32 devices in a mesh: dp: 8 (over z, x), tensor: 4 (over y, core).
Axes of the slice: x: 2, y: 2, z: 4, core: 2. Of those that a mesh axis runs over, the one named last changes fastest.
Arguments:
- inputs: bfloat16 [16384, 4096], P('tensor', 'dp'), may hold values from -6 to 6
- cotangent: bfloat16 [16384, 4096], P('tensor', 'dp'), may hold values from -6 to 6
- first_left: bfloat16 [128, 128, 128], P('tensor', 'dp'), may hold values from -0.5 to 0.5
- first_right: bfloat16 [128, 128, 128], P('tensor', 'dp'), may hold values from -0.5 to 0.5
- second_left: bfloat16 [128, 128, 128], P('tensor', 'dp'), may hold values from -0.5 to 0.5
- second_right: bfloat16 [128, 128, 128], P('tensor', 'dp'), may hold values from -0.5 to 0.5
Outputs:
- mixed: bfloat16 [16384, 4096], P('tensor', 'dp')
- input_grad: bfloat16 [16384, 4096], P('tensor', 'dp')
- first_left_grad: float32 [128, 128, 128], P('tensor', 'dp')
- first_right_grad: float32 [128, 128, 128], P('tensor', 'dp')
- second_left_grad: float32 [128, 128, 128], P('tensor', 'dp')
- second_right_grad: float32 [128, 128, 128], P('tensor', 'dp')
The draws below stay inside these ranges and needn't reach their ends.
All inputs are finite; a program needn't handle non-finite values.
Results may differ from the reference program's by a relative error of at most 0.0068.
Values may be sent and summed in bfloat16 or wider, within the bound.
No kernel may reach another device: no remote copies, remote signals or barrier semaphores. Data moves between devices by JAX's collectives and lax.ppermute only.
A program may use at most 128 MiB of HBM per device.

```python
import jax
import jax.numpy as jnp
from jax import lax

BS = 128
D = 16384
TOK_DEV = 512
TOKENS = 4096
N_DP = 8


def level_of(key, dims, pieces, low, top_value):
    loudness, own = 1.0, jax.random.fold_in(key, 6)
    for position, parts in pieces:
        heights = jnp.exp(jax.random.uniform(jax.random.fold_in(own, position), (parts,), jnp.float32, low / len(pieces), top_value / len(pieces)))
        loudness = loudness * jnp.repeat(heights, dims[position] // parts).reshape([-1 if axis == position else 1 for axis in range(len(dims))])
    return loudness


def normal_values(rng, extent, scale, limit, cuts=(), held_as=jnp.bfloat16):
    array = scale * jax.random.normal(rng, extent, jnp.float32)
    if cuts:
        array = array * level_of(rng, extent, cuts, -0.22, 0.18)
    return jnp.clip(array, -limit, limit).astype(held_as)


def setup_inputs(seed: int = 0) -> dict:
    streams_of = jax.random.split(jax.random.key(seed), 7)
    inputs = normal_values(streams_of[0], (D, TOKENS), 1.0, 6.0, ((0, 4), (1, 8)))
    cotangent = normal_values(streams_of[1], (D, TOKENS), 1.0, 6.0, ((0, 4), (1, 8)))
    first_left = normal_values(streams_of[2], (BS, BS, BS), BS ** -0.5, 0.5, ((0, 4), (1, 8)))
    first_right = normal_values(streams_of[3], (BS, BS, BS), BS ** -0.5, 0.5, ((0, 4), (1, 8)))
    second_left = normal_values(streams_of[4], (BS, BS, BS), BS ** -0.5, 0.5, ((0, 4), (1, 8)))
    second_right = normal_values(streams_of[5], (BS, BS, BS), BS ** -0.5, 0.5, ((0, 4), (1, 8)))
    return {"inputs": inputs, "cotangent": cotangent, "first_left": first_left, "first_right": first_right, "second_left": second_left, "second_right": second_right}


def gelu_value(v):
    return jax.nn.gelu(v, approximate=True)

def gelu_back(v, cot):
    return jax.vjp(gelu_value, v)[1](cot)[0]

def reference(inputs, cotangent, first_left, first_right, second_left, second_right):
    f32 = jnp.float32
    bf16 = jnp.bfloat16
    lone = first_left.astype(f32)
    rone = first_right.astype(f32)
    ltwo = second_left.astype(f32)
    rtwo = second_right.astype(f32)

    def one_block(carry, index):
        start = (index * TOK_DEV).astype(jnp.int32)
        xb = lax.dynamic_slice_in_dim(inputs, start, TOK_DEV, 1).reshape(BS, BS, TOK_DEV)
        gb = lax.dynamic_slice_in_dim(cotangent, start, TOK_DEV, 1).reshape(BS, BS, TOK_DEV)
        xf = xb.astype(f32)
        gf = gb.astype(f32)
        s1 = jnp.einsum('bjt,bjo->bot', xf, lone).astype(bf16)
        s2 = jnp.einsum('ibt,bip->bpt', s1.astype(f32), rone).astype(bf16)
        act = gelu_value(s2.astype(f32)).astype(bf16)
        s3 = jnp.einsum('jbt,bjo->bot', act.astype(f32), ltwo).astype(bf16)
        s4 = jnp.einsum('ibt,bio->bot', s3.astype(f32), rtwo).astype(bf16)
        mixed = (xf + jnp.transpose(s4.astype(f32), (1, 0, 2))).astype(bf16)
        grad_rtwo = jnp.einsum('ibt,obt->bio', s3.astype(f32), gf)
        e3 = jnp.einsum('obt,bio->bit', gf, rtwo).astype(bf16)
        e3f = e3.astype(f32)
        grad_ltwo = jnp.einsum('jbt,obt->bjo', act.astype(f32), e3f)
        back_act = jnp.einsum('obt,bjo->bjt', e3f, ltwo)
        hidden = gelu_back(jnp.transpose(s2.astype(f32), (1, 0, 2)), back_act).astype(bf16)
        hf = hidden.astype(f32)
        grad_rone = jnp.einsum('ibt,pbt->bip', s1.astype(f32), hf)
        e1 = jnp.einsum('pbt,bip->bit', hf, rone).astype(bf16)
        e1f = e1.astype(f32)
        grad_lone = jnp.einsum('bjt,obt->bjo', xf, e1f)
        input_grad = (gf + jnp.einsum('obt,bjo->bjt', e1f, lone)).astype(bf16)
        carry = (carry[0] + grad_lone, carry[1] + grad_rone, carry[2] + grad_ltwo, carry[3] + grad_rtwo)
        return (carry, (mixed.reshape(D, TOK_DEV), input_grad.reshape(D, TOK_DEV)))
    zeros = jnp.zeros((BS, BS, BS), f32)
    sums, (mixed_blocks, grad_blocks) = lax.scan(one_block, (zeros, zeros, zeros, zeros), jnp.arange(N_DP, dtype=jnp.int32))
    mixed = jnp.transpose(mixed_blocks, (1, 0, 2)).reshape(D, TOKENS)
    input_grad = jnp.transpose(grad_blocks, (1, 0, 2)).reshape(D, TOKENS)
    return (mixed, input_grad, sums[0], sums[1], sums[2], sums[3])
```

```python
import math

import jax
import jax.numpy as jnp
from jax import lax
from jax.sharding import PartitionSpec as P

BF16 = jnp.bfloat16
F32 = jnp.float32
LANES = 128


def gelu_value(values):
    return jax.nn.gelu(values, approximate=True)


def gelu_back(values, upstream):
    return jax.vjp(gelu_value, values)[1](upstream)[0]


def product(form, left, right):
    return jnp.einsum(form, left, right, preferred_element_type=F32)


class Ring:
    def __init__(self, axis, stride, size):
        self.axis, self.stride, self.size = axis, stride, size

    def here(self):
        return lax.rem(lax.axis_index(self.axis) // self.stride, self.size)

    def send(self, value, step):
        pairs = []
        for src in range(lax.axis_size(self.axis)):
            own = src // self.stride % self.size
            pairs.append((src, src + ((own + step) % self.size - own) * self.stride))
        return lax.ppermute(value, self.axis, pairs)

    def gather(self, value):
        if self.size == 1:
            return value[None]
        here = self.here()
        out = jnp.zeros((self.size,) + value.shape, value.dtype)
        out = lax.dynamic_update_index_in_dim(out, value, here, 0)
        for step in range(1, self.size):
            got = self.send(value, step)
            out = lax.dynamic_update_index_in_dim(out, got, lax.rem(here - step + self.size, self.size), 0)
        return out

    def scatter(self, value, dim):
        here = self.here()
        if self.size == 1:
            return lax.index_in_dim(value, 0, dim, keepdims=False)
        total = lax.dynamic_index_in_dim(value, here, dim, keepdims=False).astype(F32)
        for step in range(1, self.size):
            there = lax.rem(here + step, self.size)
            term = lax.dynamic_index_in_dim(value, there, dim, keepdims=False).astype(BF16)
            total = total + self.send(term, step).astype(F32)
        return total


def halves(size):
    low = 2 if size % 2 == 0 else 1
    return size // low, low


def per_device(inputs, cotangent, first_left, first_right, second_left, second_right):
    n_dp, n_tensor = lax.axis_size("dp"), lax.axis_size("tensor")
    home, rows, size = first_left.shape
    tokens = inputs.shape[1]
    share = math.gcd(n_tensor, max(1, tokens // LANES))
    groups = n_tensor // share
    held = home * share
    cut = tokens // share

    far, near = halves(share)
    ring_y, ring_core = Ring("tensor", near, far), Ring("tensor", 1, near)
    far, near = halves(n_dp)
    ring_z, ring_x = Ring("dp", near, far), Ring("dp", 1, near)

    same_tokens = [[group * share + part for group in range(groups)] for part in range(share)]

    def cross(pieces):
        return lax.all_to_all(pieces, "tensor", split_axis=0, concat_axis=0, tiled=True)

    def go(values):
        pieces = values.reshape(home, groups, held, share, cut).transpose(1, 3, 2, 0, 4)
        got = cross(pieces.reshape(n_tensor, held, home, cut))
        return got.transpose(1, 0, 2, 3).reshape(held, size, cut)

    def back(values):
        pieces = values.reshape(held, n_tensor, home, cut).transpose(1, 0, 2, 3)
        got = cross(pieces).reshape(groups, share, held, home, cut)
        return got.transpose(3, 0, 2, 1, 4).reshape(home, size, tokens)

    def turn(values):
        if groups == 1:
            return jnp.swapaxes(values, 0, 1)
        moved = lax.all_to_all(
            values.reshape(held, groups, held, cut), "tensor", split_axis=1, concat_axis=0, tiled=True, axis_index_groups=same_tokens
        )
        return jnp.swapaxes(moved.reshape(size, held, cut), 0, 1)

    def whole(factor):
        one = ring_z.gather(ring_y.gather(factor))
        all_rows = ring_core.gather(ring_x.gather(one))
        return all_rows.transpose(3, 0, 4, 2, 1, 5, 6).reshape(held, size, size)

    def own_sum(partial):
        split = partial.reshape(ring_y.size, ring_core.size, home, ring_z.size, ring_x.size, rows, size)
        split = ring_core.scatter(split, 1)
        split = ring_x.scatter(split, 3)
        split = ring_z.scatter(split, 2)
        return ring_y.scatter(split, 0)

    x_home = inputs.reshape(home, size, tokens)
    g_home = cotangent.reshape(home, size, tokens)
    g_mid = go(g_home)

    left_one = ring_x.gather(ring_z.gather(first_left)).transpose(2, 1, 0, 3, 4).reshape(home, size, size)
    right_one, left_two, right_two = whole(first_right), whole(second_left), whole(second_right)

    s_one = go(product("bjt,bjo->bot", x_home, left_one).astype(BF16))
    s_two = turn(product("bit,bip->bpt", s_one, right_one).astype(BF16))
    act = gelu_value(s_two.astype(F32)).astype(BF16)
    e_three = turn(product("bot,bio->bit", g_mid, right_two).astype(BF16))
    hidden = gelu_back(s_two.astype(F32), product("bot,bjo->bjt", e_three, left_two)).astype(BF16)
    h_mid = turn(hidden)
    e_one = back(product("bpt,bip->bit", h_mid, right_one).astype(BF16))
    s_three = turn(product("bjt,bjo->bot", act, left_two).astype(BF16))
    s_four = back(product("bit,bio->bot", s_three, right_two).astype(BF16))
    mixed = (x_home.astype(F32) + s_four.astype(F32)).astype(BF16)

    grad_rtwo = own_sum(product("bit,bot->bio", s_three, g_mid))
    grad_ltwo = own_sum(product("bjt,bot->bjo", act, e_three))
    grad_rone = own_sum(product("bit,bpt->bip", s_one, h_mid))
    grad_lone = product("bjt,bot->bjo", x_home, e_one).reshape(home, ring_z.size, ring_x.size, rows, size)
    grad_lone = ring_z.scatter(ring_x.scatter(grad_lone, 2), 1)
    input_grad = (g_home.astype(F32) + product("bot,bjo->bjt", e_one, left_one)).astype(BF16)
    return (
        mixed.reshape(home * size, tokens),
        input_grad.reshape(home * size, tokens),
        grad_lone,
        grad_rone,
        grad_ltwo,
        grad_rtwo,
    )


def solution(mesh):
    wide, factor = P("tensor", "dp"), P("tensor", "dp", None)
    return jax.shard_map(
        per_device,
        mesh=mesh,
        in_specs=(wide, wide, factor, factor, factor, factor),
        out_specs=(wide, wide, factor, factor, factor, factor),
        check_vma=False,
    )
```

```python
import functools
import math

import jax
import jax.numpy as jnp
from jax import lax
from jax.experimental import pallas as pl
from jax.experimental.pallas import tpu as pltpu
from jax.sharding import PartitionSpec as P

BF16 = jnp.bfloat16
F32 = jnp.float32
LANES = 128
PAD = 8
VMEM_BYTES = 48 * 1024 * 1024


def gelu_value(values):
    return jax.nn.gelu(values, approximate=True)


def gelu_back(values, upstream):
    return jax.vjp(gelu_value, values)[1](upstream)[0]


def gelu_both(v):
    root, cubic = 0.7978845608028654, 0.044715
    square = v * v
    t = jnp.tanh(root * (v + cubic * (v * square)))
    half = 0.5 * (1.0 + t)
    slope = half + (0.5 * v) * (1.0 - t * t) * (root + (3.0 * cubic * root) * square)
    return v * half, slope


def product(form, left, right):
    return jnp.einsum(form, left, right, preferred_element_type=F32)


def dot_nn(left, right):
    return lax.dot_general(left, right, (((1,), (0,)), ((), ())), preferred_element_type=F32)


def dot_tn(left, right):
    return lax.dot_general(left, right, (((0,), (0,)), ((), ())), preferred_element_type=F32)


def dot_nt(left, right):
    return lax.dot_general(left, right, (((1,), (1,)), ((), ())), preferred_element_type=F32)


def call(body, out, grid, in_specs, out_specs, scratch, args, scalars=None, dots=0):
    moved = sum(math.prod(a.shape) * a.dtype.itemsize for a in args)
    moved += sum(math.prod(o.shape) * o.dtype.itemsize for o in jax.tree.leaves(out))
    spec = pltpu.PrefetchScalarGridSpec(
        num_scalar_prefetch=0 if scalars is None else 1,
        grid=grid,
        in_specs=in_specs,
        out_specs=out_specs,
        scratch_shapes=scratch,
    )
    return pl.pallas_call(
        body,
        out_shape=out,
        grid_spec=spec,
        compiler_params=pltpu.CompilerParams(
            dimension_semantics=("arbitrary",) * len(grid), vmem_limit_bytes=VMEM_BYTES
        ),
        cost_estimate=pl.CostEstimate(flops=dots, bytes_accessed=moved, transcendentals=0),
    )(*(() if scalars is None else (scalars,)), *args)


def shape(dims, dtype=BF16):
    return jax.ShapeDtypeStruct(dims, dtype)


def each(count, body, unroll=4):
    def step(k, carry):
        body(k)
        return carry

    lax.fori_loop(0, count, step, 0, unroll=math.gcd(count, unroll))


def during(phase, steps):
    return lambda p, j: jnp.where(p == phase, j, jnp.where(p < phase, 0, steps - 1))


def stacked(ref, k):
    return jnp.concatenate([ref[c, k] for c in range(ref.shape[0])], axis=0)


def deal_kernel(g_ref, out_ref, turned):
    home, size, _ = g_ref.shape
    pitch = home + PAD

    def store(o):
        turned[pl.ds(o, size, stride=pitch), :] = g_ref[o].astype(F32)

    def load(b):
        out_ref[0, b] = turned[pl.ds(pl.multiple_of(b * pitch, 8), home), :].astype(BF16)

    each(home, store)
    each(size, load, 8)


def deal(g_home, share, cut):
    home, size, _ = g_home.shape
    return call(
        deal_kernel,
        shape((share, size, home, cut)),
        (share,),
        [pl.BlockSpec((home, size, cut), lambda s: (0, 0, s))],
        pl.BlockSpec((1, size, home, cut), lambda s: (s, 0, 0, 0)),
        [pltpu.VMEM((size * (home + PAD), cut), F32)],
        (g_home,),
    )


def first_kernel(x_ref, w_ref, out_ref, turned):
    home, size, _ = x_ref.shape
    pitch = home + PAD

    def store(b):
        turned[pl.ds(b, size, stride=pitch), :] = dot_tn(w_ref[b], x_ref[b])

    def load(o):
        out_ref[0, o] = turned[pl.ds(pl.multiple_of(o * pitch, 8), home), :].astype(BF16)

    each(home, store)
    each(size, load, 8)


def first_stage(x_home, left_one, share, cut):
    home, size, _ = x_home.shape
    return call(
        first_kernel,
        shape((share, size, home, cut)),
        (share,),
        [
            pl.BlockSpec((home, size, cut), lambda s: (0, 0, s)),
            pl.BlockSpec((home, size, size), lambda s: (0, 0, 0)),
        ],
        pl.BlockSpec((1, size, home, cut), lambda s: (s, 0, 0, 0)),
        [pltpu.VMEM((size * (home + PAD), cut), F32)],
        (x_home, left_one),
        dots=2 * home * size * size * share * cut,
    )


def last_kernel(e_ref, x_ref, g_ref, w_ref, out_ref, grad_ref, turned):
    _, blocks, home, _ = e_ref.shape
    pitch = blocks + PAD
    first = pl.program_id(0) == 0

    def store(o):
        turned[pl.ds(o, home, stride=pitch), :] = e_ref[0, o].astype(F32)

    def load(b):
        e_b = turned[pl.ds(pl.multiple_of(b * pitch, 8), blocks), :].astype(BF16)
        out_ref[b] = (g_ref[b].astype(F32) + dot_nn(w_ref[b], e_b)).astype(BF16)
        before = jnp.where(first, 0.0, grad_ref[b])
        grad_ref[b] = before + dot_nt(x_ref[b], e_b)

    each(blocks, store, 8)
    each(home, load)


def last_stage(e_got, x_home, g_home, left_one):
    share, blocks, home, cut = e_got.shape
    size = x_home.shape[1]
    wide = pl.BlockSpec((home, size, cut), lambda s: (0, 0, s))
    fixed = pl.BlockSpec((home, size, size), lambda s: (0, 0, 0))
    return call(
        last_kernel,
        (shape(g_home.shape), shape((home, size, size), F32)),
        (share,),
        [pl.BlockSpec((1, blocks, home, cut), lambda s: (s, 0, 0, 0)), wide, wide, fixed],
        (wide, fixed),
        [pltpu.VMEM((home * (blocks + PAD), cut), F32)],
        (e_got, x_home, g_home, left_one),
        dots=4 * home * size * size * share * cut,
    )


def mixed_kernel(s_ref, x_ref, out_ref):
    out_ref[...] = (x_ref[...].astype(F32) + s_ref[0].astype(F32)).astype(BF16)


def add_home(s_got, x_home):
    share, home, blocks, cut = s_got.shape
    per = math.gcd(home, 16)
    wide = pl.BlockSpec((per, blocks, cut), lambda s, h: (h, 0, s))
    return call(
        mixed_kernel,
        shape(x_home.shape),
        (share, home // per),
        [pl.BlockSpec((1, per, blocks, cut), lambda s, h: (s, h, 0, 0)), wide],
        wide,
        [],
        (s_got, x_home),
    )


def back_two_kernel(g_ref, w_ref, out_ref, turned):
    per, size, _ = out_ref.shape
    pitch = size + PAD
    phase, j = pl.program_id(0), pl.program_id(1)

    @pl.when(phase == 0)
    def _():
        def body(k):
            turned[pl.ds(j * per + k, size, stride=pitch), :] = dot_nn(w_ref[k], stacked(g_ref, k))

        each(per, body)

    @pl.when(phase == 1)
    def _():
        def body(k):
            out_ref[k] = turned[pl.ds(pl.multiple_of((j * per + k) * pitch, 8), size), :].astype(BF16)

        each(per, body, 8)


def middle_sizes(weights):
    blocks, size, _ = weights.shape
    per = math.gcd(blocks, 32)
    return blocks, size, per, blocks // per


def back_two(g_mid, right_two):
    blocks, size, per, steps = middle_sizes(right_two)
    n, _, home, cut = g_mid.shape
    at = [during(phase, steps) for phase in range(2)]
    return call(
        back_two_kernel,
        shape((blocks, size, cut)),
        (2, steps),
        [
            pl.BlockSpec((n, per, home, cut), lambda p, j: (0, at[0](p, j), 0, 0)),
            pl.BlockSpec((per, size, size), lambda p, j: (at[0](p, j), 0, 0)),
        ],
        pl.BlockSpec((per, size, cut), lambda p, j: (at[1](p, j), 0, 0)),
        [pltpu.VMEM((blocks * (size + PAD), cut), F32)],
        (g_mid, right_two),
        dots=2 * blocks * size * size * cut,
    )


def middle_kernel(s_ref, one_ref, two_ref, e_ref, act_ref, h_ref, out_ref, turned, hidden):
    per, size, _ = act_ref.shape
    pitch = size + PAD
    n, _, home, _ = s_ref.shape
    phase, j = pl.program_id(0), pl.program_id(1)

    def rows(k):
        return pl.ds(pl.multiple_of((j * per + k) * pitch, 8), size)

    def column(k):
        return pl.ds(j * per + k, size, stride=pitch)

    @pl.when(phase == 0)
    def _():
        def body(k):
            turned[column(k), :] = dot_tn(one_ref[k], stacked(s_ref, k))

        each(per, body)

    @pl.when(phase == 1)
    def _():
        def body(k):
            v = turned[rows(k), :].astype(BF16).astype(F32)
            value, slope = gelu_both(v)
            act_ref[k] = value.astype(BF16)
            hidden[column(k), :] = slope * dot_nn(two_ref[k], e_ref[k])

        each(per, body)

    @pl.when(phase == 2)
    def _():
        def body(k):
            h = hidden[rows(k), :].astype(BF16)
            h_ref[k] = h
            e = dot_nn(one_ref[k], h).astype(BF16)
            for c in range(n):
                out_ref[c, k] = e[c * home : (c + 1) * home]

        each(per, body)


def middle(s_mid, e_mid, right_one, left_two):
    blocks, size, per, steps = middle_sizes(right_one)
    n, _, home, cut = s_mid.shape
    at = [during(phase, steps) for phase in range(3)]
    block = (per, size, cut)
    pieces = (n, per, home, cut)

    def one(p, j):
        return (jnp.where(p == 1, 0, j), 0, 0)

    return call(
        middle_kernel,
        (shape((blocks, size, cut)), shape((blocks, size, cut)), shape(s_mid.shape)),
        (3, steps),
        [
            pl.BlockSpec(pieces, lambda p, j: (0, at[0](p, j), 0, 0)),
            pl.BlockSpec((per, size, size), one),
            pl.BlockSpec((per, size, size), lambda p, j: (at[1](p, j), 0, 0)),
            pl.BlockSpec(block, lambda p, j: (at[1](p, j), 0, 0)),
        ],
        (
            pl.BlockSpec(block, lambda p, j: (at[1](p, j), 0, 0)),
            pl.BlockSpec(block, lambda p, j: (at[2](p, j), 0, 0)),
            pl.BlockSpec(pieces, lambda p, j: (0, at[2](p, j), 0, 0)),
        ),
        [pltpu.VMEM((blocks * (size + PAD), cut), F32)] * 2,
        (s_mid, right_one, left_two, e_mid),
        dots=6 * blocks * size * size * cut,
    )


def forward_two_kernel(act_ref, left_ref, right_ref, third_ref, out_ref, turned, fourth):
    per, size, _ = third_ref.shape
    pitch = size + PAD
    phase, j = pl.program_id(0), pl.program_id(1)

    def rows(k):
        return pl.ds(pl.multiple_of((j * per + k) * pitch, 8), size)

    def column(k):
        return pl.ds(j * per + k, size, stride=pitch)

    @pl.when(phase == 0)
    def _():
        def body(k):
            turned[column(k), :] = dot_tn(left_ref[k], act_ref[k])

        each(per, body)

    @pl.when(phase == 1)
    def _():
        def body(k):
            third = turned[rows(k), :].astype(BF16)
            third_ref[k] = third
            fourth[column(k), :] = dot_tn(right_ref[k], third)

        each(per, body)

    @pl.when(phase == 2)
    def _():
        def body(k):
            out_ref[k] = fourth[rows(k), :].astype(BF16)

        each(per, body, 8)


def forward_two(act, left_two, right_two):
    blocks, size, per, steps = middle_sizes(left_two)
    cut = act.shape[2]
    at = [during(phase, steps) for phase in range(3)]
    block = (per, size, cut)
    return call(
        forward_two_kernel,
        (shape(act.shape), shape(act.shape)),
        (3, steps),
        [
            pl.BlockSpec(block, lambda p, j: (at[0](p, j), 0, 0)),
            pl.BlockSpec((per, size, size), lambda p, j: (at[0](p, j), 0, 0)),
            pl.BlockSpec((per, size, size), lambda p, j: (at[1](p, j), 0, 0)),
        ],
        (
            pl.BlockSpec(block, lambda p, j: (at[1](p, j), 0, 0)),
            pl.BlockSpec(block, lambda p, j: (at[2](p, j), 0, 0)),
        ),
        [pltpu.VMEM((blocks * (size + PAD), cut), F32)] * 2,
        (act, left_two, right_two),
        dots=4 * blocks * size * size * cut,
    )


def grads_kernel(near, split, pos_ref, *refs):
    pairs = len(split)
    keep_ref, send_ref = refs[2 * pairs :]
    rc = pl.program_id(0)
    per = keep_ref.shape[2]

    def fill(out_ref):
        def body(k):
            for n in range(pairs):
                sides = [stacked(refs[2 * n + m], k) if split[n][m] else refs[2 * n + m][k] for m in range(2)]
                out_ref[n, 0, k] = dot_nt(*sides).astype(out_ref.dtype)

        each(per, body)

    @pl.when(rc == 0)
    def _():
        fill(keep_ref)

    if near > 1:

        @pl.when(rc > 0)
        def _():
            fill(send_ref)


def grads(pairs, home, size, far, near, pos):
    per = math.gcd(home, 16)
    subs = home // per
    split = tuple(tuple(a.ndim == 4 for a in pair) for pair in pairs)

    def block(rc, y, s, pos):
        return (y * near + lax.rem(pos[1] + rc, near)) * subs + s

    specs, args = [], []
    for pair in pairs:
        for a in pair:
            args.append(a)
            if a.ndim == 4:
                specs.append(pl.BlockSpec((a.shape[0], per) + a.shape[2:], lambda rc, y, s, pos: (0, block(rc, y, s, pos), 0, 0)))
            else:
                specs.append(pl.BlockSpec((per,) + a.shape[1:], lambda rc, y, s, pos: (block(rc, y, s, pos), 0, 0)))
    n = len(pairs)
    dims = (n, far, home, size, size)

    def kept(rc, y, s, pos):
        return (0, jnp.where(rc == 0, y, far - 1), jnp.where(rc == 0, s, subs - 1), 0, 0)

    def sent(rc, y, s, pos):
        return (0, jnp.where(rc == 0, 0, y), jnp.where(rc == 0, 0, s), 0, 0)

    cut = args[0].shape[-1]
    return call(
        functools.partial(grads_kernel, near, split),
        (shape(dims, F32), shape(dims)),
        (near, far, subs),
        specs,
        (pl.BlockSpec((n, 1, per, size, size), kept), pl.BlockSpec((n, 1, per, size, size), sent)),
        [],
        tuple(args),
        scalars=pos,
        dots=2 * n * far * near * home * size * size * cut,
    )


def join_kernel(near, n_x, pos_ref, *refs):
    out_ref = refs[-1]
    rc = pl.program_id(0)
    n_z, _, _, rows, _ = refs[0].shape

    for c in range(near):

        @pl.when(rc == c)
        def _():
            for rx in range(n_x):
                for rz in range(n_z):
                    z = lax.rem(pos_ref[2] - rz + n_z, n_z)
                    x = lax.rem(pos_ref[3] - rx + n_x, n_x)
                    at = pl.multiple_of((z * n_x + x) * rows, rows)
                    out_ref[:, pl.ds(at, rows), :] = refs[c * n_x + rx][rz, 0]


def join(pieces, pos):
    near, n_x = len(pieces), len(pieces[0])
    n_z, far, home, rows, size = pieces[0][0].shape
    per = math.gcd(home, 16)
    subs = home // per
    specs = []
    for c in range(near):
        for _ in range(n_x):

            def index(rc, ry, s, pos, c=c):
                y = jnp.where(rc == c, ry, jnp.where(rc < c, 0, far - 1))
                return (0, y, jnp.where(rc == c, s, jnp.where(rc < c, 0, subs - 1)), 0, 0)

            specs.append(pl.BlockSpec((n_z, 1, per, rows, size), index))

    def out_index(rc, ry, s, pos):
        y = lax.rem(pos[0] - ry + far, far)
        core = lax.rem(pos[1] - rc + near, near)
        return ((y * near + core) * subs + s, 0, 0)

    full = n_z * n_x * rows
    return call(
        functools.partial(join_kernel, near, n_x),
        shape((near * far * home, full, size)),
        (near, far, subs),
        specs,
        pl.BlockSpec((per, full, size), out_index),
        [],
        tuple(p for row in pieces for p in row),
        scalars=pos,
    )


class Ring:
    def __init__(self, axis, stride, size):
        self.axis, self.stride, self.size = axis, stride, size

    def here(self):
        return lax.rem(lax.axis_index(self.axis) // self.stride, self.size)

    def send(self, value, step):
        pairs = []
        for src in range(lax.axis_size(self.axis)):
            own = src // self.stride % self.size
            pairs.append((src, src + ((own + step) % self.size - own) * self.stride))
        return lax.ppermute(value, self.axis, pairs)

    def sends(self, value):
        return [self.send(value, step) for step in range(1, self.size)]

    def gather(self, value):
        if self.size == 1:
            return value[None]
        here = self.here()
        out = jnp.zeros((self.size,) + value.shape, value.dtype)
        out = lax.dynamic_update_index_in_dim(out, value, here, 0)
        for step in range(1, self.size):
            got = self.send(value, step)
            out = lax.dynamic_update_index_in_dim(out, got, lax.rem(here - step + self.size, self.size), 0)
        return out

    def scatter(self, value, dim):
        here = self.here()
        if self.size == 1:
            return lax.index_in_dim(value, 0, dim, keepdims=False)
        total = lax.dynamic_index_in_dim(value, here, dim, keepdims=False).astype(F32)
        for step in range(1, self.size):
            there = lax.rem(here + step, self.size)
            term = lax.dynamic_index_in_dim(value, there, dim, keepdims=False).astype(BF16)
            total = total + self.send(term, step).astype(F32)
        return total


def halves(size):
    low = 2 if size % 2 == 0 else 1
    return size // low, low


def cross(pieces):
    return lax.all_to_all(pieces, "tensor", split_axis=0, concat_axis=0, tiled=True)


def after(value, *others):
    return lax.optimization_barrier((value,) + others)[0]


def whole_tokens(x_home, g_home, factors, rings, share, cut):
    home, size, tokens = x_home.shape
    ring_y, ring_core, ring_z, ring_x = rings
    first_left = factors[0]
    rows = first_left.shape[1]
    pos = jnp.stack([ring.here() for ring in rings]).astype(jnp.int32)

    mine = jnp.stack([factors[3], factors[1], factors[2]])
    from_y = [mine] + ring_y.sends(mine)
    one = [first_left] + ring_z.sends(first_left)
    one = jnp.stack(one)
    zero = jnp.zeros_like(pos[:1])
    one = join([[p[:, None] for p in [one] + ring_x.sends(one)]], jnp.concatenate([zero, zero, pos[2:]]))

    g_mid = cross(deal(g_home, share, cut))

    wholes, before = [], None
    for n in range(3):
        start = jnp.stack([part[n] for part in from_y])
        if before is not None:
            start = after(start, before)
        from_z = jnp.stack([start] + ring_z.sends(start))
        before = from_z
        from_x = [from_z] + ring_x.sends(from_z)
        from_core = [[p] + ring_core.sends(p) for p in from_x]
        wholes.append(join([[p[c] for p in from_core] for c in range(ring_core.size)], pos))
    right_two, right_one, left_two = wholes

    s_mid = cross(first_stage(x_home, one, share, cut))
    e_mid = back_two(g_mid, right_two)
    act, hidden, e_out = middle(s_mid, e_mid, right_one, left_two)
    e_got = cross(e_out)
    third, s_out = forward_two(act, left_two, right_two)
    s_out = s_out.reshape(share, home, size, cut)
    s_got = cross(after(s_out, e_got))

    def own_sum(pairs):
        keep, send = grads(pairs, home, size, ring_y.size, ring_core.size, pos)
        total = keep
        if ring_core.size > 1:
            total = total + ring_core.send(send, 1).astype(F32)
        split = total.reshape(len(pairs), ring_y.size, home, ring_z.size, ring_x.size, rows, size)
        split = ring_x.scatter(split, 4)
        split = ring_z.scatter(split, 3)
        return ring_y.scatter(split, 1)

    grad_ltwo, grad_rone = own_sum([(act, e_mid), (s_mid, hidden)])
    grad_rtwo = own_sum([(third, g_mid)])[0]

    input_grad, grad_lone = last_stage(e_got, x_home, g_home, one)
    grad_lone = grad_lone.reshape(home, ring_z.size, ring_x.size, rows, size)
    grad_lone = ring_z.scatter(ring_x.scatter(grad_lone, 2), 1)
    mixed = add_home(s_got, x_home)
    return mixed, input_grad, grad_lone, grad_rone, grad_ltwo, grad_rtwo


def split_blocks(x_home, g_home, factors, rings, share, cut):
    home, size, tokens = x_home.shape
    ring_y, ring_core, ring_z, ring_x = rings
    rows = factors[0].shape[1]
    n_tensor = lax.axis_size("tensor")
    groups = n_tensor // share
    held = home * share
    same_tokens = [[group * share + part for group in range(groups)] for part in range(share)]

    def go(values):
        pieces = values.reshape(home, groups, held, share, cut).transpose(1, 3, 2, 0, 4)
        got = cross(pieces.reshape(n_tensor, held, home, cut))
        return got.transpose(1, 0, 2, 3).reshape(held, size, cut)

    def back(values):
        pieces = values.reshape(held, n_tensor, home, cut).transpose(1, 0, 2, 3)
        got = cross(pieces).reshape(groups, share, held, home, cut)
        return got.transpose(3, 0, 2, 1, 4).reshape(home, size, tokens)

    def turn(values):
        moved = lax.all_to_all(
            values.reshape(held, groups, held, cut), "tensor", split_axis=1, concat_axis=0, tiled=True, axis_index_groups=same_tokens
        )
        return jnp.swapaxes(moved.reshape(size, held, cut), 0, 1)

    def whole(factor):
        one = ring_z.gather(ring_y.gather(factor))
        all_rows = ring_core.gather(ring_x.gather(one))
        return all_rows.transpose(3, 0, 4, 2, 1, 5, 6).reshape(held, size, size)

    def own_sum(partial):
        split = partial.reshape(ring_y.size, ring_core.size, home, ring_z.size, ring_x.size, rows, size)
        split = ring_core.scatter(split, 1)
        split = ring_x.scatter(split, 3)
        split = ring_z.scatter(split, 2)
        return ring_y.scatter(split, 0)

    first_left, first_right, second_left, second_right = factors
    g_mid = go(g_home)
    left_one = ring_x.gather(ring_z.gather(first_left)).transpose(2, 1, 0, 3, 4).reshape(home, size, size)
    right_one, left_two, right_two = whole(first_right), whole(second_left), whole(second_right)

    s_one = go(product("bjt,bjo->bot", x_home, left_one).astype(BF16))
    s_two = turn(product("bit,bip->bpt", s_one, right_one).astype(BF16))
    act = gelu_value(s_two.astype(F32)).astype(BF16)
    e_three = turn(product("bot,bio->bit", g_mid, right_two).astype(BF16))
    h_mid = turn(gelu_back(s_two.astype(F32), product("bot,bjo->bjt", e_three, left_two)).astype(BF16))
    e_one = back(product("bpt,bip->bit", h_mid, right_one).astype(BF16))
    s_three = turn(product("bjt,bjo->bot", act, left_two).astype(BF16))
    s_four = back(product("bit,bio->bot", s_three, right_two).astype(BF16))
    mixed = (x_home.astype(F32) + s_four.astype(F32)).astype(BF16)

    grad_rtwo = own_sum(product("bit,bot->bio", s_three, g_mid))
    grad_ltwo = own_sum(product("bjt,bot->bjo", act, e_three))
    grad_rone = own_sum(product("bit,bpt->bip", s_one, h_mid))
    grad_lone = product("bjt,bot->bjo", x_home, e_one).reshape(home, ring_z.size, ring_x.size, rows, size)
    grad_lone = ring_z.scatter(ring_x.scatter(grad_lone, 2), 1)
    input_grad = (g_home.astype(F32) + product("bot,bjo->bjt", e_one, left_one)).astype(BF16)
    return mixed, input_grad, grad_lone, grad_rone, grad_ltwo, grad_rtwo


def per_device(inputs, cotangent, first_left, first_right, second_left, second_right):
    n_dp, n_tensor = lax.axis_size("dp"), lax.axis_size("tensor")
    home, _, size = first_left.shape
    tokens = inputs.shape[1]
    share = math.gcd(n_tensor, max(1, tokens // LANES))
    cut = tokens // share
    far, near = halves(share)
    outer, inner = halves(n_dp)
    rings = (Ring("tensor", near, far), Ring("tensor", 1, near), Ring("dp", inner, outer), Ring("dp", 1, inner))
    plan = whole_tokens if share == n_tensor else split_blocks
    mixed, input_grad, *weight_grads = plan(
        inputs.reshape(home, size, tokens),
        cotangent.reshape(home, size, tokens),
        (first_left, first_right, second_left, second_right),
        rings,
        share,
        cut,
    )
    return (mixed.reshape(inputs.shape), input_grad.reshape(inputs.shape), *weight_grads)


def solution(mesh):
    wide, factor = P("tensor", "dp"), P("tensor", "dp", None)
    return jax.shard_map(
        per_device,
        mesh=mesh,
        in_specs=(wide, wide, factor, factor, factor, factor),
        out_specs=(wide, wide, factor, factor, factor, factor),
        check_vma=False,
    )
```

```python
import functools
import math

import jax
import jax.numpy as jnp
from jax import lax
from jax.experimental import pallas as pl
from jax.experimental.pallas import tpu as pltpu
from jax.sharding import PartitionSpec as P

BF16 = jnp.bfloat16
F32 = jnp.float32
LANES = 128
PAD = 8
VMEM_BYTES = 60 * 1024 * 1024


def gelu_value(values):
    return jax.nn.gelu(values, approximate=True)


def gelu_back(values, upstream):
    return jax.vjp(gelu_value, values)[1](upstream)[0]


def gelu_both(v):
    root, cubic = 0.7978845608028654, 0.044715
    square = v * v
    t = jnp.tanh(root * (v + cubic * (v * square)))
    half = 0.5 * (1.0 + t)
    slope = half + (0.5 * v) * (1.0 - t * t) * (root + (3.0 * cubic * root) * square)
    return v * half, slope


def product(form, left, right):
    return jnp.einsum(form, left, right, preferred_element_type=F32)


def dot_nn(left, right):
    return lax.dot_general(left, right, (((1,), (0,)), ((), ())), preferred_element_type=F32)


def dot_tn(left, right):
    return lax.dot_general(left, right, (((0,), (0,)), ((), ())), preferred_element_type=F32)


def dot_nt(left, right):
    return lax.dot_general(left, right, (((1,), (1,)), ((), ())), preferred_element_type=F32)


def call(body, out, grid, in_specs, out_specs, scratch, args, scalars=None):
    spec = pltpu.PrefetchScalarGridSpec(
        num_scalar_prefetch=0 if scalars is None else 1,
        grid=grid,
        in_specs=in_specs,
        out_specs=out_specs,
        scratch_shapes=scratch,
    )
    return pl.pallas_call(
        body,
        out_shape=out,
        grid_spec=spec,
        compiler_params=pltpu.CompilerParams(
            dimension_semantics=("arbitrary",) * len(grid), vmem_limit_bytes=VMEM_BYTES
        ),
        cost_estimate=pl.CostEstimate(flops=0, bytes_accessed=1024, transcendentals=0),
    )(*(() if scalars is None else (scalars,)), *args)


def shape(dims, dtype=BF16):
    return jax.ShapeDtypeStruct(dims, dtype)


def each(count, body, unroll=16):
    def step(k, carry):
        body(k)
        return carry

    lax.fori_loop(0, count, step, 0, unroll=math.gcd(count, unroll))


def during(phase, steps):
    return lambda p, j: jnp.where(p == phase, j, jnp.where(p < phase, 0, steps - 1))


def stacked(ref, k):
    return jnp.concatenate([ref[c, k] for c in range(ref.shape[0])], axis=0)


def deal_kernel(g_ref, out_ref, turned):
    home, size, _ = g_ref.shape
    cut = out_ref.shape[3]
    pitch = home + PAD
    lanes = pl.ds(pl.multiple_of(pl.program_id(0) * cut, cut), cut)

    def store(o):
        turned[pl.ds(o, size, stride=pitch), :] = g_ref[o, :, lanes].astype(F32)

    def load(b):
        out_ref[0, b] = turned[pl.ds(pl.multiple_of(b * pitch, 8), home), :].astype(BF16)

    each(home, store)
    each(size, load)


def deal(g_home, share, cut):
    home, size, tokens = g_home.shape
    return call(
        deal_kernel,
        shape((share, size, home, cut)),
        (share,),
        [pl.BlockSpec((home, size, tokens), lambda s: (0, 0, 0))],
        pl.BlockSpec((1, size, home, cut), lambda s: (s, 0, 0, 0)),
        [pltpu.VMEM((size * (home + PAD), cut), F32)],
        (g_home,),
    )


def first_kernel(x_ref, w_ref, out_ref, turned):
    home, size, _ = x_ref.shape
    cut = out_ref.shape[3]
    pitch = home + PAD
    lanes = pl.ds(pl.multiple_of(pl.program_id(0) * cut, cut), cut)

    def store(b):
        turned[pl.ds(b, size, stride=pitch), :] = dot_tn(w_ref[b], x_ref[b, :, lanes])

    def load(o):
        out_ref[0, o] = turned[pl.ds(pl.multiple_of(o * pitch, 8), home), :].astype(BF16)

    each(home, store)
    each(size, load)


def first_stage(x_home, left_one, share, cut):
    home, size, tokens = x_home.shape
    return call(
        first_kernel,
        shape((share, size, home, cut)),
        (share,),
        [
            pl.BlockSpec((home, size, tokens), lambda s: (0, 0, 0)),
            pl.BlockSpec((home, size, size), lambda s: (0, 0, 0)),
        ],
        pl.BlockSpec((1, size, home, cut), lambda s: (s, 0, 0, 0)),
        [pltpu.VMEM((size * (home + PAD), cut), F32)],
        (x_home, left_one),
    )


def last_kernel(e_ref, x_ref, g_ref, w_ref, out_ref, grad_ref, turned):
    share, blocks, per, cut = e_ref.shape
    pitch = blocks + PAD

    for s in range(share):

        def store(o):
            turned[s, pl.ds(o, per, stride=pitch), :] = e_ref[s, o].astype(F32)

        each(blocks, store)

    def load(b):
        rows = pl.ds(pl.multiple_of(b * pitch, 8), blocks)
        e_b = jnp.concatenate([turned[s, rows, :].astype(BF16) for s in range(share)], axis=1)
        out_ref[b] = (g_ref[b].astype(F32) + dot_nn(w_ref[b], e_b)).astype(BF16)
        grad_ref[b] = dot_nt(x_ref[b], e_b).astype(BF16)

    each(per, load, 4)


def last_stage(e_got, x_home, g_home, left_one):
    share, blocks, home, cut = e_got.shape
    _, size, tokens = x_home.shape
    per = math.gcd(home, 16)
    wide = pl.BlockSpec((per, size, tokens), lambda h: (h, 0, 0))
    factor = pl.BlockSpec((per, size, size), lambda h: (h, 0, 0))
    return call(
        last_kernel,
        (shape(g_home.shape), shape((home, size, size))),
        (home // per,),
        [pl.BlockSpec((share, blocks, per, cut), lambda h: (0, 0, h, 0)), wide, wide, factor],
        (wide, factor),
        [pltpu.VMEM((share, per * (blocks + PAD), cut), F32)],
        (e_got, x_home, g_home, left_one),
    )


def mixed_kernel(s_ref, x_ref, out_ref):
    cut = s_ref.shape[3]
    for s in range(s_ref.shape[0]):
        lanes = slice(s * cut, (s + 1) * cut)
        out_ref[:, :, lanes] = (x_ref[:, :, lanes].astype(F32) + s_ref[s].astype(F32)).astype(BF16)


def add_home(s_got, x_home):
    share, home, blocks, cut = s_got.shape
    per = math.gcd(home, 8)
    wide = pl.BlockSpec((per,) + x_home.shape[1:], lambda h: (h, 0, 0))
    return call(
        mixed_kernel,
        shape(x_home.shape),
        (home // per,),
        [pl.BlockSpec((share, per, blocks, cut), lambda h: (0, h, 0, 0)), wide],
        wide,
        [],
        (s_got, x_home),
    )


def back_two_kernel(g_ref, w_ref, out_ref, turned):
    per, size, _ = out_ref.shape
    pitch = size + PAD
    phase, j = pl.program_id(0), pl.program_id(1)

    @pl.when(phase == 0)
    def _():
        def body(k):
            turned[pl.ds(j * per + k, size, stride=pitch), :] = dot_nn(w_ref[k], stacked(g_ref, k))

        each(per, body)

    @pl.when(phase == 1)
    def _():
        def body(k):
            out_ref[k] = turned[pl.ds(pl.multiple_of((j * per + k) * pitch, 8), size), :].astype(BF16)

        each(per, body)


def middle_sizes(weights):
    blocks, size, _ = weights.shape
    per = math.gcd(blocks, 32)
    return blocks, size, per, blocks // per


def back_two(g_mid, right_two):
    blocks, size, per, steps = middle_sizes(right_two)
    n, _, home, cut = g_mid.shape
    at = [during(phase, steps) for phase in range(2)]
    return call(
        back_two_kernel,
        shape((blocks, size, cut)),
        (2, steps),
        [
            pl.BlockSpec((n, per, home, cut), lambda p, j: (0, at[0](p, j), 0, 0)),
            pl.BlockSpec((per, size, size), lambda p, j: (at[0](p, j), 0, 0)),
        ],
        pl.BlockSpec((per, size, cut), lambda p, j: (at[1](p, j), 0, 0)),
        [pltpu.VMEM((blocks * (size + PAD), cut), F32)],
        (g_mid, right_two),
    )


def middle_kernel(s_ref, one_ref, two_ref, e_ref, act_ref, h_ref, out_ref, turned, hidden):
    per, size, _ = act_ref.shape
    pitch = size + PAD
    n, _, home, _ = s_ref.shape
    phase, j = pl.program_id(0), pl.program_id(1)

    def rows(k):
        return pl.ds(pl.multiple_of((j * per + k) * pitch, 8), size)

    def column(k):
        return pl.ds(j * per + k, size, stride=pitch)

    @pl.when(phase == 0)
    def _():
        def body(k):
            turned[column(k), :] = dot_tn(one_ref[k], stacked(s_ref, k))

        each(per, body)

    @pl.when(phase == 1)
    def _():
        def body(k):
            v = turned[rows(k), :].astype(BF16).astype(F32)
            value, slope = gelu_both(v)
            act_ref[k] = value.astype(BF16)
            hidden[column(k), :] = slope * dot_nn(two_ref[k], e_ref[k])

        each(per, body)

    @pl.when(phase == 2)
    def _():
        def body(k):
            h = hidden[rows(k), :].astype(BF16)
            h_ref[k] = h
            e = dot_nn(one_ref[k], h).astype(BF16)
            for c in range(n):
                out_ref[c, k] = e[c * home : (c + 1) * home]

        each(per, body)


def middle(s_mid, e_mid, right_one, left_two):
    blocks, size, per, steps = middle_sizes(right_one)
    n, _, home, cut = s_mid.shape
    at = [during(phase, steps) for phase in range(3)]
    block = (per, size, cut)
    pieces = (n, per, home, cut)

    def one(p, j):
        return (jnp.where(p == 1, 0, j), 0, 0)

    return call(
        middle_kernel,
        (shape((blocks, size, cut)), shape((blocks, size, cut)), shape(s_mid.shape)),
        (3, steps),
        [
            pl.BlockSpec(pieces, lambda p, j: (0, at[0](p, j), 0, 0)),
            pl.BlockSpec((per, size, size), one),
            pl.BlockSpec((per, size, size), lambda p, j: (at[1](p, j), 0, 0)),
            pl.BlockSpec(block, lambda p, j: (at[1](p, j), 0, 0)),
        ],
        (
            pl.BlockSpec(block, lambda p, j: (at[1](p, j), 0, 0)),
            pl.BlockSpec(block, lambda p, j: (at[2](p, j), 0, 0)),
            pl.BlockSpec(pieces, lambda p, j: (0, at[2](p, j), 0, 0)),
        ),
        [pltpu.VMEM((blocks * (size + PAD), cut), F32)] * 2,
        (s_mid, right_one, left_two, e_mid),
    )


def forward_two_kernel(act_ref, left_ref, right_ref, third_ref, out_ref, turned, fourth):
    per, size, _ = third_ref.shape
    pitch = size + PAD
    phase, j = pl.program_id(0), pl.program_id(1)

    def rows(k):
        return pl.ds(pl.multiple_of((j * per + k) * pitch, 8), size)

    def column(k):
        return pl.ds(j * per + k, size, stride=pitch)

    @pl.when(phase == 0)
    def _():
        def body(k):
            turned[column(k), :] = dot_tn(left_ref[k], act_ref[k])

        each(per, body)

    @pl.when(phase == 1)
    def _():
        def body(k):
            third = turned[rows(k), :].astype(BF16)
            third_ref[k] = third
            fourth[column(k), :] = dot_tn(right_ref[k], third)

        each(per, body)

    @pl.when(phase == 2)
    def _():
        def body(k):
            out_ref[k] = fourth[rows(k), :].astype(BF16)

        each(per, body)


def forward_two(act, left_two, right_two):
    blocks, size, per, steps = middle_sizes(left_two)
    cut = act.shape[2]
    at = [during(phase, steps) for phase in range(3)]
    block = (per, size, cut)
    return call(
        forward_two_kernel,
        (shape(act.shape), shape(act.shape)),
        (3, steps),
        [
            pl.BlockSpec(block, lambda p, j: (at[0](p, j), 0, 0)),
            pl.BlockSpec((per, size, size), lambda p, j: (at[0](p, j), 0, 0)),
            pl.BlockSpec((per, size, size), lambda p, j: (at[1](p, j), 0, 0)),
        ],
        (
            pl.BlockSpec(block, lambda p, j: (at[1](p, j), 0, 0)),
            pl.BlockSpec(block, lambda p, j: (at[2](p, j), 0, 0)),
        ),
        [pltpu.VMEM((blocks * (size + PAD), cut), F32)] * 2,
        (act, left_two, right_two),
    )


def grads_kernel(near, split, pos_ref, *refs):
    pairs = len(split)
    keep_ref, send_ref = refs[2 * pairs :]
    rc = pl.program_id(0)
    per = keep_ref.shape[2]

    def fill(out_ref):
        def body(k):
            for n in range(pairs):
                sides = [stacked(refs[2 * n + m], k) if split[n][m] else refs[2 * n + m][k] for m in range(2)]
                out_ref[n, 0, k] = dot_nt(*sides).astype(out_ref.dtype)

        each(per, body)

    @pl.when(rc == 0)
    def _():
        fill(keep_ref)

    if near > 1:

        @pl.when(rc > 0)
        def _():
            fill(send_ref)


def grads(pairs, home, size, far, near, pos):
    per = math.gcd(home, 16)
    subs = home // per
    split = tuple(tuple(a.ndim == 4 for a in pair) for pair in pairs)

    def block(rc, y, s, pos):
        return (y * near + lax.rem(pos[1] + rc, near)) * subs + s

    specs, args = [], []
    for pair in pairs:
        for a in pair:
            args.append(a)
            if a.ndim == 4:
                specs.append(pl.BlockSpec((a.shape[0], per) + a.shape[2:], lambda rc, y, s, pos: (0, block(rc, y, s, pos), 0, 0)))
            else:
                specs.append(pl.BlockSpec((per,) + a.shape[1:], lambda rc, y, s, pos: (block(rc, y, s, pos), 0, 0)))
    n = len(pairs)
    dims = (n, far, home, size, size)

    def kept(rc, y, s, pos):
        return (0, jnp.where(rc == 0, y, far - 1), jnp.where(rc == 0, s, subs - 1), 0, 0)

    def sent(rc, y, s, pos):
        return (0, jnp.where(rc == 0, 0, y), jnp.where(rc == 0, 0, s), 0, 0)

    return call(
        functools.partial(grads_kernel, near, split),
        (shape(dims), shape(dims)),
        (near, far, subs),
        specs,
        (pl.BlockSpec((n, 1, per, size, size), kept), pl.BlockSpec((n, 1, per, size, size), sent)),
        [],
        tuple(args),
        scalars=pos,
    )


def join_kernel(near, n_x, pos_ref, *refs):
    out_ref = refs[-1]
    rc = pl.program_id(0)
    n_z, _, _, rows, _ = refs[0].shape

    for c in range(near):

        @pl.when(rc == c)
        def _():
            for rx in range(n_x):
                for rz in range(n_z):
                    z = lax.rem(pos_ref[2] - rz + n_z, n_z)
                    x = lax.rem(pos_ref[3] - rx + n_x, n_x)
                    at = pl.multiple_of((z * n_x + x) * rows, rows)
                    out_ref[:, pl.ds(at, rows), :] = refs[c * n_x + rx][rz, 0]


def join(pieces, pos):
    near, n_x = len(pieces), len(pieces[0])
    n_z, far, home, rows, size = pieces[0][0].shape
    per = math.gcd(home, 32)
    subs = home // per
    specs = []
    for c in range(near):
        for _ in range(n_x):

            def index(rc, ry, s, pos, c=c):
                y = jnp.where(rc == c, ry, jnp.where(rc < c, 0, far - 1))
                return (0, y, jnp.where(rc == c, s, jnp.where(rc < c, 0, subs - 1)), 0, 0)

            specs.append(pl.BlockSpec((n_z, 1, per, rows, size), index))

    def out_index(rc, ry, s, pos):
        y = lax.rem(pos[0] - ry + far, far)
        core = lax.rem(pos[1] - rc + near, near)
        return ((y * near + core) * subs + s, 0, 0)

    full = n_z * n_x * rows
    return call(
        functools.partial(join_kernel, near, n_x),
        shape((near * far * home, full, size)),
        (near, far, subs),
        specs,
        pl.BlockSpec((per, full, size), out_index),
        [],
        tuple(p for row in pieces for p in row),
        scalars=pos,
    )


class Ring:
    def __init__(self, axis, stride, size):
        self.axis, self.stride, self.size = axis, stride, size

    def here(self):
        return lax.rem(lax.axis_index(self.axis) // self.stride, self.size)

    def send(self, value, step):
        pairs = []
        for src in range(lax.axis_size(self.axis)):
            own = src // self.stride % self.size
            pairs.append((src, src + ((own + step) % self.size - own) * self.stride))
        return lax.ppermute(value, self.axis, pairs)

    def sends(self, value):
        return [self.send(value, step) for step in range(1, self.size)]

    def gather(self, value):
        if self.size == 1:
            return value[None]
        here = self.here()
        out = jnp.zeros((self.size,) + value.shape, value.dtype)
        out = lax.dynamic_update_index_in_dim(out, value, here, 0)
        for step in range(1, self.size):
            got = self.send(value, step)
            out = lax.dynamic_update_index_in_dim(out, got, lax.rem(here - step + self.size, self.size), 0)
        return out

    def scatter(self, terms, dim):
        here = self.here()
        if self.size == 1:
            return [lax.index_in_dim(t, 0, dim, keepdims=False) for t in terms]
        out = [lax.dynamic_index_in_dim(t, here, dim, keepdims=False) for t in terms]
        for step in range(1, self.size):
            there = lax.rem(here + step, self.size)
            out.append(self.send(total([lax.dynamic_index_in_dim(t, there, dim, keepdims=False) for t in terms]).astype(BF16), step))
        return out


def total(terms):
    return functools.reduce(jnp.add, [t.astype(F32) for t in terms])


def halves(size):
    low = 2 if size % 2 == 0 else 1
    return size // low, low


def cross(pieces):
    return lax.all_to_all(pieces, "tensor", split_axis=0, concat_axis=0, tiled=True)


def after(value, *others):
    return lax.optimization_barrier((value,) + others)[0]


def whole_tokens(x_home, g_home, factors, rings, share, cut):
    home, size, tokens = x_home.shape
    ring_y, ring_core, ring_z, ring_x = rings
    first_left = factors[0]
    rows = first_left.shape[1]
    pos = jnp.stack([ring.here() for ring in rings]).astype(jnp.int32)

    mine = jnp.stack([factors[3], factors[1], factors[2]])
    from_y = [mine] + ring_y.sends(mine)
    one = [first_left] + ring_z.sends(first_left)
    one = jnp.stack(one)
    zero = jnp.zeros_like(pos[:1])
    one = join([[p[:, None] for p in [one] + ring_x.sends(one)]], jnp.concatenate([zero, zero, pos[2:]]))

    g_mid = cross(after(deal(g_home, share, cut), *from_y[1:]))

    wholes, before = [], None
    for n in range(3):
        start = jnp.stack([part[n] for part in from_y])
        if before is not None:
            start = after(start, before)
        from_z = jnp.stack([start] + ring_z.sends(start))
        before = from_z
        from_x = [from_z] + ring_x.sends(from_z)
        from_core = [[p] + ring_core.sends(p) for p in from_x]
        wholes.append(join([[p[c] for p in from_core] for c in range(ring_core.size)], pos))
    right_two, right_one, left_two = wholes

    s_mid = cross(first_stage(x_home, one, share, cut))
    e_mid = back_two(g_mid, right_two)
    act, hidden, e_out = middle(s_mid, e_mid, right_one, left_two)
    e_got = cross(e_out)
    third, s_out = forward_two(act, left_two, right_two)
    s_out = s_out.reshape(share, home, size, cut)
    s_got = cross(after(s_out, e_got))

    def own_sum(pairs):
        terms = grads(pairs, home, size, ring_y.size, ring_core.size, pos)
        terms = [terms[0], ring_core.send(terms[1], 1)] if ring_core.size > 1 else terms[:1]
        terms = [t.reshape(len(pairs), ring_y.size, home, ring_z.size, ring_x.size, rows, size) for t in terms]
        return total(ring_y.scatter(ring_z.scatter(ring_x.scatter(terms, 4), 3), 1))

    grad_ltwo, grad_rone = own_sum([(act, e_mid), (s_mid, hidden)])
    grad_rtwo = own_sum([(third, g_mid)])[0]

    input_grad, grad_lone = last_stage(e_got, x_home, g_home, one)
    grad_lone = grad_lone.reshape(home, ring_z.size, ring_x.size, rows, size)
    grad_lone = total(ring_z.scatter(ring_x.scatter([grad_lone], 2), 1))
    mixed = add_home(s_got, x_home)
    return mixed, input_grad, grad_lone, grad_rone, grad_ltwo, grad_rtwo


def split_blocks(x_home, g_home, factors, rings, share, cut):
    home, size, tokens = x_home.shape
    ring_y, ring_core, ring_z, ring_x = rings
    rows = factors[0].shape[1]
    n_tensor = lax.axis_size("tensor")
    groups = n_tensor // share
    held = home * share
    same_tokens = [[group * share + part for group in range(groups)] for part in range(share)]

    def go(values):
        pieces = values.reshape(home, groups, held, share, cut).transpose(1, 3, 2, 0, 4)
        got = cross(pieces.reshape(n_tensor, held, home, cut))
        return got.transpose(1, 0, 2, 3).reshape(held, size, cut)

    def back(values):
        pieces = values.reshape(held, n_tensor, home, cut).transpose(1, 0, 2, 3)
        got = cross(pieces).reshape(groups, share, held, home, cut)
        return got.transpose(3, 0, 2, 1, 4).reshape(home, size, tokens)

    def turn(values):
        moved = lax.all_to_all(
            values.reshape(held, groups, held, cut), "tensor", split_axis=1, concat_axis=0, tiled=True, axis_index_groups=same_tokens
        )
        return jnp.swapaxes(moved.reshape(size, held, cut), 0, 1)

    def whole(factor):
        one = ring_z.gather(ring_y.gather(factor))
        all_rows = ring_core.gather(ring_x.gather(one))
        return all_rows.transpose(3, 0, 4, 2, 1, 5, 6).reshape(held, size, size)

    def own_sum(partial):
        split = partial.reshape(ring_y.size, ring_core.size, home, ring_z.size, ring_x.size, rows, size)
        terms = ring_core.scatter([split], 1)
        return total(ring_y.scatter(ring_z.scatter(ring_x.scatter(terms, 3), 2), 0))

    first_left, first_right, second_left, second_right = factors
    g_mid = go(g_home)
    left_one = ring_x.gather(ring_z.gather(first_left)).transpose(2, 1, 0, 3, 4).reshape(home, size, size)
    right_one, left_two, right_two = whole(first_right), whole(second_left), whole(second_right)

    s_one = go(product("bjt,bjo->bot", x_home, left_one).astype(BF16))
    s_two = turn(product("bit,bip->bpt", s_one, right_one).astype(BF16))
    act = gelu_value(s_two.astype(F32)).astype(BF16)
    e_three = turn(product("bot,bio->bit", g_mid, right_two).astype(BF16))
    h_mid = turn(gelu_back(s_two.astype(F32), product("bot,bjo->bjt", e_three, left_two)).astype(BF16))
    e_one = back(product("bpt,bip->bit", h_mid, right_one).astype(BF16))
    s_three = turn(product("bjt,bjo->bot", act, left_two).astype(BF16))
    s_four = back(product("bit,bio->bot", s_three, right_two).astype(BF16))
    mixed = (x_home.astype(F32) + s_four.astype(F32)).astype(BF16)

    grad_rtwo = own_sum(product("bit,bot->bio", s_three, g_mid))
    grad_ltwo = own_sum(product("bjt,bot->bjo", act, e_three))
    grad_rone = own_sum(product("bit,bpt->bip", s_one, h_mid))
    grad_lone = product("bjt,bot->bjo", x_home, e_one).reshape(home, ring_z.size, ring_x.size, rows, size)
    grad_lone = total(ring_z.scatter(ring_x.scatter([grad_lone], 2), 1))
    input_grad = (g_home.astype(F32) + product("bot,bjo->bjt", e_one, left_one)).astype(BF16)
    return mixed, input_grad, grad_lone, grad_rone, grad_ltwo, grad_rtwo


def per_device(inputs, cotangent, first_left, first_right, second_left, second_right):
    n_dp, n_tensor = lax.axis_size("dp"), lax.axis_size("tensor")
    home, _, size = first_left.shape
    tokens = inputs.shape[1]
    share = math.gcd(n_tensor, max(1, tokens // LANES))
    cut = tokens // share
    far, near = halves(share)
    outer, inner = halves(n_dp)
    rings = (Ring("tensor", near, far), Ring("tensor", 1, near), Ring("dp", inner, outer), Ring("dp", 1, inner))
    plan = whole_tokens if share == n_tensor else split_blocks
    mixed, input_grad, *weight_grads = plan(
        inputs.reshape(home, size, tokens),
        cotangent.reshape(home, size, tokens),
        (first_left, first_right, second_left, second_right),
        rings,
        share,
        cut,
    )
    return (mixed.reshape(inputs.shape), input_grad.reshape(inputs.shape), *weight_grads)


def solution(mesh):
    wide, factor = P("tensor", "dp"), P("tensor", "dp", None)
    return jax.shard_map(
        per_device,
        mesh=mesh,
        in_specs=(wide, wide, factor, factor, factor, factor),
        out_specs=(wide, wide, factor, factor, factor, factor),
        check_vma=False,
    )
```

```python
import functools
import itertools
import math

import jax
import jax.numpy as jnp
from jax import lax
from jax.experimental import pallas as pl
from jax.experimental.pallas import tpu as pltpu
from jax.sharding import PartitionSpec as P

BF16 = jnp.bfloat16
F32 = jnp.float32
LANES = 128
PAD = 8
VMEM_BYTES = 60 * 1024 * 1024


def gelu_value(values):
    return jax.nn.gelu(values, approximate=True)


def gelu_back(values, upstream):
    return jax.vjp(gelu_value, values)[1](upstream)[0]


def gelu_both(v):
    root, cubic = 0.7978845608028654, 0.044715
    square = v * v
    t = jnp.tanh(root * (v + cubic * (v * square)))
    half = 0.5 * (1.0 + t)
    slope = half + (0.5 * v) * (1.0 - t * t) * (root + (3.0 * cubic * root) * square)
    return v * half, slope


def product(form, left, right):
    return jnp.einsum(form, left, right, preferred_element_type=F32)


def dot_nn(left, right):
    return lax.dot_general(left, right, (((1,), (0,)), ((), ())), preferred_element_type=F32)


def dot_tn(left, right):
    return lax.dot_general(left, right, (((0,), (0,)), ((), ())), preferred_element_type=F32)


def dot_nt(left, right):
    return lax.dot_general(left, right, (((1,), (1,)), ((), ())), preferred_element_type=F32)


def call(body, out, grid, in_specs, out_specs, scratch, args, scalars=None):
    spec = pltpu.PrefetchScalarGridSpec(
        num_scalar_prefetch=0 if scalars is None else 1,
        grid=grid,
        in_specs=in_specs,
        out_specs=out_specs,
        scratch_shapes=scratch,
    )
    return pl.pallas_call(
        body,
        out_shape=out,
        grid_spec=spec,
        compiler_params=pltpu.CompilerParams(
            dimension_semantics=("arbitrary",) * len(grid), vmem_limit_bytes=VMEM_BYTES
        ),
        cost_estimate=pl.CostEstimate(flops=0, bytes_accessed=1024, transcendentals=0),
    )(*(() if scalars is None else (scalars,)), *args)


def shape(dims, dtype=BF16):
    return jax.ShapeDtypeStruct(dims, dtype)


def each(count, body, unroll=16):
    def step(k, carry):
        body(k)
        return carry

    lax.fori_loop(0, count, step, 0, unroll=math.gcd(count, unroll))


def during(phase, steps):
    return lambda p, j: jnp.where(p == phase, j, jnp.where(p < phase, 0, steps - 1))


def stacked(ref, k):
    return jnp.concatenate([ref[c, k] for c in range(ref.shape[0])], axis=0)


class Ring:
    def __init__(self, axis, *digits):
        self.axis, self.digits, self.last = axis, digits, None
        self.stride, self.size = digits[0]

    def here(self):
        return lax.rem(lax.axis_index(self.axis) // self.stride, self.size)

    def send(self, value, *steps):
        pairs = []
        for src in range(lax.axis_size(self.axis)):
            dst = src
            for (stride, size), step in zip(self.digits, steps):
                own = src // stride % size
                dst += ((own + step) % size - own) * stride
            pairs.append((src, dst))
        if self.last is not None:
            value = after(value, self.last)
        self.last = lax.ppermute(value, self.axis, pairs)
        return self.last

    def sends(self, value):
        return [self.send(value, step) for step in range(1, self.size)]

    def gather(self, value):
        if self.size == 1:
            return value[None]
        here = self.here()
        out = jnp.zeros((self.size,) + value.shape, value.dtype)
        out = lax.dynamic_update_index_in_dim(out, value, here, 0)
        for step in range(1, self.size):
            got = self.send(value, step)
            out = lax.dynamic_update_index_in_dim(out, got, lax.rem(here - step + self.size, self.size), 0)
        return out

    def scatter(self, terms, dim):
        here = self.here()
        if self.size == 1:
            return [lax.index_in_dim(t, 0, dim, keepdims=False) for t in terms]
        out = [lax.dynamic_index_in_dim(t, here, dim, keepdims=False) for t in terms]
        for step in range(1, self.size):
            there = lax.rem(here + step, self.size)
            out.append(self.send(total([lax.dynamic_index_in_dim(t, there, dim, keepdims=False) for t in terms]).astype(BF16), step))
        return out


def total(terms):
    return functools.reduce(jnp.add, [t.astype(F32) for t in terms])


def after(value, *others):
    return lax.optimization_barrier((value,) + others)[0]


def turned_back(here, step, size):
    return lax.rem(here - step + size, size)


class Place:
    def __init__(self, share, n_dp):
        self.far, self.near = halves(share)
        self.y, self.core = Ring("tensor", (self.near, self.far)), Ring("tensor", (1, self.near))
        self.dp, stride = [], 1
        while stride < n_dp:
            size = next(p for p in range(2, n_dp + 1) if n_dp // stride % p == 0)
            self.dp.append(Ring("dp", (stride, size)))
            stride *= size
        self.steps = [(y, c) for y in range(self.far) for c in range(self.near)]
        self.links = {step: Ring("tensor", (self.near, self.far), (1, self.near)) for step in self.steps[1:]}
        self.links[(1, 0)] = self.y if self.far > 1 else None
        if self.near > 1:
            self.links[(0, 1)] = self.core
        self.rows = [ring.size for ring in self.dp]

    def position(self):
        return jnp.stack([ring.here() for ring in [self.y, self.core] + self.dp]).astype(jnp.int32)

    def onward(self, pos, n):
        y, c = self.steps[n]
        return lax.rem(pos[0] + y, self.far) * self.near + lax.rem(pos[1] + c, self.near)

    def source(self, pos, n):
        y, c = self.steps[n]
        return turned_back(pos[0], y, self.far) * self.near + turned_back(pos[1], c, self.near)

    def exchange(self, pieces):
        got = [pieces[0]] + [None] * (len(pieces) - 1)
        for n in reversed(range(1, len(pieces))):
            y, c = self.steps[n]
            if y == 0:
                got[n] = self.core.send(pieces[n], c)
            elif c == 0:
                got[n] = self.y.send(pieces[n], y)
            else:
                got[n] = self.links[(y, c)].send(pieces[n], y, c)
        return got


def piece_copies(place, pos_ref, pieces, whole, sems):
    copies = []
    home, rows, _ = pieces[0][0].shape[-3:]
    inner = [range(ring.size) for ring in place.dp[1:]]
    strides = [ring.stride for ring in place.dp]
    for c, row in enumerate(pieces):
        for d, ref in enumerate(row):
            lead = ref.shape[:-3]
            for back in itertools.product(*inner, range(lead[-1])):
                steps = (d,) + back[:-1]
                at = sum(turned_back(pos_ref[2 + n], steps[n], place.rows[n]) * strides[n] for n in range(len(steps))) if place.dp else 0
                group = 0
                if len(pieces) > 1 or lead[-1] > 1:
                    group = turned_back(pos_ref[0], back[-1], place.far) * place.near + turned_back(pos_ref[1], c, place.near)
                dst = whole.at[pl.ds(group * home, home), pl.ds(pl.multiple_of(at * rows, rows), rows), :]
                copies.append(pltpu.make_async_copy(ref.at[back], dst, sems.at[len(copies)]))
    return copies


def share_copies(place, pos_ref, parts, whole, sems):
    return [pltpu.make_async_copy(ref, whole.at[place.source(pos_ref, n)], sems.at[n]) for n, ref in enumerate(parts)]


def run(copies):
    for copy in copies:
        copy.start()


def finish(copies):
    for copy in copies:
        copy.wait()


def n_copies(place):
    return place.far * place.near * math.prod(place.rows)


def anywhere(count):
    return [pl.BlockSpec(memory_space=pl.ANY)] * count


def flat(pieces):
    return tuple(p for row in pieces for p in row)


def unflat(place, refs):
    wide = len(refs) // place.near
    return [refs[c * wide : (c + 1) * wide] for c in range(place.near)]


def deal_kernel(pos_ref, g_ref, out_ref, turned):
    home, size, _ = g_ref.shape
    pitch = home + PAD

    def store(o):
        turned[pl.ds(o, size, stride=pitch), :] = g_ref[o].astype(F32)

    def load(b):
        out_ref[b] = turned[pl.ds(pl.multiple_of(b * pitch, 8), home), :].astype(BF16)

    each(home, store)
    each(size, load)


def deal(place, pos, g_home, cut, n):
    home, size, _ = g_home.shape
    return call(
        deal_kernel,
        shape((size, home, cut)),
        (1,),
        [pl.BlockSpec((home, size, cut), lambda i, pos: (0, 0, place.onward(pos, n)))],
        pl.BlockSpec((size, home, cut), lambda i, pos: (0, 0, 0)),
        [pltpu.VMEM((size * (home + PAD), cut), F32)],
        (g_home,),
        scalars=pos,
    )


def first_kernel(place, pos_ref, x_ref, w_ref, *refs):
    *out_refs, turned = refs
    home, size, _ = x_ref.shape
    cut = out_refs[0].shape[2]
    pitch = home + PAD

    for n, out_ref in enumerate(out_refs):

        @pl.when(pl.program_id(0) == n)
        def _():
            lanes = pl.ds(pl.multiple_of(place.onward(pos_ref, n) * cut, cut), cut)

            def store(b):
                turned[pl.ds(b, size, stride=pitch), :] = dot_tn(w_ref[b], x_ref[b, :, lanes])

            def load(o):
                out_ref[o] = turned[pl.ds(pl.multiple_of(o * pitch, 8), home), :].astype(BF16)

            each(home, store)
            each(size, load)


def first_stage(place, pos, x_home, left_one, cut):
    home, size, tokens = x_home.shape
    share = tokens // cut
    return call(
        functools.partial(first_kernel, place),
        (shape((size, home, cut)),) * share,
        (share,),
        [
            pl.BlockSpec((home, size, tokens), lambda s, pos: (0, 0, 0)),
            pl.BlockSpec((home, size, size), lambda s, pos: (0, 0, 0)),
        ],
        (pl.BlockSpec((size, home, cut), lambda s, pos: (0, 0, 0)),) * share,
        [pltpu.VMEM((size * (home + PAD), cut), F32)],
        (x_home, left_one),
        scalars=pos,
    )


def last_kernel(place, pos_ref, *refs):
    share = place.far * place.near
    e_refs = refs[:share]
    x_ref, g_ref, w_ref, out_ref, grad_ref, turned = refs[share:]
    blocks, per, cut = e_refs[0].shape
    pitch = blocks + PAD

    for n in range(share):
        s = place.source(pos_ref, n)

        def store(o):
            turned[s, pl.ds(o, per, stride=pitch), :] = e_refs[n][o].astype(F32)

        each(blocks, store)

    def load(b):
        rows = pl.ds(pl.multiple_of(b * pitch, 8), blocks)
        e_b = jnp.concatenate([turned[s, rows, :].astype(BF16) for s in range(share)], axis=1)
        out_ref[b] = (g_ref[b].astype(F32) + dot_nn(w_ref[b], e_b)).astype(BF16)
        grad_ref[b] = dot_nt(x_ref[b], e_b).astype(BF16)

    each(per, load, 4)


def last_stage(place, pos, e_got, x_home, g_home, left_one):
    share = len(e_got)
    blocks, home, cut = e_got[0].shape
    _, size, tokens = x_home.shape
    per = math.gcd(home, 16)
    wide = pl.BlockSpec((per, size, tokens), lambda h, pos: (h, 0, 0))
    factor = pl.BlockSpec((per, size, size), lambda h, pos: (h, 0, 0))
    return call(
        functools.partial(last_kernel, place),
        (shape(g_home.shape), shape((home, size, size))),
        (home // per,),
        [pl.BlockSpec((blocks, per, cut), lambda h, pos: (0, h, 0))] * share + [wide, wide, factor],
        (wide, factor),
        [pltpu.VMEM((share, per * (blocks + PAD), cut), F32)],
        (*e_got, x_home, g_home, left_one),
        scalars=pos,
    )


def mixed_kernel(place, pos_ref, *refs):
    *s_refs, x_ref, out_ref = refs
    cut = s_refs[0].shape[2]
    for n, s_ref in enumerate(s_refs):
        lanes = pl.ds(pl.multiple_of(place.source(pos_ref, n) * cut, cut), cut)
        out_ref[:, :, lanes] = (x_ref[:, :, lanes].astype(F32) + s_ref[...].astype(F32)).astype(BF16)


def add_home(place, pos, s_got, x_home):
    home, blocks, cut = s_got[0].shape
    per = math.gcd(home, 8)
    wide = pl.BlockSpec((per,) + x_home.shape[1:], lambda h, pos: (h, 0, 0))
    return call(
        functools.partial(mixed_kernel, place),
        shape(x_home.shape),
        (home // per,),
        [pl.BlockSpec((per, blocks, cut), lambda h, pos: (h, 0, 0))] * len(s_got) + [wide],
        wide,
        [],
        (*s_got, x_home),
        scalars=pos,
    )


def join_kernel(place, pos_ref, *refs):
    *pieces, out_ref, sems = refs
    copies = piece_copies(place, pos_ref, [pieces], out_ref, sems)
    run(copies)
    finish(copies)


def join(place, pos, pieces):
    home, rows, size = pieces[0].shape[-3:]
    return call(
        functools.partial(join_kernel, place),
        shape((home, rows * math.prod(place.rows), size)),
        (1,),
        anywhere(len(pieces)),
        pl.BlockSpec(memory_space=pl.ANY),
        [pltpu.SemaphoreType.DMA((math.prod(place.rows),))],
        tuple(pieces),
        scalars=pos,
    )


def back_two_kernel(place, pos_ref, *refs):
    share = place.far * place.near
    g_parts, factor = refs[:share], unflat(place, refs[share:-6])
    out_ref, turned, g_all, w_all, g_sems, w_sems = refs[-6:]
    per, size, _ = out_ref.shape
    pitch = size + PAD
    phase, j = pl.program_id(0), pl.program_id(1)

    @pl.when((phase == 0) & (j == 0))
    def _():
        copies = share_copies(place, pos_ref, g_parts, g_all, g_sems) + piece_copies(place, pos_ref, factor, w_all, w_sems)
        run(copies)
        finish(copies)

    @pl.when(phase == 0)
    def _():
        def body(k):
            b = j * per + k
            turned[pl.ds(b, size, stride=pitch), :] = dot_nn(w_all[b], stacked(g_all, b))

        each(per, body)

    @pl.when(phase == 1)
    def _():
        def body(k):
            out_ref[k] = turned[pl.ds(pl.multiple_of((j * per + k) * pitch, 8), size), :].astype(BF16)

        each(per, body)


def middle_sizes(place, parts):
    blocks, home, cut = parts[0].shape
    return blocks, home, cut, len(parts), (blocks, blocks, blocks)


def back_two(place, pos, g_mid, right_two):
    blocks, home, cut, share, whole = middle_sizes(place, g_mid)
    at = during(1, share)
    return call(
        functools.partial(back_two_kernel, place),
        shape((blocks, blocks, cut)),
        (2, share),
        anywhere(share + len(flat(right_two))),
        pl.BlockSpec((home, blocks, cut), lambda p, j, pos: (at(p, j), 0, 0)),
        [
            pltpu.VMEM((blocks * (blocks + PAD), cut), F32),
            pltpu.VMEM((share, blocks, home, cut), BF16),
            pltpu.VMEM(whole, BF16),
            pltpu.SemaphoreType.DMA((share,)),
            pltpu.SemaphoreType.DMA((n_copies(place),)),
        ],
        (*g_mid, *flat(right_two)),
        scalars=pos,
    )


def either(place, pos_ref, j, keep_ref, send_ref, body):
    mine = lax.rem(j, place.near) == pos_ref[1]

    @pl.when(mine)
    def _():
        body(keep_ref)

    @pl.when(jnp.logical_not(mine))
    def _():
        body(send_ref)


def middle_kernel(place, pos_ref, *refs):
    share = place.far * place.near
    wide = (len(refs) - (2 * share + 15)) // 2
    s_parts, rest = refs[:share], refs[share:]
    one, two, rest = unflat(place, rest[:wide]), unflat(place, rest[wide : 2 * wide]), rest[2 * wide :]
    e_ref, act_ref, keep_two, send_two, keep_one, send_one, *rest = rest
    out_refs, rest = rest[:share], rest[share:]
    turned, hidden, e_one, s_all, one_all, two_all, s_sems, one_sems, two_sems = rest
    per, size, cut = act_ref.shape
    home = s_all.shape[2]
    pitch = size + PAD
    phase, j = pl.program_id(0), pl.program_id(1)

    def rows(k):
        return pl.ds(pl.multiple_of((j * per + k) * pitch, 8), size)

    def column(k):
        return pl.ds(j * per + k, size, stride=pitch)

    def second():
        return piece_copies(place, pos_ref, two, two_all, two_sems)

    @pl.when((phase == 0) & (j == 0))
    def _():
        copies = share_copies(place, pos_ref, s_parts, s_all, s_sems) + piece_copies(place, pos_ref, one, one_all, one_sems)
        run(copies)
        run(second())
        finish(copies)

    @pl.when(phase == 0)
    def _():
        def body(k):
            b = j * per + k
            turned[column(k), :] = dot_tn(one_all[b], stacked(s_all, b))

        each(per, body)

    @pl.when((phase == 1) & (j == 0))
    def _():
        finish(second())

    @pl.when(phase == 1)
    def _():
        def with_out(grad_ref):
            def body(k):
                v = turned[rows(k), :].astype(BF16).astype(F32)
                value, slope = gelu_both(v)
                act = value.astype(BF16)
                act_ref[k] = act
                e = e_ref[k]
                hidden[column(k), :] = slope * dot_nn(two_all[j * per + k], e)
                grad_ref[0, k] = dot_nt(act, e).astype(BF16)

            each(per, body, 8)

        either(place, pos_ref, j, keep_two, send_two, with_out)

    @pl.when(phase == 2)
    def _():
        def with_out(grad_ref):
            def body(k):
                b = j * per + k
                h = hidden[rows(k), :].astype(BF16)
                e_one[k] = dot_nn(one_all[b], h).astype(BF16)
                grad_ref[0, k] = dot_nt(stacked(s_all, b), h).astype(BF16)

            each(per, body)

        either(place, pos_ref, j, keep_one, send_one, with_out)
        for n in range(share):
            at = pl.ds(pl.multiple_of(place.onward(pos_ref, n) * home, home), home)
            out_refs[n][...] = e_one[:, at, :]


def grad_specs(place, phase, home, size, share):
    at = during(phase, share)
    dims = shape((place.far, home, size, size))
    spec = pl.BlockSpec((1, home, size, size), lambda p, j, pos: (at(p, j) // place.near, 0, 0, 0))
    return [dims] * 2, [spec] * 2


def middle(place, pos, s_mid, e_mid, right_one, left_two):
    blocks, home, cut, share, whole = middle_sizes(place, s_mid)
    at = [during(phase, share) for phase in range(3)]
    block = pl.BlockSpec((home, blocks, cut), lambda p, j, pos: (at[1](p, j), 0, 0))
    two, two_specs = grad_specs(place, 1, home, blocks, share)
    one, one_specs = grad_specs(place, 2, home, blocks, share)
    piece = pl.BlockSpec((home, home, cut), lambda p, j, pos: (at[2](p, j), 0, 0))
    out = call(
        functools.partial(middle_kernel, place),
        (shape((blocks, blocks, cut)), *two, *one) + (shape((blocks, home, cut)),) * share,
        (3, share),
        anywhere(share + 2 * len(flat(right_one))) + [block],
        (block, *two_specs, *one_specs) + (piece,) * share,
        [pltpu.VMEM((blocks * (blocks + PAD), cut), F32)] * 2
        + [
            pltpu.VMEM((home, blocks, cut), BF16),
            pltpu.VMEM((share, blocks, home, cut), BF16),
            pltpu.VMEM(whole, BF16),
            pltpu.VMEM(whole, BF16),
            pltpu.SemaphoreType.DMA((share,)),
            pltpu.SemaphoreType.DMA((n_copies(place),)),
            pltpu.SemaphoreType.DMA((n_copies(place),)),
        ],
        (*s_mid, *flat(right_one), *flat(left_two), e_mid),
        scalars=pos,
    )
    return out[0], out[1:3], out[3:5], list(out[5:])


def forward_two_kernel(place, pos_ref, *refs):
    share = place.far * place.near
    wide = (len(refs) - (2 * share + 11)) // 2
    g_parts, rest = refs[:share], refs[share:]
    left, right, rest = unflat(place, rest[:wide]), unflat(place, rest[wide : 2 * wide]), rest[2 * wide :]
    act_ref, keep_ref, send_ref, *rest = rest
    out_refs, rest = rest[:share], rest[share:]
    turned, fourth, g_all, left_all, right_all, g_sems, left_sems, right_sems = rest
    per, size, _ = act_ref.shape
    pitch = size + PAD
    phase, j = pl.program_id(0), pl.program_id(1)

    def rows(k):
        return pl.ds(pl.multiple_of((j * per + k) * pitch, 8), size)

    def column(k):
        return pl.ds(j * per + k, size, stride=pitch)

    def second():
        return piece_copies(place, pos_ref, right, right_all, right_sems) + share_copies(place, pos_ref, g_parts, g_all, g_sems)

    @pl.when((phase == 0) & (j == 0))
    def _():
        copies = piece_copies(place, pos_ref, left, left_all, left_sems)
        run(copies)
        run(second())
        finish(copies)

    @pl.when(phase == 0)
    def _():
        def body(k):
            turned[column(k), :] = dot_tn(left_all[j * per + k], act_ref[k])

        each(per, body)

    @pl.when((phase == 1) & (j == 0))
    def _():
        finish(second())

    @pl.when(phase == 1)
    def _():
        def with_out(grad_ref):
            def body(k):
                b = j * per + k
                third = turned[rows(k), :].astype(BF16)
                fourth[column(k), :] = dot_tn(right_all[b], third)
                grad_ref[0, k] = dot_nt(third, stacked(g_all, b)).astype(BF16)

            each(per, body)

        either(place, pos_ref, j, keep_ref, send_ref, with_out)

    for n in range(share):

        @pl.when((phase == 2) & (j == n))
        def _():
            base = place.onward(pos_ref, n) * per

            def body(k):
                out_refs[n][k] = fourth[pl.ds(pl.multiple_of((base + k) * pitch, 8), size), :].astype(BF16)

            each(per, body)


def forward_two(place, pos, act, g_mid, left_two, right_two):
    blocks, home, cut, share, whole = middle_sizes(place, g_mid)
    at = during(0, share)
    grad, grad_spec = grad_specs(place, 1, home, blocks, share)
    out = call(
        functools.partial(forward_two_kernel, place),
        (*grad,) + (shape((home, blocks, cut)),) * share,
        (3, share),
        anywhere(share + 2 * len(flat(left_two))) + [pl.BlockSpec((home, blocks, cut), lambda p, j, pos: (at(p, j), 0, 0))],
        (*grad_spec,) + (pl.BlockSpec((home, blocks, cut), lambda p, j, pos: (0, 0, 0)),) * share,
        [pltpu.VMEM((blocks * (blocks + PAD), cut), F32)] * 2
        + [
            pltpu.VMEM((share, blocks, home, cut), BF16),
            pltpu.VMEM(whole, BF16),
            pltpu.VMEM(whole, BF16),
            pltpu.SemaphoreType.DMA((share,)),
            pltpu.SemaphoreType.DMA((n_copies(place),)),
            pltpu.SemaphoreType.DMA((n_copies(place),)),
        ],
        (*g_mid, *flat(left_two), *flat(right_two), act),
        scalars=pos,
    )
    return out[:2], list(out[2:])


def halves(size):
    low = 2 if size % 2 == 0 else 1
    return size // low, low


def cross(pieces):
    return lax.all_to_all(pieces, "tensor", split_axis=0, concat_axis=0, tiled=True)


def whole_tokens(x_home, g_home, factors, share, cut):
    home, size, tokens = x_home.shape
    first_left = factors[0]
    rows = first_left.shape[1]
    place = Place(share, lax.axis_size("dp"))
    pos = place.position()

    def spread(start):
        for ring in reversed(place.dp[1:]):
            start = jnp.stack([start] + ring.sends(start))
        return [start] + (place.dp[0].sends(start) if place.dp else [])

    mine = jnp.stack([factors[3], factors[1], factors[2]])
    from_y = [mine] + place.y.sends(mine)
    one = join(place, pos, [p[..., None, :, :, :] for p in spread(first_left)])
    order = list(reversed(range(share)))
    g_pieces = {n: deal(place, pos, g_home, cut, n) for n in order}
    g_mid = place.exchange([g_pieces[n] for n in range(share)])

    def whole(n, *before):
        pieces = spread(jnp.stack([part[n] for part in from_y]))
        pieces = [after(p, *before) for p in pieces] if before else pieces
        by_core = [[p] + place.core.sends(p) for p in pieces]
        return [[p[c] for p in by_core] for c in range(place.near)]

    right_two = whole(0)
    s_mid = place.exchange(list(first_stage(place, pos, x_home, one, cut)))
    e_mid = back_two(place, pos, g_mid, right_two)
    right_one = whole(1)
    left_two = whole(2)
    act, grad_two, grad_one, e_out = middle(place, pos, s_mid, e_mid, right_one, left_two)
    e_got = place.exchange(e_out)

    def own_sum(terms):
        terms = [terms[0], place.core.send(terms[1], 1)] if place.near > 1 else terms[:1]
        terms = [t.reshape([place.far, home] + place.rows[::-1] + [rows, size]) for t in terms]
        return total(place.y.scatter(own_rows(terms, 2), 0))

    def own_rows(terms, dim):
        for n, ring in enumerate(place.dp):
            terms = ring.scatter(terms, dim + len(place.dp) - 1 - n)
        return terms

    grad_ltwo = own_sum(grad_two)
    grad_rone = own_sum(grad_one)
    grad_rtwo, s_out = forward_two(place, pos, act, g_mid, left_two, right_two)
    s_got = place.exchange(s_out)
    grad_rtwo = own_sum(grad_rtwo)

    input_grad, grad_lone = last_stage(place, pos, e_got, x_home, g_home, one)
    grad_lone = total(own_rows([grad_lone.reshape([home] + place.rows[::-1] + [rows, size])], 1))
    mixed = add_home(place, pos, s_got, x_home)
    return mixed, input_grad, grad_lone, grad_rone, grad_ltwo, grad_rtwo


def split_blocks(x_home, g_home, factors, share, cut):
    home, size, tokens = x_home.shape
    far, near = halves(share)
    outer, inner = halves(lax.axis_size("dp"))
    ring_y, ring_core = Ring("tensor", (near, far)), Ring("tensor", (1, near))
    ring_z, ring_x = Ring("dp", (inner, outer)), Ring("dp", (1, inner))
    rows = factors[0].shape[1]
    n_tensor = lax.axis_size("tensor")
    groups = n_tensor // share
    held = home * share
    same_tokens = [[group * share + part for group in range(groups)] for part in range(share)]

    def go(values):
        pieces = values.reshape(home, groups, held, share, cut).transpose(1, 3, 2, 0, 4)
        got = cross(pieces.reshape(n_tensor, held, home, cut))
        return got.transpose(1, 0, 2, 3).reshape(held, size, cut)

    def back(values):
        pieces = values.reshape(held, n_tensor, home, cut).transpose(1, 0, 2, 3)
        got = cross(pieces).reshape(groups, share, held, home, cut)
        return got.transpose(3, 0, 2, 1, 4).reshape(home, size, tokens)

    def turn(values):
        moved = lax.all_to_all(
            values.reshape(held, groups, held, cut), "tensor", split_axis=1, concat_axis=0, tiled=True, axis_index_groups=same_tokens
        )
        return jnp.swapaxes(moved.reshape(size, held, cut), 0, 1)

    def whole(factor):
        one = ring_z.gather(ring_y.gather(factor))
        all_rows = ring_core.gather(ring_x.gather(one))
        return all_rows.transpose(3, 0, 4, 2, 1, 5, 6).reshape(held, size, size)

    def own_sum(partial):
        split = partial.reshape(ring_y.size, ring_core.size, home, ring_z.size, ring_x.size, rows, size)
        terms = ring_core.scatter([split], 1)
        return total(ring_y.scatter(ring_z.scatter(ring_x.scatter(terms, 3), 2), 0))

    first_left, first_right, second_left, second_right = factors
    g_mid = go(g_home)
    left_one = ring_x.gather(ring_z.gather(first_left)).transpose(2, 1, 0, 3, 4).reshape(home, size, size)
    right_one, left_two, right_two = whole(first_right), whole(second_left), whole(second_right)

    s_one = go(product("bjt,bjo->bot", x_home, left_one).astype(BF16))
    s_two = turn(product("bit,bip->bpt", s_one, right_one).astype(BF16))
    act = gelu_value(s_two.astype(F32)).astype(BF16)
    e_three = turn(product("bot,bio->bit", g_mid, right_two).astype(BF16))
    h_mid = turn(gelu_back(s_two.astype(F32), product("bot,bjo->bjt", e_three, left_two)).astype(BF16))
    e_one = back(product("bpt,bip->bit", h_mid, right_one).astype(BF16))
    s_three = turn(product("bjt,bjo->bot", act, left_two).astype(BF16))
    s_four = back(product("bit,bio->bot", s_three, right_two).astype(BF16))
    mixed = (x_home.astype(F32) + s_four.astype(F32)).astype(BF16)

    grad_rtwo = own_sum(product("bit,bot->bio", s_three, g_mid))
    grad_ltwo = own_sum(product("bjt,bot->bjo", act, e_three))
    grad_rone = own_sum(product("bit,bpt->bip", s_one, h_mid))
    grad_lone = product("bjt,bot->bjo", x_home, e_one).reshape(home, ring_z.size, ring_x.size, rows, size)
    grad_lone = total(ring_z.scatter(ring_x.scatter([grad_lone], 2), 1))
    input_grad = (g_home.astype(F32) + product("bot,bjo->bjt", e_one, left_one)).astype(BF16)
    return mixed, input_grad, grad_lone, grad_rone, grad_ltwo, grad_rtwo


def per_device(inputs, cotangent, first_left, first_right, second_left, second_right):
    n_tensor = lax.axis_size("tensor")
    home, _, size = first_left.shape
    tokens = inputs.shape[1]
    share = math.gcd(n_tensor, max(1, tokens // LANES))
    cut = tokens // share
    plan = whole_tokens if share == n_tensor else split_blocks
    mixed, input_grad, *weight_grads = plan(
        inputs.reshape(home, size, tokens),
        cotangent.reshape(home, size, tokens),
        (first_left, first_right, second_left, second_right),
        share,
        cut,
    )
    return (mixed.reshape(inputs.shape), input_grad.reshape(inputs.shape), *weight_grads)


def solution(mesh):
    wide, factor = P("tensor", "dp"), P("tensor", "dp", None)
    return jax.shard_map(
        per_device,
        mesh=mesh,
        in_specs=(wide, wide, factor, factor, factor, factor),
        out_specs=(wide, wide, factor, factor, factor, factor),
        check_vma=False,
    )
```

```python
import functools
import itertools
import math

import jax
import jax.numpy as jnp
from jax import lax
from jax.experimental import pallas as pl
from jax.experimental.pallas import tpu as pltpu
from jax.sharding import PartitionSpec as P

BF16 = jnp.bfloat16
F32 = jnp.float32
LANES = 128
PAD = 8
VMEM_BYTES = 60 * 1024 * 1024
BYTES_PER_US = 1_200_000


def gelu_value(values):
    return jax.nn.gelu(values, approximate=True)


def gelu_back(values, upstream):
    return jax.vjp(gelu_value, values)[1](upstream)[0]


def gelu_both(v):
    root, cubic = 0.7978845608028654, 0.044715
    square = v * v
    t = jnp.tanh(root * (v + cubic * (v * square)))
    half = 0.5 * (1.0 + t)
    slope = half + (0.5 * v) * (1.0 - t * t) * (root + (3.0 * cubic * root) * square)
    return v * half, slope


def product(form, left, right):
    return jnp.einsum(form, left, right, preferred_element_type=F32)


def dot_nn(left, right):
    return lax.dot_general(left, right, (((1,), (0,)), ((), ())), preferred_element_type=F32)


def dot_tn(left, right):
    return lax.dot_general(left, right, (((0,), (0,)), ((), ())), preferred_element_type=F32)


def dot_nt(left, right):
    return lax.dot_general(left, right, (((1,), (1,)), ((), ())), preferred_element_type=F32)


def call(body, out, grid, in_specs, out_specs, scratch, args, us, scalars=None):
    spec = pltpu.PrefetchScalarGridSpec(
        num_scalar_prefetch=0 if scalars is None else 1,
        grid=grid,
        in_specs=in_specs,
        out_specs=out_specs,
        scratch_shapes=scratch,
    )
    return pl.pallas_call(
        body,
        out_shape=out,
        grid_spec=spec,
        compiler_params=pltpu.CompilerParams(
            dimension_semantics=("arbitrary",) * len(grid), vmem_limit_bytes=VMEM_BYTES
        ),
        cost_estimate=pl.CostEstimate(flops=0, bytes_accessed=int(us * BYTES_PER_US), transcendentals=0),
    )(*(() if scalars is None else (scalars,)), *args)


def shape(dims, dtype=BF16):
    return jax.ShapeDtypeStruct(dims, dtype)


def each(count, body, unroll=16):
    def step(k, carry):
        body(k)
        return carry

    lax.fori_loop(0, count, step, 0, unroll=math.gcd(count, unroll))


def during(phase, steps):
    return lambda p, j: jnp.where(p == phase, j, jnp.where(p < phase, 0, steps - 1))


def stacked(ref, k):
    return jnp.concatenate([ref[c, k] for c in range(ref.shape[0])], axis=0)


class Ring:
    def __init__(self, axis, *digits, tied=True):
        self.axis, self.digits, self.last, self.tied = axis, digits, None, tied
        self.stride, self.size = digits[0]

    def here(self):
        return lax.rem(lax.axis_index(self.axis) // self.stride, self.size)

    def send(self, value, *steps):
        pairs = []
        for src in range(lax.axis_size(self.axis)):
            dst = src
            for (stride, size), step in zip(self.digits, steps):
                own = src // stride % size
                dst += ((own + step) % size - own) * stride
            pairs.append((src, dst))
        if self.tied and self.last is not None:
            value = after(value, self.last)
        self.last = lax.ppermute(value, self.axis, pairs)
        return self.last

    def sends(self, value):
        return [self.send(value, step) for step in range(1, self.size)]

    def gather(self, value):
        if self.size == 1:
            return value[None]
        here = self.here()
        out = jnp.zeros((self.size,) + value.shape, value.dtype)
        out = lax.dynamic_update_index_in_dim(out, value, here, 0)
        for step in range(1, self.size):
            got = self.send(value, step)
            out = lax.dynamic_update_index_in_dim(out, got, lax.rem(here - step + self.size, self.size), 0)
        return out

    def scatter(self, terms, dim, before=()):
        here = self.here()
        if self.size == 1:
            return [lax.index_in_dim(t, 0, dim, keepdims=False) for t in terms]
        out = [lax.dynamic_index_in_dim(t, here, dim, keepdims=False) for t in terms]
        for step in range(1, self.size):
            there = lax.rem(here + step, self.size)
            term = total([lax.dynamic_index_in_dim(t, there, dim, keepdims=False) for t in terms]).astype(BF16)
            out.append(self.send(after(term, *before), step))
        return out


def slot(place, values):
    values = lax.optimization_barrier(values)
    place.crossed = None
    for ring in [place.y, place.core] + place.dp + list(place.links.values()):
        ring.last = None
    return values


class Sum:
    def __init__(self, arrays, rings, tail):
        self.left = rings
        dims = [ring.size if isinstance(ring, Ring) else ring for ring in rings]
        self.arrays = [a.reshape(dims + list(tail)) for a in arrays]
        self.rings = [rings] * len(arrays)

    def cut(self, ring=None, index=None):
        out = []
        for array, rings in zip(self.arrays, self.rings):
            dim = 0
            for r in rings:
                if isinstance(r, Ring) and (r is ring or r not in self.left):
                    array = lax.dynamic_index_in_dim(array, index if r is ring else r.here(), dim, keepdims=False)
                else:
                    dim += 1
            out.append(array)
        return total(out)

    def step(self, ring):
        if ring not in self.left:
            return
        rest = [r for r in self.left if r is not ring]
        parts = [self.cut(ring, lax.rem(ring.here() + step, ring.size)).astype(BF16) for step in range(1, ring.size)]
        got = [ring.send(part, step + 1) for step, part in enumerate(parts)]
        self.arrays, self.rings, self.left = self.arrays + got, self.rings + [rest] * len(got), rest

    def finish(self):
        for ring in [r for r in self.left[::-1] if isinstance(r, Ring)]:
            self.step(ring)
        return self.cut()


def total(terms):
    return functools.reduce(jnp.add, [t.astype(F32) for t in terms])


def after(value, *others):
    if not others:
        return value
    return lax.optimization_barrier((value,) + others)[0]


def turned_back(here, step, size):
    return lax.rem(here - step + size, size)


class Place:
    def __init__(self, share, n_dp):
        self.far, self.near = halves(share)
        self.y, self.core = Ring("tensor", (self.near, self.far)), Ring("tensor", (1, self.near), tied=False)
        self.dp, stride = [], 1
        while stride < n_dp:
            size = next(p for p in range(2, n_dp + 1) if n_dp // stride % p == 0)
            self.dp.append(Ring("dp", (stride, size)))
            stride *= size
        self.steps = [(y, c) for y in range(self.far) for c in range(self.near)]
        self.crossed = None
        self.links = {step: Ring("tensor", (self.near, self.far), (1, self.near)) for step in self.steps[1:]}
        self.rows = [ring.size for ring in self.dp]

    def position(self):
        return jnp.stack([ring.here() for ring in [self.y, self.core] + self.dp]).astype(jnp.int32)

    def onward(self, pos, n):
        y, c = self.steps[n]
        return lax.rem(pos[0] + y, self.far) * self.near + lax.rem(pos[1] + c, self.near)

    def source(self, pos, n):
        y, c = self.steps[n]
        return turned_back(pos[0], y, self.far) * self.near + turned_back(pos[1], c, self.near)

    def exchange(self, pieces, n):
        y, c = self.steps[n]
        piece = pieces[n]
        if y == 0:
            return self.core.send(piece, c)
        if self.crossed is not None:
            piece = after(piece, self.crossed)
        self.crossed = self.y.send(piece, y) if c == 0 else self.links[(y, c)].send(piece, y, c)
        return self.crossed


def piece_copies(place, pos_ref, pieces, whole, sems):
    copies = []
    order = range(len(place.dp))
    home, rows, _ = pieces[0][0].shape[-3:]
    inner = [range(place.rows[n]) for n in order[1:]]
    for c, row in enumerate(pieces):
        for d, ref in enumerate(row):
            lead = ref.shape[:-3]
            for back in itertools.product(*inner, range(lead[-1])):
                at = 0
                for n, step in zip(order, (d,) + back[:-1]):
                    at += turned_back(pos_ref[2 + n], step, place.rows[n]) * place.dp[n].stride
                group = 0
                if len(pieces) > 1 or lead[-1] > 1:
                    group = turned_back(pos_ref[0], back[-1], place.far) * place.near + turned_back(pos_ref[1], c, place.near)
                dst = whole.at[pl.ds(group * home, home), pl.ds(pl.multiple_of(at * rows, rows), rows), :]
                copies.append(pltpu.make_async_copy(ref.at[back], dst, sems.at[len(copies)]))
    return copies


def share_copies(place, pos_ref, parts, whole, sems):
    return [pltpu.make_async_copy(ref, whole.at[place.source(pos_ref, n)], sems.at[n]) for n, ref in enumerate(parts)]


def run(copies):
    for copy in copies:
        copy.start()


def finish(copies):
    for copy in copies:
        copy.wait()


def n_copies(place):
    return place.far * place.near * math.prod(place.rows)


def anywhere(count):
    return [pl.BlockSpec(memory_space=pl.ANY)] * count


def flat(pieces):
    return tuple(p for row in pieces for p in row)


def unflat(place, refs):
    wide = len(refs) // place.near
    return [refs[c * wide : (c + 1) * wide] for c in range(place.near)]


def deal_kernel(pos_ref, g_ref, out_ref, turned):
    home, size, _ = g_ref.shape
    pitch = home + PAD

    def store(o):
        turned[pl.ds(o, size, stride=pitch), :] = g_ref[o].astype(F32)

    def load(b):
        out_ref[b] = turned[pl.ds(pl.multiple_of(b * pitch, 8), home), :].astype(BF16)

    each(home, store)
    each(size, load)


def deal(place, pos, g_home, cut, n):
    home, size, _ = g_home.shape
    return call(
        deal_kernel,
        shape((size, home, cut)),
        (1,),
        [pl.BlockSpec((home, size, cut), lambda i, pos: (0, 0, place.onward(pos, n)))],
        pl.BlockSpec((size, home, cut), lambda i, pos: (0, 0, 0)),
        [pltpu.VMEM((size * (home + PAD), cut), F32)],
        (g_home,),
        us=3.5,
        scalars=pos,
    )


def first_kernel(place, pos_ref, x_ref, w_ref, *refs):
    *out_refs, turned = refs
    home, size, _ = x_ref.shape
    cut = out_refs[0].shape[2]
    pitch = home + PAD

    for n, out_ref in enumerate(out_refs):

        @pl.when(pl.program_id(0) == n)
        def _():
            lanes = pl.ds(pl.multiple_of(place.onward(pos_ref, n) * cut, cut), cut)

            def store(b):
                turned[pl.ds(b, size, stride=pitch), :] = dot_tn(w_ref[b], x_ref[b, :, lanes])

            def load(o):
                out_ref[o] = turned[pl.ds(pl.multiple_of(o * pitch, 8), home), :].astype(BF16)

            each(home, store)
            each(size, load)


def first_stage(place, pos, x_home, left_one, cut):
    home, size, tokens = x_home.shape
    share = tokens // cut
    return call(
        functools.partial(first_kernel, place),
        (shape((size, home, cut)),) * share,
        (share,),
        [
            pl.BlockSpec((home, size, tokens), lambda s, pos: (0, 0, 0)),
            pl.BlockSpec((home, size, size), lambda s, pos: (0, 0, 0)),
        ],
        (pl.BlockSpec((size, home, cut), lambda s, pos: (0, 0, 0)),) * share,
        [pltpu.VMEM((size * (home + PAD), cut), F32)],
        (x_home, left_one),
        us=8,
        scalars=pos,
    )


def last_kernel(place, pos_ref, *refs):
    share = place.far * place.near
    e_refs = refs[:share]
    x_ref, g_ref, w_ref, out_ref, grad_ref, turned = refs[share:]
    blocks, per, cut = e_refs[0].shape
    pitch = blocks + PAD

    for n in range(share):
        s = place.source(pos_ref, n)

        def store(o):
            turned[s, pl.ds(o, per, stride=pitch), :] = e_refs[n][o].astype(F32)

        each(blocks, store)

    def load(b):
        rows = pl.ds(pl.multiple_of(b * pitch, 8), blocks)
        e_b = jnp.concatenate([turned[s, rows, :].astype(BF16) for s in range(share)], axis=1)
        out_ref[b] = (g_ref[b].astype(F32) + dot_nn(w_ref[b], e_b)).astype(BF16)
        grad_ref[b] = dot_nt(x_ref[b], e_b).astype(BF16)

    each(per, load, 4)


def last_stage(place, pos, e_got, x_home, g_home, left_one):
    share = len(e_got)
    blocks, home, cut = e_got[0].shape
    _, size, tokens = x_home.shape
    per = math.gcd(home, 16)
    wide = pl.BlockSpec((per, size, tokens), lambda h, pos: (h, 0, 0))
    factor = pl.BlockSpec((per, size, size), lambda h, pos: (h, 0, 0))
    return call(
        functools.partial(last_kernel, place),
        (shape(g_home.shape), shape((home, size, size))),
        (home // per,),
        [pl.BlockSpec((blocks, per, cut), lambda h, pos: (0, h, 0))] * share + [wide, wide, factor],
        (wide, factor),
        [pltpu.VMEM((share, per * (blocks + PAD), cut), F32)],
        (*e_got, x_home, g_home, left_one),
        us=10,
        scalars=pos,
    )


def mixed_kernel(place, pos_ref, *refs):
    *s_refs, x_ref, out_ref = refs
    cut = s_refs[0].shape[2]
    for n, s_ref in enumerate(s_refs):
        lanes = pl.ds(pl.multiple_of(place.source(pos_ref, n) * cut, cut), cut)
        out_ref[:, :, lanes] = (x_ref[:, :, lanes].astype(F32) + s_ref[...].astype(F32)).astype(BF16)


def add_home(place, pos, s_got, x_home):
    home, blocks, cut = s_got[0].shape
    per = math.gcd(home, 8)
    wide = pl.BlockSpec((per,) + x_home.shape[1:], lambda h, pos: (h, 0, 0))
    return call(
        functools.partial(mixed_kernel, place),
        shape(x_home.shape),
        (home // per,),
        [pl.BlockSpec((per, blocks, cut), lambda h, pos: (h, 0, 0))] * len(s_got) + [wide],
        wide,
        [],
        (*s_got, x_home),
        us=6,
        scalars=pos,
    )


def join_kernel(place, pos_ref, *refs):
    *pieces, out_ref, sems = refs
    copies = piece_copies(place, pos_ref, [pieces], out_ref, sems)
    run(copies)
    finish(copies)


def join(place, pos, pieces):
    home, rows, size = pieces[0].shape[-3:]
    return call(
        functools.partial(join_kernel, place),
        shape((home, rows * math.prod(place.rows), size)),
        (1,),
        anywhere(len(pieces)),
        pl.BlockSpec((home, rows * math.prod(place.rows), size), lambda i, pos: (0, 0, 0)),
        [pltpu.SemaphoreType.DMA((math.prod(place.rows),))],
        tuple(pieces),
        us=3,
        scalars=pos,
    )


def back_two_kernel(place, pos_ref, *refs):
    share = place.far * place.near
    g_parts, factor = refs[:share], unflat(place, refs[share:-6])
    out_ref, turned, g_all, w_all, g_sems, w_sems = refs[-6:]
    per, size, _ = out_ref.shape
    pitch = size + PAD
    phase, j = pl.program_id(0), pl.program_id(1)

    @pl.when((phase == 0) & (j == 0))
    def _():
        copies = share_copies(place, pos_ref, g_parts, g_all, g_sems) + piece_copies(place, pos_ref, factor, w_all, w_sems)
        run(copies)
        finish(copies)

    @pl.when(phase == 0)
    def _():
        def body(k):
            b = j * per + k
            turned[pl.ds(b, size, stride=pitch), :] = dot_nn(w_all[b], stacked(g_all, b))

        each(per, body)

    @pl.when(phase == 1)
    def _():
        def body(k):
            out_ref[k] = turned[pl.ds(pl.multiple_of((j * per + k) * pitch, 8), size), :].astype(BF16)

        each(per, body)


def middle_sizes(place, parts):
    blocks, home, cut = parts[0].shape
    return blocks, home, cut, len(parts), (blocks, blocks, blocks)


def back_two(place, pos, g_mid, right_two):
    blocks, home, cut, share, whole = middle_sizes(place, g_mid)
    at = during(1, share)
    return call(
        functools.partial(back_two_kernel, place),
        shape((blocks, blocks, cut)),
        (2, share),
        anywhere(share + len(flat(right_two))),
        pl.BlockSpec((home, blocks, cut), lambda p, j, pos: (at(p, j), 0, 0)),
        [
            pltpu.VMEM((blocks * (blocks + PAD), cut), F32),
            pltpu.VMEM((share, blocks, home, cut), BF16),
            pltpu.VMEM(whole, BF16),
            pltpu.SemaphoreType.DMA((share,)),
            pltpu.SemaphoreType.DMA((n_copies(place),)),
        ],
        (*g_mid, *flat(right_two)),
        us=10,
        scalars=pos,
    )


def either(place, pos_ref, j, keep_ref, send_ref, body):
    mine = lax.rem(j, place.near) == pos_ref[1]

    @pl.when(mine)
    def _():
        body(keep_ref)

    @pl.when(jnp.logical_not(mine))
    def _():
        body(send_ref)


def middle_kernel(place, pos_ref, *refs):
    share = place.far * place.near
    wide = (len(refs) - (2 * share + 15)) // 2
    s_parts, rest = refs[:share], refs[share:]
    one, two, rest = unflat(place, rest[:wide]), unflat(place, rest[wide : 2 * wide]), rest[2 * wide :]
    e_ref, act_ref, keep_two, send_two, keep_one, send_one, *rest = rest
    out_refs, rest = rest[:share], rest[share:]
    turned, hidden, e_one, s_all, one_all, two_all, s_sems, one_sems, two_sems = rest
    per, size, cut = act_ref.shape
    home = s_all.shape[2]
    pitch = size + PAD
    phase, j = pl.program_id(0), pl.program_id(1)

    def rows(k):
        return pl.ds(pl.multiple_of((j * per + k) * pitch, 8), size)

    def column(k):
        return pl.ds(j * per + k, size, stride=pitch)

    def second():
        return piece_copies(place, pos_ref, two, two_all, two_sems)

    @pl.when((phase == 0) & (j == 0))
    def _():
        copies = share_copies(place, pos_ref, s_parts, s_all, s_sems) + piece_copies(place, pos_ref, one, one_all, one_sems)
        run(copies)
        run(second())
        finish(copies)

    @pl.when(phase == 0)
    def _():
        def body(k):
            b = j * per + k
            turned[column(k), :] = dot_tn(one_all[b], stacked(s_all, b))

        each(per, body)

    @pl.when((phase == 1) & (j == 0))
    def _():
        finish(second())

    @pl.when(phase == 1)
    def _():
        def with_out(grad_ref):
            def body(k):
                v = turned[rows(k), :].astype(BF16).astype(F32)
                value, slope = gelu_both(v)
                act = value.astype(BF16)
                act_ref[k] = act
                e = e_ref[k]
                hidden[column(k), :] = slope * dot_nn(two_all[j * per + k], e)
                grad_ref[0, k] = dot_nt(act, e).astype(BF16)

            each(per, body, 8)

        either(place, pos_ref, j, keep_two, send_two, with_out)

    @pl.when(phase == 2)
    def _():
        def with_out(grad_ref):
            def body(k):
                b = j * per + k
                h = hidden[rows(k), :].astype(BF16)
                e_one[k] = dot_nn(one_all[b], h).astype(BF16)
                grad_ref[0, k] = dot_nt(stacked(s_all, b), h).astype(BF16)

            each(per, body)

        either(place, pos_ref, j, keep_one, send_one, with_out)
        for n in range(share):
            at = pl.ds(pl.multiple_of(place.onward(pos_ref, n) * home, home), home)
            out_refs[n][...] = e_one[:, at, :]


def grad_specs(place, phase, home, size, share):
    at = during(phase, share)
    dims = shape((place.far, home, size, size))
    spec = pl.BlockSpec((1, home, size, size), lambda p, j, pos: (at(p, j) // place.near, 0, 0, 0))
    return [dims] * 2, [spec] * 2


def middle(place, pos, s_mid, e_mid, right_one, left_two):
    blocks, home, cut, share, whole = middle_sizes(place, s_mid)
    at = [during(phase, share) for phase in range(3)]
    block = pl.BlockSpec((home, blocks, cut), lambda p, j, pos: (at[1](p, j), 0, 0))
    two, two_specs = grad_specs(place, 1, home, blocks, share)
    one, one_specs = grad_specs(place, 2, home, blocks, share)
    piece = pl.BlockSpec((home, home, cut), lambda p, j, pos: (at[2](p, j), 0, 0))
    out = call(
        functools.partial(middle_kernel, place),
        (shape((blocks, blocks, cut)), *two, *one) + (shape((blocks, home, cut)),) * share,
        (3, share),
        anywhere(share + 2 * len(flat(right_one))) + [block],
        (block, *two_specs, *one_specs) + (piece,) * share,
        [pltpu.VMEM((blocks * (blocks + PAD), cut), F32)] * 2
        + [
            pltpu.VMEM((home, blocks, cut), BF16),
            pltpu.VMEM((share, blocks, home, cut), BF16),
            pltpu.VMEM(whole, BF16),
            pltpu.VMEM(whole, BF16),
            pltpu.SemaphoreType.DMA((share,)),
            pltpu.SemaphoreType.DMA((n_copies(place),)),
            pltpu.SemaphoreType.DMA((n_copies(place),)),
        ],
        (*s_mid, *flat(right_one), *flat(left_two), e_mid),
        us=26,
        scalars=pos,
    )
    return out[0], out[1:3], out[3:5], list(out[5:])


def forward_two_kernel(place, pos_ref, *refs):
    share = place.far * place.near
    wide = (len(refs) - (2 * share + 11)) // 2
    g_parts, rest = refs[:share], refs[share:]
    left, right, rest = unflat(place, rest[:wide]), unflat(place, rest[wide : 2 * wide]), rest[2 * wide :]
    act_ref, keep_ref, send_ref, *rest = rest
    out_refs, rest = rest[:share], rest[share:]
    turned, fourth, g_all, left_all, right_all, g_sems, left_sems, right_sems = rest
    per, size, _ = act_ref.shape
    pitch = size + PAD
    phase, j = pl.program_id(0), pl.program_id(1)

    def rows(k):
        return pl.ds(pl.multiple_of((j * per + k) * pitch, 8), size)

    def column(k):
        return pl.ds(j * per + k, size, stride=pitch)

    def second():
        return piece_copies(place, pos_ref, right, right_all, right_sems) + share_copies(place, pos_ref, g_parts, g_all, g_sems)

    @pl.when((phase == 0) & (j == 0))
    def _():
        copies = piece_copies(place, pos_ref, left, left_all, left_sems)
        run(copies)
        run(second())
        finish(copies)

    @pl.when(phase == 0)
    def _():
        def body(k):
            turned[column(k), :] = dot_tn(left_all[j * per + k], act_ref[k])

        each(per, body)

    @pl.when((phase == 1) & (j == 0))
    def _():
        finish(second())

    @pl.when(phase == 1)
    def _():
        def with_out(grad_ref):
            def body(k):
                b = j * per + k
                third = turned[rows(k), :].astype(BF16)
                fourth[column(k), :] = dot_tn(right_all[b], third)
                grad_ref[0, k] = dot_nt(third, stacked(g_all, b)).astype(BF16)

            each(per, body)

        either(place, pos_ref, j, keep_ref, send_ref, with_out)

    for n in range(share):

        @pl.when((phase == 2) & (j == n))
        def _():
            base = place.onward(pos_ref, n) * per

            def body(k):
                out_refs[n][k] = fourth[pl.ds(pl.multiple_of((base + k) * pitch, 8), size), :].astype(BF16)

            each(per, body)


def forward_two(place, pos, act, g_mid, left_two, right_two):
    blocks, home, cut, share, whole = middle_sizes(place, g_mid)
    at = during(0, share)
    grad, grad_spec = grad_specs(place, 1, home, blocks, share)
    out = call(
        functools.partial(forward_two_kernel, place),
        (*grad,) + (shape((home, blocks, cut)),) * share,
        (3, share),
        anywhere(share + 2 * len(flat(left_two))) + [pl.BlockSpec((home, blocks, cut), lambda p, j, pos: (at(p, j), 0, 0))],
        (*grad_spec,) + (pl.BlockSpec((home, blocks, cut), lambda p, j, pos: (0, 0, 0)),) * share,
        [pltpu.VMEM((blocks * (blocks + PAD), cut), F32)] * 2
        + [
            pltpu.VMEM((share, blocks, home, cut), BF16),
            pltpu.VMEM(whole, BF16),
            pltpu.VMEM(whole, BF16),
            pltpu.SemaphoreType.DMA((share,)),
            pltpu.SemaphoreType.DMA((n_copies(place),)),
            pltpu.SemaphoreType.DMA((n_copies(place),)),
        ],
        (*g_mid, *flat(left_two), *flat(right_two), act),
        us=20,
        scalars=pos,
    )
    return out[:2], list(out[2:])


def halves(size):
    low = 2 if size % 2 == 0 else 1
    return size // low, low


def cross(pieces):
    return lax.all_to_all(pieces, "tensor", split_axis=0, concat_axis=0, tiled=True)


def whole_tokens(x_home, g_home, factors, share, cut):
    home, size, tokens = x_home.shape
    first_left = factors[0]
    rows = first_left.shape[1]
    place = Place(share, lax.axis_size("dp"))
    pos = place.position()

    def gather(start, skip, *before):
        ring = place.dp[skip]
        got = [start] + ring.sends(after(start, *before))
        return got if skip == 0 else jnp.stack(got)

    def gathers(start):
        for n in reversed(range(1, len(place.dp))):
            start = gather(start, n)
        return start

    last_dp = (lambda start: gather(start, 0)) if place.dp else (lambda start: [start])

    def cores(piece):
        return [piece] + place.core.sends(piece)

    def by_core(own):
        return [[p[c] for p in own] for c in range(place.near)]

    def cross(pieces, n):
        return place.exchange(pieces, n) if n < share else None

    n_one, n_two, n_three = (place.steps.index(step) if step in place.steps else share for step in [(0, 1), (1, 0), (1, 1)])
    mine = jnp.stack([factors[3], factors[1], factors[2]])
    from_y = [mine] + place.y.sends(mine)
    one = first_left
    g = {n: deal(place, pos, g_home, cut, n) for n in range(share) if n >= 2}
    from_y, g = slot(place, (from_y, g))

    wholes = [jnp.stack([part[n] for part in from_y]) for n in range(3)]
    got_three = cross(g, n_three)
    one = last_dp(gathers(one))
    wholes[0] = gathers(wholes[0])
    g |= {n: deal(place, pos, g_home, cut, n) for n in range(share) if n < 2}
    got_one = cross(g, n_one)
    got_three, got_one, one, wholes, g = slot(place, (got_three, got_one, one, wholes, g))

    got_two = cross(g, n_two)
    right_two = last_dp(wholes[0])
    wholes[1] = gathers(wholes[1])
    one = join(place, pos, [p[..., None, :, :, :] for p in one])
    s = first_stage(place, pos, x_home, one, cut)
    got_two, right_two, wholes, one, s = slot(place, (got_two, right_two, wholes, one, list(s)))
    g_mid = [g[0], got_one, got_two, got_three][:share]

    got_three = cross(s, n_three)
    got_one = cross(s, n_one)
    right_one = last_dp(wholes[1])
    wholes[2] = gathers(wholes[2])
    right_two = by_core([cores(p) for p in right_two])
    got_three, got_one, right_one, wholes, right_two = slot(place, (got_three, got_one, right_one, wholes, right_two))

    got_two = cross(s, n_two)
    left_two = last_dp(wholes[2])
    left_core = cores(left_two[0])
    right_one = by_core([cores(p) for p in right_one])
    e_mid = back_two(place, pos, g_mid, right_two)
    got_two, left_two, left_core, right_one, e_mid = slot(place, (got_two, left_two, left_core, right_one, e_mid))
    s_mid = [s[0], got_one, got_two, got_three][:share]
    left_two = by_core([left_core] + [cores(p) for p in left_two[1:]])

    act, grad_two, grad_one, e = middle(place, pos, s_mid, e_mid, right_one, left_two)

    def start_sum(keep, send):
        arrays = [keep, place.core.send(send, 1)] if place.near > 1 else [keep]
        return Sum(arrays, [place.y, home] + place.dp[::-1], (rows, size))

    def hold(parts, arrays):
        for part, kept in zip(parts, arrays):
            part.arrays = kept

    def arrays_of(*parts):
        return [part.arrays for part in parts]

    x_step, near_step, far_step = (place.dp + [None] * 3)[:3]

    e_three = cross(e, n_three)
    two = start_sum(*grad_two)
    grad_three, s = forward_two(place, pos, act, g_mid, left_two, right_two)
    e_three, kept, grad_three, s, e, grad_one = slot(place, (e_three, arrays_of(two), grad_three, s, e, grad_one))
    hold([two], kept)

    e_two = cross(e, n_two)
    two.step(x_step)
    one_part, three = start_sum(*grad_one), start_sum(*grad_three)
    e_one = cross(e, n_one)
    e_two, e_one, kept, s = slot(place, (e_two, e_one, arrays_of(two, one_part, three), s))
    hold([two, one_part, three], kept)
    e_got = [e[0], e_one, e_two, e_three][:share]

    s_three = cross(s, n_three)
    three.step(x_step)
    one_part.step(near_step)
    input_grad, lone = last_stage(place, pos, e_got, x_home, g_home, one)
    s_three, kept, lone, input_grad, s = slot(place, (s_three, arrays_of(two, one_part, three), lone, input_grad, s))
    hold([two, one_part, three], kept)
    lone = Sum([lone], [home] + place.dp[::-1], (rows, size))

    s_two, s_one = cross(s, n_two), cross(s, n_one)
    one_part.step(x_step)
    two.step(near_step)
    three.step(near_step)
    lone.step(x_step)
    one_part.step(far_step)
    two.step(far_step)
    s_got = [s[0], s_one, s_two, s_three][:share]
    grad_rone = one_part.finish()
    lone.step(near_step)
    grad_ltwo = two.finish()
    three.step(far_step)
    grad_lone = lone.finish()
    grad_rtwo = three.finish()
    mixed = add_home(place, pos, s_got, x_home)
    return mixed, input_grad, grad_lone, grad_rone, grad_ltwo, grad_rtwo


def split_blocks(x_home, g_home, factors, share, cut):
    home, size, tokens = x_home.shape
    far, near = halves(share)
    outer, inner = halves(lax.axis_size("dp"))
    ring_y, ring_core = Ring("tensor", (near, far)), Ring("tensor", (1, near))
    ring_z, ring_x = Ring("dp", (inner, outer)), Ring("dp", (1, inner))
    rows = factors[0].shape[1]
    n_tensor = lax.axis_size("tensor")
    groups = n_tensor // share
    held = home * share
    same_tokens = [[group * share + part for group in range(groups)] for part in range(share)]

    def go(values):
        pieces = values.reshape(home, groups, held, share, cut).transpose(1, 3, 2, 0, 4)
        got = cross(pieces.reshape(n_tensor, held, home, cut))
        return got.transpose(1, 0, 2, 3).reshape(held, size, cut)

    def back(values):
        pieces = values.reshape(held, n_tensor, home, cut).transpose(1, 0, 2, 3)
        got = cross(pieces).reshape(groups, share, held, home, cut)
        return got.transpose(3, 0, 2, 1, 4).reshape(home, size, tokens)

    def turn(values):
        moved = lax.all_to_all(
            values.reshape(held, groups, held, cut), "tensor", split_axis=1, concat_axis=0, tiled=True, axis_index_groups=same_tokens
        )
        return jnp.swapaxes(moved.reshape(size, held, cut), 0, 1)

    def whole(factor):
        one = ring_z.gather(ring_y.gather(factor))
        all_rows = ring_core.gather(ring_x.gather(one))
        return all_rows.transpose(3, 0, 4, 2, 1, 5, 6).reshape(held, size, size)

    def own_sum(partial):
        split = partial.reshape(ring_y.size, ring_core.size, home, ring_z.size, ring_x.size, rows, size)
        terms = ring_core.scatter([split], 1)
        return total(ring_y.scatter(ring_z.scatter(ring_x.scatter(terms, 3), 2), 0))

    first_left, first_right, second_left, second_right = factors
    g_mid = go(g_home)
    left_one = ring_x.gather(ring_z.gather(first_left)).transpose(2, 1, 0, 3, 4).reshape(home, size, size)
    right_one, left_two, right_two = whole(first_right), whole(second_left), whole(second_right)

    s_one = go(product("bjt,bjo->bot", x_home, left_one).astype(BF16))
    s_two = turn(product("bit,bip->bpt", s_one, right_one).astype(BF16))
    act = gelu_value(s_two.astype(F32)).astype(BF16)
    e_three = turn(product("bot,bio->bit", g_mid, right_two).astype(BF16))
    h_mid = turn(gelu_back(s_two.astype(F32), product("bot,bjo->bjt", e_three, left_two)).astype(BF16))
    e_one = back(product("bpt,bip->bit", h_mid, right_one).astype(BF16))
    s_three = turn(product("bjt,bjo->bot", act, left_two).astype(BF16))
    s_four = back(product("bit,bio->bot", s_three, right_two).astype(BF16))
    mixed = (x_home.astype(F32) + s_four.astype(F32)).astype(BF16)

    grad_rtwo = own_sum(product("bit,bot->bio", s_three, g_mid))
    grad_ltwo = own_sum(product("bjt,bot->bjo", act, e_three))
    grad_rone = own_sum(product("bit,bpt->bip", s_one, h_mid))
    grad_lone = product("bjt,bot->bjo", x_home, e_one).reshape(home, ring_z.size, ring_x.size, rows, size)
    grad_lone = total(ring_z.scatter(ring_x.scatter([grad_lone], 2), 1))
    input_grad = (g_home.astype(F32) + product("bot,bjo->bjt", e_one, left_one)).astype(BF16)
    return mixed, input_grad, grad_lone, grad_rone, grad_ltwo, grad_rtwo


def per_device(inputs, cotangent, first_left, first_right, second_left, second_right):
    n_tensor = lax.axis_size("tensor")
    home, _, size = first_left.shape
    tokens = inputs.shape[1]
    share = math.gcd(n_tensor, max(1, tokens // LANES))
    cut = tokens // share
    plan = whole_tokens if share == n_tensor else split_blocks
    mixed, input_grad, *weight_grads = plan(
        inputs.reshape(home, size, tokens),
        cotangent.reshape(home, size, tokens),
        (first_left, first_right, second_left, second_right),
        share,
        cut,
    )
    return (mixed.reshape(inputs.shape), input_grad.reshape(inputs.shape), *weight_grads)


def solution(mesh):
    wide, factor = P("tensor", "dp"), P("tensor", "dp", None)
    return jax.shard_map(
        per_device,
        mesh=mesh,
        in_specs=(wide, wide, factor, factor, factor, factor),
        out_specs=(wide, wide, factor, factor, factor, factor),
        check_vma=False,
    )
```

```python
import functools
import itertools
import math

import jax
import jax.numpy as jnp
from jax import lax
from jax.experimental import pallas as pl
from jax.experimental.pallas import tpu as pltpu
from jax.sharding import PartitionSpec as P

BF16 = jnp.bfloat16
F32 = jnp.float32
LANES = 128
PAD = 1
VMEM_BYTES = 60 * 1024 * 1024
BYTES_PER_US = 1_200_000


def gelu_value(values):
    return jax.nn.gelu(values, approximate=True)


def gelu_back(values, upstream):
    return jax.vjp(gelu_value, values)[1](upstream)[0]


def gelu_both(v):
    root, cubic = 0.7978845608028654, 0.044715
    square = v * v
    t = jnp.tanh(root * (v + cubic * (v * square)))
    half = 0.5 * (1.0 + t)
    slope = half + (0.5 * v) * (1.0 - t * t) * (root + (3.0 * cubic * root) * square)
    return v * half, slope


def product(form, left, right):
    return jnp.einsum(form, left, right, preferred_element_type=F32)


def dot_nn(left, right):
    return lax.dot_general(left, right, (((1,), (0,)), ((), ())), preferred_element_type=F32)


def dot_tn(left, right):
    return lax.dot_general(left, right, (((0,), (0,)), ((), ())), preferred_element_type=F32)


def dot_nt(left, right):
    return lax.dot_general(left, right, (((1,), (1,)), ((), ())), preferred_element_type=F32)


def call(body, out, grid, in_specs, out_specs, scratch, args, us, scalars=None):
    spec = pltpu.PrefetchScalarGridSpec(
        num_scalar_prefetch=0 if scalars is None else 1,
        grid=grid,
        in_specs=in_specs,
        out_specs=out_specs,
        scratch_shapes=scratch,
    )
    return pl.pallas_call(
        body,
        out_shape=out,
        grid_spec=spec,
        compiler_params=pltpu.CompilerParams(
            dimension_semantics=("arbitrary",) * len(grid), vmem_limit_bytes=VMEM_BYTES
        ),
        cost_estimate=pl.CostEstimate(flops=0, bytes_accessed=int(us * BYTES_PER_US), transcendentals=0),
    )(*(() if scalars is None else (scalars,)), *args)


def shape(dims, dtype=BF16):
    return jax.ShapeDtypeStruct(dims, dtype)


def each(count, body, unroll=16):
    def step(k, carry):
        body(k)
        return carry

    lax.fori_loop(0, count, step, 0, unroll=math.gcd(count, unroll))


def during(phase, steps):
    return lambda p, j: jnp.where(p == phase, j, jnp.where(p < phase, 0, steps - 1))


def stacked(ref, k):
    return jnp.concatenate([ref[c, k] for c in range(ref.shape[0])], axis=0)


class Ring:
    def __init__(self, axis, *digits, tied=True):
        self.axis, self.digits, self.last, self.tied = axis, digits, None, tied
        self.stride, self.size = digits[0]

    def here(self):
        return lax.rem(lax.axis_index(self.axis) // self.stride, self.size)

    def send(self, value, *steps):
        pairs = []
        for src in range(lax.axis_size(self.axis)):
            dst = src
            for (stride, size), step in zip(self.digits, steps):
                own = src // stride % size
                dst += ((own + step) % size - own) * stride
            pairs.append((src, dst))
        if self.tied and self.last is not None:
            value = after(value, self.last)
        self.last = lax.ppermute(value, self.axis, pairs)
        return self.last

    def sends(self, value):
        return [self.send(value, step) for step in range(1, self.size)]

    def gather(self, value):
        if self.size == 1:
            return value[None]
        here = self.here()
        out = jnp.zeros((self.size,) + value.shape, value.dtype)
        out = lax.dynamic_update_index_in_dim(out, value, here, 0)
        for step in range(1, self.size):
            got = self.send(value, step)
            out = lax.dynamic_update_index_in_dim(out, got, lax.rem(here - step + self.size, self.size), 0)
        return out

    def scatter(self, terms, dim, before=()):
        here = self.here()
        if self.size == 1:
            return [lax.index_in_dim(t, 0, dim, keepdims=False) for t in terms]
        out = [lax.dynamic_index_in_dim(t, here, dim, keepdims=False) for t in terms]
        for step in range(1, self.size):
            there = lax.rem(here + step, self.size)
            term = total([lax.dynamic_index_in_dim(t, there, dim, keepdims=False) for t in terms]).astype(BF16)
            out.append(self.send(after(term, *before), step))
        return out


def slot(place, values):
    values = lax.optimization_barrier(values)
    place.crossed = None
    for ring in [place.y, place.core] + place.dp + list(place.links.values()):
        ring.last = None
    return values


class Sum:
    def __init__(self, arrays, rings, tail):
        self.left = rings
        dims = [ring.size if isinstance(ring, Ring) else ring for ring in rings]
        self.arrays = [a.reshape(dims + list(tail)) for a in arrays]
        self.rings = [rings] * len(arrays)

    def cut(self, ring=None, index=None):
        out = []
        for array, rings in zip(self.arrays, self.rings):
            dim = 0
            for r in rings:
                if isinstance(r, Ring) and (r is ring or r not in self.left):
                    array = lax.dynamic_index_in_dim(array, index if r is ring else r.here(), dim, keepdims=False)
                else:
                    dim += 1
            out.append(array)
        return total(out)

    def step(self, ring):
        if ring not in self.left:
            return
        rest = [r for r in self.left if r is not ring]
        parts = [self.cut(ring, lax.rem(ring.here() + step, ring.size)).astype(BF16) for step in range(1, ring.size)]
        got = [ring.send(part, step + 1) for step, part in enumerate(parts)]
        self.arrays, self.rings, self.left = self.arrays + got, self.rings + [rest] * len(got), rest

    def finish(self):
        for ring in [r for r in self.left[::-1] if isinstance(r, Ring)]:
            self.step(ring)
        return self.cut()


def total(terms):
    return functools.reduce(jnp.add, [t.astype(F32) for t in terms])


def after(value, *others):
    if not others:
        return value
    return lax.optimization_barrier((value,) + others)[0]


def turned_back(here, step, size):
    return lax.rem(here - step + size, size)


class Place:
    def __init__(self, share, n_dp):
        self.far, self.near = halves(share)
        self.y, self.core = Ring("tensor", (self.near, self.far)), Ring("tensor", (1, self.near), tied=False)
        self.dp, stride = [], 1
        while stride < n_dp:
            size = next(p for p in range(2, n_dp + 1) if n_dp // stride % p == 0)
            self.dp.append(Ring("dp", (stride, size)))
            stride *= size
        self.steps = [(y, c) for y in range(self.far) for c in range(self.near)]
        self.crossed = None
        self.links = {step: Ring("tensor", (self.near, self.far), (1, self.near)) for step in self.steps[1:]}
        self.rows = [ring.size for ring in self.dp]

    def position(self):
        return jnp.stack([ring.here() for ring in [self.y, self.core] + self.dp]).astype(jnp.int32)

    def onward(self, pos, n):
        y, c = self.steps[n]
        return lax.rem(pos[0] + y, self.far) * self.near + lax.rem(pos[1] + c, self.near)

    def source(self, pos, n):
        y, c = self.steps[n]
        return turned_back(pos[0], y, self.far) * self.near + turned_back(pos[1], c, self.near)

    def exchange(self, pieces, n):
        y, c = self.steps[n]
        piece = pieces[n]
        if y == 0:
            return self.core.send(piece, c)
        if self.crossed is not None:
            piece = after(piece, self.crossed)
        self.crossed = self.y.send(piece, y) if c == 0 else self.links[(y, c)].send(piece, y, c)
        return self.crossed


def piece_copies(place, pos_ref, pieces, whole, sems):
    copies = []
    order = range(len(place.dp))
    home, rows, _ = pieces[0][0].shape[-3:]
    inner = [range(place.rows[n]) for n in order[1:]]
    for c, row in enumerate(pieces):
        for d, ref in enumerate(row):
            lead = ref.shape[:-3]
            for back in itertools.product(*inner, range(lead[-1])):
                at = 0
                for n, step in zip(order, (d,) + back[:-1]):
                    at += turned_back(pos_ref[2 + n], step, place.rows[n]) * place.dp[n].stride
                group = 0
                if len(pieces) > 1 or lead[-1] > 1:
                    group = turned_back(pos_ref[0], back[-1], place.far) * place.near + turned_back(pos_ref[1], c, place.near)
                dst = whole.at[pl.ds(group * home, home), pl.ds(pl.multiple_of(at * rows, rows), rows), :]
                copies.append(pltpu.make_async_copy(ref.at[back], dst, sems.at[len(copies)]))
    return copies


def share_copies(place, pos_ref, parts, whole, sems):
    return [pltpu.make_async_copy(ref, whole.at[place.source(pos_ref, n)], sems.at[n]) for n, ref in enumerate(parts)]


def run(copies):
    for copy in copies:
        copy.start()


def finish(copies):
    for copy in copies:
        copy.wait()


def n_copies(place):
    return place.far * place.near * math.prod(place.rows)


def anywhere(count):
    return [pl.BlockSpec(memory_space=pl.ANY)] * count


def flat(pieces):
    return tuple(p for row in pieces for p in row)


def unflat(place, refs):
    wide = len(refs) // place.near
    return [refs[c * wide : (c + 1) * wide] for c in range(place.near)]


def deal_kernel(pos_ref, g_ref, out_ref, turned):
    home, size, _ = g_ref.shape
    pitch = home + PAD

    def store(o):
        turned[pl.ds(o, size, stride=pitch), :] = g_ref[o].astype(F32)

    def load(b):
        out_ref[b] = turned[pl.ds(b * pitch, home), :].astype(BF16)

    each(home, store)
    each(size, load)


def deal(place, pos, g_home, cut, n):
    home, size, _ = g_home.shape
    return call(
        deal_kernel,
        shape((size, home, cut)),
        (1,),
        [pl.BlockSpec((home, size, cut), lambda i, pos: (0, 0, place.onward(pos, n)))],
        pl.BlockSpec((size, home, cut), lambda i, pos: (0, 0, 0)),
        [pltpu.VMEM((size * (home + PAD), cut), F32)],
        (g_home,),
        us=3.5,
        scalars=pos,
    )


def first_kernel(place, pos_ref, x_ref, w_ref, *refs):
    *out_refs, turned = refs
    home, size, _ = x_ref.shape
    cut = out_refs[0].shape[2]
    pitch = home + PAD

    for n, out_ref in enumerate(out_refs):

        @pl.when(pl.program_id(0) == n)
        def _():
            lanes = pl.ds(pl.multiple_of(place.onward(pos_ref, n) * cut, cut), cut)

            def store(b):
                turned[pl.ds(b, size, stride=pitch), :] = dot_tn(w_ref[b], x_ref[b, :, lanes])

            def load(o):
                out_ref[o] = turned[pl.ds(o * pitch, home), :].astype(BF16)

            each(home, store)
            each(size, load)


def first_stage(place, pos, x_home, left_one, cut):
    home, size, tokens = x_home.shape
    share = tokens // cut
    return call(
        functools.partial(first_kernel, place),
        (shape((size, home, cut)),) * share,
        (share,),
        [
            pl.BlockSpec((home, size, tokens), lambda s, pos: (0, 0, 0)),
            pl.BlockSpec((home, size, size), lambda s, pos: (0, 0, 0)),
        ],
        (pl.BlockSpec((size, home, cut), lambda s, pos: (0, 0, 0)),) * share,
        [pltpu.VMEM((size * (home + PAD), cut), F32)],
        (x_home, left_one),
        us=8,
        scalars=pos,
    )


def last_kernel(place, pos_ref, *refs):
    share = place.far * place.near
    e_refs = refs[:share]
    x_ref, g_ref, w_ref, out_ref, grad_ref, turned = refs[share:]
    blocks, per, cut = e_refs[0].shape
    pitch = blocks + PAD

    for n in range(share):
        s = place.source(pos_ref, n)

        def store(o):
            turned[s, pl.ds(o, per, stride=pitch), :] = e_refs[n][o].astype(F32)

        each(blocks, store)

    def load(b):
        rows = pl.ds(b * pitch, blocks)
        e_b = jnp.concatenate([turned[s, rows, :].astype(BF16) for s in range(share)], axis=1)
        out_ref[b] = (g_ref[b].astype(F32) + dot_nn(w_ref[b], e_b)).astype(BF16)
        grad_ref[b] = dot_nt(x_ref[b], e_b).astype(BF16)

    each(per, load, 4)


def last_stage(place, pos, e_got, x_home, g_home, left_one):
    share = len(e_got)
    blocks, home, cut = e_got[0].shape
    _, size, tokens = x_home.shape
    per = math.gcd(home, 16)
    wide = pl.BlockSpec((per, size, tokens), lambda h, pos: (h, 0, 0))
    factor = pl.BlockSpec((per, size, size), lambda h, pos: (h, 0, 0))
    return call(
        functools.partial(last_kernel, place),
        (shape(g_home.shape), shape((home, size, size))),
        (home // per,),
        [pl.BlockSpec((blocks, per, cut), lambda h, pos: (0, h, 0))] * share + [wide, wide, factor],
        (wide, factor),
        [pltpu.VMEM((share, per * (blocks + PAD), cut), F32)],
        (*e_got, x_home, g_home, left_one),
        us=10,
        scalars=pos,
    )


def mixed_kernel(place, pos_ref, *refs):
    *s_refs, x_ref, out_ref = refs
    cut = s_refs[0].shape[2]
    for n, s_ref in enumerate(s_refs):
        lanes = pl.ds(pl.multiple_of(place.source(pos_ref, n) * cut, cut), cut)
        out_ref[:, :, lanes] = (x_ref[:, :, lanes].astype(F32) + s_ref[...].astype(F32)).astype(BF16)


def add_home(place, pos, s_got, x_home):
    home, blocks, cut = s_got[0].shape
    per = math.gcd(home, 8)
    wide = pl.BlockSpec((per,) + x_home.shape[1:], lambda h, pos: (h, 0, 0))
    return call(
        functools.partial(mixed_kernel, place),
        shape(x_home.shape),
        (home // per,),
        [pl.BlockSpec((per, blocks, cut), lambda h, pos: (h, 0, 0))] * len(s_got) + [wide],
        wide,
        [],
        (*s_got, x_home),
        us=6,
        scalars=pos,
    )


def join_kernel(place, pos_ref, *refs):
    *pieces, out_ref, sems = refs
    copies = piece_copies(place, pos_ref, [pieces], out_ref, sems)
    run(copies)
    finish(copies)


def join(place, pos, pieces):
    home, rows, size = pieces[0].shape[-3:]
    return call(
        functools.partial(join_kernel, place),
        shape((home, rows * math.prod(place.rows), size)),
        (1,),
        anywhere(len(pieces)),
        pl.BlockSpec((home, rows * math.prod(place.rows), size), lambda i, pos: (0, 0, 0)),
        [pltpu.SemaphoreType.DMA((math.prod(place.rows),))],
        tuple(pieces),
        us=3,
        scalars=pos,
    )


def back_two_kernel(place, pos_ref, *refs):
    share = place.far * place.near
    g_parts, factor = refs[:share], unflat(place, refs[share:-6])
    out_ref, turned, g_all, w_all, g_sems, w_sems = refs[-6:]
    per, size, _ = out_ref.shape
    pitch = size + PAD
    phase, j = pl.program_id(0), pl.program_id(1)

    @pl.when((phase == 0) & (j == 0))
    def _():
        copies = share_copies(place, pos_ref, g_parts, g_all, g_sems) + piece_copies(place, pos_ref, factor, w_all, w_sems)
        run(copies)
        finish(copies)

    @pl.when(phase == 0)
    def _():
        def body(k):
            b = j * per + k
            turned[pl.ds(b, size, stride=pitch), :] = dot_nn(w_all[b], stacked(g_all, b))

        each(per, body)

    @pl.when(phase == 1)
    def _():
        def body(k):
            out_ref[k] = turned[pl.ds((j * per + k) * pitch, size), :].astype(BF16)

        each(per, body)


def middle_sizes(place, parts):
    blocks, home, cut = parts[0].shape
    return blocks, home, cut, len(parts), (blocks, blocks, blocks)


def back_two(place, pos, g_mid, right_two):
    blocks, home, cut, share, whole = middle_sizes(place, g_mid)
    at = during(1, share)
    return call(
        functools.partial(back_two_kernel, place),
        shape((blocks, blocks, cut)),
        (2, share),
        anywhere(share + len(flat(right_two))),
        pl.BlockSpec((home, blocks, cut), lambda p, j, pos: (at(p, j), 0, 0)),
        [
            pltpu.VMEM((blocks * (blocks + PAD), cut), F32),
            pltpu.VMEM((share, blocks, home, cut), BF16),
            pltpu.VMEM(whole, BF16),
            pltpu.SemaphoreType.DMA((share,)),
            pltpu.SemaphoreType.DMA((n_copies(place),)),
        ],
        (*g_mid, *flat(right_two)),
        us=10,
        scalars=pos,
    )


def either(place, pos_ref, j, keep_ref, send_ref, body):
    mine = lax.rem(j, place.near) == pos_ref[1]

    @pl.when(mine)
    def _():
        body(keep_ref)

    @pl.when(jnp.logical_not(mine))
    def _():
        body(send_ref)


def middle_kernel(place, pos_ref, *refs):
    share = place.far * place.near
    wide = (len(refs) - (2 * share + 15)) // 2
    s_parts, rest = refs[:share], refs[share:]
    one, two, rest = unflat(place, rest[:wide]), unflat(place, rest[wide : 2 * wide]), rest[2 * wide :]
    e_ref, act_ref, keep_two, send_two, keep_one, send_one, *rest = rest
    out_refs, rest = rest[:share], rest[share:]
    turned, hidden, e_one, s_all, one_all, two_all, s_sems, one_sems, two_sems = rest
    per, size, cut = act_ref.shape
    home = s_all.shape[2]
    pitch = size + PAD
    phase, j = pl.program_id(0), pl.program_id(1)

    def rows(k):
        return pl.ds((j * per + k) * pitch, size)

    def column(k):
        return pl.ds(j * per + k, size, stride=pitch)

    def second():
        return piece_copies(place, pos_ref, two, two_all, two_sems)

    @pl.when((phase == 0) & (j == 0))
    def _():
        copies = share_copies(place, pos_ref, s_parts, s_all, s_sems) + piece_copies(place, pos_ref, one, one_all, one_sems)
        run(copies)
        run(second())
        finish(copies)

    @pl.when(phase == 0)
    def _():
        def body(k):
            b = j * per + k
            turned[column(k), :] = dot_tn(one_all[b], stacked(s_all, b))

        each(per, body)

    @pl.when((phase == 1) & (j == 0))
    def _():
        finish(second())

    @pl.when(phase == 1)
    def _():
        def with_out(grad_ref):
            def body(k):
                v = turned[rows(k), :].astype(BF16).astype(F32)
                value, slope = gelu_both(v)
                act = value.astype(BF16)
                act_ref[k] = act
                e = e_ref[k]
                hidden[column(k), :] = slope * dot_nn(two_all[j * per + k], e)
                grad_ref[0, k] = dot_nt(act, e).astype(BF16)

            each(per, body, 8)

        either(place, pos_ref, j, keep_two, send_two, with_out)

    @pl.when(phase == 2)
    def _():
        def with_out(grad_ref):
            def body(k):
                b = j * per + k
                h = hidden[rows(k), :].astype(BF16)
                e_one[k] = dot_nn(one_all[b], h).astype(BF16)
                grad_ref[0, k] = dot_nt(stacked(s_all, b), h).astype(BF16)

            each(per, body)

        either(place, pos_ref, j, keep_one, send_one, with_out)
        for n in range(share):
            at = pl.ds(pl.multiple_of(place.onward(pos_ref, n) * home, home), home)
            out_refs[n][...] = e_one[:, at, :]


def grad_specs(place, phase, home, size, share):
    at = during(phase, share)
    dims = shape((place.far, home, size, size))
    spec = pl.BlockSpec((1, home, size, size), lambda p, j, pos: (at(p, j) // place.near, 0, 0, 0))
    return [dims] * 2, [spec] * 2


def middle(place, pos, s_mid, e_mid, right_one, left_two):
    blocks, home, cut, share, whole = middle_sizes(place, s_mid)
    at = [during(phase, share) for phase in range(3)]
    block = pl.BlockSpec((home, blocks, cut), lambda p, j, pos: (at[1](p, j), 0, 0))
    two, two_specs = grad_specs(place, 1, home, blocks, share)
    one, one_specs = grad_specs(place, 2, home, blocks, share)
    piece = pl.BlockSpec((home, home, cut), lambda p, j, pos: (at[2](p, j), 0, 0))
    out = call(
        functools.partial(middle_kernel, place),
        (shape((blocks, blocks, cut)), *two, *one) + (shape((blocks, home, cut)),) * share,
        (3, share),
        anywhere(share + 2 * len(flat(right_one))) + [block],
        (block, *two_specs, *one_specs) + (piece,) * share,
        [pltpu.VMEM((blocks * (blocks + PAD), cut), F32)] * 2
        + [
            pltpu.VMEM((home, blocks, cut), BF16),
            pltpu.VMEM((share, blocks, home, cut), BF16),
            pltpu.VMEM(whole, BF16),
            pltpu.VMEM(whole, BF16),
            pltpu.SemaphoreType.DMA((share,)),
            pltpu.SemaphoreType.DMA((n_copies(place),)),
            pltpu.SemaphoreType.DMA((n_copies(place),)),
        ],
        (*s_mid, *flat(right_one), *flat(left_two), e_mid),
        us=26,
        scalars=pos,
    )
    return out[0], out[1:3], out[3:5], list(out[5:])


def forward_two_kernel(place, pos_ref, *refs):
    share = place.far * place.near
    wide = (len(refs) - (2 * share + 11)) // 2
    g_parts, rest = refs[:share], refs[share:]
    left, right, rest = unflat(place, rest[:wide]), unflat(place, rest[wide : 2 * wide]), rest[2 * wide :]
    act_ref, keep_ref, send_ref, *rest = rest
    out_refs, rest = rest[:share], rest[share:]
    turned, fourth, g_all, left_all, right_all, g_sems, left_sems, right_sems = rest
    per, size, _ = act_ref.shape
    pitch = size + PAD
    phase, j = pl.program_id(0), pl.program_id(1)

    def rows(k):
        return pl.ds((j * per + k) * pitch, size)

    def column(k):
        return pl.ds(j * per + k, size, stride=pitch)

    def second():
        return piece_copies(place, pos_ref, right, right_all, right_sems) + share_copies(place, pos_ref, g_parts, g_all, g_sems)

    @pl.when((phase == 0) & (j == 0))
    def _():
        copies = piece_copies(place, pos_ref, left, left_all, left_sems)
        run(copies)
        run(second())
        finish(copies)

    @pl.when(phase == 0)
    def _():
        def body(k):
            turned[column(k), :] = dot_tn(left_all[j * per + k], act_ref[k])

        each(per, body)

    @pl.when((phase == 1) & (j == 0))
    def _():
        finish(second())

    @pl.when(phase == 1)
    def _():
        def with_out(grad_ref):
            def body(k):
                b = j * per + k
                third = turned[rows(k), :].astype(BF16)
                fourth[column(k), :] = dot_tn(right_all[b], third)
                grad_ref[0, k] = dot_nt(third, stacked(g_all, b)).astype(BF16)

            each(per, body)

        either(place, pos_ref, j, keep_ref, send_ref, with_out)

    for n in range(share):

        @pl.when((phase == 2) & (j == n))
        def _():
            base = place.onward(pos_ref, n) * per

            def body(k):
                out_refs[n][k] = fourth[pl.ds((base + k) * pitch, size), :].astype(BF16)

            each(per, body)


def forward_two(place, pos, act, g_mid, left_two, right_two):
    blocks, home, cut, share, whole = middle_sizes(place, g_mid)
    at = during(0, share)
    grad, grad_spec = grad_specs(place, 1, home, blocks, share)
    out = call(
        functools.partial(forward_two_kernel, place),
        (*grad,) + (shape((home, blocks, cut)),) * share,
        (3, share),
        anywhere(share + 2 * len(flat(left_two))) + [pl.BlockSpec((home, blocks, cut), lambda p, j, pos: (at(p, j), 0, 0))],
        (*grad_spec,) + (pl.BlockSpec((home, blocks, cut), lambda p, j, pos: (0, 0, 0)),) * share,
        [pltpu.VMEM((blocks * (blocks + PAD), cut), F32)] * 2
        + [
            pltpu.VMEM((share, blocks, home, cut), BF16),
            pltpu.VMEM(whole, BF16),
            pltpu.VMEM(whole, BF16),
            pltpu.SemaphoreType.DMA((share,)),
            pltpu.SemaphoreType.DMA((n_copies(place),)),
            pltpu.SemaphoreType.DMA((n_copies(place),)),
        ],
        (*g_mid, *flat(left_two), *flat(right_two), act),
        us=20,
        scalars=pos,
    )
    return out[:2], list(out[2:])


def halves(size):
    low = 2 if size % 2 == 0 else 1
    return size // low, low


def cross(pieces):
    return lax.all_to_all(pieces, "tensor", split_axis=0, concat_axis=0, tiled=True)


def whole_tokens(x_home, g_home, factors, share, cut):
    home, size, tokens = x_home.shape
    first_left = factors[0]
    rows = first_left.shape[1]
    place = Place(share, lax.axis_size("dp"))
    pos = place.position()

    def gather(start, n):
        if n >= len(place.dp):
            return start
        got = [start] + place.dp[n].sends(start)
        return got if n == 0 else jnp.stack(got)

    def gather_far(start):
        for n in reversed(range(2, len(place.dp))):
            start = gather(start, n)
        return start

    def last_dp(start):
        return gather(start, 0) if place.dp else [start]

    def cores(piece):
        return [piece] + place.core.sends(piece)

    def by_core(own):
        return [[p[c] for p in own] for c in range(place.near)]

    def cross(pieces, n):
        return place.exchange(pieces, n) if n < share else None

    def from_y(start):
        return jnp.stack([start] + place.y.sends(start))

    n_one, n_two, n_three = (place.steps.index(step) if step in place.steps else share for step in [(0, 1), (1, 0), (1, 1)])
    one = gather_far(first_left)
    w_two = from_y(factors[3])
    rest = from_y(jnp.stack([factors[1], factors[2]]))
    g = {n: deal(place, pos, g_home, cut, n) for n in reversed(range(share))}
    got_three = cross(g, n_three)
    w_two = gather_far(after(w_two, g[share - 1]))
    one = last_dp(gather(after(one, rest), 1))
    w_two = gather(w_two, 1)
    got_three, one, w_two, rest, g = slot(place, (got_three, one, w_two, rest, g))

    got_two = cross(g, n_two)
    right_two = last_dp(w_two)
    w_one = gather(gather_far(rest[:, 0]), 1)
    w_left = gather_far(rest[:, 1])
    one = join(place, pos, [p[..., None, :, :, :] for p in one])
    s = first_stage(place, pos, x_home, one, cut)
    got_two, right_two, w_one, w_left, one, s, pos = slot(place, (got_two, right_two, w_one, w_left, one, list(s), pos))

    s_three = cross(s, n_three)
    right_one = last_dp(w_one)
    w_left = gather(w_left, 1)
    right_two = by_core([cores(p) for p in right_two])
    s_one = cross(s, n_one)
    got_one = cross(g, n_one)
    s_three, s_one, right_one, w_left, right_two, g, got_one = slot(
        place, (s_three, s_one, right_one, w_left, right_two, g, got_one)
    )
    g_mid = [g[0], got_one, got_two, got_three][:share]

    s_two = cross(s, n_two)
    left_two = last_dp(w_left)
    left_core = cores(left_two[0])
    right_one = by_core([cores(p) for p in right_one])
    e_mid = back_two(place, pos, g_mid, right_two)
    s_two, left_two, left_core, right_one, e_mid = slot(place, (s_two, left_two, left_core, right_one, e_mid))
    s_mid = [s[0], s_one, s_two, s_three][:share]
    left_two = by_core([left_core] + [cores(p) for p in left_two[1:]])

    act, grad_two, grad_one, e = middle(place, pos, s_mid, e_mid, right_one, left_two)

    def start_sum(keep, send):
        arrays = [keep, place.core.send(send, 1)] if place.near > 1 else [keep]
        return Sum(arrays, [place.y, home] + place.dp[::-1], (rows, size))

    def hold(parts, arrays):
        for part, kept in zip(parts, arrays):
            part.arrays = kept

    def arrays_of(*parts):
        return [part.arrays for part in parts]

    x_step, near_step, far_step = (place.dp + [None] * 3)[:3]

    e_three = cross(e, n_three)
    two, one_part = start_sum(*grad_two), start_sum(*grad_one)
    grad_three, s = forward_two(place, pos, act, g_mid, left_two, right_two)
    e_three, kept, grad_three, s, e = slot(place, (e_three, arrays_of(two, one_part), grad_three, s, e))
    hold([two, one_part], kept)

    e_two = cross(e, n_two)
    two.step(x_step)
    one_part.step(near_step)
    three = start_sum(*grad_three)
    e_one = cross(e, n_one)
    e_two, e_one, kept, s = slot(place, (e_two, e_one, arrays_of(two, one_part, three), s))
    hold([two, one_part, three], kept)
    e_got = [e[0], e_one, e_two, e_three][:share]

    s_three = cross(s, n_three)
    three.step(x_step)
    two.step(near_step)
    input_grad, lone = last_stage(place, pos, e_got, x_home, g_home, one)
    s_three, kept, lone, input_grad, s = slot(place, (s_three, arrays_of(two, one_part, three), lone, input_grad, s))
    hold([two, one_part, three], kept)
    lone = Sum([lone], [home] + place.dp[::-1], (rows, size))

    s_two, s_one = cross(s, n_two), cross(s, n_one)
    one_part.step(x_step)
    three.step(near_step)
    two.step(far_step)
    lone.step(x_step)
    one_part.step(far_step)
    three.step(far_step)
    lone.step(near_step)
    s_got = [after(s[0], lone.arrays[-1]), s_one, s_two, s_three][:share]
    grad_ltwo = two.finish()
    grad_rone = one_part.finish()
    grad_rtwo = three.finish()
    grad_lone = lone.finish()
    mixed = add_home(place, pos, s_got, x_home)
    return mixed, input_grad, grad_lone, grad_rone, grad_ltwo, grad_rtwo


def split_blocks(x_home, g_home, factors, share, cut):
    home, size, tokens = x_home.shape
    far, near = halves(share)
    outer, inner = halves(lax.axis_size("dp"))
    ring_y, ring_core = Ring("tensor", (near, far)), Ring("tensor", (1, near))
    ring_z, ring_x = Ring("dp", (inner, outer)), Ring("dp", (1, inner))
    rows = factors[0].shape[1]
    n_tensor = lax.axis_size("tensor")
    groups = n_tensor // share
    held = home * share
    same_tokens = [[group * share + part for group in range(groups)] for part in range(share)]

    def go(values):
        pieces = values.reshape(home, groups, held, share, cut).transpose(1, 3, 2, 0, 4)
        got = cross(pieces.reshape(n_tensor, held, home, cut))
        return got.transpose(1, 0, 2, 3).reshape(held, size, cut)

    def back(values):
        pieces = values.reshape(held, n_tensor, home, cut).transpose(1, 0, 2, 3)
        got = cross(pieces).reshape(groups, share, held, home, cut)
        return got.transpose(3, 0, 2, 1, 4).reshape(home, size, tokens)

    def turn(values):
        moved = lax.all_to_all(
            values.reshape(held, groups, held, cut), "tensor", split_axis=1, concat_axis=0, tiled=True, axis_index_groups=same_tokens
        )
        return jnp.swapaxes(moved.reshape(size, held, cut), 0, 1)

    def whole(factor):
        one = ring_z.gather(ring_y.gather(factor))
        all_rows = ring_core.gather(ring_x.gather(one))
        return all_rows.transpose(3, 0, 4, 2, 1, 5, 6).reshape(held, size, size)

    def own_sum(partial):
        split = partial.reshape(ring_y.size, ring_core.size, home, ring_z.size, ring_x.size, rows, size)
        terms = ring_core.scatter([split], 1)
        return total(ring_y.scatter(ring_z.scatter(ring_x.scatter(terms, 3), 2), 0))

    first_left, first_right, second_left, second_right = factors
    g_mid = go(g_home)
    left_one = ring_x.gather(ring_z.gather(first_left)).transpose(2, 1, 0, 3, 4).reshape(home, size, size)
    right_one, left_two, right_two = whole(first_right), whole(second_left), whole(second_right)

    s_one = go(product("bjt,bjo->bot", x_home, left_one).astype(BF16))
    s_two = turn(product("bit,bip->bpt", s_one, right_one).astype(BF16))
    act = gelu_value(s_two.astype(F32)).astype(BF16)
    e_three = turn(product("bot,bio->bit", g_mid, right_two).astype(BF16))
    h_mid = turn(gelu_back(s_two.astype(F32), product("bot,bjo->bjt", e_three, left_two)).astype(BF16))
    e_one = back(product("bpt,bip->bit", h_mid, right_one).astype(BF16))
    s_three = turn(product("bjt,bjo->bot", act, left_two).astype(BF16))
    s_four = back(product("bit,bio->bot", s_three, right_two).astype(BF16))
    mixed = (x_home.astype(F32) + s_four.astype(F32)).astype(BF16)

    grad_rtwo = own_sum(product("bit,bot->bio", s_three, g_mid))
    grad_ltwo = own_sum(product("bjt,bot->bjo", act, e_three))
    grad_rone = own_sum(product("bit,bpt->bip", s_one, h_mid))
    grad_lone = product("bjt,bot->bjo", x_home, e_one).reshape(home, ring_z.size, ring_x.size, rows, size)
    grad_lone = total(ring_z.scatter(ring_x.scatter([grad_lone], 2), 1))
    input_grad = (g_home.astype(F32) + product("bot,bjo->bjt", e_one, left_one)).astype(BF16)
    return mixed, input_grad, grad_lone, grad_rone, grad_ltwo, grad_rtwo


def per_device(inputs, cotangent, first_left, first_right, second_left, second_right):
    n_tensor = lax.axis_size("tensor")
    home, _, size = first_left.shape
    tokens = inputs.shape[1]
    share = math.gcd(n_tensor, max(1, tokens // LANES))
    cut = tokens // share
    plan = whole_tokens if share == n_tensor else split_blocks
    mixed, input_grad, *weight_grads = plan(
        inputs.reshape(home, size, tokens),
        cotangent.reshape(home, size, tokens),
        (first_left, first_right, second_left, second_right),
        share,
        cut,
    )
    return (mixed.reshape(inputs.shape), input_grad.reshape(inputs.shape), *weight_grads)


def solution(mesh):
    wide, factor = P("tensor", "dp"), P("tensor", "dp", None)
    return jax.shard_map(
        per_device,
        mesh=mesh,
        in_specs=(wide, wide, factor, factor, factor, factor),
        out_specs=(wide, wide, factor, factor, factor, factor),
        check_vma=False,
    )
```

```python
import functools
import itertools
import math

import jax
import jax.numpy as jnp
from jax import lax
from jax.experimental import pallas as pl
from jax.experimental.pallas import tpu as pltpu
from jax.sharding import PartitionSpec as P

BF16 = jnp.bfloat16
F32 = jnp.float32
LANES = 128
PAD = 1
VMEM_BYTES = 60 * 1024 * 1024
BYTES_PER_US = 1_200_000


def gelu_value(values):
    return jax.nn.gelu(values, approximate=True)


def gelu_back(values, upstream):
    return jax.vjp(gelu_value, values)[1](upstream)[0]


def gelu_both(v):
    root, cubic = 0.7978845608028654, 0.044715
    square = v * v
    t = jnp.tanh(root * (v + cubic * (v * square)))
    half = 0.5 * (1.0 + t)
    slope = half + (0.5 * v) * (1.0 - t * t) * (root + (3.0 * cubic * root) * square)
    return v * half, slope


def product(form, left, right):
    return jnp.einsum(form, left, right, preferred_element_type=F32)


def dot_nn(left, right):
    return lax.dot_general(left, right, (((1,), (0,)), ((), ())), preferred_element_type=F32)


def dot_tn(left, right):
    return lax.dot_general(left, right, (((0,), (0,)), ((), ())), preferred_element_type=F32)


def dot_nt(left, right):
    return lax.dot_general(left, right, (((1,), (1,)), ((), ())), preferred_element_type=F32)


def call(body, out, grid, in_specs, out_specs, scratch, args, us, scalars=None):
    spec = pltpu.PrefetchScalarGridSpec(
        num_scalar_prefetch=0 if scalars is None else 1,
        grid=grid,
        in_specs=in_specs,
        out_specs=out_specs,
        scratch_shapes=scratch,
    )
    return pl.pallas_call(
        body,
        out_shape=out,
        grid_spec=spec,
        compiler_params=pltpu.CompilerParams(
            dimension_semantics=("arbitrary",) * len(grid), vmem_limit_bytes=VMEM_BYTES
        ),
        cost_estimate=pl.CostEstimate(flops=0, bytes_accessed=int(us * BYTES_PER_US), transcendentals=0),
    )(*(() if scalars is None else (scalars,)), *args)


def shape(dims, dtype=BF16):
    return jax.ShapeDtypeStruct(dims, dtype)


def each(count, body, unroll=16):
    def step(k, carry):
        body(k)
        return carry

    lax.fori_loop(0, count, step, 0, unroll=math.gcd(count, unroll))


def during(phase, steps):
    return lambda p, j: jnp.where(p == phase, j, jnp.where(p < phase, 0, steps - 1))


def stacked(ref, k):
    return jnp.concatenate([ref[c, k] for c in range(ref.shape[0])], axis=0)


class Ring:
    def __init__(self, axis, *digits, tied=True):
        self.axis, self.digits, self.last, self.tied = axis, digits, None, tied
        self.stride, self.size = digits[0]

    def here(self):
        return lax.rem(lax.axis_index(self.axis) // self.stride, self.size)

    def send(self, value, *steps):
        pairs = []
        for src in range(lax.axis_size(self.axis)):
            dst = src
            for (stride, size), step in zip(self.digits, steps):
                own = src // stride % size
                dst += ((own + step) % size - own) * stride
            pairs.append((src, dst))
        if self.tied and self.last is not None:
            value = after(value, self.last)
        self.last = lax.ppermute(value, self.axis, pairs)
        return self.last

    def sends(self, value):
        return [self.send(value, step) for step in range(1, self.size)]

    def gather(self, value):
        if self.size == 1:
            return value[None]
        here = self.here()
        out = jnp.zeros((self.size,) + value.shape, value.dtype)
        out = lax.dynamic_update_index_in_dim(out, value, here, 0)
        for step in range(1, self.size):
            got = self.send(value, step)
            out = lax.dynamic_update_index_in_dim(out, got, lax.rem(here - step + self.size, self.size), 0)
        return out

    def scatter(self, terms, dim, before=()):
        here = self.here()
        if self.size == 1:
            return [lax.index_in_dim(t, 0, dim, keepdims=False) for t in terms]
        out = [lax.dynamic_index_in_dim(t, here, dim, keepdims=False) for t in terms]
        for step in range(1, self.size):
            there = lax.rem(here + step, self.size)
            term = total([lax.dynamic_index_in_dim(t, there, dim, keepdims=False) for t in terms]).astype(BF16)
            out.append(self.send(after(term, *before), step))
        return out


def slot(place, values):
    values = lax.optimization_barrier(values)
    place.crossed = None
    for ring in [place.y, place.core] + place.dp + list(place.links.values()):
        ring.last = None
    return values


class Sum:
    def __init__(self, arrays, rings, tail):
        self.left = rings
        dims = [ring.size if isinstance(ring, Ring) else ring for ring in rings]
        self.arrays = [a.reshape(dims + list(tail)) for a in arrays]
        self.rings = [rings] * len(arrays)
        self.ready = []

    def cut(self, ring=None, index=None):
        out = []
        for array, rings in zip(self.arrays, self.rings):
            dim = 0
            for r in rings:
                if isinstance(r, Ring) and (r is ring or r not in self.left):
                    array = lax.dynamic_index_in_dim(array, index if r is ring else r.here(), dim, keepdims=False)
                else:
                    dim += 1
            out.append(array)
        return total(out)

    def parts(self, ring):
        return [self.cut(ring, lax.rem(ring.here() + step, ring.size)).astype(BF16) for step in range(1, ring.size)]

    def prepare(self, ring):
        self.ready = self.parts(ring) if ring in self.left else []

    def step(self, ring):
        if ring not in self.left:
            return
        rest = [r for r in self.left if r is not ring]
        parts = self.ready or self.parts(ring)
        self.ready = []
        got = [ring.send(part, step + 1) for step, part in enumerate(parts)]
        self.arrays, self.rings, self.left = self.arrays + got, self.rings + [rest] * len(got), rest

    def finish(self):
        for ring in [r for r in self.left[::-1] if isinstance(r, Ring)]:
            self.step(ring)
        return self.cut()


def total(terms):
    return functools.reduce(jnp.add, [t.astype(F32) for t in terms])


def after(value, *others):
    if not others:
        return value
    return lax.optimization_barrier((value,) + others)[0]


def turned_back(here, step, size):
    return lax.rem(here - step + size, size)


class Place:
    def __init__(self, share, n_dp):
        self.far, self.near = halves(share)
        self.y, self.core = Ring("tensor", (self.near, self.far)), Ring("tensor", (1, self.near), tied=False)
        self.dp, stride = [], 1
        while stride < n_dp:
            size = next(p for p in range(2, n_dp + 1) if n_dp // stride % p == 0)
            self.dp.append(Ring("dp", (stride, size)))
            stride *= size
        self.steps = [(y, c) for y in range(self.far) for c in range(self.near)]
        self.crossed = None
        self.links = {step: Ring("tensor", (self.near, self.far), (1, self.near)) for step in self.steps[1:]}
        self.rows = [ring.size for ring in self.dp]

    def position(self):
        return jnp.stack([ring.here() for ring in [self.y, self.core] + self.dp]).astype(jnp.int32)

    def onward(self, pos, n):
        y, c = self.steps[n]
        return lax.rem(pos[0] + y, self.far) * self.near + lax.rem(pos[1] + c, self.near)

    def source(self, pos, n):
        y, c = self.steps[n]
        return turned_back(pos[0], y, self.far) * self.near + turned_back(pos[1], c, self.near)

    def exchange(self, pieces, n):
        y, c = self.steps[n]
        piece = pieces[n]
        if y == 0:
            return self.core.send(piece, c)
        if self.crossed is not None:
            piece = after(piece, self.crossed)
        self.crossed = self.y.send(piece, y) if c == 0 else self.links[(y, c)].send(piece, y, c)
        return self.crossed


def piece_copies(pieces, whole, sems):
    flat_whole = [whole.at[c, d] for c in range(len(pieces)) for d in range(len(pieces[0]))]
    return [pltpu.make_async_copy(ref, dst, sems.at[n]) for n, (ref, dst) in enumerate(zip(flat(pieces), flat_whole))]


def block_reader(place, pos_ref, whole, group):
    lead = ()
    if group is not None:
        lead = (turned_back(pos_ref[0], group // place.near, place.far),)
    core = 0 if group is None else turned_back(pos_ref[1], lax.rem(group, place.near), place.near)
    places = []
    for d in range(math.prod(place.rows)):
        steps = [turned_back(pos_ref[2 + n], d // ring.stride % ring.size, ring.size) for n, ring in enumerate(place.dp)]
        places.append((core, *(steps or [0]), *lead))
    return lambda k: jnp.concatenate([whole[(*at, k)] for at in places], axis=0)


def whole_scratch(pieces):
    dims = (len(pieces), len(pieces[0])) + pieces[0][0].shape
    return [pltpu.VMEM(dims, BF16), pltpu.SemaphoreType.DMA((dims[0] * dims[1],))]


def share_copies(place, pos_ref, parts, whole, sems):
    return [pltpu.make_async_copy(ref, whole.at[place.source(pos_ref, n)], sems.at[n]) for n, ref in enumerate(parts)]


def run(copies):
    for copy in copies:
        copy.start()


def finish(copies):
    for copy in copies:
        copy.wait()


def anywhere(count):
    return [pl.BlockSpec(memory_space=pl.ANY)] * count


def flat(pieces):
    return tuple(p for row in pieces for p in row)


def unflat(place, refs):
    wide = len(refs) // place.near
    return [refs[c * wide : (c + 1) * wide] for c in range(place.near)]


def deal_kernel(pos_ref, g_ref, out_ref, turned):
    home, size, _ = g_ref.shape
    pitch = home + PAD

    def store(o):
        turned[pl.ds(o, size, stride=pitch), :] = g_ref[o].astype(F32)

    def load(b):
        out_ref[b] = turned[pl.ds(b * pitch, home), :].astype(BF16)

    each(home, store)
    each(size, load)


def deal(place, pos, g_home, cut, n):
    home, size, _ = g_home.shape
    return call(
        deal_kernel,
        shape((size, home, cut)),
        (1,),
        [pl.BlockSpec((home, size, cut), lambda i, pos: (0, 0, place.onward(pos, n)))],
        pl.BlockSpec((size, home, cut), lambda i, pos: (0, 0, 0)),
        [pltpu.VMEM((size * (home + PAD), cut), F32)],
        (g_home,),
        us=3.5,
        scalars=pos,
    )


def first_kernel(place, pos_ref, x_ref, *refs):
    share = place.far * place.near
    pieces, out_refs = refs[: -share - 3], refs[-share - 3 : -3]
    turned, whole, sems = refs[-3:]
    home, size, _ = x_ref.shape
    cut = out_refs[0].shape[2]
    pitch = home + PAD
    copies = piece_copies([pieces], whole, sems)
    block = block_reader(place, pos_ref, whole, None)

    @pl.when(pl.program_id(0) == 0)
    def _():
        run(copies)
        finish(copies)

    for n, out_ref in enumerate(out_refs):

        @pl.when(pl.program_id(0) == n)
        def _():
            lanes = pl.ds(pl.multiple_of(place.onward(pos_ref, n) * cut, cut), cut)

            def store(b):
                turned[pl.ds(b, size, stride=pitch), :] = dot_tn(block(b), x_ref[b, :, lanes])

            def load(o):
                out_ref[o] = turned[pl.ds(o * pitch, home), :].astype(BF16)

            each(home, store)
            each(size, load)


def first_stage(place, pos, x_home, left_one, cut):
    home, size, tokens = x_home.shape
    share = tokens // cut
    return call(
        functools.partial(first_kernel, place),
        (shape((size, home, cut)),) * share,
        (share,),
        [pl.BlockSpec((home, size, tokens), lambda s, pos: (0, 0, 0))] + anywhere(len(left_one)),
        (pl.BlockSpec((size, home, cut), lambda s, pos: (0, 0, 0)),) * share,
        [pltpu.VMEM((size * (home + PAD), cut), F32)] + whole_scratch([left_one]),
        (x_home, *left_one),
        us=8,
        scalars=pos,
    )


def last_kernel(place, pos_ref, *refs):
    share = place.far * place.near
    e_refs, x_ref, g_ref = refs[:share], refs[share], refs[share + 1]
    pieces, (out_ref, grad_ref, turned, whole, sems) = refs[share + 2 : -5], refs[-5:]
    blocks, per, cut = e_refs[0].shape
    pitch = blocks + PAD
    copies = piece_copies([pieces], whole, sems)
    block = block_reader(place, pos_ref, whole, None)
    first = pl.program_id(0) * per

    @pl.when(pl.program_id(0) == 0)
    def _():
        run(copies)

    for n in range(share):
        s = place.source(pos_ref, n)

        def store(o):
            turned[s, pl.ds(o, per, stride=pitch), :] = e_refs[n][o].astype(F32)

        each(blocks, store)

    @pl.when(pl.program_id(0) == 0)
    def _():
        finish(copies)

    def load(b):
        rows = pl.ds(b * pitch, blocks)
        e_b = jnp.concatenate([turned[s, rows, :].astype(BF16) for s in range(share)], axis=1)
        out_ref[b] = (g_ref[b].astype(F32) + dot_nn(block(first + b), e_b)).astype(BF16)
        grad_ref[b] = dot_nt(x_ref[b], e_b).astype(BF16)

    each(per, load, 4)


def last_stage(place, pos, e_got, x_home, g_home, left_one):
    share = len(e_got)
    blocks, home, cut = e_got[0].shape
    _, size, tokens = x_home.shape
    per = math.gcd(home, 16)
    wide = pl.BlockSpec((per, size, tokens), lambda h, pos: (h, 0, 0))
    factor = pl.BlockSpec((per, size, size), lambda h, pos: (h, 0, 0))
    return call(
        functools.partial(last_kernel, place),
        (shape(g_home.shape), shape((home, size, size))),
        (home // per,),
        [pl.BlockSpec((blocks, per, cut), lambda h, pos: (0, h, 0))] * share + [wide, wide] + anywhere(len(left_one)),
        (wide, factor),
        [pltpu.VMEM((share, per * (blocks + PAD), cut), F32)] + whole_scratch([left_one]),
        (*e_got, x_home, g_home, *left_one),
        us=10,
        scalars=pos,
    )


def mixed_kernel(place, pos_ref, *refs):
    *s_refs, x_ref, out_ref = refs
    cut = s_refs[0].shape[2]
    for n, s_ref in enumerate(s_refs):
        lanes = pl.ds(pl.multiple_of(place.source(pos_ref, n) * cut, cut), cut)
        out_ref[:, :, lanes] = (x_ref[:, :, lanes].astype(F32) + s_ref[...].astype(F32)).astype(BF16)


def add_home(place, pos, s_got, x_home):
    home, blocks, cut = s_got[0].shape
    per = math.gcd(home, 8)
    wide = pl.BlockSpec((per,) + x_home.shape[1:], lambda h, pos: (h, 0, 0))
    return call(
        functools.partial(mixed_kernel, place),
        shape(x_home.shape),
        (home // per,),
        [pl.BlockSpec((per, blocks, cut), lambda h, pos: (h, 0, 0))] * len(s_got) + [wide],
        wide,
        [],
        (*s_got, x_home),
        us=6,
        scalars=pos,
    )


def back_two_kernel(place, pos_ref, *refs):
    share = place.far * place.near
    g_parts, factor = refs[:share], unflat(place, refs[share:-6])
    out_ref, turned, g_all, g_sems, w_all, w_sems = refs[-6:]
    per, size, _ = out_ref.shape
    pitch = size + PAD
    phase, j = pl.program_id(0), pl.program_id(1)

    @pl.when((phase == 0) & (j == 0))
    def _():
        copies = share_copies(place, pos_ref, g_parts, g_all, g_sems) + piece_copies(factor, w_all, w_sems)
        run(copies)
        finish(copies)

    @pl.when(phase == 0)
    def _():
        block = block_reader(place, pos_ref, w_all, j)

        def body(k):
            b = j * per + k
            turned[pl.ds(b, size, stride=pitch), :] = dot_nn(block(k), stacked(g_all, b))

        each(per, body)

    @pl.when(phase == 1)
    def _():
        def body(k):
            out_ref[k] = turned[pl.ds((j * per + k) * pitch, size), :].astype(BF16)

        each(per, body)


def middle_sizes(place, parts):
    blocks, home, cut = parts[0].shape
    return blocks, home, cut, len(parts)


def back_two(place, pos, g_mid, right_two):
    blocks, home, cut, share = middle_sizes(place, g_mid)
    at = during(1, share)
    return call(
        functools.partial(back_two_kernel, place),
        shape((blocks, blocks, cut)),
        (2, share),
        anywhere(share + len(flat(right_two))),
        pl.BlockSpec((home, blocks, cut), lambda p, j, pos: (at(p, j), 0, 0)),
        [
            pltpu.VMEM((blocks * (blocks + PAD), cut), F32),
            pltpu.VMEM((share, blocks, home, cut), BF16),
            pltpu.SemaphoreType.DMA((share,)),
        ]
        + whole_scratch(right_two),
        (*g_mid, *flat(right_two)),
        us=10,
        scalars=pos,
    )


def either(place, pos_ref, j, keep_ref, send_ref, body):
    mine = lax.rem(j, place.near) == pos_ref[1]

    @pl.when(mine)
    def _():
        body(keep_ref)

    @pl.when(jnp.logical_not(mine))
    def _():
        body(send_ref)


def middle_kernel(place, pos_ref, *refs):
    share = place.far * place.near
    wide = (len(refs) - (2 * share + 15)) // 2
    s_parts, rest = refs[:share], refs[share:]
    one, two, rest = unflat(place, rest[:wide]), unflat(place, rest[wide : 2 * wide]), rest[2 * wide :]
    e_ref, act_ref, keep_two, send_two, keep_one, send_one, *rest = rest
    out_refs, rest = rest[:share], rest[share:]
    turned, hidden, e_one, s_all, s_sems, one_all, one_sems, two_all, two_sems = rest
    per, size, cut = act_ref.shape
    home = s_all.shape[2]
    pitch = size + PAD
    phase, j = pl.program_id(0), pl.program_id(1)

    def rows(k):
        return pl.ds((j * per + k) * pitch, size)

    def column(k):
        return pl.ds(j * per + k, size, stride=pitch)

    def second():
        return piece_copies(two, two_all, two_sems)

    @pl.when((phase == 0) & (j == 0))
    def _():
        copies = share_copies(place, pos_ref, s_parts, s_all, s_sems) + piece_copies(one, one_all, one_sems)
        run(copies)
        run(second())
        finish(copies)

    @pl.when(phase == 0)
    def _():
        block = block_reader(place, pos_ref, one_all, j)

        def body(k):
            turned[column(k), :] = dot_tn(block(k), stacked(s_all, j * per + k))

        each(per, body)

    @pl.when((phase == 1) & (j == 0))
    def _():
        finish(second())

    @pl.when(phase == 1)
    def _():
        block = block_reader(place, pos_ref, two_all, j)

        def with_out(grad_ref):
            def body(k):
                v = turned[rows(k), :].astype(BF16).astype(F32)
                value, slope = gelu_both(v)
                act = value.astype(BF16)
                act_ref[k] = act
                e = e_ref[k]
                hidden[column(k), :] = slope * dot_nn(block(k), e)
                grad_ref[0, k] = dot_nt(act, e).astype(BF16)

            each(per, body, 8)

        either(place, pos_ref, j, keep_two, send_two, with_out)

    @pl.when(phase == 2)
    def _():
        block = block_reader(place, pos_ref, one_all, j)

        def with_out(grad_ref):
            def body(k):
                b = j * per + k
                h = hidden[rows(k), :].astype(BF16)
                e_one[k] = dot_nn(block(k), h).astype(BF16)
                grad_ref[0, k] = dot_nt(stacked(s_all, b), h).astype(BF16)

            each(per, body)

        either(place, pos_ref, j, keep_one, send_one, with_out)
        for n in range(share):
            at = pl.ds(pl.multiple_of(place.onward(pos_ref, n) * home, home), home)
            out_refs[n][...] = e_one[:, at, :]


def grad_specs(place, phase, home, size, share):
    at = during(phase, share)
    dims = shape((place.far, home, size, size))
    spec = pl.BlockSpec((1, home, size, size), lambda p, j, pos: (at(p, j) // place.near, 0, 0, 0))
    return [dims] * 2, [spec] * 2


def middle(place, pos, s_mid, e_mid, right_one, left_two):
    blocks, home, cut, share = middle_sizes(place, s_mid)
    at = [during(phase, share) for phase in range(3)]
    block = pl.BlockSpec((home, blocks, cut), lambda p, j, pos: (at[1](p, j), 0, 0))
    two, two_specs = grad_specs(place, 1, home, blocks, share)
    one, one_specs = grad_specs(place, 2, home, blocks, share)
    piece = pl.BlockSpec((home, home, cut), lambda p, j, pos: (at[2](p, j), 0, 0))
    out = call(
        functools.partial(middle_kernel, place),
        (shape((blocks, blocks, cut)), *two, *one) + (shape((blocks, home, cut)),) * share,
        (3, share),
        anywhere(share + 2 * len(flat(right_one))) + [block],
        (block, *two_specs, *one_specs) + (piece,) * share,
        [pltpu.VMEM((blocks * (blocks + PAD), cut), F32)] * 2
        + [
            pltpu.VMEM((home, blocks, cut), BF16),
            pltpu.VMEM((share, blocks, home, cut), BF16),
            pltpu.SemaphoreType.DMA((share,)),
        ]
        + whole_scratch(right_one)
        + whole_scratch(left_two),
        (*s_mid, *flat(right_one), *flat(left_two), e_mid),
        us=26,
        scalars=pos,
    )
    return out[0], out[1:3], out[3:5], list(out[5:])


def forward_two_kernel(place, pos_ref, *refs):
    share = place.far * place.near
    wide = (len(refs) - (2 * share + 11)) // 2
    g_parts, rest = refs[:share], refs[share:]
    left, right, rest = unflat(place, rest[:wide]), unflat(place, rest[wide : 2 * wide]), rest[2 * wide :]
    act_ref, keep_ref, send_ref, *rest = rest
    out_refs, rest = rest[:share], rest[share:]
    turned, fourth, g_all, g_sems, left_all, left_sems, right_all, right_sems = rest
    per, size, _ = act_ref.shape
    pitch = size + PAD
    phase, j = pl.program_id(0), pl.program_id(1)

    def rows(k):
        return pl.ds((j * per + k) * pitch, size)

    def column(k):
        return pl.ds(j * per + k, size, stride=pitch)

    def second():
        return piece_copies(right, right_all, right_sems) + share_copies(place, pos_ref, g_parts, g_all, g_sems)

    @pl.when((phase == 0) & (j == 0))
    def _():
        copies = piece_copies(left, left_all, left_sems)
        run(copies)
        run(second())
        finish(copies)

    @pl.when(phase == 0)
    def _():
        block = block_reader(place, pos_ref, left_all, j)

        def body(k):
            turned[column(k), :] = dot_tn(block(k), act_ref[k])

        each(per, body)

    @pl.when((phase == 1) & (j == 0))
    def _():
        finish(second())

    @pl.when(phase == 1)
    def _():
        block = block_reader(place, pos_ref, right_all, j)

        def with_out(grad_ref):
            def body(k):
                b = j * per + k
                third = turned[rows(k), :].astype(BF16)
                fourth[column(k), :] = dot_tn(block(k), third)
                grad_ref[0, k] = dot_nt(third, stacked(g_all, b)).astype(BF16)

            each(per, body)

        either(place, pos_ref, j, keep_ref, send_ref, with_out)

    for n in range(share):

        @pl.when((phase == 2) & (j == n))
        def _():
            base = place.onward(pos_ref, n) * per

            def body(k):
                out_refs[n][k] = fourth[pl.ds((base + k) * pitch, size), :].astype(BF16)

            each(per, body)


def forward_two(place, pos, act, g_mid, left_two, right_two):
    blocks, home, cut, share = middle_sizes(place, g_mid)
    at = during(0, share)
    grad, grad_spec = grad_specs(place, 1, home, blocks, share)
    out = call(
        functools.partial(forward_two_kernel, place),
        (*grad,) + (shape((home, blocks, cut)),) * share,
        (3, share),
        anywhere(share + 2 * len(flat(left_two))) + [pl.BlockSpec((home, blocks, cut), lambda p, j, pos: (at(p, j), 0, 0))],
        (*grad_spec,) + (pl.BlockSpec((home, blocks, cut), lambda p, j, pos: (0, 0, 0)),) * share,
        [pltpu.VMEM((blocks * (blocks + PAD), cut), F32)] * 2
        + [
            pltpu.VMEM((share, blocks, home, cut), BF16),
            pltpu.SemaphoreType.DMA((share,)),
        ]
        + whole_scratch(left_two)
        + whole_scratch(right_two),
        (*g_mid, *flat(left_two), *flat(right_two), act),
        us=20,
        scalars=pos,
    )
    return out[:2], list(out[2:])


def halves(size):
    low = 2 if size % 2 == 0 else 1
    return size // low, low


def cross(pieces):
    return lax.all_to_all(pieces, "tensor", split_axis=0, concat_axis=0, tiled=True)


def whole_tokens(x_home, g_home, factors, share, cut):
    home, size, tokens = x_home.shape
    first_left = factors[0]
    rows = first_left.shape[1]
    place = Place(share, lax.axis_size("dp"))
    pos = place.position()

    def gather(start, n):
        if n >= len(place.dp):
            return start
        got = [start] + place.dp[n].sends(start)
        return got if n == 0 else jnp.stack(got)

    def gather_far(start):
        for n in reversed(range(2, len(place.dp))):
            start = gather(start, n)
        return start

    def last_dp(start):
        return gather(start, 0) if place.dp else [start]

    def cores(piece):
        return [piece] + place.core.sends(piece)

    def by_core(own):
        return [[p[c] for p in own] for c in range(place.near)]

    def cross(pieces, n):
        return place.exchange(pieces, n) if n < share else None

    def from_y(start):
        return jnp.stack([start] + place.y.sends(start))

    n_one, n_two, n_three = (place.steps.index(step) if step in place.steps else share for step in [(0, 1), (1, 0), (1, 1)])
    one = gather_far(first_left)
    w_two = from_y(factors[3])
    rest = from_y(after(jnp.stack([factors[1], factors[2]]), one))
    g = {n: deal(place, pos, g_home, cut, n) for n in reversed(range(share))}
    got_three = cross(g, n_three)
    w_two = gather_far(after(w_two, g[share - 1]))
    one = last_dp(gather(one, 1))
    w_two = gather(w_two, 1)
    got_three, one, w_two, rest, g = slot(place, (got_three, one, w_two, rest, g))

    got_two = cross(g, n_two)
    right_two = last_dp(w_two)
    w_one = gather(gather_far(rest[:, 0]), 1)
    w_left = gather_far(rest[:, 1])
    s = first_stage(place, pos, x_home, one, cut)
    got_two, right_two, w_one, w_left, one, s, pos = slot(place, (got_two, right_two, w_one, w_left, one, list(s), pos))

    s_three = cross(s, n_three)
    right_one = last_dp(w_one)
    w_left = gather(w_left, 1)
    right_two = by_core([cores(p) for p in right_two])
    s_one = cross(s, n_one)
    got_one = cross(g, n_one)
    s_three, s_one, right_one, w_left, right_two, g, got_one = slot(
        place, (s_three, s_one, right_one, w_left, right_two, g, got_one)
    )
    g_mid = [g[0], got_one, got_two, got_three][:share]

    s_two = cross(s, n_two)
    left_two = last_dp(w_left)
    left_core = cores(left_two[0])
    right_one = by_core([cores(p) for p in right_one])
    e_mid = back_two(place, pos, g_mid, right_two)
    s_two, left_two, left_core, right_one, e_mid = slot(place, (s_two, left_two, left_core, right_one, e_mid))
    s_mid = [s[0], s_one, s_two, s_three][:share]
    left_two = by_core([left_core] + [cores(p) for p in left_two[1:]])

    act, grad_two, grad_one, e = middle(place, pos, s_mid, e_mid, right_one, left_two)

    def start_sum(keep, send):
        arrays = [keep, place.core.send(send, 1)] if place.near > 1 else [keep]
        return Sum(arrays, [place.y, home] + place.dp[::-1], (rows, size))

    def hold(parts, arrays):
        for part, kept in zip(parts, arrays):
            part.arrays, part.ready = kept

    def arrays_of(*parts):
        return [(part.arrays, part.ready) for part in parts]

    x_step, near_step, far_step = (place.dp + [None] * 3)[:3]

    e_three = cross(e, n_three)
    two, one_part = start_sum(*grad_two), start_sum(*grad_one)
    grad_three, s = forward_two(place, pos, act, g_mid, left_two, right_two)
    two.prepare(x_step)
    one_part.prepare(near_step)
    e_three, kept, grad_three, s, e = slot(place, (e_three, arrays_of(two, one_part), grad_three, s, e))
    hold([two, one_part], kept)

    e_two = cross(e, n_two)
    two.step(x_step)
    one_part.step(near_step)
    three = start_sum(*grad_three)
    e_one = cross(e, n_one)
    three.prepare(x_step)
    e_two, e_one, kept, s = slot(place, (e_two, e_one, arrays_of(two, one_part, three), s))
    hold([two, one_part, three], kept)
    e_got = [e[0], e_one, e_two, e_three][:share]

    s_three = cross(s, n_three)
    three.step(x_step)
    two.step(near_step)
    input_grad, lone = last_stage(place, pos, e_got, x_home, g_home, one)
    lone = Sum([lone], [home] + place.dp[::-1], (rows, size))
    one_part.prepare(x_step)
    lone.prepare(x_step)
    s_three, kept, input_grad, s = slot(place, (s_three, arrays_of(two, one_part, three, lone), input_grad, s))
    hold([two, one_part, three, lone], kept)

    s_two = cross(s, n_two)
    lone.step(x_step)
    three.step(near_step)
    two.step(far_step)
    kept = slot(place, arrays_of(two, one_part, three, lone))
    hold([two, one_part, three, lone], kept)

    one_part.step(x_step)
    lone.step(near_step)
    three.step(far_step)
    s_one = cross(s, n_one)
    s_two, s_one, kept = slot(place, (s_two, s_one, arrays_of(two, one_part, three, lone)))
    hold([two, one_part, three, lone], kept)

    one_part.step(far_step)
    lone.step(far_step)
    s_got = [s[0], s_one, s_two, s_three][:share]
    grad_ltwo = two.finish()
    grad_rone = one_part.finish()
    grad_rtwo = three.finish()
    grad_lone = lone.finish()
    mixed = add_home(place, pos, s_got, x_home)
    return mixed, input_grad, grad_lone, grad_rone, grad_ltwo, grad_rtwo


def split_blocks(x_home, g_home, factors, share, cut):
    home, size, tokens = x_home.shape
    far, near = halves(share)
    outer, inner = halves(lax.axis_size("dp"))
    ring_y, ring_core = Ring("tensor", (near, far)), Ring("tensor", (1, near))
    ring_z, ring_x = Ring("dp", (inner, outer)), Ring("dp", (1, inner))
    rows = factors[0].shape[1]
    n_tensor = lax.axis_size("tensor")
    groups = n_tensor // share
    held = home * share
    same_tokens = [[group * share + part for group in range(groups)] for part in range(share)]

    def go(values):
        pieces = values.reshape(home, groups, held, share, cut).transpose(1, 3, 2, 0, 4)
        got = cross(pieces.reshape(n_tensor, held, home, cut))
        return got.transpose(1, 0, 2, 3).reshape(held, size, cut)

    def back(values):
        pieces = values.reshape(held, n_tensor, home, cut).transpose(1, 0, 2, 3)
        got = cross(pieces).reshape(groups, share, held, home, cut)
        return got.transpose(3, 0, 2, 1, 4).reshape(home, size, tokens)

    def turn(values):
        moved = lax.all_to_all(
            values.reshape(held, groups, held, cut), "tensor", split_axis=1, concat_axis=0, tiled=True, axis_index_groups=same_tokens
        )
        return jnp.swapaxes(moved.reshape(size, held, cut), 0, 1)

    def whole(factor):
        one = ring_z.gather(ring_y.gather(factor))
        all_rows = ring_core.gather(ring_x.gather(one))
        return all_rows.transpose(3, 0, 4, 2, 1, 5, 6).reshape(held, size, size)

    def own_sum(partial):
        split = partial.reshape(ring_y.size, ring_core.size, home, ring_z.size, ring_x.size, rows, size)
        terms = ring_core.scatter([split], 1)
        return total(ring_y.scatter(ring_z.scatter(ring_x.scatter(terms, 3), 2), 0))

    first_left, first_right, second_left, second_right = factors
    g_mid = go(g_home)
    left_one = ring_x.gather(ring_z.gather(first_left)).transpose(2, 1, 0, 3, 4).reshape(home, size, size)
    right_one, left_two, right_two = whole(first_right), whole(second_left), whole(second_right)

    s_one = go(product("bjt,bjo->bot", x_home, left_one).astype(BF16))
    s_two = turn(product("bit,bip->bpt", s_one, right_one).astype(BF16))
    act = gelu_value(s_two.astype(F32)).astype(BF16)
    e_three = turn(product("bot,bio->bit", g_mid, right_two).astype(BF16))
    h_mid = turn(gelu_back(s_two.astype(F32), product("bot,bjo->bjt", e_three, left_two)).astype(BF16))
    e_one = back(product("bpt,bip->bit", h_mid, right_one).astype(BF16))
    s_three = turn(product("bjt,bjo->bot", act, left_two).astype(BF16))
    s_four = back(product("bit,bio->bot", s_three, right_two).astype(BF16))
    mixed = (x_home.astype(F32) + s_four.astype(F32)).astype(BF16)

    grad_rtwo = own_sum(product("bit,bot->bio", s_three, g_mid))
    grad_ltwo = own_sum(product("bjt,bot->bjo", act, e_three))
    grad_rone = own_sum(product("bit,bpt->bip", s_one, h_mid))
    grad_lone = product("bjt,bot->bjo", x_home, e_one).reshape(home, ring_z.size, ring_x.size, rows, size)
    grad_lone = total(ring_z.scatter(ring_x.scatter([grad_lone], 2), 1))
    input_grad = (g_home.astype(F32) + product("bot,bjo->bjt", e_one, left_one)).astype(BF16)
    return mixed, input_grad, grad_lone, grad_rone, grad_ltwo, grad_rtwo


def per_device(inputs, cotangent, first_left, first_right, second_left, second_right):
    n_tensor = lax.axis_size("tensor")
    home, _, size = first_left.shape
    tokens = inputs.shape[1]
    share = math.gcd(n_tensor, max(1, tokens // LANES))
    cut = tokens // share
    plan = whole_tokens if share == n_tensor else split_blocks
    mixed, input_grad, *weight_grads = plan(
        inputs.reshape(home, size, tokens),
        cotangent.reshape(home, size, tokens),
        (first_left, first_right, second_left, second_right),
        share,
        cut,
    )
    return (mixed.reshape(inputs.shape), input_grad.reshape(inputs.shape), *weight_grads)


def solution(mesh):
    wide, factor = P("tensor", "dp"), P("tensor", "dp", None)
    return jax.shard_map(
        per_device,
        mesh=mesh,
        in_specs=(wide, wide, factor, factor, factor, factor),
        out_specs=(wide, wide, factor, factor, factor, factor),
        check_vma=False,
    )
```

```python
import functools
import itertools
import math

import jax
import jax.numpy as jnp
from jax import lax
from jax.experimental import pallas as pl
from jax.experimental.pallas import tpu as pltpu
from jax.sharding import PartitionSpec as P

BF16 = jnp.bfloat16
F32 = jnp.float32
LANES = 128
PAD = 1
VMEM_BYTES = 60 * 1024 * 1024
BYTES_PER_US = 1_200_000


def gelu_value(values):
    return jax.nn.gelu(values, approximate=True)


def gelu_back(values, upstream):
    return jax.vjp(gelu_value, values)[1](upstream)[0]


def gelu_both(v):
    root, cubic = 0.7978845608028654, 0.044715
    square = v * v
    t = jnp.tanh(root * (v + cubic * (v * square)))
    half = 0.5 * (1.0 + t)
    slope = half + (0.5 * v) * (1.0 - t * t) * (root + (3.0 * cubic * root) * square)
    return v * half, slope


def product(form, left, right):
    return jnp.einsum(form, left, right, preferred_element_type=F32)


def dot(left, right, left_dim, right_dim):
    return lax.dot_general(left, right, (((left_dim,), (right_dim,)), ((), ())), preferred_element_type=F32)


def dots(lefts, rights, left_dim, right_dim):
    if len(lefts) == 1:
        return [dot(lefts[0], rights[0], left_dim, right_dim)]
    zero = jnp.zeros_like(rights[0])
    upper = jnp.concatenate([rights[0], zero], axis=1)
    lower = jnp.concatenate([zero, rights[1]], axis=1)
    out = dot(jnp.concatenate(lefts, axis=left_dim), jnp.concatenate([upper, lower], axis=0), left_dim, right_dim)
    half = out.shape[1] // 2
    return [out[:, :half], out[:, half:]]


def dots_nn(lefts, rights):
    return dots(lefts, rights, 1, 0)


def dots_tn(lefts, rights):
    return dots(lefts, rights, 0, 0)


def dots_nt(lefts, rights):
    return dots(lefts, rights, 1, 1)


def dot_nn(left, right):
    return dot(left, right, 1, 0)


def dot_nt(left, right):
    return dot(left, right, 1, 1)


def call(body, out, grid, in_specs, out_specs, scratch, args, us, scalars=None):
    spec = pltpu.PrefetchScalarGridSpec(
        num_scalar_prefetch=0 if scalars is None else 1,
        grid=grid,
        in_specs=in_specs,
        out_specs=out_specs,
        scratch_shapes=scratch,
    )
    return pl.pallas_call(
        body,
        out_shape=out,
        grid_spec=spec,
        compiler_params=pltpu.CompilerParams(
            dimension_semantics=("arbitrary",) * len(grid), vmem_limit_bytes=VMEM_BYTES
        ),
        cost_estimate=pl.CostEstimate(flops=0, bytes_accessed=int(us * BYTES_PER_US), transcendentals=0),
    )(*(() if scalars is None else (scalars,)), *args)


def pairs(count, body, unroll=8):
    group = 2 if count % 2 == 0 else 1
    each(count // group, lambda n: body([n * group + i for i in range(group)]), unroll)


def shape(dims, dtype=BF16):
    return jax.ShapeDtypeStruct(dims, dtype)


def each(count, body, unroll=16):
    def step(k, carry):
        body(k)
        return carry

    lax.fori_loop(0, count, step, 0, unroll=math.gcd(count, unroll))


def during(phase, steps):
    return lambda p, j: jnp.where(p == phase, j, jnp.where(p < phase, 0, steps - 1))


def stacked(ref, k):
    return jnp.concatenate([ref[c, k] for c in range(ref.shape[0])], axis=0)


class Ring:
    def __init__(self, axis, *digits, tied=True):
        self.axis, self.digits, self.last, self.tied = axis, digits, None, tied
        self.stride, self.size = digits[0]

    def here(self):
        return lax.rem(lax.axis_index(self.axis) // self.stride, self.size)

    def send(self, value, *steps):
        pairs = []
        for src in range(lax.axis_size(self.axis)):
            dst = src
            for (stride, size), step in zip(self.digits, steps):
                own = src // stride % size
                dst += ((own + step) % size - own) * stride
            pairs.append((src, dst))
        if self.tied and self.last is not None:
            value = after(value, self.last)
        self.last = lax.ppermute(value, self.axis, pairs)
        return self.last

    def sends(self, value):
        return [self.send(value, step) for step in range(1, self.size)]

    def gather(self, value):
        if self.size == 1:
            return value[None]
        here = self.here()
        out = jnp.zeros((self.size,) + value.shape, value.dtype)
        out = lax.dynamic_update_index_in_dim(out, value, here, 0)
        for step in range(1, self.size):
            got = self.send(value, step)
            out = lax.dynamic_update_index_in_dim(out, got, lax.rem(here - step + self.size, self.size), 0)
        return out

    def scatter(self, terms, dim, before=()):
        here = self.here()
        if self.size == 1:
            return [lax.index_in_dim(t, 0, dim, keepdims=False) for t in terms]
        out = [lax.dynamic_index_in_dim(t, here, dim, keepdims=False) for t in terms]
        for step in range(1, self.size):
            there = lax.rem(here + step, self.size)
            term = total([lax.dynamic_index_in_dim(t, there, dim, keepdims=False) for t in terms]).astype(BF16)
            out.append(self.send(after(term, *before), step))
        return out


def slot(place, values):
    values = lax.optimization_barrier(values)
    place.crossed = None
    for ring in [place.y, place.core] + place.dp + list(place.links.values()):
        ring.last = None
    return values


class Sum:
    def __init__(self, arrays, rings, tail):
        self.left = rings
        dims = [ring.size if isinstance(ring, Ring) else ring for ring in rings]
        self.arrays = [a.reshape(dims + list(tail)) for a in arrays]
        self.rings = [rings] * len(arrays)
        self.ready = []

    def cut(self, ring=None, index=None):
        out = []
        for array, rings in zip(self.arrays, self.rings):
            dim = 0
            for r in rings:
                if isinstance(r, Ring) and (r is ring or r not in self.left):
                    array = lax.dynamic_index_in_dim(array, index if r is ring else r.here(), dim, keepdims=False)
                else:
                    dim += 1
            out.append(array)
        return total(out)

    def parts(self, ring):
        return [self.cut(ring, lax.rem(ring.here() + step, ring.size)).astype(BF16) for step in range(1, ring.size)]

    def prepare(self, ring):
        self.ready = self.parts(ring) if ring in self.left else []

    def step(self, ring):
        if ring not in self.left:
            return
        rest = [r for r in self.left if r is not ring]
        parts = self.ready or self.parts(ring)
        self.ready = []
        got = [ring.send(part, step + 1) for step, part in enumerate(parts)]
        self.arrays, self.rings, self.left = self.arrays + got, self.rings + [rest] * len(got), rest

    def finish(self):
        for ring in [r for r in self.left[::-1] if isinstance(r, Ring)]:
            self.step(ring)
        return self.cut()


def finish_together(sums, rings, last):
    for part in sums:
        for ring in rings:
            part.step(ring)
    sends = list(zip(*[part.parts(last) for part in sums]))
    got = [last.send(jnp.stack(send), step + 1) for step, send in enumerate(sends)]
    for n, part in enumerate(sums):
        part.left = [r for r in part.left if r is not last]
        part.arrays, part.rings = part.arrays + [g[n] for g in got], part.rings + [part.left] * len(got)
    return [part.cut() for part in sums]


def total(terms):
    return functools.reduce(jnp.add, [t.astype(F32) for t in terms])


def after(value, *others):
    if not others:
        return value
    return lax.optimization_barrier((value,) + others)[0]


def turned_back(here, step, size):
    return lax.rem(here - step + size, size)


class Place:
    def __init__(self, share, n_dp):
        self.far, self.near = halves(share)
        self.y, self.core = Ring("tensor", (self.near, self.far)), Ring("tensor", (1, self.near), tied=False)
        self.dp, stride = [], 1
        while stride < n_dp:
            size = next(p for p in range(2, n_dp + 1) if n_dp // stride % p == 0)
            self.dp.append(Ring("dp", (stride, size)))
            stride *= size
        self.steps = [(y, c) for y in range(self.far) for c in range(self.near)]
        self.crossed = None
        self.links = {step: Ring("tensor", (self.near, self.far), (1, self.near)) for step in self.steps[1:]}
        self.rows = [ring.size for ring in self.dp]

    def position(self):
        return jnp.stack([ring.here() for ring in [self.y, self.core] + self.dp]).astype(jnp.int32)

    def onward(self, pos, n):
        y, c = self.steps[n]
        return lax.rem(pos[0] + y, self.far) * self.near + lax.rem(pos[1] + c, self.near)

    def source(self, pos, n):
        y, c = self.steps[n]
        return turned_back(pos[0], y, self.far) * self.near + turned_back(pos[1], c, self.near)

    def exchange(self, pieces, n):
        y, c = self.steps[n]
        piece = pieces[n]
        if y == 0:
            return self.core.send(piece, c)
        if self.crossed is not None:
            piece = after(piece, self.crossed)
        self.crossed = self.y.send(piece, y) if c == 0 else self.links[(y, c)].send(piece, y, c)
        return self.crossed


def piece_copies(pieces, whole, sems):
    flat_whole = [whole.at[c, d] for c in range(len(pieces)) for d in range(len(pieces[0]))]
    return [pltpu.make_async_copy(ref, dst, sems.at[n]) for n, (ref, dst) in enumerate(zip(flat(pieces), flat_whole))]


def block_reader(place, pos_ref, whole, group):
    lead = ()
    if group is not None:
        lead = (turned_back(pos_ref[0], group // place.near, place.far),)
    core = 0 if group is None else turned_back(pos_ref[1], lax.rem(group, place.near), place.near)
    places = []
    for d in range(math.prod(place.rows)):
        steps = [turned_back(pos_ref[2 + n], d // ring.stride % ring.size, ring.size) for n, ring in enumerate(place.dp)]
        places.append((core, *(steps or [0]), *lead))
    return lambda k: jnp.concatenate([whole[(*at, k)] for at in places], axis=0)


def whole_scratch(pieces):
    dims = (len(pieces), len(pieces[0])) + pieces[0][0].shape
    return [pltpu.VMEM(dims, BF16), pltpu.SemaphoreType.DMA((dims[0] * dims[1],))]


def share_copies(place, pos_ref, parts, whole, sems):
    return [pltpu.make_async_copy(ref, whole.at[place.source(pos_ref, n)], sems.at[n]) for n, ref in enumerate(parts)]


def run(copies):
    for copy in copies:
        copy.start()


def finish(copies):
    for copy in copies:
        copy.wait()


def anywhere(count):
    return [pl.BlockSpec(memory_space=pl.ANY)] * count


def flat(pieces):
    return tuple(p for row in pieces for p in row)


def unflat(place, refs):
    wide = len(refs) // place.near
    return [refs[c * wide : (c + 1) * wide] for c in range(place.near)]


def deal_kernel(pos_ref, g_ref, out_ref, turned):
    home, size, _ = g_ref.shape
    pitch = home + PAD

    def store(o):
        turned[pl.ds(o, size, stride=pitch), :] = g_ref[o].astype(F32)

    def load(b):
        out_ref[b] = turned[pl.ds(b * pitch, home), :].astype(BF16)

    each(home, store)
    each(size, load)


def deal(place, pos, g_home, cut, n):
    home, size, _ = g_home.shape
    return call(
        deal_kernel,
        shape((size, home, cut)),
        (1,),
        [pl.BlockSpec((home, size, cut), lambda i, pos: (0, 0, place.onward(pos, n)))],
        pl.BlockSpec((size, home, cut), lambda i, pos: (0, 0, 0)),
        [pltpu.VMEM((size * (home + PAD), cut), F32)],
        (g_home,),
        us=3.5,
        scalars=pos,
    )


def first_kernel(place, pos_ref, x_ref, *refs):
    share = place.far * place.near
    pieces, out_refs = refs[: -share - 3], refs[-share - 3 : -3]
    turned, whole, sems = refs[-3:]
    home, size, _ = x_ref.shape
    cut = out_refs[0].shape[2]
    pitch = home + PAD
    copies = piece_copies([pieces], whole, sems)
    block = block_reader(place, pos_ref, whole, None)

    @pl.when(pl.program_id(0) == 0)
    def _():
        run(copies)
        finish(copies)

    for n, out_ref in enumerate(out_refs):

        @pl.when(pl.program_id(0) == n)
        def _():
            lanes = pl.ds(pl.multiple_of(place.onward(pos_ref, n) * cut, cut), cut)

            def store(bs):
                out = dots_tn([block(b) for b in bs], [x_ref[b, :, lanes] for b in bs])
                for b, y in zip(bs, out):
                    turned[pl.ds(b, size, stride=pitch), :] = y

            def load(o):
                out_ref[o] = turned[pl.ds(o * pitch, home), :].astype(BF16)

            pairs(home, store)
            each(size, load)


def first_stage(place, pos, x_home, left_one, cut):
    home, size, tokens = x_home.shape
    share = tokens // cut
    return call(
        functools.partial(first_kernel, place),
        (shape((size, home, cut)),) * share,
        (share,),
        [pl.BlockSpec((home, size, tokens), lambda s, pos: (0, 0, 0))] + anywhere(len(left_one)),
        (pl.BlockSpec((size, home, cut), lambda s, pos: (0, 0, 0)),) * share,
        [pltpu.VMEM((size * (home + PAD), cut), F32)] + whole_scratch([left_one]),
        (x_home, *left_one),
        us=8,
        scalars=pos,
    )


def last_kernel(place, pos_ref, *refs):
    share = place.far * place.near
    e_refs, x_ref, g_ref = refs[:share], refs[share], refs[share + 1]
    pieces, (out_ref, grad_ref, turned, whole, sems) = refs[share + 2 : -5], refs[-5:]
    blocks, per, cut = e_refs[0].shape
    pitch = blocks + PAD
    copies = piece_copies([pieces], whole, sems)
    block = block_reader(place, pos_ref, whole, None)
    first = pl.program_id(0) * per

    @pl.when(pl.program_id(0) == 0)
    def _():
        run(copies)

    for n in range(share):
        s = place.source(pos_ref, n)

        def store(o):
            turned[s, pl.ds(o, per, stride=pitch), :] = e_refs[n][o].astype(F32)

        each(blocks, store)

    @pl.when(pl.program_id(0) == 0)
    def _():
        finish(copies)

    def load(b):
        rows = pl.ds(b * pitch, blocks)
        e_b = jnp.concatenate([turned[s, rows, :].astype(BF16) for s in range(share)], axis=1)
        out_ref[b] = (g_ref[b].astype(F32) + dot_nn(block(first + b), e_b)).astype(BF16)
        grad_ref[b] = dot_nt(x_ref[b], e_b).astype(BF16)

    each(per, load, 4)


def last_stage(place, pos, e_got, x_home, g_home, left_one):
    share = len(e_got)
    blocks, home, cut = e_got[0].shape
    _, size, tokens = x_home.shape
    per = math.gcd(home, 16)
    wide = pl.BlockSpec((per, size, tokens), lambda h, pos: (h, 0, 0))
    factor = pl.BlockSpec((per, size, size), lambda h, pos: (h, 0, 0))
    return call(
        functools.partial(last_kernel, place),
        (shape(g_home.shape), shape((home, size, size))),
        (home // per,),
        [pl.BlockSpec((blocks, per, cut), lambda h, pos: (0, h, 0))] * share + [wide, wide] + anywhere(len(left_one)),
        (wide, factor),
        [pltpu.VMEM((share, per * (blocks + PAD), cut), F32)] + whole_scratch([left_one]),
        (*e_got, x_home, g_home, *left_one),
        us=10,
        scalars=pos,
    )


def mixed_kernel(place, pos_ref, *refs):
    *s_refs, x_ref, out_ref = refs
    cut = s_refs[0].shape[2]
    for n, s_ref in enumerate(s_refs):
        lanes = pl.ds(pl.multiple_of(place.source(pos_ref, n) * cut, cut), cut)
        out_ref[:, :, lanes] = (x_ref[:, :, lanes].astype(F32) + s_ref[...].astype(F32)).astype(BF16)


def add_home(place, pos, s_got, x_home):
    home, blocks, cut = s_got[0].shape
    per = math.gcd(home, 8)
    wide = pl.BlockSpec((per,) + x_home.shape[1:], lambda h, pos: (h, 0, 0))
    return call(
        functools.partial(mixed_kernel, place),
        shape(x_home.shape),
        (home // per,),
        [pl.BlockSpec((per, blocks, cut), lambda h, pos: (h, 0, 0))] * len(s_got) + [wide],
        wide,
        [],
        (*s_got, x_home),
        us=6,
        scalars=pos,
    )


def back_two_kernel(place, pos_ref, *refs):
    share = place.far * place.near
    g_parts, factor = refs[:share], unflat(place, refs[share:-6])
    out_ref, turned, g_all, g_sems, w_all, w_sems = refs[-6:]
    per, size, _ = out_ref.shape
    pitch = size + PAD
    phase, j = pl.program_id(0), pl.program_id(1)

    @pl.when((phase == 0) & (j == 0))
    def _():
        copies = share_copies(place, pos_ref, g_parts, g_all, g_sems) + piece_copies(factor, w_all, w_sems)
        run(copies)
        finish(copies)

    @pl.when(phase == 0)
    def _():
        block = block_reader(place, pos_ref, w_all, j)

        def body(ks):
            out = dots_nn([block(k) for k in ks], [stacked(g_all, j * per + k) for k in ks])
            for k, y in zip(ks, out):
                turned[pl.ds(j * per + k, size, stride=pitch), :] = y

        pairs(per, body)

    @pl.when(phase == 1)
    def _():
        def body(k):
            out_ref[k] = turned[pl.ds((j * per + k) * pitch, size), :].astype(BF16)

        each(per, body)


def middle_sizes(place, parts):
    blocks, home, cut = parts[0].shape
    return blocks, home, cut, len(parts)


def back_two(place, pos, g_mid, right_two):
    blocks, home, cut, share = middle_sizes(place, g_mid)
    at = during(1, share)
    return call(
        functools.partial(back_two_kernel, place),
        shape((blocks, blocks, cut)),
        (2, share),
        anywhere(share + len(flat(right_two))),
        pl.BlockSpec((home, blocks, cut), lambda p, j, pos: (at(p, j), 0, 0)),
        [
            pltpu.VMEM((blocks * (blocks + PAD), cut), F32),
            pltpu.VMEM((share, blocks, home, cut), BF16),
            pltpu.SemaphoreType.DMA((share,)),
        ]
        + whole_scratch(right_two),
        (*g_mid, *flat(right_two)),
        us=10,
        scalars=pos,
    )


def either(place, pos_ref, j, keep_ref, send_ref, body):
    mine = lax.rem(j, place.near) == pos_ref[1]

    @pl.when(mine)
    def _():
        body(keep_ref)

    @pl.when(jnp.logical_not(mine))
    def _():
        body(send_ref)


def middle_kernel(place, pos_ref, *refs):
    share = place.far * place.near
    wide = (len(refs) - (2 * share + 15)) // 2
    s_parts, rest = refs[:share], refs[share:]
    one, two, rest = unflat(place, rest[:wide]), unflat(place, rest[wide : 2 * wide]), rest[2 * wide :]
    e_ref, act_ref, keep_two, send_two, keep_one, send_one, *rest = rest
    out_refs, rest = rest[:share], rest[share:]
    turned, hidden, e_one, s_all, s_sems, one_all, one_sems, two_all, two_sems = rest
    per, size, cut = act_ref.shape
    home = s_all.shape[2]
    pitch = size + PAD
    phase, j = pl.program_id(0), pl.program_id(1)

    def rows(k):
        return pl.ds((j * per + k) * pitch, size)

    def column(k):
        return pl.ds(j * per + k, size, stride=pitch)

    def second():
        return piece_copies(two, two_all, two_sems)

    @pl.when((phase == 0) & (j == 0))
    def _():
        copies = share_copies(place, pos_ref, s_parts, s_all, s_sems) + piece_copies(one, one_all, one_sems)
        run(copies)
        run(second())
        finish(copies)

    @pl.when(phase == 0)
    def _():
        block = block_reader(place, pos_ref, one_all, j)

        def body(ks):
            out = dots_tn([block(k) for k in ks], [stacked(s_all, j * per + k) for k in ks])
            for k, y in zip(ks, out):
                turned[column(k), :] = y

        pairs(per, body)

    @pl.when((phase == 1) & (j == 0))
    def _():
        finish(second())

    @pl.when(phase == 1)
    def _():
        block = block_reader(place, pos_ref, two_all, j)

        def with_out(grad_ref):
            def body(ks):
                acts, slopes, es = [], [], [e_ref[k] for k in ks]
                for k in ks:
                    value, slope = gelu_both(turned[rows(k), :].astype(BF16).astype(F32))
                    acts.append(value.astype(BF16))
                    slopes.append(slope)
                    act_ref[k] = acts[-1]
                for k, slope, y in zip(ks, slopes, dots_nn([block(k) for k in ks], es)):
                    hidden[column(k), :] = slope * y
                for k, y in zip(ks, dots_nt(acts, es)):
                    grad_ref[0, k] = y.astype(BF16)

            pairs(per, body, 4)

        either(place, pos_ref, j, keep_two, send_two, with_out)

    @pl.when(phase == 2)
    def _():
        block = block_reader(place, pos_ref, one_all, j)

        def with_out(grad_ref):
            def body(ks):
                hs = [hidden[rows(k), :].astype(BF16) for k in ks]
                for k, y in zip(ks, dots_nn([block(k) for k in ks], hs)):
                    e_one[k] = y.astype(BF16)
                for k, y in zip(ks, dots_nt([stacked(s_all, j * per + k) for k in ks], hs)):
                    grad_ref[0, k] = y.astype(BF16)

            pairs(per, body)

        either(place, pos_ref, j, keep_one, send_one, with_out)
        for n in range(share):
            at = pl.ds(pl.multiple_of(place.onward(pos_ref, n) * home, home), home)
            out_refs[n][...] = e_one[:, at, :]


def grad_specs(place, phase, home, size, share):
    at = during(phase, share)
    dims = shape((place.far, home, size, size))
    spec = pl.BlockSpec((1, home, size, size), lambda p, j, pos: (at(p, j) // place.near, 0, 0, 0))
    return [dims] * 2, [spec] * 2


def middle(place, pos, s_mid, e_mid, right_one, left_two):
    blocks, home, cut, share = middle_sizes(place, s_mid)
    at = [during(phase, share) for phase in range(3)]
    block = pl.BlockSpec((home, blocks, cut), lambda p, j, pos: (at[1](p, j), 0, 0))
    two, two_specs = grad_specs(place, 1, home, blocks, share)
    one, one_specs = grad_specs(place, 2, home, blocks, share)
    piece = pl.BlockSpec((home, home, cut), lambda p, j, pos: (at[2](p, j), 0, 0))
    out = call(
        functools.partial(middle_kernel, place),
        (shape((blocks, blocks, cut)), *two, *one) + (shape((blocks, home, cut)),) * share,
        (3, share),
        anywhere(share + 2 * len(flat(right_one))) + [block],
        (block, *two_specs, *one_specs) + (piece,) * share,
        [pltpu.VMEM((blocks * (blocks + PAD), cut), F32)] * 2
        + [
            pltpu.VMEM((home, blocks, cut), BF16),
            pltpu.VMEM((share, blocks, home, cut), BF16),
            pltpu.SemaphoreType.DMA((share,)),
        ]
        + whole_scratch(right_one)
        + whole_scratch(left_two),
        (*s_mid, *flat(right_one), *flat(left_two), e_mid),
        us=26,
        scalars=pos,
    )
    return out[0], out[1:3], out[3:5], list(out[5:])


def forward_two_kernel(place, pos_ref, *refs):
    share = place.far * place.near
    wide = (len(refs) - (2 * share + 11)) // 2
    g_parts, rest = refs[:share], refs[share:]
    left, right, rest = unflat(place, rest[:wide]), unflat(place, rest[wide : 2 * wide]), rest[2 * wide :]
    act_ref, keep_ref, send_ref, *rest = rest
    out_refs, rest = rest[:share], rest[share:]
    turned, fourth, g_all, g_sems, left_all, left_sems, right_all, right_sems = rest
    per, size, _ = act_ref.shape
    pitch = size + PAD
    phase, j = pl.program_id(0), pl.program_id(1)

    def rows(k):
        return pl.ds((j * per + k) * pitch, size)

    def column(k):
        return pl.ds(j * per + k, size, stride=pitch)

    def second():
        return piece_copies(right, right_all, right_sems) + share_copies(place, pos_ref, g_parts, g_all, g_sems)

    @pl.when((phase == 0) & (j == 0))
    def _():
        copies = piece_copies(left, left_all, left_sems)
        run(copies)
        run(second())
        finish(copies)

    @pl.when(phase == 0)
    def _():
        block = block_reader(place, pos_ref, left_all, j)

        def body(ks):
            for k, y in zip(ks, dots_tn([block(k) for k in ks], [act_ref[k] for k in ks])):
                turned[column(k), :] = y

        pairs(per, body)

    @pl.when((phase == 1) & (j == 0))
    def _():
        finish(second())

    @pl.when(phase == 1)
    def _():
        block = block_reader(place, pos_ref, right_all, j)

        def with_out(grad_ref):
            def body(ks):
                thirds = [turned[rows(k), :].astype(BF16) for k in ks]
                for k, y in zip(ks, dots_tn([block(k) for k in ks], thirds)):
                    fourth[column(k), :] = y
                for k, y in zip(ks, dots_nt(thirds, [stacked(g_all, j * per + k) for k in ks])):
                    grad_ref[0, k] = y.astype(BF16)

            pairs(per, body)

        either(place, pos_ref, j, keep_ref, send_ref, with_out)

    for n in range(share):

        @pl.when((phase == 2) & (j == n))
        def _():
            base = place.onward(pos_ref, n) * per

            def body(k):
                out_refs[n][k] = fourth[pl.ds((base + k) * pitch, size), :].astype(BF16)

            each(per, body)


def forward_two(place, pos, act, g_mid, left_two, right_two):
    blocks, home, cut, share = middle_sizes(place, g_mid)
    at = during(0, share)
    grad, grad_spec = grad_specs(place, 1, home, blocks, share)
    out = call(
        functools.partial(forward_two_kernel, place),
        (*grad,) + (shape((home, blocks, cut)),) * share,
        (3, share),
        anywhere(share + 2 * len(flat(left_two))) + [pl.BlockSpec((home, blocks, cut), lambda p, j, pos: (at(p, j), 0, 0))],
        (*grad_spec,) + (pl.BlockSpec((home, blocks, cut), lambda p, j, pos: (0, 0, 0)),) * share,
        [pltpu.VMEM((blocks * (blocks + PAD), cut), F32)] * 2
        + [
            pltpu.VMEM((share, blocks, home, cut), BF16),
            pltpu.SemaphoreType.DMA((share,)),
        ]
        + whole_scratch(left_two)
        + whole_scratch(right_two),
        (*g_mid, *flat(left_two), *flat(right_two), act),
        us=20,
        scalars=pos,
    )
    return out[:2], list(out[2:])


def halves(size):
    low = 2 if size % 2 == 0 else 1
    return size // low, low


def cross(pieces):
    return lax.all_to_all(pieces, "tensor", split_axis=0, concat_axis=0, tiled=True)


def whole_tokens(x_home, g_home, factors, share, cut):
    home, size, tokens = x_home.shape
    first_left = factors[0]
    rows = first_left.shape[1]
    place = Place(share, lax.axis_size("dp"))
    pos = place.position()

    def gather(start, n):
        if n >= len(place.dp):
            return start
        got = [start] + place.dp[n].sends(start)
        return got if n == 0 else jnp.stack(got)

    def gather_far(start):
        for n in reversed(range(2, len(place.dp))):
            start = gather(start, n)
        return start

    def last_dp(start):
        return gather(start, 0) if place.dp else [start]

    def cores(piece):
        return [piece] + place.core.sends(piece)

    def by_core(own):
        return [[p[c] for p in own] for c in range(place.near)]

    def cross(pieces, n):
        return place.exchange(pieces, n) if n < share else None

    def from_y(start):
        return jnp.stack([start] + place.y.sends(start))

    n_one, n_two, n_three = (place.steps.index(step) if step in place.steps else share for step in [(0, 1), (1, 0), (1, 1)])
    one = gather_far(first_left)
    w_two = from_y(factors[3])
    rest = from_y(after(jnp.stack([factors[1], factors[2]]), one))
    g = {n: deal(place, pos, g_home, cut, n) for n in reversed(range(share))}
    got_three = cross(g, n_three)
    w_two = gather_far(after(w_two, g[share - 1]))
    one = last_dp(gather(one, 1))
    w_two = gather(w_two, 1)
    got_three, one, w_two, rest, g = slot(place, (got_three, one, w_two, rest, g))

    got_two = cross(g, n_two)
    right_two = last_dp(w_two)
    w_one = gather(gather_far(rest[:, 0]), 1)
    w_left = gather_far(rest[:, 1])
    s = first_stage(place, pos, x_home, one, cut)
    got_two, right_two, w_one, w_left, one, s, pos = slot(place, (got_two, right_two, w_one, w_left, one, list(s), pos))

    s_three = cross(s, n_three)
    right_one = last_dp(w_one)
    w_left = gather(w_left, 1)
    right_two = by_core([cores(p) for p in right_two])
    s_one = cross(s, n_one)
    got_one = cross(g, n_one)
    s_three, s_one, right_one, w_left, right_two, g, got_one = slot(
        place, (s_three, s_one, right_one, w_left, right_two, g, got_one)
    )
    g_mid = [g[0], got_one, got_two, got_three][:share]

    s_two = cross(s, n_two)
    left_two = last_dp(w_left)
    left_core = cores(left_two[0])
    right_one = by_core([cores(p) for p in right_one])
    e_mid = back_two(place, pos, g_mid, right_two)
    s_two, left_two, left_core, right_one, e_mid = slot(place, (s_two, left_two, left_core, right_one, e_mid))
    s_mid = [s[0], s_one, s_two, s_three][:share]
    left_two = by_core([left_core] + [cores(p) for p in left_two[1:]])

    act, grad_two, grad_one, e = middle(place, pos, s_mid, e_mid, right_one, left_two)

    def start_sum(keep, send):
        arrays = [keep, place.core.send(send, 1)] if place.near > 1 else [keep]
        return Sum(arrays, [place.y, home] + place.dp[::-1], (rows, size))

    def hold(parts, arrays):
        for part, kept in zip(parts, arrays):
            part.arrays, part.ready = kept

    def arrays_of(*parts):
        return [(part.arrays, part.ready) for part in parts]

    x_step, near_step, far_step = (place.dp + [None] * 3)[:3]

    e_three = cross(e, n_three)
    two, one_part = start_sum(*grad_two), start_sum(*grad_one)
    grad_three, s = forward_two(place, pos, act, g_mid, left_two, right_two)
    two.prepare(x_step)
    one_part.prepare(near_step)
    e_three, kept, grad_three, s, e = slot(place, (e_three, arrays_of(two, one_part), grad_three, s, e))
    hold([two, one_part], kept)

    e_two = cross(e, n_two)
    two.step(x_step)
    one_part.step(near_step)
    three = start_sum(*grad_three)
    e_one = cross(e, n_one)
    three.prepare(x_step)
    e_two, e_one, kept, s = slot(place, (e_two, e_one, arrays_of(two, one_part, three), s))
    hold([two, one_part, three], kept)
    e_got = [e[0], e_one, e_two, e_three][:share]

    s_three = cross(s, n_three)
    three.step(x_step)
    one_part.step(far_step)
    two.step(near_step)
    input_grad, lone = last_stage(place, pos, e_got, x_home, g_home, one)
    lone = Sum([lone], [home] + place.dp[::-1], (rows, size))
    lone.prepare(x_step)
    s_three, kept, input_grad, s = slot(place, (s_three, arrays_of(two, one_part, three, lone), input_grad, s))
    hold([two, one_part, three, lone], kept)

    s_two = cross(s, n_two)
    lone.step(x_step)
    two.step(far_step)
    three.step(near_step)
    one_part.step(x_step)
    lone.step(near_step)
    three.step(far_step)
    s_one = cross(s, n_one)
    s_got = [s[0], s_one, s_two, s_three][:share]
    grad_ltwo, grad_rone, grad_rtwo = finish_together([two, one_part, three], place.dp, place.y)
    grad_lone = lone.finish()
    mixed = add_home(place, pos, s_got, x_home)
    return mixed, input_grad, grad_lone, grad_rone, grad_ltwo, grad_rtwo


def split_blocks(x_home, g_home, factors, share, cut):
    home, size, tokens = x_home.shape
    far, near = halves(share)
    outer, inner = halves(lax.axis_size("dp"))
    ring_y, ring_core = Ring("tensor", (near, far)), Ring("tensor", (1, near))
    ring_z, ring_x = Ring("dp", (inner, outer)), Ring("dp", (1, inner))
    rows = factors[0].shape[1]
    n_tensor = lax.axis_size("tensor")
    groups = n_tensor // share
    held = home * share
    same_tokens = [[group * share + part for group in range(groups)] for part in range(share)]

    def go(values):
        pieces = values.reshape(home, groups, held, share, cut).transpose(1, 3, 2, 0, 4)
        got = cross(pieces.reshape(n_tensor, held, home, cut))
        return got.transpose(1, 0, 2, 3).reshape(held, size, cut)

    def back(values):
        pieces = values.reshape(held, n_tensor, home, cut).transpose(1, 0, 2, 3)
        got = cross(pieces).reshape(groups, share, held, home, cut)
        return got.transpose(3, 0, 2, 1, 4).reshape(home, size, tokens)

    def turn(values):
        moved = lax.all_to_all(
            values.reshape(held, groups, held, cut), "tensor", split_axis=1, concat_axis=0, tiled=True, axis_index_groups=same_tokens
        )
        return jnp.swapaxes(moved.reshape(size, held, cut), 0, 1)

    def whole(factor):
        one = ring_z.gather(ring_y.gather(factor))
        all_rows = ring_core.gather(ring_x.gather(one))
        return all_rows.transpose(3, 0, 4, 2, 1, 5, 6).reshape(held, size, size)

    def own_sum(partial):
        split = partial.reshape(ring_y.size, ring_core.size, home, ring_z.size, ring_x.size, rows, size)
        terms = ring_core.scatter([split], 1)
        return total(ring_y.scatter(ring_z.scatter(ring_x.scatter(terms, 3), 2), 0))

    first_left, first_right, second_left, second_right = factors
    g_mid = go(g_home)
    left_one = ring_x.gather(ring_z.gather(first_left)).transpose(2, 1, 0, 3, 4).reshape(home, size, size)
    right_one, left_two, right_two = whole(first_right), whole(second_left), whole(second_right)

    s_one = go(product("bjt,bjo->bot", x_home, left_one).astype(BF16))
    s_two = turn(product("bit,bip->bpt", s_one, right_one).astype(BF16))
    act = gelu_value(s_two.astype(F32)).astype(BF16)
    e_three = turn(product("bot,bio->bit", g_mid, right_two).astype(BF16))
    h_mid = turn(gelu_back(s_two.astype(F32), product("bot,bjo->bjt", e_three, left_two)).astype(BF16))
    e_one = back(product("bpt,bip->bit", h_mid, right_one).astype(BF16))
    s_three = turn(product("bjt,bjo->bot", act, left_two).astype(BF16))
    s_four = back(product("bit,bio->bot", s_three, right_two).astype(BF16))
    mixed = (x_home.astype(F32) + s_four.astype(F32)).astype(BF16)

    grad_rtwo = own_sum(product("bit,bot->bio", s_three, g_mid))
    grad_ltwo = own_sum(product("bjt,bot->bjo", act, e_three))
    grad_rone = own_sum(product("bit,bpt->bip", s_one, h_mid))
    grad_lone = product("bjt,bot->bjo", x_home, e_one).reshape(home, ring_z.size, ring_x.size, rows, size)
    grad_lone = total(ring_z.scatter(ring_x.scatter([grad_lone], 2), 1))
    input_grad = (g_home.astype(F32) + product("bot,bjo->bjt", e_one, left_one)).astype(BF16)
    return mixed, input_grad, grad_lone, grad_rone, grad_ltwo, grad_rtwo


def per_device(inputs, cotangent, first_left, first_right, second_left, second_right):
    n_tensor = lax.axis_size("tensor")
    home, _, size = first_left.shape
    tokens = inputs.shape[1]
    share = math.gcd(n_tensor, max(1, tokens // LANES))
    cut = tokens // share
    plan = whole_tokens if share == n_tensor else split_blocks
    mixed, input_grad, *weight_grads = plan(
        inputs.reshape(home, size, tokens),
        cotangent.reshape(home, size, tokens),
        (first_left, first_right, second_left, second_right),
        share,
        cut,
    )
    return (mixed.reshape(inputs.shape), input_grad.reshape(inputs.shape), *weight_grads)


def solution(mesh):
    wide, factor = P("tensor", "dp"), P("tensor", "dp", None)
    return jax.shard_map(
        per_device,
        mesh=mesh,
        in_specs=(wide, wide, factor, factor, factor, factor),
        out_specs=(wide, wide, factor, factor, factor, factor),
        check_vma=False,
    )
```

```python
import functools
import itertools
import math

import jax
import jax.numpy as jnp
from jax import lax
from jax.experimental import pallas as pl
from jax.experimental.pallas import tpu as pltpu
from jax.sharding import PartitionSpec as P

BF16 = jnp.bfloat16
F32 = jnp.float32
LANES = 128
TILE = 16
VMEM_BYTES = 60 * 1024 * 1024
BYTES_PER_US = 1_200_000


def gelu_value(values):
    return jax.nn.gelu(values, approximate=True)


def gelu_back(values, upstream):
    return jax.vjp(gelu_value, values)[1](upstream)[0]


def gelu_both(v):
    root, cubic = 0.7978845608028654, 0.044715
    square = v * v
    t = jnp.tanh(root * (v + cubic * (v * square)))
    half = 0.5 * (1.0 + t)
    slope = half + (0.5 * v) * (1.0 - t * t) * (root + (3.0 * cubic * root) * square)
    return v * half, slope


def product(form, left, right):
    return jnp.einsum(form, left, right, preferred_element_type=F32)


def dot(left, right, left_dim, right_dim):
    return lax.dot_general(left, right, (((left_dim,), (right_dim,)), ((), ())), preferred_element_type=F32)


def dots(lefts, rights, left_dim, right_dim):
    if len(lefts) == 1:
        return [dot(lefts[0], rights[0], left_dim, right_dim)]
    zero = jnp.zeros_like(rights[0])
    upper = jnp.concatenate([rights[0], zero], axis=1)
    lower = jnp.concatenate([zero, rights[1]], axis=1)
    out = dot(jnp.concatenate(lefts, axis=left_dim), jnp.concatenate([upper, lower], axis=0), left_dim, right_dim)
    half = out.shape[1] // 2
    return [out[:, :half], out[:, half:]]


def dots_nn(lefts, rights):
    return dots(lefts, rights, 1, 0)


def dots_tn(lefts, rights):
    return dots(lefts, rights, 0, 0)


def dots_nt(lefts, rights):
    return dots(lefts, rights, 1, 1)


def dot_nn(left, right):
    return dot(left, right, 1, 0)


def dot_nt(left, right):
    return dot(left, right, 1, 1)


def call(body, out, grid, in_specs, out_specs, scratch, args, us, scalars=None):
    spec = pltpu.PrefetchScalarGridSpec(
        num_scalar_prefetch=0 if scalars is None else 1,
        grid=grid,
        in_specs=in_specs,
        out_specs=out_specs,
        scratch_shapes=scratch,
    )
    return pl.pallas_call(
        body,
        out_shape=out,
        grid_spec=spec,
        compiler_params=pltpu.CompilerParams(
            dimension_semantics=("arbitrary",) * len(grid), vmem_limit_bytes=VMEM_BYTES
        ),
        cost_estimate=pl.CostEstimate(flops=0, bytes_accessed=int(us * BYTES_PER_US), transcendentals=0),
    )(*(() if scalars is None else (scalars,)), *args)


def pairs(count, body, unroll=8):
    group = 2 if count % 2 == 0 else 1
    each(count // group, lambda n: body([n * group + i for i in range(group)]), unroll)


def turn(source, out_ref, at):
    n, size, _ = source.shape
    for i in range(0, size, TILE):
        out_ref[i : i + TILE, pl.ds(pl.multiple_of(at, TILE), n), :] = jnp.swapaxes(source[:, i : i + TILE, :], 0, 1)


def shape(dims, dtype=BF16):
    return jax.ShapeDtypeStruct(dims, dtype)


def each(count, body, unroll=16):
    def step(k, carry):
        body(k)
        return carry

    lax.fori_loop(0, count, step, 0, unroll=math.gcd(count, unroll))


def during(phase, steps):
    return lambda p, j: jnp.where(p == phase, j, jnp.where(p < phase, 0, steps - 1))


def stacked(ref, k):
    return jnp.concatenate([ref[c, k] for c in range(ref.shape[0])], axis=0)


class Ring:
    def __init__(self, axis, *digits, tied=True):
        self.axis, self.digits, self.last, self.tied = axis, digits, None, tied
        self.stride, self.size = digits[0]

    def here(self):
        return lax.rem(lax.axis_index(self.axis) // self.stride, self.size)

    def send(self, value, *steps):
        pairs = []
        for src in range(lax.axis_size(self.axis)):
            dst = src
            for (stride, size), step in zip(self.digits, steps):
                own = src // stride % size
                dst += ((own + step) % size - own) * stride
            pairs.append((src, dst))
        if self.tied and self.last is not None:
            value = after(value, self.last)
        self.last = lax.ppermute(value, self.axis, pairs)
        return self.last

    def sends(self, value):
        return [self.send(value, step) for step in range(1, self.size)]

    def gather(self, value):
        if self.size == 1:
            return value[None]
        here = self.here()
        out = jnp.zeros((self.size,) + value.shape, value.dtype)
        out = lax.dynamic_update_index_in_dim(out, value, here, 0)
        for step in range(1, self.size):
            got = self.send(value, step)
            out = lax.dynamic_update_index_in_dim(out, got, lax.rem(here - step + self.size, self.size), 0)
        return out

    def scatter(self, terms, dim, before=()):
        here = self.here()
        if self.size == 1:
            return [lax.index_in_dim(t, 0, dim, keepdims=False) for t in terms]
        out = [lax.dynamic_index_in_dim(t, here, dim, keepdims=False) for t in terms]
        for step in range(1, self.size):
            there = lax.rem(here + step, self.size)
            term = total([lax.dynamic_index_in_dim(t, there, dim, keepdims=False) for t in terms]).astype(BF16)
            out.append(self.send(after(term, *before), step))
        return out


def slot(place, values):
    values = lax.optimization_barrier(values)
    place.crossed = None
    for ring in [place.y, place.core] + place.dp + list(place.links.values()):
        ring.last = None
    return values


class Sum:
    def __init__(self, arrays, rings, tail):
        self.left = rings
        dims = [ring.size if isinstance(ring, Ring) else ring for ring in rings]
        self.arrays = [a.reshape(dims + list(tail)) for a in arrays]
        self.rings = [rings] * len(arrays)
        self.ready = []

    def cut(self, ring=None, index=None):
        out = []
        for array, rings in zip(self.arrays, self.rings):
            dim = 0
            for r in rings:
                if isinstance(r, Ring) and (r is ring or r not in self.left):
                    array = lax.dynamic_index_in_dim(array, index if r is ring else r.here(), dim, keepdims=False)
                else:
                    dim += 1
            out.append(array)
        return total(out)

    def parts(self, ring):
        return [self.cut(ring, lax.rem(ring.here() + step, ring.size)).astype(BF16) for step in range(1, ring.size)]

    def prepare(self, ring):
        self.ready = self.parts(ring) if ring in self.left else []

    def step(self, ring):
        if ring not in self.left:
            return
        rest = [r for r in self.left if r is not ring]
        parts = self.ready or self.parts(ring)
        self.ready = []
        got = [ring.send(part, step + 1) for step, part in enumerate(parts)]
        self.arrays, self.rings, self.left = self.arrays + got, self.rings + [rest] * len(got), rest

    def finish(self):
        for ring in [r for r in self.left[::-1] if isinstance(r, Ring)]:
            self.step(ring)
        return self.cut()


def finish_together(sums, rings, last):
    for part in sums:
        for ring in rings:
            part.step(ring)
    sends = list(zip(*[part.parts(last) for part in sums]))
    got = [last.send(jnp.stack(send), step + 1) for step, send in enumerate(sends)]
    for n, part in enumerate(sums):
        part.left = [r for r in part.left if r is not last]
        part.arrays, part.rings = part.arrays + [g[n] for g in got], part.rings + [part.left] * len(got)
    return [part.cut() for part in sums]


def total(terms):
    return functools.reduce(jnp.add, [t.astype(F32) for t in terms])


def after(value, *others):
    if not others:
        return value
    return lax.optimization_barrier((value,) + others)[0]


def turned_back(here, step, size):
    return lax.rem(here - step + size, size)


class Place:
    def __init__(self, share, n_dp):
        self.far, self.near = halves(share)
        self.y, self.core = Ring("tensor", (self.near, self.far)), Ring("tensor", (1, self.near), tied=False)
        self.dp, stride = [], 1
        while stride < n_dp:
            size = next(p for p in range(2, n_dp + 1) if n_dp // stride % p == 0)
            self.dp.append(Ring("dp", (stride, size)))
            stride *= size
        self.steps = [(y, c) for y in range(self.far) for c in range(self.near)]
        self.crossed = None
        self.links = {step: Ring("tensor", (self.near, self.far), (1, self.near)) for step in self.steps[1:]}
        self.rows = [ring.size for ring in self.dp]

    def position(self):
        return jnp.stack([ring.here() for ring in [self.y, self.core] + self.dp]).astype(jnp.int32)

    def onward(self, pos, n):
        y, c = self.steps[n]
        return lax.rem(pos[0] + y, self.far) * self.near + lax.rem(pos[1] + c, self.near)

    def source(self, pos, n):
        y, c = self.steps[n]
        return turned_back(pos[0], y, self.far) * self.near + turned_back(pos[1], c, self.near)

    def exchange(self, pieces, n):
        y, c = self.steps[n]
        piece = pieces[n]
        if y == 0:
            return self.core.send(piece, c)
        if self.crossed is not None:
            piece = after(piece, self.crossed)
        self.crossed = self.y.send(piece, y) if c == 0 else self.links[(y, c)].send(piece, y, c)
        return self.crossed


def piece_copies(pieces, whole, sems):
    flat_whole = [whole.at[c, d] for c in range(len(pieces)) for d in range(len(pieces[0]))]
    return [pltpu.make_async_copy(ref, dst, sems.at[n]) for n, (ref, dst) in enumerate(zip(flat(pieces), flat_whole))]


def block_reader(place, pos_ref, whole, group):
    lead = ()
    if group is not None:
        lead = (turned_back(pos_ref[0], group // place.near, place.far),)
    core = 0 if group is None else turned_back(pos_ref[1], lax.rem(group, place.near), place.near)
    places = []
    for d in range(math.prod(place.rows)):
        steps = [turned_back(pos_ref[2 + n], d // ring.stride % ring.size, ring.size) for n, ring in enumerate(place.dp)]
        places.append((core, *(steps or [0]), *lead))
    return lambda k: jnp.concatenate([whole[(*at, k)] for at in places], axis=0)


def whole_scratch(pieces):
    dims = (len(pieces), len(pieces[0])) + pieces[0][0].shape
    return [pltpu.VMEM(dims, BF16), pltpu.SemaphoreType.DMA((dims[0] * dims[1],))]


def share_copies(place, pos_ref, parts, whole, sems):
    return [pltpu.make_async_copy(ref, whole.at[place.source(pos_ref, n)], sems.at[n]) for n, ref in enumerate(parts)]


def run(copies):
    for copy in copies:
        copy.start()


def finish(copies):
    for copy in copies:
        copy.wait()


def anywhere(count):
    return [pl.BlockSpec(memory_space=pl.ANY)] * count


def flat(pieces):
    return tuple(p for row in pieces for p in row)


def unflat(place, refs):
    wide = len(refs) // place.near
    return [refs[c * wide : (c + 1) * wide] for c in range(place.near)]


def deal_kernel(pos_ref, g_ref, out_ref):
    for o in range(0, g_ref.shape[0], TILE):
        turn(g_ref.at[o : o + TILE], out_ref, o)


def deal(place, pos, g_home, cut, n):
    home, size, _ = g_home.shape
    return call(
        deal_kernel,
        shape((size, home, cut)),
        (1,),
        [pl.BlockSpec((home, size, cut), lambda i, pos: (0, 0, place.onward(pos, n)))],
        pl.BlockSpec((size, home, cut), lambda i, pos: (0, 0, 0)),
        [],
        (g_home,),
        us=3.5,
        scalars=pos,
    )


def first_kernel(place, pos_ref, x_ref, *refs):
    share = place.far * place.near
    pieces, out_refs = refs[: -share - 3], refs[-share - 3 : -3]
    stage, whole, sems = refs[-3:]
    home = x_ref.shape[0]
    cut = out_refs[0].shape[2]
    copies = piece_copies([pieces], whole, sems)
    block = block_reader(place, pos_ref, whole, None)

    @pl.when(pl.program_id(0) == 0)
    def _():
        run(copies)
        finish(copies)

    for n, out_ref in enumerate(out_refs):

        @pl.when(pl.program_id(0) == n)
        def _():
            lanes = pl.ds(pl.multiple_of(place.onward(pos_ref, n) * cut, cut), cut)

            for b in range(0, home, TILE):

                def store(ks):
                    out = dots_tn([block(b + k) for k in ks], [x_ref[b + k, :, lanes] for k in ks])
                    for k, y in zip(ks, out):
                        stage[b + k] = y.astype(BF16)

                pairs(TILE, store)
                turn(stage.at[b : b + TILE], out_ref, b)


def first_stage(place, pos, x_home, left_one, cut):
    home, size, tokens = x_home.shape
    share = tokens // cut
    return call(
        functools.partial(first_kernel, place),
        (shape((size, home, cut)),) * share,
        (share,),
        [pl.BlockSpec((home, size, tokens), lambda s, pos: (0, 0, 0))] + anywhere(len(left_one)),
        (pl.BlockSpec((size, home, cut), lambda s, pos: (0, 0, 0)),) * share,
        [pltpu.VMEM((home, size, cut), BF16)] + whole_scratch([left_one]),
        (x_home, *left_one),
        us=8,
        scalars=pos,
    )


def last_kernel(place, pos_ref, *refs):
    share = place.far * place.near
    e_refs, x_ref, g_ref = refs[:share], refs[share], refs[share + 1]
    pieces, (out_ref, grad_ref, turned, whole, sems) = refs[share + 2 : -5], refs[-5:]
    blocks, per, _ = e_refs[0].shape
    copies = piece_copies([pieces], whole, sems)
    block = block_reader(place, pos_ref, whole, None)
    first = pl.program_id(0) * per

    @pl.when(pl.program_id(0) == 0)
    def _():
        run(copies)

    for n in range(share):
        into = turned.at[place.source(pos_ref, n)]
        for o in range(0, blocks, TILE):
            turn(e_refs[n].at[o : o + TILE], into, o)

    @pl.when(pl.program_id(0) == 0)
    def _():
        finish(copies)

    def load(b):
        e_b = jnp.concatenate([turned[s, b] for s in range(share)], axis=1)
        out_ref[b] = (g_ref[b].astype(F32) + dot_nn(block(first + b), e_b)).astype(BF16)
        grad_ref[b] = dot_nt(x_ref[b], e_b).astype(BF16)

    each(per, load, 4)


def last_stage(place, pos, e_got, x_home, g_home, left_one):
    share = len(e_got)
    blocks, home, cut = e_got[0].shape
    _, size, tokens = x_home.shape
    per = math.gcd(home, 16)
    wide = pl.BlockSpec((per, size, tokens), lambda h, pos: (h, 0, 0))
    factor = pl.BlockSpec((per, size, size), lambda h, pos: (h, 0, 0))
    return call(
        functools.partial(last_kernel, place),
        (shape(g_home.shape), shape((home, size, size))),
        (home // per,),
        [pl.BlockSpec((blocks, per, cut), lambda h, pos: (0, h, 0))] * share + [wide, wide] + anywhere(len(left_one)),
        (wide, factor),
        [pltpu.VMEM((share, per, blocks, cut), BF16)] + whole_scratch([left_one]),
        (*e_got, x_home, g_home, *left_one),
        us=10,
        scalars=pos,
    )


def mixed_kernel(place, pos_ref, *refs):
    *s_refs, x_ref, out_ref = refs
    cut = s_refs[0].shape[2]
    for n, s_ref in enumerate(s_refs):
        lanes = pl.ds(pl.multiple_of(place.source(pos_ref, n) * cut, cut), cut)
        out_ref[:, :, lanes] = (x_ref[:, :, lanes].astype(F32) + s_ref[...].astype(F32)).astype(BF16)


def add_home(place, pos, s_got, x_home):
    home, blocks, cut = s_got[0].shape
    per = math.gcd(home, 8)
    wide = pl.BlockSpec((per,) + x_home.shape[1:], lambda h, pos: (h, 0, 0))
    return call(
        functools.partial(mixed_kernel, place),
        shape(x_home.shape),
        (home // per,),
        [pl.BlockSpec((per, blocks, cut), lambda h, pos: (h, 0, 0))] * len(s_got) + [wide],
        wide,
        [],
        (*s_got, x_home),
        us=6,
        scalars=pos,
    )


def back_two_kernel(place, pos_ref, *refs):
    share = place.far * place.near
    g_parts, factor = refs[:share], unflat(place, refs[share:-7])
    out_ref, turned, stage, g_all, g_sems, w_all, w_sems = refs[-7:]
    per = out_ref.shape[0]
    phase, j = pl.program_id(0), pl.program_id(1)

    @pl.when((phase == 0) & (j == 0))
    def _():
        copies = share_copies(place, pos_ref, g_parts, g_all, g_sems) + piece_copies(factor, w_all, w_sems)
        run(copies)
        finish(copies)

    @pl.when(phase == 0)
    def _():
        block = block_reader(place, pos_ref, w_all, j)

        def body(ks):
            out = dots_nn([block(k) for k in ks], [stacked(g_all, j * per + k) for k in ks])
            for k, y in zip(ks, out):
                stage[k] = y.astype(BF16)

        staged(per, body, stage, turned, j)

    @pl.when(phase == 1)
    def _():
        def body(k):
            out_ref[k] = turned[j * per + k]

        each(per, body)


def staged(per, body, stage, turned, j):
    for k in range(0, per, TILE):
        pairs(TILE, lambda ks: body([k + i for i in ks]))
        turn(stage.at[k : k + TILE], turned, j * per + k)


def middle_sizes(place, parts):
    blocks, home, cut = parts[0].shape
    return blocks, home, cut, len(parts)


def back_two(place, pos, g_mid, right_two):
    blocks, home, cut, share = middle_sizes(place, g_mid)
    at = during(1, share)
    return call(
        functools.partial(back_two_kernel, place),
        shape((blocks, blocks, cut)),
        (2, share),
        anywhere(share + len(flat(right_two))),
        pl.BlockSpec((home, blocks, cut), lambda p, j, pos: (at(p, j), 0, 0)),
        [
            pltpu.VMEM((blocks, blocks, cut), BF16),
            pltpu.VMEM((home, blocks, cut), BF16),
            pltpu.VMEM((share, blocks, home, cut), BF16),
            pltpu.SemaphoreType.DMA((share,)),
        ]
        + whole_scratch(right_two),
        (*g_mid, *flat(right_two)),
        us=10,
        scalars=pos,
    )


def either(place, pos_ref, j, keep_ref, send_ref, body):
    mine = lax.rem(j, place.near) == pos_ref[1]

    @pl.when(mine)
    def _():
        body(keep_ref)

    @pl.when(jnp.logical_not(mine))
    def _():
        body(send_ref)


def middle_kernel(place, pos_ref, *refs):
    share = place.far * place.near
    wide = (len(refs) - (2 * share + 15)) // 2
    s_parts, rest = refs[:share], refs[share:]
    one, two, rest = unflat(place, rest[:wide]), unflat(place, rest[wide : 2 * wide]), rest[2 * wide :]
    e_ref, act_ref, keep_two, send_two, keep_one, send_one, *rest = rest
    out_refs, rest = rest[:share], rest[share:]
    turned, hidden, e_one, s_all, s_sems, one_all, one_sems, two_all, two_sems = rest
    per, home = act_ref.shape[0], s_all.shape[2]
    phase, j = pl.program_id(0), pl.program_id(1)

    def second():
        return piece_copies(two, two_all, two_sems)

    @pl.when((phase == 0) & (j == 0))
    def _():
        copies = share_copies(place, pos_ref, s_parts, s_all, s_sems) + piece_copies(one, one_all, one_sems)
        run(copies)
        run(second())
        finish(copies)

    @pl.when(phase == 0)
    def _():
        block = block_reader(place, pos_ref, one_all, j)

        def body(ks):
            out = dots_tn([block(k) for k in ks], [stacked(s_all, j * per + k) for k in ks])
            for k, y in zip(ks, out):
                e_one[k] = y.astype(BF16)

        staged(per, body, e_one, turned, j)

    @pl.when((phase == 1) & (j == 0))
    def _():
        finish(second())

    @pl.when(phase == 1)
    def _():
        block = block_reader(place, pos_ref, two_all, j)

        def with_out(grad_ref):
            def body(ks):
                acts, slopes, es = [], [], [e_ref[k] for k in ks]
                for k in ks:
                    value, slope = gelu_both(turned[j * per + k].astype(F32))
                    acts.append(value.astype(BF16))
                    slopes.append(slope)
                    act_ref[k] = acts[-1]
                for k, slope, y in zip(ks, slopes, dots_nn([block(k) for k in ks], es)):
                    e_one[k] = (slope * y).astype(BF16)
                for k, y in zip(ks, dots_nt(acts, es)):
                    grad_ref[0, k] = y.astype(BF16)

            staged(per, body, e_one, hidden, j)

        either(place, pos_ref, j, keep_two, send_two, with_out)

    @pl.when(phase == 2)
    def _():
        block = block_reader(place, pos_ref, one_all, j)

        def with_out(grad_ref):
            def body(ks):
                hs = [hidden[j * per + k] for k in ks]
                for k, y in zip(ks, dots_nn([block(k) for k in ks], hs)):
                    e_one[k] = y.astype(BF16)
                for k, y in zip(ks, dots_nt([stacked(s_all, j * per + k) for k in ks], hs)):
                    grad_ref[0, k] = y.astype(BF16)

            pairs(per, body)

        either(place, pos_ref, j, keep_one, send_one, with_out)
        for n in range(share):
            at = pl.ds(pl.multiple_of(place.onward(pos_ref, n) * home, home), home)
            out_refs[n][...] = e_one[:, at, :]


def grad_specs(place, phase, home, size, share):
    at = during(phase, share)
    dims = shape((place.far, home, size, size))
    spec = pl.BlockSpec((1, home, size, size), lambda p, j, pos: (at(p, j) // place.near, 0, 0, 0))
    return [dims] * 2, [spec] * 2


def middle(place, pos, s_mid, e_mid, right_one, left_two):
    blocks, home, cut, share = middle_sizes(place, s_mid)
    at = [during(phase, share) for phase in range(3)]
    block = pl.BlockSpec((home, blocks, cut), lambda p, j, pos: (at[1](p, j), 0, 0))
    two, two_specs = grad_specs(place, 1, home, blocks, share)
    one, one_specs = grad_specs(place, 2, home, blocks, share)
    piece = pl.BlockSpec((home, home, cut), lambda p, j, pos: (at[2](p, j), 0, 0))
    out = call(
        functools.partial(middle_kernel, place),
        (shape((blocks, blocks, cut)), *two, *one) + (shape((blocks, home, cut)),) * share,
        (3, share),
        anywhere(share + 2 * len(flat(right_one))) + [block],
        (block, *two_specs, *one_specs) + (piece,) * share,
        [pltpu.VMEM((blocks, blocks, cut), BF16)] * 2
        + [
            pltpu.VMEM((home, blocks, cut), BF16),
            pltpu.VMEM((share, blocks, home, cut), BF16),
            pltpu.SemaphoreType.DMA((share,)),
        ]
        + whole_scratch(right_one)
        + whole_scratch(left_two),
        (*s_mid, *flat(right_one), *flat(left_two), e_mid),
        us=26,
        scalars=pos,
    )
    return out[0], out[1:3], out[3:5], list(out[5:])


def forward_two_kernel(place, pos_ref, *refs):
    share = place.far * place.near
    wide = (len(refs) - (2 * share + 12)) // 2
    g_parts, rest = refs[:share], refs[share:]
    left, right, rest = unflat(place, rest[:wide]), unflat(place, rest[wide : 2 * wide]), rest[2 * wide :]
    act_ref, keep_ref, send_ref, *rest = rest
    out_refs, rest = rest[:share], rest[share:]
    turned, fourth, stage, g_all, g_sems, left_all, left_sems, right_all, right_sems = rest
    per = act_ref.shape[0]
    phase, j = pl.program_id(0), pl.program_id(1)

    def second():
        return piece_copies(right, right_all, right_sems) + share_copies(place, pos_ref, g_parts, g_all, g_sems)

    @pl.when((phase == 0) & (j == 0))
    def _():
        copies = piece_copies(left, left_all, left_sems)
        run(copies)
        run(second())
        finish(copies)

    @pl.when(phase == 0)
    def _():
        block = block_reader(place, pos_ref, left_all, j)

        def body(ks):
            for k, y in zip(ks, dots_tn([block(k) for k in ks], [act_ref[k] for k in ks])):
                stage[k] = y.astype(BF16)

        staged(per, body, stage, turned, j)

    @pl.when((phase == 1) & (j == 0))
    def _():
        finish(second())

    @pl.when(phase == 1)
    def _():
        block = block_reader(place, pos_ref, right_all, j)

        def with_out(grad_ref):
            def body(ks):
                thirds = [turned[j * per + k] for k in ks]
                for k, y in zip(ks, dots_tn([block(k) for k in ks], thirds)):
                    stage[k] = y.astype(BF16)
                for k, y in zip(ks, dots_nt(thirds, [stacked(g_all, j * per + k) for k in ks])):
                    grad_ref[0, k] = y.astype(BF16)

            staged(per, body, stage, fourth, j)

        either(place, pos_ref, j, keep_ref, send_ref, with_out)

    for n in range(share):

        @pl.when((phase == 2) & (j == n))
        def _():
            base = place.onward(pos_ref, n) * per

            def body(k):
                out_refs[n][k] = fourth[base + k]

            each(per, body)


def forward_two(place, pos, act, g_mid, left_two, right_two):
    blocks, home, cut, share = middle_sizes(place, g_mid)
    at = during(0, share)
    grad, grad_spec = grad_specs(place, 1, home, blocks, share)
    out = call(
        functools.partial(forward_two_kernel, place),
        (*grad,) + (shape((home, blocks, cut)),) * share,
        (3, share),
        anywhere(share + 2 * len(flat(left_two))) + [pl.BlockSpec((home, blocks, cut), lambda p, j, pos: (at(p, j), 0, 0))],
        (*grad_spec,) + (pl.BlockSpec((home, blocks, cut), lambda p, j, pos: (0, 0, 0)),) * share,
        [pltpu.VMEM((blocks, blocks, cut), BF16)] * 2
        + [
            pltpu.VMEM((home, blocks, cut), BF16),
            pltpu.VMEM((share, blocks, home, cut), BF16),
            pltpu.SemaphoreType.DMA((share,)),
        ]
        + whole_scratch(left_two)
        + whole_scratch(right_two),
        (*g_mid, *flat(left_two), *flat(right_two), act),
        us=20,
        scalars=pos,
    )
    return out[:2], list(out[2:])


def halves(size):
    low = 2 if size % 2 == 0 else 1
    return size // low, low


def cross(pieces):
    return lax.all_to_all(pieces, "tensor", split_axis=0, concat_axis=0, tiled=True)


def whole_tokens(x_home, g_home, factors, share, cut):
    home, size, tokens = x_home.shape
    first_left = factors[0]
    rows = first_left.shape[1]
    place = Place(share, lax.axis_size("dp"))
    pos = place.position()

    def gather(start, n):
        if n >= len(place.dp):
            return start
        got = [start] + place.dp[n].sends(start)
        return got if n == 0 else jnp.stack(got)

    def gather_far(start):
        for n in reversed(range(2, len(place.dp))):
            start = gather(start, n)
        return start

    def last_dp(start):
        return gather(start, 0) if place.dp else [start]

    def cores(piece):
        return [piece] + place.core.sends(piece)

    def by_core(own):
        return [[p[c] for p in own] for c in range(place.near)]

    def cross(pieces, n):
        return place.exchange(pieces, n) if n < share else None

    def from_y(start):
        return jnp.stack([start] + place.y.sends(start))

    n_one, n_two, n_three = (place.steps.index(step) if step in place.steps else share for step in [(0, 1), (1, 0), (1, 1)])
    one = gather_far(first_left)
    w_two = from_y(factors[3])
    rest = from_y(after(jnp.stack([factors[1], factors[2]]), one))
    g = {n: deal(place, pos, g_home, cut, n) for n in reversed(range(share))}
    got_three = cross(g, n_three)
    w_two = gather_far(after(w_two, g[share - 1]))
    one = last_dp(gather(one, 1))
    w_two = gather(w_two, 1)
    got_three, one, w_two, rest, g = slot(place, (got_three, one, w_two, rest, g))

    got_two = cross(g, n_two)
    right_two = last_dp(w_two)
    w_one = gather(gather_far(rest[:, 0]), 1)
    w_left = gather_far(rest[:, 1])
    s = first_stage(place, pos, x_home, one, cut)
    got_two, right_two, w_one, w_left, one, s, pos = slot(place, (got_two, right_two, w_one, w_left, one, list(s), pos))

    s_three = cross(s, n_three)
    right_one = last_dp(w_one)
    w_left = gather(w_left, 1)
    right_two = by_core([cores(p) for p in right_two])
    s_one = cross(s, n_one)
    got_one = cross(g, n_one)
    s_three, s_one, right_one, w_left, right_two, g, got_one = slot(
        place, (s_three, s_one, right_one, w_left, right_two, g, got_one)
    )
    g_mid = [g[0], got_one, got_two, got_three][:share]

    s_two = cross(s, n_two)
    left_two = last_dp(w_left)
    left_core = cores(left_two[0])
    right_one = by_core([cores(p) for p in right_one])
    e_mid = back_two(place, pos, g_mid, right_two)
    s_two, left_two, left_core, right_one, e_mid = slot(place, (s_two, left_two, left_core, right_one, e_mid))
    s_mid = [s[0], s_one, s_two, s_three][:share]
    left_two = by_core([left_core] + [cores(p) for p in left_two[1:]])

    act, grad_two, grad_one, e = middle(place, pos, s_mid, e_mid, right_one, left_two)

    def start_sum(keep, send):
        arrays = [keep, place.core.send(send, 1)] if place.near > 1 else [keep]
        return Sum(arrays, [place.y, home] + place.dp[::-1], (rows, size))

    def hold(parts, arrays):
        for part, kept in zip(parts, arrays):
            part.arrays, part.ready = kept

    def arrays_of(*parts):
        return [(part.arrays, part.ready) for part in parts]

    x_step, near_step, far_step = (place.dp + [None] * 3)[:3]

    e_three = cross(e, n_three)
    two, one_part = start_sum(*grad_two), start_sum(*grad_one)
    grad_three, s = forward_two(place, pos, act, g_mid, left_two, right_two)
    two.prepare(x_step)
    one_part.prepare(near_step)
    e_three, kept, grad_three, s, e = slot(place, (e_three, arrays_of(two, one_part), grad_three, s, e))
    hold([two, one_part], kept)

    e_two = cross(e, n_two)
    two.step(x_step)
    one_part.step(near_step)
    three = start_sum(*grad_three)
    e_one = cross(e, n_one)
    three.prepare(x_step)
    e_two, e_one, kept, s = slot(place, (e_two, e_one, arrays_of(two, one_part, three), s))
    hold([two, one_part, three], kept)
    e_got = [e[0], e_one, e_two, e_three][:share]

    s_three = cross(s, n_three)
    three.step(x_step)
    one_part.step(far_step)
    two.step(near_step)
    input_grad, lone = last_stage(place, pos, e_got, x_home, g_home, one)
    lone = Sum([lone], [home] + place.dp[::-1], (rows, size))
    lone.prepare(x_step)
    s_three, kept, input_grad, s = slot(place, (s_three, arrays_of(two, one_part, three, lone), input_grad, s))
    hold([two, one_part, three, lone], kept)

    s_two = cross(s, n_two)
    lone.step(x_step)
    two.step(far_step)
    three.step(near_step)
    one_part.step(x_step)
    lone.step(near_step)
    three.step(far_step)
    s_one = cross(s, n_one)
    s_got = [s[0], s_one, s_two, s_three][:share]
    grad_ltwo, grad_rone, grad_rtwo = finish_together([two, one_part, three], place.dp, place.y)
    grad_lone = lone.finish()
    mixed = add_home(place, pos, s_got, x_home)
    return mixed, input_grad, grad_lone, grad_rone, grad_ltwo, grad_rtwo


def split_blocks(x_home, g_home, factors, share, cut):
    home, size, tokens = x_home.shape
    far, near = halves(share)
    outer, inner = halves(lax.axis_size("dp"))
    ring_y, ring_core = Ring("tensor", (near, far)), Ring("tensor", (1, near))
    ring_z, ring_x = Ring("dp", (inner, outer)), Ring("dp", (1, inner))
    rows = factors[0].shape[1]
    n_tensor = lax.axis_size("tensor")
    groups = n_tensor // share
    held = home * share
    same_tokens = [[group * share + part for group in range(groups)] for part in range(share)]

    def go(values):
        pieces = values.reshape(home, groups, held, share, cut).transpose(1, 3, 2, 0, 4)
        got = cross(pieces.reshape(n_tensor, held, home, cut))
        return got.transpose(1, 0, 2, 3).reshape(held, size, cut)

    def back(values):
        pieces = values.reshape(held, n_tensor, home, cut).transpose(1, 0, 2, 3)
        got = cross(pieces).reshape(groups, share, held, home, cut)
        return got.transpose(3, 0, 2, 1, 4).reshape(home, size, tokens)

    def turn(values):
        moved = lax.all_to_all(
            values.reshape(held, groups, held, cut), "tensor", split_axis=1, concat_axis=0, tiled=True, axis_index_groups=same_tokens
        )
        return jnp.swapaxes(moved.reshape(size, held, cut), 0, 1)

    def whole(factor):
        one = ring_z.gather(ring_y.gather(factor))
        all_rows = ring_core.gather(ring_x.gather(one))
        return all_rows.transpose(3, 0, 4, 2, 1, 5, 6).reshape(held, size, size)

    def own_sum(partial):
        split = partial.reshape(ring_y.size, ring_core.size, home, ring_z.size, ring_x.size, rows, size)
        terms = ring_core.scatter([split], 1)
        return total(ring_y.scatter(ring_z.scatter(ring_x.scatter(terms, 3), 2), 0))

    first_left, first_right, second_left, second_right = factors
    g_mid = go(g_home)
    left_one = ring_x.gather(ring_z.gather(first_left)).transpose(2, 1, 0, 3, 4).reshape(home, size, size)
    right_one, left_two, right_two = whole(first_right), whole(second_left), whole(second_right)

    s_one = go(product("bjt,bjo->bot", x_home, left_one).astype(BF16))
    s_two = turn(product("bit,bip->bpt", s_one, right_one).astype(BF16))
    act = gelu_value(s_two.astype(F32)).astype(BF16)
    e_three = turn(product("bot,bio->bit", g_mid, right_two).astype(BF16))
    h_mid = turn(gelu_back(s_two.astype(F32), product("bot,bjo->bjt", e_three, left_two)).astype(BF16))
    e_one = back(product("bpt,bip->bit", h_mid, right_one).astype(BF16))
    s_three = turn(product("bjt,bjo->bot", act, left_two).astype(BF16))
    s_four = back(product("bit,bio->bot", s_three, right_two).astype(BF16))
    mixed = (x_home.astype(F32) + s_four.astype(F32)).astype(BF16)

    grad_rtwo = own_sum(product("bit,bot->bio", s_three, g_mid))
    grad_ltwo = own_sum(product("bjt,bot->bjo", act, e_three))
    grad_rone = own_sum(product("bit,bpt->bip", s_one, h_mid))
    grad_lone = product("bjt,bot->bjo", x_home, e_one).reshape(home, ring_z.size, ring_x.size, rows, size)
    grad_lone = total(ring_z.scatter(ring_x.scatter([grad_lone], 2), 1))
    input_grad = (g_home.astype(F32) + product("bot,bjo->bjt", e_one, left_one)).astype(BF16)
    return mixed, input_grad, grad_lone, grad_rone, grad_ltwo, grad_rtwo


def per_device(inputs, cotangent, first_left, first_right, second_left, second_right):
    n_tensor = lax.axis_size("tensor")
    home, _, size = first_left.shape
    tokens = inputs.shape[1]
    share = math.gcd(n_tensor, max(1, tokens // LANES))
    cut = tokens // share
    plan = whole_tokens if share == n_tensor else split_blocks
    mixed, input_grad, *weight_grads = plan(
        inputs.reshape(home, size, tokens),
        cotangent.reshape(home, size, tokens),
        (first_left, first_right, second_left, second_right),
        share,
        cut,
    )
    return (mixed.reshape(inputs.shape), input_grad.reshape(inputs.shape), *weight_grads)


def solution(mesh):
    wide, factor = P("tensor", "dp"), P("tensor", "dp", None)
    return jax.shard_map(
        per_device,
        mesh=mesh,
        in_specs=(wide, wide, factor, factor, factor, factor),
        out_specs=(wide, wide, factor, factor, factor, factor),
        check_vma=False,
    )
```

```python
import functools
import itertools
import math

import jax
import jax.numpy as jnp
from jax import lax
from jax.experimental import pallas as pl
from jax.experimental.pallas import tpu as pltpu
from jax.sharding import PartitionSpec as P

BF16 = jnp.bfloat16
F32 = jnp.float32
LANES = 128
TILE = 16
VMEM_BYTES = 60 * 1024 * 1024
BYTES_PER_US = 1_200_000


def gelu_value(values):
    return jax.nn.gelu(values, approximate=True)


def gelu_back(values, upstream):
    return jax.vjp(gelu_value, values)[1](upstream)[0]


def gelu_both(v):
    root, cubic = 0.7978845608028654, 0.044715
    square = v * v
    t = jnp.tanh(root * (v + cubic * (v * square)))
    half = 0.5 * (1.0 + t)
    slope = half + (0.5 * v) * (1.0 - t * t) * (root + (3.0 * cubic * root) * square)
    return v * half, slope


def product(form, left, right):
    return jnp.einsum(form, left, right, preferred_element_type=F32)


def dot(left, right, left_dim, right_dim):
    return lax.dot_general(left, right, (((left_dim,), (right_dim,)), ((), ())), preferred_element_type=F32)


def dots(lefts, rights, left_dim, right_dim):
    if len(lefts) == 1:
        return [dot(lefts[0], rights[0], left_dim, right_dim)]
    zero = jnp.zeros_like(rights[0])
    upper = jnp.concatenate([rights[0], zero], axis=1)
    lower = jnp.concatenate([zero, rights[1]], axis=1)
    out = dot(jnp.concatenate(lefts, axis=left_dim), jnp.concatenate([upper, lower], axis=0), left_dim, right_dim)
    half = out.shape[1] // 2
    return [out[:, :half], out[:, half:]]


def dots_nn(lefts, rights):
    return dots(lefts, rights, 1, 0)


def dots_tn(lefts, rights):
    return dots(lefts, rights, 0, 0)


def dots_nt(lefts, rights):
    return dots(lefts, rights, 1, 1)


def dot_nn(left, right):
    return dot(left, right, 1, 0)


def dot_nt(left, right):
    return dot(left, right, 1, 1)


def call(body, out, grid, in_specs, out_specs, scratch, args, us, scalars=None):
    spec = pltpu.PrefetchScalarGridSpec(
        num_scalar_prefetch=0 if scalars is None else 1,
        grid=grid,
        in_specs=in_specs,
        out_specs=out_specs,
        scratch_shapes=scratch,
    )
    return pl.pallas_call(
        body,
        out_shape=out,
        grid_spec=spec,
        compiler_params=pltpu.CompilerParams(
            dimension_semantics=("arbitrary",) * len(grid), vmem_limit_bytes=VMEM_BYTES
        ),
        cost_estimate=pl.CostEstimate(flops=0, bytes_accessed=int(us * BYTES_PER_US), transcendentals=0),
    )(*(() if scalars is None else (scalars,)), *args)


def pairs(count, body, unroll=8):
    group = 2 if count % 2 == 0 else 1
    each(count // group, lambda n: body([n * group + i for i in range(group)]), unroll)


def turn(source, out_ref, at):
    n, size, _ = source.shape
    for i in range(0, size, TILE):
        out_ref[i : i + TILE, pl.ds(pl.multiple_of(at, TILE), n), :] = jnp.swapaxes(source[:, i : i + TILE, :], 0, 1)


def shape(dims, dtype=BF16):
    return jax.ShapeDtypeStruct(dims, dtype)


def each(count, body, unroll=16):
    def step(k, carry):
        body(k)
        return carry

    lax.fori_loop(0, count, step, 0, unroll=math.gcd(count, unroll))


def during(phase, steps):
    return lambda p, j: jnp.where(p == phase, j, jnp.where(p < phase, 0, steps - 1))


def stacked(ref, k):
    return jnp.concatenate([ref[c, k] for c in range(ref.shape[0])], axis=0)


class Ring:
    def __init__(self, axis, *digits, tied=True):
        self.axis, self.digits, self.last, self.tied = axis, digits, None, tied
        self.stride, self.size = digits[0]

    def here(self):
        return lax.rem(lax.axis_index(self.axis) // self.stride, self.size)

    def send(self, value, *steps):
        pairs = []
        for src in range(lax.axis_size(self.axis)):
            dst = src
            for (stride, size), step in zip(self.digits, steps):
                own = src // stride % size
                dst += ((own + step) % size - own) * stride
            pairs.append((src, dst))
        if self.tied and self.last is not None:
            value = after(value, self.last)
        self.last = lax.ppermute(value, self.axis, pairs)
        return self.last

    def sends(self, value):
        return [self.send(value, step) for step in range(1, self.size)]

    def gather(self, value):
        if self.size == 1:
            return value[None]
        here = self.here()
        out = jnp.zeros((self.size,) + value.shape, value.dtype)
        out = lax.dynamic_update_index_in_dim(out, value, here, 0)
        for step in range(1, self.size):
            got = self.send(value, step)
            out = lax.dynamic_update_index_in_dim(out, got, lax.rem(here - step + self.size, self.size), 0)
        return out

    def scatter(self, terms, dim, before=()):
        here = self.here()
        if self.size == 1:
            return [lax.index_in_dim(t, 0, dim, keepdims=False) for t in terms]
        out = [lax.dynamic_index_in_dim(t, here, dim, keepdims=False) for t in terms]
        for step in range(1, self.size):
            there = lax.rem(here + step, self.size)
            term = total([lax.dynamic_index_in_dim(t, there, dim, keepdims=False) for t in terms]).astype(BF16)
            out.append(self.send(after(term, *before), step))
        return out


def slot(place, values):
    values = lax.optimization_barrier(values)
    place.crossed = None
    for ring in [place.y, place.core] + place.dp + list(place.links.values()):
        ring.last = None
    return values


class Sum:
    def __init__(self, arrays, rings, tail):
        self.left = rings
        dims = [ring.size if isinstance(ring, Ring) else ring for ring in rings]
        self.arrays = [a.reshape(dims + list(tail)) for a in arrays]
        self.rings = [rings] * len(arrays)
        self.ready = []

    def cut(self, ring=None, index=None):
        out = []
        for array, rings in zip(self.arrays, self.rings):
            dim = 0
            for r in rings:
                if isinstance(r, Ring) and (r is ring or r not in self.left):
                    array = lax.dynamic_index_in_dim(array, index if r is ring else r.here(), dim, keepdims=False)
                else:
                    dim += 1
            out.append(array)
        return total(out)

    def parts(self, ring):
        return [self.cut(ring, lax.rem(ring.here() + step, ring.size)).astype(BF16) for step in range(1, ring.size)]

    def prepare(self, ring):
        self.ready = self.parts(ring) if ring in self.left else []

    def step(self, ring, *before):
        if ring not in self.left:
            return
        rest = [r for r in self.left if r is not ring]
        parts = self.ready or self.parts(ring)
        self.ready = []
        got = [ring.send(after(part, *before), step + 1) for step, part in enumerate(parts)]
        self.arrays, self.rings, self.left = self.arrays + got, self.rings + [rest] * len(got), rest

    def finish(self):
        for ring in [r for r in self.left[::-1] if isinstance(r, Ring)]:
            self.step(ring)
        return self.cut()


def finish_together(sums, rings, last, *before):
    for part in sums:
        for ring in rings:
            part.step(ring)
    sends = list(zip(*[part.parts(last) for part in sums]))
    got = [last.send(after(jnp.stack(send), *before), step + 1) for step, send in enumerate(sends)]
    for n, part in enumerate(sums):
        part.left = [r for r in part.left if r is not last]
        part.arrays, part.rings = part.arrays + [g[n] for g in got], part.rings + [part.left] * len(got)
    return [part.cut() for part in sums]


def total(terms):
    return functools.reduce(jnp.add, [t.astype(F32) for t in terms])


def after(value, *others):
    if not others:
        return value
    return lax.optimization_barrier((value,) + others)[0]


def turned_back(here, step, size):
    return lax.rem(here - step + size, size)


class Place:
    def __init__(self, share, n_dp):
        self.far, self.near = halves(share)
        self.y, self.core = Ring("tensor", (self.near, self.far)), Ring("tensor", (1, self.near), tied=False)
        self.dp, stride = [], 1
        while stride < n_dp:
            size = next(p for p in range(2, n_dp + 1) if n_dp // stride % p == 0)
            self.dp.append(Ring("dp", (stride, size)))
            stride *= size
        self.steps = [(y, c) for y in range(self.far) for c in range(self.near)]
        self.crossed = None
        self.links = {step: Ring("tensor", (self.near, self.far), (1, self.near)) for step in self.steps[1:]}
        self.rows = [ring.size for ring in self.dp]

    def position(self):
        return jnp.stack([ring.here() for ring in [self.y, self.core] + self.dp]).astype(jnp.int32)

    def onward(self, pos, n):
        y, c = self.steps[n]
        return lax.rem(pos[0] + y, self.far) * self.near + lax.rem(pos[1] + c, self.near)

    def source(self, pos, n):
        y, c = self.steps[n]
        return turned_back(pos[0], y, self.far) * self.near + turned_back(pos[1], c, self.near)

    def exchange(self, pieces, n):
        y, c = self.steps[n]
        piece = pieces[n]
        if y == 0:
            return self.core.send(piece, c)
        if self.crossed is not None:
            piece = after(piece, self.crossed)
        self.crossed = self.y.send(piece, y) if c == 0 else self.links[(y, c)].send(piece, y, c)
        return self.crossed


def piece_copies(pieces, whole, sems):
    flat_whole = [whole.at[c, d] for c in range(len(pieces)) for d in range(len(pieces[0]))]
    return [pltpu.make_async_copy(ref, dst, sems.at[n]) for n, (ref, dst) in enumerate(zip(flat(pieces), flat_whole))]


def block_reader(place, pos_ref, whole, group):
    lead = ()
    if group is not None:
        lead = (turned_back(pos_ref[0], group // place.near, place.far),)
    core = 0 if group is None else turned_back(pos_ref[1], lax.rem(group, place.near), place.near)
    places = []
    for d in range(math.prod(place.rows)):
        steps = [turned_back(pos_ref[2 + n], d // ring.stride % ring.size, ring.size) for n, ring in enumerate(place.dp)]
        places.append((core, *(steps or [0]), *lead))
    return lambda k: jnp.concatenate([whole[(*at, k)] for at in places], axis=0)


def whole_scratch(pieces):
    dims = (len(pieces), len(pieces[0])) + pieces[0][0].shape
    return [pltpu.VMEM(dims, BF16), pltpu.SemaphoreType.DMA((dims[0] * dims[1],))]


def share_copies(place, pos_ref, parts, whole, sems):
    return [pltpu.make_async_copy(ref, whole.at[place.source(pos_ref, n)], sems.at[n]) for n, ref in enumerate(parts)]


def run(copies):
    for copy in copies:
        copy.start()


def finish(copies):
    for copy in copies:
        copy.wait()


def anywhere(count):
    return [pl.BlockSpec(memory_space=pl.ANY)] * count


def flat(pieces):
    return tuple(p for row in pieces for p in row)


def unflat(place, refs):
    wide = len(refs) // place.near
    return [refs[c * wide : (c + 1) * wide] for c in range(place.near)]


def deal_kernel(pos_ref, g_ref, out_ref):
    for o in range(0, g_ref.shape[0], TILE):
        turn(g_ref.at[o : o + TILE], out_ref, o)


def deal(place, pos, g_home, cut, n):
    home, size, _ = g_home.shape
    return call(
        deal_kernel,
        shape((size, home, cut)),
        (1,),
        [pl.BlockSpec((home, size, cut), lambda i, pos: (0, 0, place.onward(pos, n)))],
        pl.BlockSpec((size, home, cut), lambda i, pos: (0, 0, 0)),
        [],
        (g_home,),
        us=3.5,
        scalars=pos,
    )


def first_kernel(place, pos_ref, x_ref, *refs):
    share = place.far * place.near
    pieces, out_refs = refs[: -share - 3], refs[-share - 3 : -3]
    stage, whole, sems = refs[-3:]
    home = x_ref.shape[0]
    cut = out_refs[0].shape[2]
    copies = piece_copies([pieces], whole, sems)
    block = block_reader(place, pos_ref, whole, None)

    @pl.when(pl.program_id(0) == 0)
    def _():
        run(copies)
        finish(copies)

    for n, out_ref in enumerate(out_refs):

        @pl.when(pl.program_id(0) == n)
        def _():
            lanes = pl.ds(pl.multiple_of(place.onward(pos_ref, n) * cut, cut), cut)

            for b in range(0, home, TILE):

                def store(ks):
                    out = dots_tn([block(b + k) for k in ks], [x_ref[b + k, :, lanes] for k in ks])
                    for k, y in zip(ks, out):
                        stage[b + k] = y.astype(BF16)

                pairs(TILE, store)
                turn(stage.at[b : b + TILE], out_ref, b)


def first_stage(place, pos, x_home, left_one, cut):
    home, size, tokens = x_home.shape
    share = tokens // cut
    return call(
        functools.partial(first_kernel, place),
        (shape((size, home, cut)),) * share,
        (share,),
        [pl.BlockSpec((home, size, tokens), lambda s, pos: (0, 0, 0))] + anywhere(len(left_one)),
        (pl.BlockSpec((size, home, cut), lambda s, pos: (0, 0, 0)),) * share,
        [pltpu.VMEM((home, size, cut), BF16)] + whole_scratch([left_one]),
        (x_home, *left_one),
        us=8,
        scalars=pos,
    )


def last_kernel(place, pos_ref, *refs):
    share = place.far * place.near
    e_refs, x_ref, g_ref = refs[:share], refs[share], refs[share + 1]
    pieces, (out_ref, grad_ref, turned, whole, sems) = refs[share + 2 : -5], refs[-5:]
    blocks, per, _ = e_refs[0].shape
    copies = piece_copies([pieces], whole, sems)
    block = block_reader(place, pos_ref, whole, None)
    first = pl.program_id(0) * per

    @pl.when(pl.program_id(0) == 0)
    def _():
        run(copies)

    for n in range(share):
        into = turned.at[place.source(pos_ref, n)]
        for o in range(0, blocks, TILE):
            turn(e_refs[n].at[o : o + TILE], into, o)

    @pl.when(pl.program_id(0) == 0)
    def _():
        finish(copies)

    def load(b):
        e_b = jnp.concatenate([turned[s, b] for s in range(share)], axis=1)
        out_ref[b] = (g_ref[b].astype(F32) + dot_nn(block(first + b), e_b)).astype(BF16)
        grad_ref[b] = dot_nt(x_ref[b], e_b).astype(BF16)

    each(per, load, 4)


def last_stage(place, pos, e_got, x_home, g_home, left_one):
    share = len(e_got)
    blocks, home, cut = e_got[0].shape
    _, size, tokens = x_home.shape
    per = math.gcd(home, 16)
    wide = pl.BlockSpec((per, size, tokens), lambda h, pos: (h, 0, 0))
    factor = pl.BlockSpec((per, size, size), lambda h, pos: (h, 0, 0))
    return call(
        functools.partial(last_kernel, place),
        (shape(g_home.shape), shape((home, size, size))),
        (home // per,),
        [pl.BlockSpec((blocks, per, cut), lambda h, pos: (0, h, 0))] * share + [wide, wide] + anywhere(len(left_one)),
        (wide, factor),
        [pltpu.VMEM((share, per, blocks, cut), BF16)] + whole_scratch([left_one]),
        (*e_got, x_home, g_home, *left_one),
        us=10,
        scalars=pos,
    )


def mixed_kernel(place, pos_ref, *refs):
    *s_refs, x_ref, out_ref = refs
    cut = s_refs[0].shape[2]
    for n, s_ref in enumerate(s_refs):
        lanes = pl.ds(pl.multiple_of(place.source(pos_ref, n) * cut, cut), cut)
        out_ref[:, :, lanes] = (x_ref[:, :, lanes].astype(F32) + s_ref[...].astype(F32)).astype(BF16)


def add_home(place, pos, s_got, x_home):
    home, blocks, cut = s_got[0].shape
    per = math.gcd(home, 8)
    wide = pl.BlockSpec((per,) + x_home.shape[1:], lambda h, pos: (h, 0, 0))
    return call(
        functools.partial(mixed_kernel, place),
        shape(x_home.shape),
        (home // per,),
        [pl.BlockSpec((per, blocks, cut), lambda h, pos: (h, 0, 0))] * len(s_got) + [wide],
        wide,
        [],
        (*s_got, x_home),
        us=6,
        scalars=pos,
    )


def back_two_kernel(place, pos_ref, *refs):
    share = place.far * place.near
    g_parts, factor = refs[:share], unflat(place, refs[share:-7])
    out_ref, turned, stage, g_all, g_sems, w_all, w_sems = refs[-7:]
    per = out_ref.shape[0]
    phase, j = pl.program_id(0), pl.program_id(1)

    @pl.when((phase == 0) & (j == 0))
    def _():
        copies = share_copies(place, pos_ref, g_parts, g_all, g_sems) + piece_copies(factor, w_all, w_sems)
        run(copies)
        finish(copies)

    @pl.when(phase == 0)
    def _():
        block = block_reader(place, pos_ref, w_all, j)

        def body(ks):
            out = dots_nn([block(k) for k in ks], [stacked(g_all, j * per + k) for k in ks])
            for k, y in zip(ks, out):
                stage[k] = y.astype(BF16)

        staged(per, body, stage, turned, j)

    @pl.when(phase == 1)
    def _():
        def body(k):
            out_ref[k] = turned[j * per + k]

        each(per, body)


def staged(per, body, stage, turned, j):
    for k in range(0, per, TILE):
        pairs(TILE, lambda ks: body([k + i for i in ks]))
        turn(stage.at[k : k + TILE], turned, j * per + k)


def middle_sizes(place, parts):
    blocks, home, cut = parts[0].shape
    return blocks, home, cut, len(parts)


def back_two(place, pos, g_mid, right_two):
    blocks, home, cut, share = middle_sizes(place, g_mid)
    at = during(1, share)
    return call(
        functools.partial(back_two_kernel, place),
        shape((blocks, blocks, cut)),
        (2, share),
        anywhere(share + len(flat(right_two))),
        pl.BlockSpec((home, blocks, cut), lambda p, j, pos: (at(p, j), 0, 0)),
        [
            pltpu.VMEM((blocks, blocks, cut), BF16),
            pltpu.VMEM((home, blocks, cut), BF16),
            pltpu.VMEM((share, blocks, home, cut), BF16),
            pltpu.SemaphoreType.DMA((share,)),
        ]
        + whole_scratch(right_two),
        (*g_mid, *flat(right_two)),
        us=10,
        scalars=pos,
    )


def either(place, pos_ref, j, keep_ref, send_ref, body):
    mine = lax.rem(j, place.near) == pos_ref[1]

    @pl.when(mine)
    def _():
        body(keep_ref)

    @pl.when(jnp.logical_not(mine))
    def _():
        body(send_ref)


def middle_kernel(place, pos_ref, *refs):
    share = place.far * place.near
    wide = (len(refs) - (2 * share + 15)) // 2
    s_parts, rest = refs[:share], refs[share:]
    one, two, rest = unflat(place, rest[:wide]), unflat(place, rest[wide : 2 * wide]), rest[2 * wide :]
    e_ref, act_ref, keep_two, send_two, keep_one, send_one, *rest = rest
    out_refs, rest = rest[:share], rest[share:]
    turned, hidden, e_one, s_all, s_sems, one_all, one_sems, two_all, two_sems = rest
    per, home = act_ref.shape[0], s_all.shape[2]
    phase, j = pl.program_id(0), pl.program_id(1)

    def second():
        return piece_copies(two, two_all, two_sems)

    @pl.when((phase == 0) & (j == 0))
    def _():
        copies = share_copies(place, pos_ref, s_parts, s_all, s_sems) + piece_copies(one, one_all, one_sems)
        run(copies)
        run(second())
        finish(copies)

    @pl.when(phase == 0)
    def _():
        block = block_reader(place, pos_ref, one_all, j)

        def body(ks):
            out = dots_tn([block(k) for k in ks], [stacked(s_all, j * per + k) for k in ks])
            for k, y in zip(ks, out):
                e_one[k] = y.astype(BF16)

        staged(per, body, e_one, turned, j)

    @pl.when((phase == 1) & (j == 0))
    def _():
        finish(second())

    @pl.when(phase == 1)
    def _():
        block = block_reader(place, pos_ref, two_all, j)

        def with_out(grad_ref):
            def body(ks):
                acts, slopes, es = [], [], [e_ref[k] for k in ks]
                for k in ks:
                    value, slope = gelu_both(turned[j * per + k].astype(F32))
                    acts.append(value.astype(BF16))
                    slopes.append(slope)
                    act_ref[k] = acts[-1]
                for k, slope, y in zip(ks, slopes, dots_nn([block(k) for k in ks], es)):
                    e_one[k] = (slope * y).astype(BF16)
                for k, y in zip(ks, dots_nt(acts, es)):
                    grad_ref[0, k] = y.astype(BF16)

            staged(per, body, e_one, hidden, j)

        either(place, pos_ref, j, keep_two, send_two, with_out)

    @pl.when(phase == 2)
    def _():
        block = block_reader(place, pos_ref, one_all, j)

        def with_out(grad_ref):
            def body(ks):
                hs = [hidden[j * per + k] for k in ks]
                for k, y in zip(ks, dots_nn([block(k) for k in ks], hs)):
                    e_one[k] = y.astype(BF16)
                for k, y in zip(ks, dots_nt([stacked(s_all, j * per + k) for k in ks], hs)):
                    grad_ref[0, k] = y.astype(BF16)

            pairs(per, body)

        either(place, pos_ref, j, keep_one, send_one, with_out)
        for n in range(share):
            at = pl.ds(pl.multiple_of(place.onward(pos_ref, n) * home, home), home)
            out_refs[n][...] = e_one[:, at, :]


def grad_specs(place, phase, home, size, share):
    at = during(phase, share)
    dims = shape((place.far, home, size, size))
    spec = pl.BlockSpec((1, home, size, size), lambda p, j, pos: (at(p, j) // place.near, 0, 0, 0))
    return [dims] * 2, [spec] * 2


def middle(place, pos, s_mid, e_mid, right_one, left_two):
    blocks, home, cut, share = middle_sizes(place, s_mid)
    at = [during(phase, share) for phase in range(3)]
    block = pl.BlockSpec((home, blocks, cut), lambda p, j, pos: (at[1](p, j), 0, 0))
    two, two_specs = grad_specs(place, 1, home, blocks, share)
    one, one_specs = grad_specs(place, 2, home, blocks, share)
    piece = pl.BlockSpec((home, home, cut), lambda p, j, pos: (at[2](p, j), 0, 0))
    out = call(
        functools.partial(middle_kernel, place),
        (shape((blocks, blocks, cut)), *two, *one) + (shape((blocks, home, cut)),) * share,
        (3, share),
        anywhere(share + 2 * len(flat(right_one))) + [block],
        (block, *two_specs, *one_specs) + (piece,) * share,
        [pltpu.VMEM((blocks, blocks, cut), BF16)] * 2
        + [
            pltpu.VMEM((home, blocks, cut), BF16),
            pltpu.VMEM((share, blocks, home, cut), BF16),
            pltpu.SemaphoreType.DMA((share,)),
        ]
        + whole_scratch(right_one)
        + whole_scratch(left_two),
        (*s_mid, *flat(right_one), *flat(left_two), e_mid),
        us=26,
        scalars=pos,
    )
    return out[0], out[1:3], out[3:5], list(out[5:])


def forward_two_kernel(place, pos_ref, *refs):
    share = place.far * place.near
    wide = (len(refs) - (2 * share + 12)) // 2
    g_parts, rest = refs[:share], refs[share:]
    left, right, rest = unflat(place, rest[:wide]), unflat(place, rest[wide : 2 * wide]), rest[2 * wide :]
    act_ref, keep_ref, send_ref, *rest = rest
    out_refs, rest = rest[:share], rest[share:]
    turned, fourth, stage, g_all, g_sems, left_all, left_sems, right_all, right_sems = rest
    per = act_ref.shape[0]
    phase, j = pl.program_id(0), pl.program_id(1)

    def second():
        return piece_copies(right, right_all, right_sems) + share_copies(place, pos_ref, g_parts, g_all, g_sems)

    @pl.when((phase == 0) & (j == 0))
    def _():
        copies = piece_copies(left, left_all, left_sems)
        run(copies)
        run(second())
        finish(copies)

    @pl.when(phase == 0)
    def _():
        block = block_reader(place, pos_ref, left_all, j)

        def body(ks):
            for k, y in zip(ks, dots_tn([block(k) for k in ks], [act_ref[k] for k in ks])):
                stage[k] = y.astype(BF16)

        staged(per, body, stage, turned, j)

    @pl.when((phase == 1) & (j == 0))
    def _():
        finish(second())

    @pl.when(phase == 1)
    def _():
        block = block_reader(place, pos_ref, right_all, j)

        def with_out(grad_ref):
            def body(ks):
                thirds = [turned[j * per + k] for k in ks]
                for k, y in zip(ks, dots_tn([block(k) for k in ks], thirds)):
                    stage[k] = y.astype(BF16)
                for k, y in zip(ks, dots_nt(thirds, [stacked(g_all, j * per + k) for k in ks])):
                    grad_ref[0, k] = y.astype(BF16)

            staged(per, body, stage, fourth, j)

        either(place, pos_ref, j, keep_ref, send_ref, with_out)

    for n in range(share):

        @pl.when((phase == 2) & (j == n))
        def _():
            base = place.onward(pos_ref, n) * per

            def body(k):
                out_refs[n][k] = fourth[base + k]

            each(per, body)


def forward_two(place, pos, act, g_mid, left_two, right_two):
    blocks, home, cut, share = middle_sizes(place, g_mid)
    at = during(0, share)
    grad, grad_spec = grad_specs(place, 1, home, blocks, share)
    out = call(
        functools.partial(forward_two_kernel, place),
        (*grad,) + (shape((home, blocks, cut)),) * share,
        (3, share),
        anywhere(share + 2 * len(flat(left_two))) + [pl.BlockSpec((home, blocks, cut), lambda p, j, pos: (at(p, j), 0, 0))],
        (*grad_spec,) + (pl.BlockSpec((home, blocks, cut), lambda p, j, pos: (0, 0, 0)),) * share,
        [pltpu.VMEM((blocks, blocks, cut), BF16)] * 2
        + [
            pltpu.VMEM((home, blocks, cut), BF16),
            pltpu.VMEM((share, blocks, home, cut), BF16),
            pltpu.SemaphoreType.DMA((share,)),
        ]
        + whole_scratch(left_two)
        + whole_scratch(right_two),
        (*g_mid, *flat(left_two), *flat(right_two), act),
        us=20,
        scalars=pos,
    )
    return out[:2], list(out[2:])


def halves(size):
    low = 2 if size % 2 == 0 else 1
    return size // low, low


def cross(pieces):
    return lax.all_to_all(pieces, "tensor", split_axis=0, concat_axis=0, tiled=True)


def whole_tokens(x_home, g_home, factors, share, cut):
    home, size, tokens = x_home.shape
    first_left = factors[0]
    rows = first_left.shape[1]
    place = Place(share, lax.axis_size("dp"))
    pos = place.position()

    def gather(start, n):
        if n >= len(place.dp):
            return start
        got = [start] + place.dp[n].sends(start)
        return got if n == 0 else jnp.stack(got)

    def gather_far(start):
        for n in reversed(range(2, len(place.dp))):
            start = gather(start, n)
        return start

    def last_dp(start):
        return gather(start, 0) if place.dp else [start]

    def cores(piece):
        return [piece] + place.core.sends(piece)

    def by_core(own):
        return [[p[c] for p in own] for c in range(place.near)]

    def cross(pieces, n):
        return place.exchange(pieces, n) if n < share else None

    def from_y(start):
        return jnp.stack([start] + place.y.sends(start))

    n_one, n_two, n_three = (place.steps.index(step) if step in place.steps else share for step in [(0, 1), (1, 0), (1, 1)])
    one = gather_far(first_left)
    rest = from_y(jnp.stack([factors[3], factors[1], factors[2]]))
    g = {n: deal(place, pos, g_home, cut, n) for n in reversed(range(share))}
    got_three = cross(g, n_three)
    w_two = gather_far(after(rest[:, 0], g[share - 1]))
    one = last_dp(gather(one, 1))
    w_one = gather_far(rest[:, 1])
    w_two = gather(w_two, 1)
    got_three, one, w_two, w_one, rest, g = slot(place, (got_three, one, w_two, w_one, rest, g))

    got_two = cross(g, n_two)
    right_two = last_dp(w_two)
    w_one = gather(w_one, 1)
    w_left = gather_far(rest[:, 2])
    s = first_stage(place, pos, x_home, one, cut)
    got_two, right_two, w_one, w_left, one, s, pos = slot(place, (got_two, right_two, w_one, w_left, one, list(s), pos))

    s_three = cross(s, n_three)
    right_one = last_dp(w_one)
    w_left = gather(w_left, 1)
    right_two = by_core([cores(p) for p in right_two])
    s_one = cross(s, n_one)
    got_one = cross(g, n_one)
    s_three, s_one, right_one, w_left, right_two, g, got_one = slot(
        place, (s_three, s_one, right_one, w_left, right_two, g, got_one)
    )
    g_mid = [g[0], got_one, got_two, got_three][:share]

    s_two = cross(s, n_two)
    left_two = last_dp(w_left)
    left_core = cores(left_two[0])
    right_one = by_core([cores(p) for p in right_one])
    e_mid = back_two(place, pos, g_mid, right_two)
    s_two, left_two, left_core, right_one, e_mid = slot(place, (s_two, left_two, left_core, right_one, e_mid))
    s_mid = [s[0], s_one, s_two, s_three][:share]
    left_two = by_core([left_core] + [cores(p) for p in left_two[1:]])

    act, grad_two, grad_one, e = middle(place, pos, s_mid, e_mid, right_one, left_two)

    def start_sum(keep, send):
        arrays = [keep, place.core.send(send, 1)] if place.near > 1 else [keep]
        return Sum(arrays, [place.y, home] + place.dp[::-1], (rows, size))

    def hold(parts, arrays):
        for part, kept in zip(parts, arrays):
            part.arrays, part.ready = kept

    def arrays_of(*parts):
        return [(part.arrays, part.ready) for part in parts]

    x_step, near_step, far_step = (place.dp + [None] * 3)[:3]

    e_three = cross(e, n_three)
    two, one_part = start_sum(*grad_two), start_sum(*grad_one)
    grad_three, s = forward_two(place, pos, act, g_mid, left_two, right_two)
    two.prepare(x_step)
    one_part.prepare(near_step)
    e_three, kept, grad_three, s, e = slot(place, (e_three, arrays_of(two, one_part), grad_three, s, e))
    hold([two, one_part], kept)

    e_two = cross(e, n_two)
    two.step(x_step)
    one_part.step(near_step)
    three = start_sum(*grad_three)
    e_one = cross(e, n_one)
    three.prepare(x_step)
    e_two, e_one, kept, s = slot(place, (e_two, e_one, arrays_of(two, one_part, three), s))
    hold([two, one_part, three], kept)
    e_got = [e[0], e_one, e_two, e_three][:share]

    s_three = cross(s, n_three)
    three.step(x_step)
    one_part.step(far_step)
    two.step(near_step)
    input_grad, lone = last_stage(place, pos, e_got, x_home, g_home, one)
    lone = Sum([lone], [home] + place.dp[::-1], (rows, size))
    lone.prepare(x_step)
    s_three, kept, input_grad, s = slot(place, (s_three, arrays_of(two, one_part, three, lone), input_grad, s))
    hold([two, one_part, three, lone], kept)

    s_two = cross(s, n_two)
    lone.step(x_step)
    two.step(far_step)
    three.step(near_step)
    one_part.step(x_step)
    lone.step(near_step)
    three.step(far_step, lone.arrays[-1], *([s_two] if n_two < share else []))
    s_one = cross(s, n_one)
    s_got = [s[0], s_one, s_two, s_three][:share]
    mixed = add_home(place, pos, s_got, x_home)
    grad_ltwo, grad_rone, grad_rtwo = finish_together([two, one_part, three], place.dp, place.y, mixed)
    grad_lone = lone.finish()
    return mixed, input_grad, grad_lone, grad_rone, grad_ltwo, grad_rtwo


def split_blocks(x_home, g_home, factors, share, cut):
    home, size, tokens = x_home.shape
    far, near = halves(share)
    outer, inner = halves(lax.axis_size("dp"))
    ring_y, ring_core = Ring("tensor", (near, far)), Ring("tensor", (1, near))
    ring_z, ring_x = Ring("dp", (inner, outer)), Ring("dp", (1, inner))
    rows = factors[0].shape[1]
    n_tensor = lax.axis_size("tensor")
    groups = n_tensor // share
    held = home * share
    same_tokens = [[group * share + part for group in range(groups)] for part in range(share)]

    def go(values):
        pieces = values.reshape(home, groups, held, share, cut).transpose(1, 3, 2, 0, 4)
        got = cross(pieces.reshape(n_tensor, held, home, cut))
        return got.transpose(1, 0, 2, 3).reshape(held, size, cut)

    def back(values):
        pieces = values.reshape(held, n_tensor, home, cut).transpose(1, 0, 2, 3)
        got = cross(pieces).reshape(groups, share, held, home, cut)
        return got.transpose(3, 0, 2, 1, 4).reshape(home, size, tokens)

    def turn(values):
        moved = lax.all_to_all(
            values.reshape(held, groups, held, cut), "tensor", split_axis=1, concat_axis=0, tiled=True, axis_index_groups=same_tokens
        )
        return jnp.swapaxes(moved.reshape(size, held, cut), 0, 1)

    def whole(factor):
        one = ring_z.gather(ring_y.gather(factor))
        all_rows = ring_core.gather(ring_x.gather(one))
        return all_rows.transpose(3, 0, 4, 2, 1, 5, 6).reshape(held, size, size)

    def own_sum(partial):
        split = partial.reshape(ring_y.size, ring_core.size, home, ring_z.size, ring_x.size, rows, size)
        terms = ring_core.scatter([split], 1)
        return total(ring_y.scatter(ring_z.scatter(ring_x.scatter(terms, 3), 2), 0))

    first_left, first_right, second_left, second_right = factors
    g_mid = go(g_home)
    left_one = ring_x.gather(ring_z.gather(first_left)).transpose(2, 1, 0, 3, 4).reshape(home, size, size)
    right_one, left_two, right_two = whole(first_right), whole(second_left), whole(second_right)

    s_one = go(product("bjt,bjo->bot", x_home, left_one).astype(BF16))
    s_two = turn(product("bit,bip->bpt", s_one, right_one).astype(BF16))
    act = gelu_value(s_two.astype(F32)).astype(BF16)
    e_three = turn(product("bot,bio->bit", g_mid, right_two).astype(BF16))
    h_mid = turn(gelu_back(s_two.astype(F32), product("bot,bjo->bjt", e_three, left_two)).astype(BF16))
    e_one = back(product("bpt,bip->bit", h_mid, right_one).astype(BF16))
    s_three = turn(product("bjt,bjo->bot", act, left_two).astype(BF16))
    s_four = back(product("bit,bio->bot", s_three, right_two).astype(BF16))
    mixed = (x_home.astype(F32) + s_four.astype(F32)).astype(BF16)

    grad_rtwo = own_sum(product("bit,bot->bio", s_three, g_mid))
    grad_ltwo = own_sum(product("bjt,bot->bjo", act, e_three))
    grad_rone = own_sum(product("bit,bpt->bip", s_one, h_mid))
    grad_lone = product("bjt,bot->bjo", x_home, e_one).reshape(home, ring_z.size, ring_x.size, rows, size)
    grad_lone = total(ring_z.scatter(ring_x.scatter([grad_lone], 2), 1))
    input_grad = (g_home.astype(F32) + product("bot,bjo->bjt", e_one, left_one)).astype(BF16)
    return mixed, input_grad, grad_lone, grad_rone, grad_ltwo, grad_rtwo


def per_device(inputs, cotangent, first_left, first_right, second_left, second_right):
    n_tensor = lax.axis_size("tensor")
    home, _, size = first_left.shape
    tokens = inputs.shape[1]
    share = math.gcd(n_tensor, max(1, tokens // LANES))
    cut = tokens // share
    plan = whole_tokens if share == n_tensor else split_blocks
    mixed, input_grad, *weight_grads = plan(
        inputs.reshape(home, size, tokens),
        cotangent.reshape(home, size, tokens),
        (first_left, first_right, second_left, second_right),
        share,
        cut,
    )
    return (mixed.reshape(inputs.shape), input_grad.reshape(inputs.shape), *weight_grads)


def solution(mesh):
    wide, factor = P("tensor", "dp"), P("tensor", "dp", None)
    return jax.shard_map(
        per_device,
        mesh=mesh,
        in_specs=(wide, wide, factor, factor, factor, factor),
        out_specs=(wide, wide, factor, factor, factor, factor),
        check_vma=False,
    )
```

```python
import functools
import itertools
import math

import jax
import jax.numpy as jnp
from jax import lax
from jax.experimental import pallas as pl
from jax.experimental.pallas import tpu as pltpu
from jax.sharding import PartitionSpec as P

BF16 = jnp.bfloat16
F32 = jnp.float32
LANES = 128
TILE = 16
VMEM_BYTES = 60 * 1024 * 1024
BYTES_PER_US = 1_200_000


def gelu_value(values):
    return jax.nn.gelu(values, approximate=True)


def gelu_back(values, upstream):
    return jax.vjp(gelu_value, values)[1](upstream)[0]


def gelu_both(v):
    root, cubic = 0.7978845608028654, 0.044715
    square = v * v
    t = jnp.tanh(root * (v + cubic * (v * square)))
    half = 0.5 * (1.0 + t)
    slope = half + (0.5 * v) * (1.0 - t * t) * (root + (3.0 * cubic * root) * square)
    return v * half, slope


def product(form, left, right):
    return jnp.einsum(form, left, right, preferred_element_type=F32)


def dot(left, right, left_dim, right_dim):
    return lax.dot_general(left, right, (((left_dim,), (right_dim,)), ((), ())), preferred_element_type=F32)


def dots(lefts, rights, left_dim, right_dim):
    if len(lefts) == 1:
        return [dot(lefts[0], rights[0], left_dim, right_dim)]
    zero = jnp.zeros_like(rights[0])
    upper = jnp.concatenate([rights[0], zero], axis=1)
    lower = jnp.concatenate([zero, rights[1]], axis=1)
    out = dot(jnp.concatenate(lefts, axis=left_dim), jnp.concatenate([upper, lower], axis=0), left_dim, right_dim)
    half = out.shape[1] // 2
    return [out[:, :half], out[:, half:]]


def dots_nn(lefts, rights):
    return dots(lefts, rights, 1, 0)


def dots_tn(lefts, rights):
    return dots(lefts, rights, 0, 0)


def dots_nt(lefts, rights):
    return dots(lefts, rights, 1, 1)


def dot_nn(left, right):
    return dot(left, right, 1, 0)


def dot_nt(left, right):
    return dot(left, right, 1, 1)


def call(body, out, grid, in_specs, out_specs, scratch, args, us, scalars=None):
    spec = pltpu.PrefetchScalarGridSpec(
        num_scalar_prefetch=0 if scalars is None else 1,
        grid=grid,
        in_specs=in_specs,
        out_specs=out_specs,
        scratch_shapes=scratch,
    )
    return pl.pallas_call(
        body,
        out_shape=out,
        grid_spec=spec,
        compiler_params=pltpu.CompilerParams(
            dimension_semantics=("arbitrary",) * len(grid), vmem_limit_bytes=VMEM_BYTES
        ),
        cost_estimate=pl.CostEstimate(flops=0, bytes_accessed=int(us * BYTES_PER_US), transcendentals=0),
    )(*(() if scalars is None else (scalars,)), *args)


def pairs(count, body, unroll=8):
    group = 2 if count % 2 == 0 else 1
    each(count // group, lambda n: body([n * group + i for i in range(group)]), unroll)


def turn(source, out_ref, at):
    n, size, _ = source.shape
    for i in range(0, size, TILE):
        out_ref[i : i + TILE, pl.ds(pl.multiple_of(at, TILE), n), :] = jnp.swapaxes(source[:, i : i + TILE, :], 0, 1)


def shape(dims, dtype=BF16):
    return jax.ShapeDtypeStruct(dims, dtype)


def each(count, body, unroll=16):
    def step(k, carry):
        body(k)
        return carry

    lax.fori_loop(0, count, step, 0, unroll=math.gcd(count, unroll))


def during(phase, steps):
    return lambda p, j: jnp.where(p == phase, j, jnp.where(p < phase, 0, steps - 1))


def stacked(ref, k):
    return jnp.concatenate([ref[c, k] for c in range(ref.shape[0])], axis=0)


class Ring:
    def __init__(self, axis, *digits, tied=True):
        self.axis, self.digits, self.last, self.tied = axis, digits, None, tied
        self.stride, self.size = digits[0]

    def here(self):
        return lax.rem(lax.axis_index(self.axis) // self.stride, self.size)

    def send(self, value, *steps):
        pairs = []
        for src in range(lax.axis_size(self.axis)):
            dst = src
            for (stride, size), step in zip(self.digits, steps):
                own = src // stride % size
                dst += ((own + step) % size - own) * stride
            pairs.append((src, dst))
        if self.tied and self.last is not None:
            value = after(value, self.last)
        self.last = lax.ppermute(value, self.axis, pairs)
        return self.last

    def sends(self, value):
        return [self.send(value, step) for step in range(1, self.size)]

    def gather(self, value):
        if self.size == 1:
            return value[None]
        here = self.here()
        out = jnp.zeros((self.size,) + value.shape, value.dtype)
        out = lax.dynamic_update_index_in_dim(out, value, here, 0)
        for step in range(1, self.size):
            got = self.send(value, step)
            out = lax.dynamic_update_index_in_dim(out, got, lax.rem(here - step + self.size, self.size), 0)
        return out

    def scatter(self, terms, dim, before=()):
        here = self.here()
        if self.size == 1:
            return [lax.index_in_dim(t, 0, dim, keepdims=False) for t in terms]
        out = [lax.dynamic_index_in_dim(t, here, dim, keepdims=False) for t in terms]
        for step in range(1, self.size):
            there = lax.rem(here + step, self.size)
            term = total([lax.dynamic_index_in_dim(t, there, dim, keepdims=False) for t in terms]).astype(BF16)
            out.append(self.send(after(term, *before), step))
        return out


def slot(place, values):
    values = lax.optimization_barrier(values)
    place.crossed = None
    for ring in [place.y, place.core] + place.dp + list(place.links.values()):
        ring.last = None
    return values


class Sum:
    def __init__(self, arrays, rings, tail):
        self.left = rings
        dims = [ring.size if isinstance(ring, Ring) else ring for ring in rings]
        self.arrays = [a.reshape(dims + list(tail)) for a in arrays]
        self.rings = [rings] * len(arrays)
        self.ready = []

    def cut(self, ring=None, index=None):
        out = []
        for array, rings in zip(self.arrays, self.rings):
            dim = 0
            for r in rings:
                if isinstance(r, Ring) and (r is ring or r not in self.left):
                    array = lax.dynamic_index_in_dim(array, index if r is ring else r.here(), dim, keepdims=False)
                else:
                    dim += 1
            out.append(array)
        return total(out)

    def parts(self, ring):
        return [self.cut(ring, lax.rem(ring.here() + step, ring.size)).astype(BF16) for step in range(1, ring.size)]

    def prepare(self, ring):
        self.ready = self.parts(ring) if ring in self.left else []

    def step(self, ring, *before):
        if ring not in self.left:
            return
        rest = [r for r in self.left if r is not ring]
        parts = self.ready or self.parts(ring)
        self.ready = []
        got = [ring.send(after(part, *before), step + 1) for step, part in enumerate(parts)]
        self.arrays, self.rings, self.left = self.arrays + got, self.rings + [rest] * len(got), rest

    def finish(self):
        for ring in [r for r in self.left[::-1] if isinstance(r, Ring)]:
            count = len(self.arrays)
            self.step(ring)
        if not any(isinstance(r, Ring) for r in self.rings[0]):
            return self.cut()
        got, self.arrays = self.arrays[count:], self.arrays[:count]
        own, got = lax.optimization_barrier((self.cut(), got))
        return total([own] + got)


def finish_together(sums, rings, last, *before):
    for part in sums:
        for ring in rings:
            part.step(ring)
    sends = list(zip(*[part.parts(last) for part in sums]))
    got = [last.send(after(jnp.stack(send), *before), step + 1) for step, send in enumerate(sends)]
    for part in sums:
        part.left = [r for r in part.left if r is not last]
    own, got = lax.optimization_barrier(([part.cut() for part in sums], got))
    return [total([mine] + [g[n] for g in got]) for n, mine in enumerate(own)]


def total(terms):
    return functools.reduce(jnp.add, [t.astype(F32) for t in terms])


def after(value, *others):
    if not others:
        return value
    return lax.optimization_barrier((value,) + others)[0]


def turned_back(here, step, size):
    return lax.rem(here - step + size, size)


class Place:
    def __init__(self, share, n_dp):
        self.far, self.near = halves(share)
        self.y, self.core = Ring("tensor", (self.near, self.far)), Ring("tensor", (1, self.near), tied=False)
        self.dp, stride = [], 1
        while stride < n_dp:
            size = next(p for p in range(2, n_dp + 1) if n_dp // stride % p == 0)
            self.dp.append(Ring("dp", (stride, size)))
            stride *= size
        self.steps = [(y, c) for y in range(self.far) for c in range(self.near)]
        self.crossed = None
        self.links = {step: Ring("tensor", (self.near, self.far), (1, self.near)) for step in self.steps[1:]}
        self.rows = [ring.size for ring in self.dp]

    def position(self):
        return jnp.stack([ring.here() for ring in [self.y, self.core] + self.dp]).astype(jnp.int32)

    def onward(self, pos, n):
        y, c = self.steps[n]
        return lax.rem(pos[0] + y, self.far) * self.near + lax.rem(pos[1] + c, self.near)

    def source(self, pos, n):
        y, c = self.steps[n]
        return turned_back(pos[0], y, self.far) * self.near + turned_back(pos[1], c, self.near)

    def exchange(self, pieces, n):
        y, c = self.steps[n]
        piece = pieces[n]
        if y == 0:
            return self.core.send(piece, c)
        if self.crossed is not None:
            piece = after(piece, self.crossed)
        self.crossed = self.y.send(piece, y) if c == 0 else self.links[(y, c)].send(piece, y, c)
        return self.crossed


def piece_copies(pieces, whole, sems):
    flat_whole = [whole.at[c, d] for c in range(len(pieces)) for d in range(len(pieces[0]))]
    return [pltpu.make_async_copy(ref, dst, sems.at[n]) for n, (ref, dst) in enumerate(zip(flat(pieces), flat_whole))]


def block_reader(place, pos_ref, whole, group):
    lead = ()
    if group is not None:
        lead = (turned_back(pos_ref[0], group // place.near, place.far),)
    core = 0 if group is None else turned_back(pos_ref[1], lax.rem(group, place.near), place.near)
    places = []
    for d in range(math.prod(place.rows)):
        steps = [turned_back(pos_ref[2 + n], d // ring.stride % ring.size, ring.size) for n, ring in enumerate(place.dp)]
        places.append((core, *(steps or [0]), *lead))
    return lambda k: jnp.concatenate([whole[(*at, k)] for at in places], axis=0)


def whole_scratch(pieces):
    dims = (len(pieces), len(pieces[0])) + pieces[0][0].shape
    return [pltpu.VMEM(dims, BF16), pltpu.SemaphoreType.DMA((dims[0] * dims[1],))]


def share_copies(place, pos_ref, parts, whole, sems):
    return [pltpu.make_async_copy(ref, whole.at[place.source(pos_ref, n)], sems.at[n]) for n, ref in enumerate(parts)]


def run(copies):
    for copy in copies:
        copy.start()


def finish(copies):
    for copy in copies:
        copy.wait()


def anywhere(count):
    return [pl.BlockSpec(memory_space=pl.ANY)] * count


def flat(pieces):
    return tuple(p for row in pieces for p in row)


def unflat(place, refs):
    wide = len(refs) // place.near
    return [refs[c * wide : (c + 1) * wide] for c in range(place.near)]


def deal_kernel(pos_ref, g_ref, out_ref):
    for o in range(0, g_ref.shape[0], TILE):
        turn(g_ref.at[o : o + TILE], out_ref, o)


def deal(place, pos, g_home, cut, n):
    home, size, _ = g_home.shape
    return call(
        deal_kernel,
        shape((size, home, cut)),
        (1,),
        [pl.BlockSpec((home, size, cut), lambda i, pos: (0, 0, place.onward(pos, n)))],
        pl.BlockSpec((size, home, cut), lambda i, pos: (0, 0, 0)),
        [],
        (g_home,),
        us=3.5,
        scalars=pos,
    )


def first_kernel(place, pos_ref, x_ref, *refs):
    share = place.far * place.near
    pieces, out_refs = refs[: -share - 3], refs[-share - 3 : -3]
    stage, whole, sems = refs[-3:]
    home = x_ref.shape[0]
    cut = out_refs[0].shape[2]
    copies = piece_copies([pieces], whole, sems)
    block = block_reader(place, pos_ref, whole, None)

    @pl.when(pl.program_id(0) == 0)
    def _():
        run(copies)
        finish(copies)

    for n, out_ref in enumerate(out_refs):

        @pl.when(pl.program_id(0) == n)
        def _():
            lanes = pl.ds(pl.multiple_of(place.onward(pos_ref, n) * cut, cut), cut)

            for b in range(0, home, TILE):

                def store(ks):
                    out = dots_tn([block(b + k) for k in ks], [x_ref[b + k, :, lanes] for k in ks])
                    for k, y in zip(ks, out):
                        stage[b + k] = y.astype(BF16)

                pairs(TILE, store)
                turn(stage.at[b : b + TILE], out_ref, b)


def first_stage(place, pos, x_home, left_one, cut):
    home, size, tokens = x_home.shape
    share = tokens // cut
    return call(
        functools.partial(first_kernel, place),
        (shape((size, home, cut)),) * share,
        (share,),
        [pl.BlockSpec((home, size, tokens), lambda s, pos: (0, 0, 0))] + anywhere(len(left_one)),
        (pl.BlockSpec((size, home, cut), lambda s, pos: (0, 0, 0)),) * share,
        [pltpu.VMEM((home, size, cut), BF16)] + whole_scratch([left_one]),
        (x_home, *left_one),
        us=8,
        scalars=pos,
    )


def last_kernel(place, pos_ref, *refs):
    share = place.far * place.near
    e_refs, x_ref, g_ref = refs[:share], refs[share], refs[share + 1]
    pieces, (out_ref, grad_ref, turned, whole, sems) = refs[share + 2 : -5], refs[-5:]
    blocks, per, _ = e_refs[0].shape
    copies = piece_copies([pieces], whole, sems)
    block = block_reader(place, pos_ref, whole, None)
    first = pl.program_id(0) * per

    @pl.when(pl.program_id(0) == 0)
    def _():
        run(copies)

    for n in range(share):
        into = turned.at[place.source(pos_ref, n)]
        for o in range(0, blocks, TILE):
            turn(e_refs[n].at[o : o + TILE], into, o)

    @pl.when(pl.program_id(0) == 0)
    def _():
        finish(copies)

    def load(b):
        e_b = jnp.concatenate([turned[s, b] for s in range(share)], axis=1)
        out_ref[b] = (g_ref[b].astype(F32) + dot_nn(block(first + b), e_b)).astype(BF16)
        grad_ref[b] = dot_nt(x_ref[b], e_b).astype(BF16)

    each(per, load, 4)


def last_stage(place, pos, e_got, x_home, g_home, left_one):
    share = len(e_got)
    blocks, home, cut = e_got[0].shape
    _, size, tokens = x_home.shape
    per = math.gcd(home, 16)
    wide = pl.BlockSpec((per, size, tokens), lambda h, pos: (h, 0, 0))
    factor = pl.BlockSpec((per, size, size), lambda h, pos: (h, 0, 0))
    return call(
        functools.partial(last_kernel, place),
        (shape(g_home.shape), shape((home, size, size))),
        (home // per,),
        [pl.BlockSpec((blocks, per, cut), lambda h, pos: (0, h, 0))] * share + [wide, wide] + anywhere(len(left_one)),
        (wide, factor),
        [pltpu.VMEM((share, per, blocks, cut), BF16)] + whole_scratch([left_one]),
        (*e_got, x_home, g_home, *left_one),
        us=10,
        scalars=pos,
    )


def mixed_kernel(place, pos_ref, *refs):
    *s_refs, x_ref, out_ref = refs
    cut = s_refs[0].shape[2]
    for n, s_ref in enumerate(s_refs):
        lanes = pl.ds(pl.multiple_of(place.source(pos_ref, n) * cut, cut), cut)
        out_ref[:, :, lanes] = (x_ref[:, :, lanes].astype(F32) + s_ref[...].astype(F32)).astype(BF16)


def add_home(place, pos, s_got, x_home):
    home, blocks, cut = s_got[0].shape
    per = math.gcd(home, 8)
    wide = pl.BlockSpec((per,) + x_home.shape[1:], lambda h, pos: (h, 0, 0))
    return call(
        functools.partial(mixed_kernel, place),
        shape(x_home.shape),
        (home // per,),
        [pl.BlockSpec((per, blocks, cut), lambda h, pos: (h, 0, 0))] * len(s_got) + [wide],
        wide,
        [],
        (*s_got, x_home),
        us=6,
        scalars=pos,
    )


def back_two_kernel(place, pos_ref, *refs):
    share = place.far * place.near
    g_parts, factor = refs[:share], unflat(place, refs[share:-7])
    out_ref, turned, stage, g_all, g_sems, w_all, w_sems = refs[-7:]
    per = out_ref.shape[0]
    phase, j = pl.program_id(0), pl.program_id(1)

    @pl.when((phase == 0) & (j == 0))
    def _():
        copies = share_copies(place, pos_ref, g_parts, g_all, g_sems) + piece_copies(factor, w_all, w_sems)
        run(copies)
        finish(copies)

    @pl.when(phase == 0)
    def _():
        block = block_reader(place, pos_ref, w_all, j)

        def body(ks):
            out = dots_nn([block(k) for k in ks], [stacked(g_all, j * per + k) for k in ks])
            for k, y in zip(ks, out):
                stage[k] = y.astype(BF16)

        staged(per, body, stage, turned, j)

    @pl.when(phase == 1)
    def _():
        def body(k):
            out_ref[k] = turned[j * per + k]

        each(per, body)


def staged(per, body, stage, turned, j):
    for k in range(0, per, TILE):
        pairs(TILE, lambda ks: body([k + i for i in ks]))
        turn(stage.at[k : k + TILE], turned, j * per + k)


def middle_sizes(place, parts):
    blocks, home, cut = parts[0].shape
    return blocks, home, cut, len(parts)


def back_two(place, pos, g_mid, right_two):
    blocks, home, cut, share = middle_sizes(place, g_mid)
    at = during(1, share)
    return call(
        functools.partial(back_two_kernel, place),
        shape((blocks, blocks, cut)),
        (2, share),
        anywhere(share + len(flat(right_two))),
        pl.BlockSpec((home, blocks, cut), lambda p, j, pos: (at(p, j), 0, 0)),
        [
            pltpu.VMEM((blocks, blocks, cut), BF16),
            pltpu.VMEM((home, blocks, cut), BF16),
            pltpu.VMEM((share, blocks, home, cut), BF16),
            pltpu.SemaphoreType.DMA((share,)),
        ]
        + whole_scratch(right_two),
        (*g_mid, *flat(right_two)),
        us=10,
        scalars=pos,
    )


def either(place, pos_ref, j, keep_ref, send_ref, body):
    mine = lax.rem(j, place.near) == pos_ref[1]

    @pl.when(mine)
    def _():
        body(keep_ref)

    @pl.when(jnp.logical_not(mine))
    def _():
        body(send_ref)


def middle_kernel(place, pos_ref, *refs):
    share = place.far * place.near
    wide = (len(refs) - (2 * share + 15)) // 2
    s_parts, rest = refs[:share], refs[share:]
    one, two, rest = unflat(place, rest[:wide]), unflat(place, rest[wide : 2 * wide]), rest[2 * wide :]
    e_ref, act_ref, keep_two, send_two, keep_one, send_one, *rest = rest
    out_refs, rest = rest[:share], rest[share:]
    turned, hidden, e_one, s_all, s_sems, one_all, one_sems, two_all, two_sems = rest
    per, home = act_ref.shape[0], s_all.shape[2]
    phase, j = pl.program_id(0), pl.program_id(1)

    def second():
        return piece_copies(two, two_all, two_sems)

    @pl.when((phase == 0) & (j == 0))
    def _():
        copies = share_copies(place, pos_ref, s_parts, s_all, s_sems) + piece_copies(one, one_all, one_sems)
        run(copies)
        finish(copies)
        run(second())

    @pl.when(phase == 0)
    def _():
        block = block_reader(place, pos_ref, one_all, j)

        def body(ks):
            out = dots_tn([block(k) for k in ks], [stacked(s_all, j * per + k) for k in ks])
            for k, y in zip(ks, out):
                e_one[k] = y.astype(BF16)

        staged(per, body, e_one, turned, j)

    @pl.when((phase == 1) & (j == 0))
    def _():
        finish(second())

    @pl.when(phase == 1)
    def _():
        block = block_reader(place, pos_ref, two_all, j)

        def with_out(grad_ref):
            def body(ks):
                acts, slopes, es = [], [], [e_ref[k] for k in ks]
                for k in ks:
                    value, slope = gelu_both(turned[j * per + k].astype(F32))
                    acts.append(value.astype(BF16))
                    slopes.append(slope)
                    act_ref[k] = acts[-1]
                for k, slope, y in zip(ks, slopes, dots_nn([block(k) for k in ks], es)):
                    e_one[k] = (slope * y).astype(BF16)
                for k, y in zip(ks, dots_nt(acts, es)):
                    grad_ref[0, k] = y.astype(BF16)

            staged(per, body, e_one, hidden, j)

        either(place, pos_ref, j, keep_two, send_two, with_out)

    @pl.when(phase == 2)
    def _():
        block = block_reader(place, pos_ref, one_all, j)

        def with_out(grad_ref):
            def body(ks):
                hs = [hidden[j * per + k] for k in ks]
                for k, y in zip(ks, dots_nn([block(k) for k in ks], hs)):
                    e_one[k] = y.astype(BF16)
                for k, y in zip(ks, dots_nt([stacked(s_all, j * per + k) for k in ks], hs)):
                    grad_ref[0, k] = y.astype(BF16)

            pairs(per, body)

        either(place, pos_ref, j, keep_one, send_one, with_out)
        for n in range(share):
            at = pl.ds(pl.multiple_of(place.onward(pos_ref, n) * home, home), home)
            out_refs[n][...] = e_one[:, at, :]


def grad_specs(place, phase, home, size, share):
    at = during(phase, share)
    dims = shape((place.far, home, size, size))
    spec = pl.BlockSpec((1, home, size, size), lambda p, j, pos: (at(p, j) // place.near, 0, 0, 0))
    return [dims] * 2, [spec] * 2


def middle(place, pos, s_mid, e_mid, right_one, left_two):
    blocks, home, cut, share = middle_sizes(place, s_mid)
    at = [during(phase, share) for phase in range(3)]
    block = pl.BlockSpec((home, blocks, cut), lambda p, j, pos: (at[1](p, j), 0, 0))
    two, two_specs = grad_specs(place, 1, home, blocks, share)
    one, one_specs = grad_specs(place, 2, home, blocks, share)
    piece = pl.BlockSpec((home, home, cut), lambda p, j, pos: (at[2](p, j), 0, 0))
    out = call(
        functools.partial(middle_kernel, place),
        (shape((blocks, blocks, cut)), *two, *one) + (shape((blocks, home, cut)),) * share,
        (3, share),
        anywhere(share + 2 * len(flat(right_one))) + [block],
        (block, *two_specs, *one_specs) + (piece,) * share,
        [pltpu.VMEM((blocks, blocks, cut), BF16)] * 2
        + [
            pltpu.VMEM((home, blocks, cut), BF16),
            pltpu.VMEM((share, blocks, home, cut), BF16),
            pltpu.SemaphoreType.DMA((share,)),
        ]
        + whole_scratch(right_one)
        + whole_scratch(left_two),
        (*s_mid, *flat(right_one), *flat(left_two), e_mid),
        us=26,
        scalars=pos,
    )
    return out[0], out[1:3], out[3:5], list(out[5:])


def forward_two_kernel(place, pos_ref, *refs):
    share = place.far * place.near
    wide = (len(refs) - (2 * share + 12)) // 2
    g_parts, rest = refs[:share], refs[share:]
    left, right, rest = unflat(place, rest[:wide]), unflat(place, rest[wide : 2 * wide]), rest[2 * wide :]
    act_ref, keep_ref, send_ref, *rest = rest
    out_refs, rest = rest[:share], rest[share:]
    turned, fourth, stage, g_all, g_sems, left_all, left_sems, right_all, right_sems = rest
    per = act_ref.shape[0]
    phase, j = pl.program_id(0), pl.program_id(1)

    def second():
        return piece_copies(right, right_all, right_sems) + share_copies(place, pos_ref, g_parts, g_all, g_sems)

    @pl.when((phase == 0) & (j == 0))
    def _():
        copies = piece_copies(left, left_all, left_sems)
        run(copies)
        finish(copies)
        run(second())

    @pl.when(phase == 0)
    def _():
        block = block_reader(place, pos_ref, left_all, j)

        def body(ks):
            for k, y in zip(ks, dots_tn([block(k) for k in ks], [act_ref[k] for k in ks])):
                stage[k] = y.astype(BF16)

        staged(per, body, stage, turned, j)

    @pl.when((phase == 1) & (j == 0))
    def _():
        finish(second())

    @pl.when(phase == 1)
    def _():
        block = block_reader(place, pos_ref, right_all, j)

        def with_out(grad_ref):
            def body(ks):
                thirds = [turned[j * per + k] for k in ks]
                for k, y in zip(ks, dots_tn([block(k) for k in ks], thirds)):
                    stage[k] = y.astype(BF16)
                for k, y in zip(ks, dots_nt(thirds, [stacked(g_all, j * per + k) for k in ks])):
                    grad_ref[0, k] = y.astype(BF16)

            staged(per, body, stage, fourth, j)

        either(place, pos_ref, j, keep_ref, send_ref, with_out)

    for n in range(share):

        @pl.when((phase == 2) & (j == n))
        def _():
            base = place.onward(pos_ref, n) * per

            def body(k):
                out_refs[n][k] = fourth[base + k]

            each(per, body)


def forward_two(place, pos, act, g_mid, left_two, right_two):
    blocks, home, cut, share = middle_sizes(place, g_mid)
    at = during(0, share)
    grad, grad_spec = grad_specs(place, 1, home, blocks, share)
    out = call(
        functools.partial(forward_two_kernel, place),
        (*grad,) + (shape((home, blocks, cut)),) * share,
        (3, share),
        anywhere(share + 2 * len(flat(left_two))) + [pl.BlockSpec((home, blocks, cut), lambda p, j, pos: (at(p, j), 0, 0))],
        (*grad_spec,) + (pl.BlockSpec((home, blocks, cut), lambda p, j, pos: (0, 0, 0)),) * share,
        [pltpu.VMEM((blocks, blocks, cut), BF16)] * 2
        + [
            pltpu.VMEM((home, blocks, cut), BF16),
            pltpu.VMEM((share, blocks, home, cut), BF16),
            pltpu.SemaphoreType.DMA((share,)),
        ]
        + whole_scratch(left_two)
        + whole_scratch(right_two),
        (*g_mid, *flat(left_two), *flat(right_two), act),
        us=20,
        scalars=pos,
    )
    return out[:2], list(out[2:])


def halves(size):
    low = 2 if size % 2 == 0 else 1
    return size // low, low


def cross(pieces):
    return lax.all_to_all(pieces, "tensor", split_axis=0, concat_axis=0, tiled=True)


def whole_tokens(x_home, g_home, factors, share, cut):
    home, size, tokens = x_home.shape
    first_left = factors[0]
    rows = first_left.shape[1]
    place = Place(share, lax.axis_size("dp"))
    pos = place.position()

    def gather(start, n):
        if n >= len(place.dp):
            return start
        got = [start] + place.dp[n].sends(start)
        return got if n == 0 else jnp.stack(got)

    def gather_far(start):
        for n in reversed(range(2, len(place.dp))):
            start = gather(start, n)
        return start

    def last_dp(start):
        return gather(start, 0) if place.dp else [start]

    def cores(piece):
        return [piece] + place.core.sends(piece)

    def by_core(own):
        return [[p[c] for p in own] for c in range(place.near)]

    def cross(pieces, n):
        return place.exchange(pieces, n) if n < share else None

    def from_y(start):
        return jnp.stack([start] + place.y.sends(start))

    n_one, n_two, n_three = (place.steps.index(step) if step in place.steps else share for step in [(0, 1), (1, 0), (1, 1)])
    one = gather_far(first_left)
    rest = from_y(jnp.stack([factors[3], factors[1], factors[2]]))
    g = {n: deal(place, pos, g_home, cut, n) for n in reversed(range(share))}
    got_three = cross(g, n_three)
    w_two = gather_far(after(rest[:, 0], g[share - 1]))
    one = last_dp(gather(one, 1))
    w_one = gather_far(rest[:, 1])
    w_two = gather(w_two, 1)
    got_three, one, w_two, w_one, rest, g = slot(place, (got_three, one, w_two, w_one, rest, g))

    got_two = cross(g, n_two)
    right_two = last_dp(w_two)
    w_one = gather(w_one, 1)
    w_left = gather_far(rest[:, 2])
    s = first_stage(place, pos, x_home, one, cut)
    got_two, right_two, w_one, w_left, one, s, pos = slot(place, (got_two, right_two, w_one, w_left, one, list(s), pos))

    s_three = cross(s, n_three)
    right_one = last_dp(w_one)
    w_left = gather(w_left, 1)
    right_two = by_core([cores(p) for p in right_two])
    s_one = cross(s, n_one)
    got_one = cross(g, n_one)
    s_three, s_one, right_one, w_left, right_two, g, got_one = slot(
        place, (s_three, s_one, right_one, w_left, right_two, g, got_one)
    )
    g_mid = [g[0], got_one, got_two, got_three][:share]

    s_two = cross(s, n_two)
    left_two = last_dp(w_left)
    left_core = cores(left_two[0])
    right_one = by_core([cores(p) for p in right_one])
    e_mid = back_two(place, pos, g_mid, right_two)
    s_two, left_two, left_core, right_one, e_mid = slot(place, (s_two, left_two, left_core, right_one, e_mid))
    s_mid = [s[0], s_one, s_two, s_three][:share]
    left_two = by_core([left_core] + [cores(p) for p in left_two[1:]])

    act, grad_two, grad_one, e = middle(place, pos, s_mid, e_mid, right_one, left_two)

    def start_sum(keep, send):
        arrays = [keep, place.core.send(send, 1)] if place.near > 1 else [keep]
        return Sum(arrays, [place.y, home] + place.dp[::-1], (rows, size))

    def hold(parts, arrays):
        for part, kept in zip(parts, arrays):
            part.arrays, part.ready = kept

    def arrays_of(*parts):
        return [(part.arrays, part.ready) for part in parts]

    x_step, near_step, far_step = (place.dp + [None] * 3)[:3]

    e_three = cross(e, n_three)
    two, one_part = start_sum(*grad_two), start_sum(*grad_one)
    grad_three, s = forward_two(place, pos, act, g_mid, left_two, right_two)
    two.prepare(x_step)
    one_part.prepare(near_step)
    e_three, kept, grad_three, s, e = slot(place, (e_three, arrays_of(two, one_part), grad_three, s, e))
    hold([two, one_part], kept)

    e_two = cross(e, n_two)
    two.step(x_step)
    one_part.step(near_step)
    three = start_sum(*grad_three)
    e_one = cross(e, n_one)
    three.prepare(x_step)
    e_two, e_one, kept, s = slot(place, (e_two, e_one, arrays_of(two, one_part, three), s))
    hold([two, one_part, three], kept)
    e_got = [e[0], e_one, e_two, e_three][:share]

    s_three = cross(s, n_three)
    three.step(x_step)
    one_part.step(far_step)
    two.step(near_step)
    input_grad, lone = last_stage(place, pos, e_got, x_home, g_home, one)
    lone = Sum([lone], [home] + place.dp[::-1], (rows, size))
    lone.prepare(x_step)
    s_three, kept, input_grad, s = slot(place, (s_three, arrays_of(two, one_part, three, lone), input_grad, s))
    hold([two, one_part, three, lone], kept)

    s_two = cross(s, n_two)
    lone.step(x_step)
    two.step(far_step)
    three.step(near_step)
    one_part.step(x_step)
    lone.step(near_step)
    three.step(far_step, lone.arrays[-1])
    s_one = cross(s, n_one)
    s_got = [s[0], s_one, s_two, s_three][:share]
    mixed = add_home(place, pos, s_got, x_home)
    grad_ltwo, grad_rone, grad_rtwo = finish_together([two, one_part, three], place.dp, place.y, mixed)
    grad_lone = lone.finish()
    return mixed, input_grad, grad_lone, grad_rone, grad_ltwo, grad_rtwo


def split_blocks(x_home, g_home, factors, share, cut):
    home, size, tokens = x_home.shape
    far, near = halves(share)
    outer, inner = halves(lax.axis_size("dp"))
    ring_y, ring_core = Ring("tensor", (near, far)), Ring("tensor", (1, near))
    ring_z, ring_x = Ring("dp", (inner, outer)), Ring("dp", (1, inner))
    rows = factors[0].shape[1]
    n_tensor = lax.axis_size("tensor")
    groups = n_tensor // share
    held = home * share
    same_tokens = [[group * share + part for group in range(groups)] for part in range(share)]

    def go(values):
        pieces = values.reshape(home, groups, held, share, cut).transpose(1, 3, 2, 0, 4)
        got = cross(pieces.reshape(n_tensor, held, home, cut))
        return got.transpose(1, 0, 2, 3).reshape(held, size, cut)

    def back(values):
        pieces = values.reshape(held, n_tensor, home, cut).transpose(1, 0, 2, 3)
        got = cross(pieces).reshape(groups, share, held, home, cut)
        return got.transpose(3, 0, 2, 1, 4).reshape(home, size, tokens)

    def turn(values):
        moved = lax.all_to_all(
            values.reshape(held, groups, held, cut), "tensor", split_axis=1, concat_axis=0, tiled=True, axis_index_groups=same_tokens
        )
        return jnp.swapaxes(moved.reshape(size, held, cut), 0, 1)

    def whole(factor):
        one = ring_z.gather(ring_y.gather(factor))
        all_rows = ring_core.gather(ring_x.gather(one))
        return all_rows.transpose(3, 0, 4, 2, 1, 5, 6).reshape(held, size, size)

    def own_sum(partial):
        split = partial.reshape(ring_y.size, ring_core.size, home, ring_z.size, ring_x.size, rows, size)
        terms = ring_core.scatter([split], 1)
        return total(ring_y.scatter(ring_z.scatter(ring_x.scatter(terms, 3), 2), 0))

    first_left, first_right, second_left, second_right = factors
    g_mid = go(g_home)
    left_one = ring_x.gather(ring_z.gather(first_left)).transpose(2, 1, 0, 3, 4).reshape(home, size, size)
    right_one, left_two, right_two = whole(first_right), whole(second_left), whole(second_right)

    s_one = go(product("bjt,bjo->bot", x_home, left_one).astype(BF16))
    s_two = turn(product("bit,bip->bpt", s_one, right_one).astype(BF16))
    act = gelu_value(s_two.astype(F32)).astype(BF16)
    e_three = turn(product("bot,bio->bit", g_mid, right_two).astype(BF16))
    h_mid = turn(gelu_back(s_two.astype(F32), product("bot,bjo->bjt", e_three, left_two)).astype(BF16))
    e_one = back(product("bpt,bip->bit", h_mid, right_one).astype(BF16))
    s_three = turn(product("bjt,bjo->bot", act, left_two).astype(BF16))
    s_four = back(product("bit,bio->bot", s_three, right_two).astype(BF16))
    mixed = (x_home.astype(F32) + s_four.astype(F32)).astype(BF16)

    grad_rtwo = own_sum(product("bit,bot->bio", s_three, g_mid))
    grad_ltwo = own_sum(product("bjt,bot->bjo", act, e_three))
    grad_rone = own_sum(product("bit,bpt->bip", s_one, h_mid))
    grad_lone = product("bjt,bot->bjo", x_home, e_one).reshape(home, ring_z.size, ring_x.size, rows, size)
    grad_lone = total(ring_z.scatter(ring_x.scatter([grad_lone], 2), 1))
    input_grad = (g_home.astype(F32) + product("bot,bjo->bjt", e_one, left_one)).astype(BF16)
    return mixed, input_grad, grad_lone, grad_rone, grad_ltwo, grad_rtwo


def per_device(inputs, cotangent, first_left, first_right, second_left, second_right):
    n_tensor = lax.axis_size("tensor")
    home, _, size = first_left.shape
    tokens = inputs.shape[1]
    share = math.gcd(n_tensor, max(1, tokens // LANES))
    cut = tokens // share
    plan = whole_tokens if share == n_tensor else split_blocks
    mixed, input_grad, *weight_grads = plan(
        inputs.reshape(home, size, tokens),
        cotangent.reshape(home, size, tokens),
        (first_left, first_right, second_left, second_right),
        share,
        cut,
    )
    return (mixed.reshape(inputs.shape), input_grad.reshape(inputs.shape), *weight_grads)


def solution(mesh):
    wide, factor = P("tensor", "dp"), P("tensor", "dp", None)
    return jax.shard_map(
        per_device,
        mesh=mesh,
        in_specs=(wide, wide, factor, factor, factor, factor),
        out_specs=(wide, wide, factor, factor, factor, factor),
        check_vma=False,
    )
```

```python
import functools
import itertools
import math

import jax
import jax.numpy as jnp
from jax import lax
from jax.experimental import pallas as pl
from jax.experimental.pallas import tpu as pltpu
from jax.sharding import PartitionSpec as P

BF16 = jnp.bfloat16
F32 = jnp.float32
LANES = 128
TILE = 16
VMEM_BYTES = 60 * 1024 * 1024
BYTES_PER_US = 1_200_000


def gelu_value(values):
    return jax.nn.gelu(values, approximate=True)


def gelu_back(values, upstream):
    return jax.vjp(gelu_value, values)[1](upstream)[0]


def gelu_both(v):
    root, cubic = 0.7978845608028654, 0.044715
    square = v * v
    t = jnp.tanh(root * (v + cubic * (v * square)))
    half = 0.5 * (1.0 + t)
    slope = half + (0.5 * v) * (1.0 - t * t) * (root + (3.0 * cubic * root) * square)
    return v * half, slope


def product(form, left, right):
    return jnp.einsum(form, left, right, preferred_element_type=F32)


def dot(left, right, left_dim, right_dim):
    return lax.dot_general(left, right, (((left_dim,), (right_dim,)), ((), ())), preferred_element_type=F32)


def dots(lefts, rights, left_dim, right_dim):
    if len(lefts) == 1:
        return [dot(lefts[0], rights[0], left_dim, right_dim)]
    zero = jnp.zeros_like(rights[0])
    upper = jnp.concatenate([rights[0], zero], axis=1)
    lower = jnp.concatenate([zero, rights[1]], axis=1)
    out = dot(jnp.concatenate(lefts, axis=left_dim), jnp.concatenate([upper, lower], axis=0), left_dim, right_dim)
    half = out.shape[1] // 2
    return [out[:, :half], out[:, half:]]


def dots_nn(lefts, rights):
    return dots(lefts, rights, 1, 0)


def dots_tn(lefts, rights):
    return dots(lefts, rights, 0, 0)


def dots_nt(lefts, rights):
    return dots(lefts, rights, 1, 1)


def dot_nn(left, right):
    return dot(left, right, 1, 0)


def dot_nt(left, right):
    return dot(left, right, 1, 1)


def call(body, out, grid, in_specs, out_specs, scratch, args, us, scalars=None):
    spec = pltpu.PrefetchScalarGridSpec(
        num_scalar_prefetch=0 if scalars is None else 1,
        grid=grid,
        in_specs=in_specs,
        out_specs=out_specs,
        scratch_shapes=scratch,
    )
    return pl.pallas_call(
        body,
        out_shape=out,
        grid_spec=spec,
        compiler_params=pltpu.CompilerParams(
            dimension_semantics=("arbitrary",) * len(grid), vmem_limit_bytes=VMEM_BYTES
        ),
        cost_estimate=pl.CostEstimate(flops=0, bytes_accessed=int(us * BYTES_PER_US), transcendentals=0),
    )(*(() if scalars is None else (scalars,)), *args)


def pairs(count, body, unroll=8):
    group = 2 if count % 2 == 0 else 1
    each(count // group, lambda n: body([n * group + i for i in range(group)]), unroll)


def turn(source, out_ref, at):
    n, size, _ = source.shape
    for i in range(0, size, TILE):
        out_ref[i : i + TILE, pl.ds(pl.multiple_of(at, TILE), n), :] = jnp.swapaxes(source[:, i : i + TILE, :], 0, 1)


def shape(dims, dtype=BF16):
    return jax.ShapeDtypeStruct(dims, dtype)


def each(count, body, unroll=16):
    def step(k, carry):
        body(k)
        return carry

    lax.fori_loop(0, count, step, 0, unroll=math.gcd(count, unroll))


def during(phase, steps):
    return lambda p, j: jnp.where(p == phase, j, jnp.where(p < phase, 0, steps - 1))


def stacked(ref, k):
    return jnp.concatenate([ref[c, k] for c in range(ref.shape[0])], axis=0)


class Ring:
    def __init__(self, axis, *digits, tied=True):
        self.axis, self.digits, self.last, self.tied = axis, digits, None, tied
        self.stride, self.size = digits[0]

    def here(self):
        return lax.rem(lax.axis_index(self.axis) // self.stride, self.size)

    def send(self, value, *steps):
        pairs = []
        for src in range(lax.axis_size(self.axis)):
            dst = src
            for (stride, size), step in zip(self.digits, steps):
                own = src // stride % size
                dst += ((own + step) % size - own) * stride
            pairs.append((src, dst))
        if self.tied and self.last is not None:
            value = after(value, self.last)
        self.last = lax.ppermute(value, self.axis, pairs)
        return self.last

    def sends(self, value):
        return [self.send(value, step) for step in range(1, self.size)]

    def gather(self, value):
        if self.size == 1:
            return value[None]
        here = self.here()
        out = jnp.zeros((self.size,) + value.shape, value.dtype)
        out = lax.dynamic_update_index_in_dim(out, value, here, 0)
        for step in range(1, self.size):
            got = self.send(value, step)
            out = lax.dynamic_update_index_in_dim(out, got, lax.rem(here - step + self.size, self.size), 0)
        return out

    def scatter(self, terms, dim, before=()):
        here = self.here()
        if self.size == 1:
            return [lax.index_in_dim(t, 0, dim, keepdims=False) for t in terms]
        out = [lax.dynamic_index_in_dim(t, here, dim, keepdims=False) for t in terms]
        for step in range(1, self.size):
            there = lax.rem(here + step, self.size)
            term = total([lax.dynamic_index_in_dim(t, there, dim, keepdims=False) for t in terms]).astype(BF16)
            out.append(self.send(after(term, *before), step))
        return out


def slot(place, values):
    values = lax.optimization_barrier(values)
    place.crossed = None
    for ring in [place.y, place.core] + place.dp + list(place.links.values()):
        ring.last = None
    return values


class Sum:
    def __init__(self, arrays, rings, tail):
        self.left = rings
        dims = [ring.size if isinstance(ring, Ring) else ring for ring in rings]
        self.arrays = [a.reshape(dims + list(tail)) for a in arrays]
        self.rings = [rings] * len(arrays)
        self.ready = []

    def cut(self, ring=None, index=None):
        out = []
        for array, rings in zip(self.arrays, self.rings):
            dim = 0
            for r in rings:
                if isinstance(r, Ring) and (r is ring or r not in self.left):
                    array = lax.dynamic_index_in_dim(array, index if r is ring else r.here(), dim, keepdims=False)
                else:
                    dim += 1
            out.append(array)
        return total(out)

    def parts(self, ring):
        return [self.cut(ring, lax.rem(ring.here() + step, ring.size)).astype(BF16) for step in range(1, ring.size)]

    def prepare(self, ring):
        self.ready = self.parts(ring) if ring in self.left else []

    def step(self, ring, *before):
        if ring not in self.left:
            return
        rest = [r for r in self.left if r is not ring]
        parts = self.ready or self.parts(ring)
        self.ready = []
        got = [ring.send(after(part, *before), step + 1) for step, part in enumerate(parts)]
        self.arrays, self.rings, self.left = self.arrays + got, self.rings + [rest] * len(got), rest

    def finish(self):
        for ring in [r for r in self.left[::-1] if isinstance(r, Ring)]:
            count = len(self.arrays)
            self.step(ring)
        if not any(isinstance(r, Ring) for r in self.rings[0]):
            return self.cut()
        got, self.arrays = self.arrays[count:], self.arrays[:count]
        own, got = lax.optimization_barrier((self.cut(), got))
        return total([own] + got)


def finish_together(sums, rings, last, *before):
    for part in sums:
        for ring in rings:
            part.step(ring)
    sends = list(zip(*[part.parts(last) for part in sums]))
    got = [last.send(after(jnp.stack(send), *before), step + 1) for step, send in enumerate(sends)]
    for part in sums:
        part.left = [r for r in part.left if r is not last]
    own, got = lax.optimization_barrier(([part.cut() for part in sums], got))
    return [total([mine] + [g[n] for g in got]) for n, mine in enumerate(own)]


def total(terms):
    return functools.reduce(jnp.add, [t.astype(F32) for t in terms])


def after(value, *others):
    if not others:
        return value
    return lax.optimization_barrier((value,) + others)[0]


def turned_back(here, step, size):
    return lax.rem(here - step + size, size)


class Place:
    def __init__(self, share, n_dp):
        self.far, self.near = halves(share)
        self.y, self.core = Ring("tensor", (self.near, self.far)), Ring("tensor", (1, self.near), tied=False)
        self.dp, stride = [], 1
        while stride < n_dp:
            size = next(p for p in range(2, n_dp + 1) if n_dp // stride % p == 0)
            self.dp.append(Ring("dp", (stride, size)))
            stride *= size
        self.steps = [(y, c) for y in range(self.far) for c in range(self.near)]
        self.crossed = None
        self.links = {step: Ring("tensor", (self.near, self.far), (1, self.near)) for step in self.steps[1:]}
        self.rows = [ring.size for ring in self.dp]

    def position(self):
        return jnp.stack([ring.here() for ring in [self.y, self.core] + self.dp]).astype(jnp.int32)

    def onward(self, pos, n):
        y, c = self.steps[n]
        return lax.rem(pos[0] + y, self.far) * self.near + lax.rem(pos[1] + c, self.near)

    def source(self, pos, n):
        y, c = self.steps[n]
        return turned_back(pos[0], y, self.far) * self.near + turned_back(pos[1], c, self.near)

    def exchange(self, pieces, n):
        y, c = self.steps[n]
        piece = pieces[n]
        if y == 0:
            return self.core.send(piece, c)
        if self.crossed is not None:
            piece = after(piece, self.crossed)
        self.crossed = self.y.send(piece, y) if c == 0 else self.links[(y, c)].send(piece, y, c)
        return self.crossed


def piece_copies(pieces, whole, sems):
    flat_whole = [whole.at[c, d] for c in range(len(pieces)) for d in range(len(pieces[0]))]
    return [pltpu.make_async_copy(ref, dst, sems.at[n]) for n, (ref, dst) in enumerate(zip(flat(pieces), flat_whole))]


def block_reader(place, pos_ref, whole, group):
    lead = ()
    if group is not None:
        lead = (turned_back(pos_ref[0], group // place.near, place.far),)
    core = 0 if group is None else turned_back(pos_ref[1], lax.rem(group, place.near), place.near)
    places = []
    for d in range(math.prod(place.rows)):
        steps = [turned_back(pos_ref[2 + n], d // ring.stride % ring.size, ring.size) for n, ring in enumerate(place.dp)]
        places.append((core, *(steps or [0]), *lead))
    return lambda k: jnp.concatenate([whole[(*at, k)] for at in places], axis=0)


def whole_scratch(pieces, grouped=False):
    dims = (len(pieces), len(pieces[0])) + pieces[0][0].shape
    sems = (dims[0], dims[1], dims[-4]) if grouped else (dims[0] * dims[1],)
    return [pltpu.VMEM(dims, BF16), pltpu.SemaphoreType.DMA(sems)]


def group_of(ref, y):
    return ref.at[(slice(None),) * (len(ref.shape) - 4) + (y,)]


def group_copies(pieces, whole, sems):
    copies = []
    for c, row in enumerate(pieces):
        for d, ref in enumerate(row):
            for y in range(ref.shape[-4]):
                dst = group_of(whole.at[c, d], y)
                copies.append(pltpu.make_async_copy(group_of(ref, y), dst, sems.at[c, d, y]))
    return copies


def copies_of_group(place, pos_ref, pieces, whole, sems, group):
    y = turned_back(pos_ref[0], group // place.near, place.far)
    c = turned_back(pos_ref[1], lax.rem(group, place.near), place.near)
    copies = []
    for d, ref in enumerate(pieces[0]):
        dst = group_of(whole.at[c, d], y)
        copies.append(pltpu.make_async_copy(group_of(ref, y), dst, sems.at[c, d, y]))
    return copies


def share_group(place, pos_ref, parts, whole, sems, group, per):
    at = pl.ds(group * per, per)
    return [
        pltpu.make_async_copy(ref.at[at], whole.at[place.source(pos_ref, n), at], sems.at[n, group])
        for n, ref in enumerate(parts)
    ]


def share_copies(place, pos_ref, parts, whole, sems):
    return [pltpu.make_async_copy(ref, whole.at[place.source(pos_ref, n)], sems.at[n]) for n, ref in enumerate(parts)]


def run(copies):
    for copy in copies:
        copy.start()


def finish(copies):
    for copy in copies:
        copy.wait()


def anywhere(count):
    return [pl.BlockSpec(memory_space=pl.ANY)] * count


def flat(pieces):
    return tuple(p for row in pieces for p in row)


def unflat(place, refs):
    wide = len(refs) // place.near
    return [refs[c * wide : (c + 1) * wide] for c in range(place.near)]


def deal_kernel(pos_ref, g_ref, out_ref):
    for o in range(0, g_ref.shape[0], TILE):
        turn(g_ref.at[o : o + TILE], out_ref, o)


def deal(place, pos, g_home, cut, n):
    home, size, _ = g_home.shape
    return call(
        deal_kernel,
        shape((size, home, cut)),
        (1,),
        [pl.BlockSpec((home, size, cut), lambda i, pos: (0, 0, place.onward(pos, n)))],
        pl.BlockSpec((size, home, cut), lambda i, pos: (0, 0, 0)),
        [],
        (g_home,),
        us=3.5,
        scalars=pos,
    )


def first_kernel(place, pos_ref, x_ref, *refs):
    share = place.far * place.near
    pieces, out_refs = refs[: -share - 3], refs[-share - 3 : -3]
    stage, whole, sems = refs[-3:]
    home = x_ref.shape[0]
    cut = out_refs[0].shape[2]
    copies = piece_copies([pieces], whole, sems)
    block = block_reader(place, pos_ref, whole, None)

    @pl.when(pl.program_id(0) == 0)
    def _():
        run(copies)
        finish(copies)

    for n, out_ref in enumerate(out_refs):

        @pl.when(pl.program_id(0) == n)
        def _():
            lanes = pl.ds(pl.multiple_of(place.onward(pos_ref, n) * cut, cut), cut)

            for b in range(0, home, TILE):

                def store(ks):
                    out = dots_tn([block(b + k) for k in ks], [x_ref[b + k, :, lanes] for k in ks])
                    for k, y in zip(ks, out):
                        stage[b + k] = y.astype(BF16)

                pairs(TILE, store)
                turn(stage.at[b : b + TILE], out_ref, b)


def first_stage(place, pos, x_home, left_one, cut):
    home, size, tokens = x_home.shape
    share = tokens // cut
    return call(
        functools.partial(first_kernel, place),
        (shape((size, home, cut)),) * share,
        (share,),
        [pl.BlockSpec((home, size, tokens), lambda s, pos: (0, 0, 0))] + anywhere(len(left_one)),
        (pl.BlockSpec((size, home, cut), lambda s, pos: (0, 0, 0)),) * share,
        [pltpu.VMEM((home, size, cut), BF16)] + whole_scratch([left_one]),
        (x_home, *left_one),
        us=8,
        scalars=pos,
    )


def last_kernel(place, pos_ref, *refs):
    share = place.far * place.near
    e_refs, x_ref, g_ref = refs[:share], refs[share], refs[share + 1]
    pieces, (out_ref, grad_ref, turned, whole, sems) = refs[share + 2 : -5], refs[-5:]
    blocks, per, _ = e_refs[0].shape
    copies = piece_copies([pieces], whole, sems)
    block = block_reader(place, pos_ref, whole, None)
    first = pl.program_id(0) * per

    @pl.when(pl.program_id(0) == 0)
    def _():
        run(copies)

    for n in range(share):
        into = turned.at[place.source(pos_ref, n)]
        for o in range(0, blocks, TILE):
            turn(e_refs[n].at[o : o + TILE], into, o)

    @pl.when(pl.program_id(0) == 0)
    def _():
        finish(copies)

    def load(b):
        e_b = jnp.concatenate([turned[s, b] for s in range(share)], axis=1)
        out_ref[b] = (g_ref[b].astype(F32) + dot_nn(block(first + b), e_b)).astype(BF16)
        grad_ref[b] = dot_nt(x_ref[b], e_b).astype(BF16)

    each(per, load, 4)


def last_stage(place, pos, e_got, x_home, g_home, left_one):
    share = len(e_got)
    blocks, home, cut = e_got[0].shape
    _, size, tokens = x_home.shape
    per = math.gcd(home, 16)
    wide = pl.BlockSpec((per, size, tokens), lambda h, pos: (h, 0, 0))
    factor = pl.BlockSpec((per, size, size), lambda h, pos: (h, 0, 0))
    return call(
        functools.partial(last_kernel, place),
        (shape(g_home.shape), shape((home, size, size))),
        (home // per,),
        [pl.BlockSpec((blocks, per, cut), lambda h, pos: (0, h, 0))] * share + [wide, wide] + anywhere(len(left_one)),
        (wide, factor),
        [pltpu.VMEM((share, per, blocks, cut), BF16)] + whole_scratch([left_one]),
        (*e_got, x_home, g_home, *left_one),
        us=10,
        scalars=pos,
    )


def mixed_kernel(place, pos_ref, *refs):
    *s_refs, x_ref, out_ref = refs
    cut = s_refs[0].shape[2]
    for n, s_ref in enumerate(s_refs):
        lanes = pl.ds(pl.multiple_of(place.source(pos_ref, n) * cut, cut), cut)
        out_ref[:, :, lanes] = (x_ref[:, :, lanes].astype(F32) + s_ref[...].astype(F32)).astype(BF16)


def add_home(place, pos, s_got, x_home):
    home, blocks, cut = s_got[0].shape
    per = math.gcd(home, 8)
    wide = pl.BlockSpec((per,) + x_home.shape[1:], lambda h, pos: (h, 0, 0))
    return call(
        functools.partial(mixed_kernel, place),
        shape(x_home.shape),
        (home // per,),
        [pl.BlockSpec((per, blocks, cut), lambda h, pos: (h, 0, 0))] * len(s_got) + [wide],
        wide,
        [],
        (*s_got, x_home),
        us=6,
        scalars=pos,
    )


def back_two_kernel(place, pos_ref, *refs):
    share = place.far * place.near
    g_parts, factor = refs[:share], unflat(place, refs[share:-7])
    out_ref, turned, stage, g_all, g_sems, w_all, w_sems = refs[-7:]
    per = out_ref.shape[0]
    phase, j = pl.program_id(0), pl.program_id(1)

    @pl.when((phase == 0) & (j == 0))
    def _():
        copies = share_copies(place, pos_ref, g_parts, g_all, g_sems) + piece_copies(factor, w_all, w_sems)
        run(copies)
        finish(copies)

    @pl.when(phase == 0)
    def _():
        block = block_reader(place, pos_ref, w_all, j)

        def body(ks):
            out = dots_nn([block(k) for k in ks], [stacked(g_all, j * per + k) for k in ks])
            for k, y in zip(ks, out):
                stage[k] = y.astype(BF16)

        staged(per, body, stage, turned, j)

    @pl.when(phase == 1)
    def _():
        def body(k):
            out_ref[k] = turned[j * per + k]

        each(per, body)


def staged(per, body, stage, turned, j):
    for k in range(0, per, TILE):
        pairs(TILE, lambda ks: body([k + i for i in ks]))
        turn(stage.at[k : k + TILE], turned, j * per + k)


def middle_sizes(place, parts):
    blocks, home, cut = parts[0].shape
    return blocks, home, cut, len(parts)


def back_two(place, pos, g_mid, right_two):
    blocks, home, cut, share = middle_sizes(place, g_mid)
    at = during(1, share)
    return call(
        functools.partial(back_two_kernel, place),
        shape((blocks, blocks, cut)),
        (2, share),
        anywhere(share + len(flat(right_two))),
        pl.BlockSpec((home, blocks, cut), lambda p, j, pos: (at(p, j), 0, 0)),
        [
            pltpu.VMEM((blocks, blocks, cut), BF16),
            pltpu.VMEM((home, blocks, cut), BF16),
            pltpu.VMEM((share, blocks, home, cut), BF16),
            pltpu.SemaphoreType.DMA((share,)),
        ]
        + whole_scratch(right_two),
        (*g_mid, *flat(right_two)),
        us=10,
        scalars=pos,
    )


def either(place, pos_ref, j, keep_ref, send_ref, body):
    mine = lax.rem(j, place.near) == pos_ref[1]

    @pl.when(mine)
    def _():
        body(keep_ref)

    @pl.when(jnp.logical_not(mine))
    def _():
        body(send_ref)


def middle_kernel(place, pos_ref, *refs):
    share = place.far * place.near
    wide = (len(refs) - (2 * share + 15)) // 2
    s_parts, rest = refs[:share], refs[share:]
    one, two, rest = unflat(place, rest[:wide]), unflat(place, rest[wide : 2 * wide]), rest[2 * wide :]
    e_ref, act_ref, keep_two, send_two, keep_one, send_one, *rest = rest
    out_refs, rest = rest[:share], rest[share:]
    turned, hidden, e_one, s_all, s_sems, one_all, one_sems, two_all, two_sems = rest
    per, home = act_ref.shape[0], s_all.shape[2]
    phase, j = pl.program_id(0), pl.program_id(1)

    def second():
        return piece_copies(two, two_all, two_sems)

    @pl.when((phase == 0) & (j == 0))
    def _():
        run(group_copies(one, one_all, one_sems))
        for group in range(share):
            run(share_group(place, pos_ref, s_parts, s_all, s_sems, group, per))

    @pl.when((phase == 0) & (j == min(1, share - 1)))
    def _():
        run(second())

    @pl.when(phase == 0)
    def _():
        finish(copies_of_group(place, pos_ref, one, one_all, one_sems, j))
        finish(share_group(place, pos_ref, s_parts, s_all, s_sems, j, per))

    @pl.when(phase == 0)
    def _():
        block = block_reader(place, pos_ref, one_all, j)

        def body(ks):
            out = dots_tn([block(k) for k in ks], [stacked(s_all, j * per + k) for k in ks])
            for k, y in zip(ks, out):
                e_one[k] = y.astype(BF16)

        staged(per, body, e_one, turned, j)

    @pl.when((phase == 1) & (j == 0))
    def _():
        finish(second())

    @pl.when(phase == 1)
    def _():
        block = block_reader(place, pos_ref, two_all, j)

        def with_out(grad_ref):
            def body(ks):
                acts, slopes, es = [], [], [e_ref[k] for k in ks]
                for k in ks:
                    value, slope = gelu_both(turned[j * per + k].astype(F32))
                    acts.append(value.astype(BF16))
                    slopes.append(slope)
                    act_ref[k] = acts[-1]
                for k, slope, y in zip(ks, slopes, dots_nn([block(k) for k in ks], es)):
                    e_one[k] = (slope * y).astype(BF16)
                for k, y in zip(ks, dots_nt(acts, es)):
                    grad_ref[0, k] = y.astype(BF16)

            staged(per, body, e_one, hidden, j)

        either(place, pos_ref, j, keep_two, send_two, with_out)

    @pl.when(phase == 2)
    def _():
        block = block_reader(place, pos_ref, one_all, j)

        def with_out(grad_ref):
            def body(ks):
                hs = [hidden[j * per + k] for k in ks]
                for k, y in zip(ks, dots_nn([block(k) for k in ks], hs)):
                    e_one[k] = y.astype(BF16)
                for k, y in zip(ks, dots_nt([stacked(s_all, j * per + k) for k in ks], hs)):
                    grad_ref[0, k] = y.astype(BF16)

            pairs(per, body)

        either(place, pos_ref, j, keep_one, send_one, with_out)
        for n in range(share):
            at = pl.ds(pl.multiple_of(place.onward(pos_ref, n) * home, home), home)
            out_refs[n][...] = e_one[:, at, :]


def grad_specs(place, phase, home, size, share):
    at = during(phase, share)
    dims = shape((place.far, home, size, size))
    spec = pl.BlockSpec((1, home, size, size), lambda p, j, pos: (at(p, j) // place.near, 0, 0, 0))
    return [dims] * 2, [spec] * 2


def middle(place, pos, s_mid, e_mid, right_one, left_two):
    blocks, home, cut, share = middle_sizes(place, s_mid)
    at = [during(phase, share) for phase in range(3)]
    block = pl.BlockSpec((home, blocks, cut), lambda p, j, pos: (at[1](p, j), 0, 0))
    two, two_specs = grad_specs(place, 1, home, blocks, share)
    one, one_specs = grad_specs(place, 2, home, blocks, share)
    piece = pl.BlockSpec((home, home, cut), lambda p, j, pos: (at[2](p, j), 0, 0))
    out = call(
        functools.partial(middle_kernel, place),
        (shape((blocks, blocks, cut)), *two, *one) + (shape((blocks, home, cut)),) * share,
        (3, share),
        anywhere(share + 2 * len(flat(right_one))) + [block],
        (block, *two_specs, *one_specs) + (piece,) * share,
        [pltpu.VMEM((blocks, blocks, cut), BF16)] * 2
        + [
            pltpu.VMEM((home, blocks, cut), BF16),
            pltpu.VMEM((share, blocks, home, cut), BF16),
            pltpu.SemaphoreType.DMA((share, share)),
        ]
        + whole_scratch(right_one, True)
        + whole_scratch(left_two),
        (*s_mid, *flat(right_one), *flat(left_two), e_mid),
        us=26,
        scalars=pos,
    )
    return out[0], out[1:3], out[3:5], list(out[5:])


def forward_two_kernel(place, pos_ref, *refs):
    share = place.far * place.near
    wide = (len(refs) - (2 * share + 12)) // 2
    g_parts, rest = refs[:share], refs[share:]
    left, right, rest = unflat(place, rest[:wide]), unflat(place, rest[wide : 2 * wide]), rest[2 * wide :]
    act_ref, keep_ref, send_ref, *rest = rest
    out_refs, rest = rest[:share], rest[share:]
    turned, fourth, stage, g_all, g_sems, left_all, left_sems, right_all, right_sems = rest
    per = act_ref.shape[0]
    phase, j = pl.program_id(0), pl.program_id(1)

    def second():
        return piece_copies(right, right_all, right_sems) + share_copies(place, pos_ref, g_parts, g_all, g_sems)

    @pl.when((phase == 0) & (j == 0))
    def _():
        run(group_copies(left, left_all, left_sems))

    @pl.when((phase == 0) & (j == min(1, share - 1)))
    def _():
        run(second())

    @pl.when(phase == 0)
    def _():
        finish(copies_of_group(place, pos_ref, left, left_all, left_sems, j))

    @pl.when(phase == 0)
    def _():
        block = block_reader(place, pos_ref, left_all, j)

        def body(ks):
            for k, y in zip(ks, dots_tn([block(k) for k in ks], [act_ref[k] for k in ks])):
                stage[k] = y.astype(BF16)

        staged(per, body, stage, turned, j)

    @pl.when((phase == 1) & (j == 0))
    def _():
        finish(second())

    @pl.when(phase == 1)
    def _():
        block = block_reader(place, pos_ref, right_all, j)

        def with_out(grad_ref):
            def body(ks):
                thirds = [turned[j * per + k] for k in ks]
                for k, y in zip(ks, dots_tn([block(k) for k in ks], thirds)):
                    stage[k] = y.astype(BF16)
                for k, y in zip(ks, dots_nt(thirds, [stacked(g_all, j * per + k) for k in ks])):
                    grad_ref[0, k] = y.astype(BF16)

            staged(per, body, stage, fourth, j)

        either(place, pos_ref, j, keep_ref, send_ref, with_out)

    for n in range(share):

        @pl.when((phase == 2) & (j == n))
        def _():
            base = place.onward(pos_ref, n) * per

            def body(k):
                out_refs[n][k] = fourth[base + k]

            each(per, body)


def forward_two(place, pos, act, g_mid, left_two, right_two):
    blocks, home, cut, share = middle_sizes(place, g_mid)
    at = during(0, share)
    grad, grad_spec = grad_specs(place, 1, home, blocks, share)
    out = call(
        functools.partial(forward_two_kernel, place),
        (*grad,) + (shape((home, blocks, cut)),) * share,
        (3, share),
        anywhere(share + 2 * len(flat(left_two))) + [pl.BlockSpec((home, blocks, cut), lambda p, j, pos: (at(p, j), 0, 0))],
        (*grad_spec,) + (pl.BlockSpec((home, blocks, cut), lambda p, j, pos: (0, 0, 0)),) * share,
        [pltpu.VMEM((blocks, blocks, cut), BF16)] * 2
        + [
            pltpu.VMEM((home, blocks, cut), BF16),
            pltpu.VMEM((share, blocks, home, cut), BF16),
            pltpu.SemaphoreType.DMA((share,)),
        ]
        + whole_scratch(left_two, True)
        + whole_scratch(right_two),
        (*g_mid, *flat(left_two), *flat(right_two), act),
        us=20,
        scalars=pos,
    )
    return out[:2], list(out[2:])


def halves(size):
    low = 2 if size % 2 == 0 else 1
    return size // low, low


def cross(pieces):
    return lax.all_to_all(pieces, "tensor", split_axis=0, concat_axis=0, tiled=True)


def whole_tokens(x_home, g_home, factors, share, cut):
    home, size, tokens = x_home.shape
    first_left = factors[0]
    rows = first_left.shape[1]
    place = Place(share, lax.axis_size("dp"))
    pos = place.position()

    def gather(start, n):
        if n >= len(place.dp):
            return start
        got = [start] + place.dp[n].sends(start)
        return got if n == 0 else jnp.stack(got)

    def gather_far(start):
        for n in reversed(range(2, len(place.dp))):
            start = gather(start, n)
        return start

    def last_dp(start):
        return gather(start, 0) if place.dp else [start]

    def cores(piece):
        return [piece] + place.core.sends(piece)

    def by_core(own):
        return [[p[c] for p in own] for c in range(place.near)]

    def cross(pieces, n):
        return place.exchange(pieces, n) if n < share else None

    def from_y(start):
        return jnp.stack([start] + place.y.sends(start))

    n_one, n_two, n_three = (place.steps.index(step) if step in place.steps else share for step in [(0, 1), (1, 0), (1, 1)])
    one = gather_far(first_left)
    rest = from_y(jnp.stack([factors[3], factors[1], factors[2]]))
    g = {n: deal(place, pos, g_home, cut, n) for n in reversed(range(share))}
    got_three = cross(g, n_three)
    w_two = gather_far(after(rest[:, 0], g[share - 1]))
    one = last_dp(gather(one, 1))
    w_one = gather_far(rest[:, 1])
    w_two = gather(w_two, 1)
    got_three, one, w_two, w_one, rest, g = slot(place, (got_three, one, w_two, w_one, rest, g))

    got_two = cross(g, n_two)
    right_two = last_dp(w_two)
    w_one = gather(w_one, 1)
    w_left = gather_far(rest[:, 2])
    s = first_stage(place, pos, x_home, one, cut)
    got_two, right_two, w_one, w_left, one, s, pos = slot(place, (got_two, right_two, w_one, w_left, one, list(s), pos))

    s_three = cross(s, n_three)
    right_one = last_dp(w_one)
    w_left = gather(w_left, 1)
    right_two = by_core([cores(p) for p in right_two])
    s_one = cross(s, n_one)
    got_one = cross(g, n_one)
    s_three, s_one, right_one, w_left, right_two, g, got_one = slot(
        place, (s_three, s_one, right_one, w_left, right_two, g, got_one)
    )
    g_mid = [g[0], got_one, got_two, got_three][:share]

    s_two = cross(s, n_two)
    left_two = last_dp(w_left)
    left_core = cores(left_two[0])
    right_one = by_core([cores(p) for p in right_one])
    e_mid = back_two(place, pos, g_mid, right_two)
    s_two, left_two, left_core, right_one, e_mid = slot(place, (s_two, left_two, left_core, right_one, e_mid))
    s_mid = [s[0], s_one, s_two, s_three][:share]
    left_two = by_core([left_core] + [cores(p) for p in left_two[1:]])

    act, grad_two, grad_one, e = middle(place, pos, s_mid, e_mid, right_one, left_two)

    def start_sum(keep, send):
        arrays = [keep, place.core.send(send, 1)] if place.near > 1 else [keep]
        return Sum(arrays, [place.y, home] + place.dp[::-1], (rows, size))

    def hold(parts, arrays):
        for part, kept in zip(parts, arrays):
            part.arrays, part.ready = kept

    def arrays_of(*parts):
        return [(part.arrays, part.ready) for part in parts]

    x_step, near_step, far_step = (place.dp + [None] * 3)[:3]

    e_three = cross(e, n_three)
    two, one_part = start_sum(*grad_two), start_sum(*grad_one)
    grad_three, s = forward_two(place, pos, act, g_mid, left_two, right_two)
    two.prepare(x_step)
    one_part.prepare(near_step)
    e_three, kept, grad_three, s, e = slot(place, (e_three, arrays_of(two, one_part), grad_three, s, e))
    hold([two, one_part], kept)

    e_two = cross(e, n_two)
    two.step(x_step)
    one_part.step(near_step)
    three = start_sum(*grad_three)
    e_one = cross(e, n_one)
    three.prepare(x_step)
    e_two, e_one, kept, s = slot(place, (e_two, e_one, arrays_of(two, one_part, three), s))
    hold([two, one_part, three], kept)
    e_got = [e[0], e_one, e_two, e_three][:share]

    s_three = cross(s, n_three)
    three.step(x_step)
    one_part.step(far_step)
    two.step(near_step)
    input_grad, lone = last_stage(place, pos, e_got, x_home, g_home, one)
    lone = Sum([lone], [home] + place.dp[::-1], (rows, size))
    lone.prepare(x_step)
    s_three, kept, input_grad, s = slot(place, (s_three, arrays_of(two, one_part, three, lone), input_grad, s))
    hold([two, one_part, three, lone], kept)

    s_two = cross(s, n_two)
    lone.step(x_step)
    two.step(far_step)
    three.step(near_step)
    one_part.step(x_step)
    lone.step(near_step)
    three.step(far_step, lone.arrays[-1])
    s_one = cross(s, n_one)
    s_got = [s[0], s_one, s_two, s_three][:share]
    mixed = add_home(place, pos, s_got, x_home)
    grad_ltwo, grad_rone, grad_rtwo = finish_together([two, one_part, three], place.dp, place.y, mixed)
    grad_lone = lone.finish()
    return mixed, input_grad, grad_lone, grad_rone, grad_ltwo, grad_rtwo


def split_blocks(x_home, g_home, factors, share, cut):
    home, size, tokens = x_home.shape
    far, near = halves(share)
    outer, inner = halves(lax.axis_size("dp"))
    ring_y, ring_core = Ring("tensor", (near, far)), Ring("tensor", (1, near))
    ring_z, ring_x = Ring("dp", (inner, outer)), Ring("dp", (1, inner))
    rows = factors[0].shape[1]
    n_tensor = lax.axis_size("tensor")
    groups = n_tensor // share
    held = home * share
    same_tokens = [[group * share + part for group in range(groups)] for part in range(share)]

    def go(values):
        pieces = values.reshape(home, groups, held, share, cut).transpose(1, 3, 2, 0, 4)
        got = cross(pieces.reshape(n_tensor, held, home, cut))
        return got.transpose(1, 0, 2, 3).reshape(held, size, cut)

    def back(values):
        pieces = values.reshape(held, n_tensor, home, cut).transpose(1, 0, 2, 3)
        got = cross(pieces).reshape(groups, share, held, home, cut)
        return got.transpose(3, 0, 2, 1, 4).reshape(home, size, tokens)

    def turn(values):
        moved = lax.all_to_all(
            values.reshape(held, groups, held, cut), "tensor", split_axis=1, concat_axis=0, tiled=True, axis_index_groups=same_tokens
        )
        return jnp.swapaxes(moved.reshape(size, held, cut), 0, 1)

    def whole(factor):
        one = ring_z.gather(ring_y.gather(factor))
        all_rows = ring_core.gather(ring_x.gather(one))
        return all_rows.transpose(3, 0, 4, 2, 1, 5, 6).reshape(held, size, size)

    def own_sum(partial):
        split = partial.reshape(ring_y.size, ring_core.size, home, ring_z.size, ring_x.size, rows, size)
        terms = ring_core.scatter([split], 1)
        return total(ring_y.scatter(ring_z.scatter(ring_x.scatter(terms, 3), 2), 0))

    first_left, first_right, second_left, second_right = factors
    g_mid = go(g_home)
    left_one = ring_x.gather(ring_z.gather(first_left)).transpose(2, 1, 0, 3, 4).reshape(home, size, size)
    right_one, left_two, right_two = whole(first_right), whole(second_left), whole(second_right)

    s_one = go(product("bjt,bjo->bot", x_home, left_one).astype(BF16))
    s_two = turn(product("bit,bip->bpt", s_one, right_one).astype(BF16))
    act = gelu_value(s_two.astype(F32)).astype(BF16)
    e_three = turn(product("bot,bio->bit", g_mid, right_two).astype(BF16))
    h_mid = turn(gelu_back(s_two.astype(F32), product("bot,bjo->bjt", e_three, left_two)).astype(BF16))
    e_one = back(product("bpt,bip->bit", h_mid, right_one).astype(BF16))
    s_three = turn(product("bjt,bjo->bot", act, left_two).astype(BF16))
    s_four = back(product("bit,bio->bot", s_three, right_two).astype(BF16))
    mixed = (x_home.astype(F32) + s_four.astype(F32)).astype(BF16)

    grad_rtwo = own_sum(product("bit,bot->bio", s_three, g_mid))
    grad_ltwo = own_sum(product("bjt,bot->bjo", act, e_three))
    grad_rone = own_sum(product("bit,bpt->bip", s_one, h_mid))
    grad_lone = product("bjt,bot->bjo", x_home, e_one).reshape(home, ring_z.size, ring_x.size, rows, size)
    grad_lone = total(ring_z.scatter(ring_x.scatter([grad_lone], 2), 1))
    input_grad = (g_home.astype(F32) + product("bot,bjo->bjt", e_one, left_one)).astype(BF16)
    return mixed, input_grad, grad_lone, grad_rone, grad_ltwo, grad_rtwo


def per_device(inputs, cotangent, first_left, first_right, second_left, second_right):
    n_tensor = lax.axis_size("tensor")
    home, _, size = first_left.shape
    tokens = inputs.shape[1]
    share = math.gcd(n_tensor, max(1, tokens // LANES))
    cut = tokens // share
    plan = whole_tokens if share == n_tensor else split_blocks
    mixed, input_grad, *weight_grads = plan(
        inputs.reshape(home, size, tokens),
        cotangent.reshape(home, size, tokens),
        (first_left, first_right, second_left, second_right),
        share,
        cut,
    )
    return (mixed.reshape(inputs.shape), input_grad.reshape(inputs.shape), *weight_grads)


def solution(mesh):
    wide, factor = P("tensor", "dp"), P("tensor", "dp", None)
    return jax.shard_map(
        per_device,
        mesh=mesh,
        in_specs=(wide, wide, factor, factor, factor, factor),
        out_specs=(wide, wide, factor, factor, factor, factor),
        check_vma=False,
    )
```

```python
import functools
import itertools
import math

import jax
import jax.numpy as jnp
from jax import lax
from jax.experimental import pallas as pl
from jax.experimental.pallas import tpu as pltpu
from jax.sharding import PartitionSpec as P

BF16 = jnp.bfloat16
F32 = jnp.float32
LANES = 128
TILE = 16
VMEM_BYTES = 60 * 1024 * 1024
BYTES_PER_US = 1_200_000


def gelu_value(values):
    return jax.nn.gelu(values, approximate=True)


def gelu_back(values, upstream):
    return jax.vjp(gelu_value, values)[1](upstream)[0]


def gelu_both(v):
    root, cubic = 0.7978845608028654, 0.044715
    square = v * v
    t = jnp.tanh(root * (v + cubic * (v * square)))
    half = 0.5 * (1.0 + t)
    slope = half + (0.5 * v) * (1.0 - t * t) * (root + (3.0 * cubic * root) * square)
    return v * half, slope


def product(form, left, right):
    return jnp.einsum(form, left, right, preferred_element_type=F32)


def dot(left, right, left_dim, right_dim):
    return lax.dot_general(left, right, (((left_dim,), (right_dim,)), ((), ())), preferred_element_type=F32)


def dots(lefts, rights, left_dim, right_dim):
    if len(lefts) == 1:
        return [dot(lefts[0], rights[0], left_dim, right_dim)]
    zero = jnp.zeros_like(rights[0])
    upper = jnp.concatenate([rights[0], zero], axis=1)
    lower = jnp.concatenate([zero, rights[1]], axis=1)
    out = dot(jnp.concatenate(lefts, axis=left_dim), jnp.concatenate([upper, lower], axis=0), left_dim, right_dim)
    half = out.shape[1] // 2
    return [out[:, :half], out[:, half:]]


def dots_nn(lefts, rights):
    return dots(lefts, rights, 1, 0)


def dots_tn(lefts, rights):
    return dots(lefts, rights, 0, 0)


def dots_nt(lefts, rights):
    return dots(lefts, rights, 1, 1)


def dot_nn(left, right):
    return dot(left, right, 1, 0)


def dot_nt(left, right):
    return dot(left, right, 1, 1)


def call(body, out, grid, in_specs, out_specs, scratch, args, us, scalars=None):
    spec = pltpu.PrefetchScalarGridSpec(
        num_scalar_prefetch=0 if scalars is None else 1,
        grid=grid,
        in_specs=in_specs,
        out_specs=out_specs,
        scratch_shapes=scratch,
    )
    return pl.pallas_call(
        body,
        out_shape=out,
        grid_spec=spec,
        compiler_params=pltpu.CompilerParams(
            dimension_semantics=("arbitrary",) * len(grid), vmem_limit_bytes=VMEM_BYTES
        ),
        cost_estimate=pl.CostEstimate(flops=0, bytes_accessed=int(us * BYTES_PER_US), transcendentals=0),
    )(*(() if scalars is None else (scalars,)), *args)


def pairs(count, body, unroll=8):
    group = 2 if count % 2 == 0 else 1
    each(count // group, lambda n: body([n * group + i for i in range(group)]), unroll)


def turn(source, out_ref, at):
    n, size, _ = source.shape
    for i in range(0, size, TILE):
        out_ref[i : i + TILE, pl.ds(pl.multiple_of(at, TILE), n), :] = jnp.swapaxes(source[:, i : i + TILE, :], 0, 1)


def shape(dims, dtype=BF16):
    return jax.ShapeDtypeStruct(dims, dtype)


def each(count, body, unroll=16):
    def step(k, carry):
        body(k)
        return carry

    lax.fori_loop(0, count, step, 0, unroll=math.gcd(count, unroll))


def during(phase, steps):
    return lambda p, j: jnp.where(p == phase, j, jnp.where(p < phase, 0, steps - 1))


def stacked(ref, k):
    return jnp.concatenate([ref[c, k] for c in range(ref.shape[0])], axis=0)


class Ring:
    def __init__(self, axis, *digits, tied=True):
        self.axis, self.digits, self.last, self.tied = axis, digits, None, tied
        self.stride, self.size = digits[0]

    def here(self):
        return lax.rem(lax.axis_index(self.axis) // self.stride, self.size)

    def send(self, value, *steps):
        pairs = []
        for src in range(lax.axis_size(self.axis)):
            dst = src
            for (stride, size), step in zip(self.digits, steps):
                own = src // stride % size
                dst += ((own + step) % size - own) * stride
            pairs.append((src, dst))
        if self.tied and self.last is not None:
            value = after(value, self.last)
        self.last = lax.ppermute(value, self.axis, pairs)
        return self.last

    def sends(self, value):
        return [self.send(value, step) for step in range(1, self.size)]

    def gather(self, value):
        if self.size == 1:
            return value[None]
        here = self.here()
        out = jnp.zeros((self.size,) + value.shape, value.dtype)
        out = lax.dynamic_update_index_in_dim(out, value, here, 0)
        for step in range(1, self.size):
            got = self.send(value, step)
            out = lax.dynamic_update_index_in_dim(out, got, lax.rem(here - step + self.size, self.size), 0)
        return out

    def scatter(self, terms, dim, before=()):
        here = self.here()
        if self.size == 1:
            return [lax.index_in_dim(t, 0, dim, keepdims=False) for t in terms]
        out = [lax.dynamic_index_in_dim(t, here, dim, keepdims=False) for t in terms]
        for step in range(1, self.size):
            there = lax.rem(here + step, self.size)
            term = total([lax.dynamic_index_in_dim(t, there, dim, keepdims=False) for t in terms]).astype(BF16)
            out.append(self.send(after(term, *before), step))
        return out


def slot(place, values):
    values = lax.optimization_barrier(values)
    place.crossed = None
    for ring in [place.y, place.core] + place.dp + list(place.links.values()):
        ring.last = None
    return values


class Sum:
    def __init__(self, arrays, rings, tail):
        self.left = rings
        dims = [ring.size if isinstance(ring, Ring) else ring for ring in rings]
        self.arrays = [a.reshape(dims + list(tail)) for a in arrays]
        self.rings = [rings] * len(arrays)
        self.ready = []

    def cut(self, ring=None, index=None):
        out = []
        for array, rings in zip(self.arrays, self.rings):
            dim = 0
            for r in rings:
                if isinstance(r, Ring) and (r is ring or r not in self.left):
                    array = lax.dynamic_index_in_dim(array, index if r is ring else r.here(), dim, keepdims=False)
                else:
                    dim += 1
            out.append(array)
        return total(out)

    def parts(self, ring):
        return [self.cut(ring, lax.rem(ring.here() + step, ring.size)).astype(BF16) for step in range(1, ring.size)]

    def prepare(self, ring):
        self.ready = self.parts(ring) if ring in self.left else []

    def step(self, ring, *before):
        if ring not in self.left:
            return
        rest = [r for r in self.left if r is not ring]
        parts = self.ready or self.parts(ring)
        self.ready = []
        got = [ring.send(after(part, *before), step + 1) for step, part in enumerate(parts)]
        self.arrays, self.rings, self.left = self.arrays + got, self.rings + [rest] * len(got), rest

    def finish(self):
        for ring in [r for r in self.left[::-1] if isinstance(r, Ring)]:
            count = len(self.arrays)
            self.step(ring)
        if not any(isinstance(r, Ring) for r in self.rings[0]):
            return self.cut()
        got, self.arrays = self.arrays[count:], self.arrays[:count]
        own, got = lax.optimization_barrier((self.cut(), got))
        return total([own] + got)


def finish_together(sums, rings, last, *before):
    for part in sums:
        for ring in rings:
            part.step(ring)
    sends = list(zip(*[part.parts(last) for part in sums]))
    got = [last.send(after(jnp.stack(send), *before), step + 1) for step, send in enumerate(sends)]
    for part in sums:
        part.left = [r for r in part.left if r is not last]
    own, got = lax.optimization_barrier(([part.cut() for part in sums], got))
    return [total([mine] + [g[n] for g in got]) for n, mine in enumerate(own)]


def total(terms):
    return functools.reduce(jnp.add, [t.astype(F32) for t in terms])


def after(value, *others):
    if not others:
        return value
    return lax.optimization_barrier((value,) + others)[0]


def turned_back(here, step, size):
    return lax.rem(here - step + size, size)


class Place:
    def __init__(self, share, n_dp):
        self.far, self.near = halves(share)
        self.y, self.core = Ring("tensor", (self.near, self.far)), Ring("tensor", (1, self.near), tied=False)
        self.dp, stride = [], 1
        while stride < n_dp:
            size = next(p for p in range(2, n_dp + 1) if n_dp // stride % p == 0)
            self.dp.append(Ring("dp", (stride, size)))
            stride *= size
        self.steps = [(y, c) for y in range(self.far) for c in range(self.near)]
        self.crossed = None
        self.links = {step: Ring("tensor", (self.near, self.far), (1, self.near)) for step in self.steps[1:]}
        self.rows = [ring.size for ring in self.dp]

    def position(self):
        return jnp.stack([ring.here() for ring in [self.y, self.core] + self.dp]).astype(jnp.int32)

    def onward(self, pos, n):
        y, c = self.steps[n]
        return lax.rem(pos[0] + y, self.far) * self.near + lax.rem(pos[1] + c, self.near)

    def source(self, pos, n):
        y, c = self.steps[n]
        return turned_back(pos[0], y, self.far) * self.near + turned_back(pos[1], c, self.near)

    def exchange(self, pieces, n):
        y, c = self.steps[n]
        piece = pieces[n]
        if y == 0:
            return self.core.send(piece, c)
        if self.crossed is not None:
            piece = after(piece, self.crossed)
        self.crossed = self.y.send(piece, y) if c == 0 else self.links[(y, c)].send(piece, y, c)
        return self.crossed


def piece_copies(pieces, whole, sems):
    flat_whole = [whole.at[c, d] for c in range(len(pieces)) for d in range(len(pieces[0]))]
    return [pltpu.make_async_copy(ref, dst, sems.at[n]) for n, (ref, dst) in enumerate(zip(flat(pieces), flat_whole))]


def block_reader(place, pos_ref, whole, group):
    lead = ()
    if group is not None:
        lead = (turned_back(pos_ref[0], group // place.near, place.far),)
    core = 0 if group is None else turned_back(pos_ref[1], lax.rem(group, place.near), place.near)
    places = []
    for d in range(math.prod(place.rows)):
        steps = [turned_back(pos_ref[2 + n], d // ring.stride % ring.size, ring.size) for n, ring in enumerate(place.dp)]
        places.append((core, *(steps or [0]), *lead))
    return lambda k: jnp.concatenate([whole[(*at, k)] for at in places], axis=0)


def whole_scratch(pieces, grouped=False):
    dims = (len(pieces), len(pieces[0])) + pieces[0][0].shape
    sems = (dims[0], dims[1], dims[-4]) if grouped else (dims[0] * dims[1],)
    return [pltpu.VMEM(dims, BF16), pltpu.SemaphoreType.DMA(sems)]


def group_of(ref, y):
    return ref.at[(slice(None),) * (len(ref.shape) - 4) + (y,)]


def group_copies(pieces, whole, sems):
    copies = []
    for c, row in enumerate(pieces):
        for d, ref in enumerate(row):
            for y in range(ref.shape[-4]):
                dst = group_of(whole.at[c, d], y)
                copies.append(pltpu.make_async_copy(group_of(ref, y), dst, sems.at[c, d, y]))
    return copies


def copies_of_group(place, pos_ref, pieces, whole, sems, group):
    y = turned_back(pos_ref[0], group // place.near, place.far)
    c = turned_back(pos_ref[1], lax.rem(group, place.near), place.near)
    copies = []
    for d, ref in enumerate(pieces[0]):
        dst = group_of(whole.at[c, d], y)
        copies.append(pltpu.make_async_copy(group_of(ref, y), dst, sems.at[c, d, y]))
    return copies


def share_group(place, pos_ref, parts, whole, sems, group, per):
    at = pl.ds(group * per, per)
    return [
        pltpu.make_async_copy(ref.at[at], whole.at[place.source(pos_ref, n), at], sems.at[n, group])
        for n, ref in enumerate(parts)
    ]


def share_copies(place, pos_ref, parts, whole, sems):
    return [pltpu.make_async_copy(ref, whole.at[place.source(pos_ref, n)], sems.at[n]) for n, ref in enumerate(parts)]


def run(copies):
    for copy in copies:
        copy.start()


def finish(copies):
    for copy in copies:
        copy.wait()


def anywhere(count):
    return [pl.BlockSpec(memory_space=pl.ANY)] * count


def flat(pieces):
    return tuple(p for row in pieces for p in row)


def unflat(place, refs):
    wide = len(refs) // place.near
    return [refs[c * wide : (c + 1) * wide] for c in range(place.near)]


def deal_kernel(pos_ref, g_ref, out_ref):
    for o in range(0, g_ref.shape[0], TILE):
        turn(g_ref.at[o : o + TILE], out_ref, o)


def deal(place, pos, g_home, cut, n):
    home, size, _ = g_home.shape
    return call(
        deal_kernel,
        shape((size, home, cut)),
        (1,),
        [pl.BlockSpec((home, size, cut), lambda i, pos: (0, 0, place.onward(pos, n)))],
        pl.BlockSpec((size, home, cut), lambda i, pos: (0, 0, 0)),
        [],
        (g_home,),
        us=3.5,
        scalars=pos,
    )


def first_kernel(place, pos_ref, x_ref, *refs):
    share = place.far * place.near
    pieces, out_refs = refs[: -share - 3], refs[-share - 3 : -3]
    stage, whole, sems = refs[-3:]
    home = x_ref.shape[0]
    cut = out_refs[0].shape[2]
    copies = piece_copies([pieces], whole, sems)
    block = block_reader(place, pos_ref, whole, None)

    @pl.when(pl.program_id(0) == 0)
    def _():
        run(copies)
        finish(copies)

    for n, out_ref in enumerate(out_refs):

        @pl.when(pl.program_id(0) == n)
        def _():
            lanes = pl.ds(pl.multiple_of(place.onward(pos_ref, n) * cut, cut), cut)

            for b in range(0, home, TILE):

                def store(ks):
                    out = dots_tn([block(b + k) for k in ks], [x_ref[b + k, :, lanes] for k in ks])
                    for k, y in zip(ks, out):
                        stage[b + k] = y.astype(BF16)

                pairs(TILE, store)
                turn(stage.at[b : b + TILE], out_ref, b)


def first_stage(place, pos, x_home, left_one, cut):
    home, size, tokens = x_home.shape
    share = tokens // cut
    return call(
        functools.partial(first_kernel, place),
        (shape((size, home, cut)),) * share,
        (share,),
        [pl.BlockSpec((home, size, tokens), lambda s, pos: (0, 0, 0))] + anywhere(len(left_one)),
        (pl.BlockSpec((size, home, cut), lambda s, pos: (0, 0, 0)),) * share,
        [pltpu.VMEM((home, size, cut), BF16)] + whole_scratch([left_one]),
        (x_home, *left_one),
        us=8,
        scalars=pos,
    )


def last_kernel(place, pos_ref, *refs):
    share = place.far * place.near
    e_refs, x_ref, g_ref = refs[:share], refs[share], refs[share + 1]
    pieces, (out_ref, grad_ref, turned, whole, sems) = refs[share + 2 : -5], refs[-5:]
    blocks, per, _ = e_refs[0].shape
    copies = piece_copies([pieces], whole, sems)
    block = block_reader(place, pos_ref, whole, None)
    first = pl.program_id(0) * per

    @pl.when(pl.program_id(0) == 0)
    def _():
        run(copies)

    for n in range(share):
        into = turned.at[place.source(pos_ref, n)]
        for o in range(0, blocks, TILE):
            turn(e_refs[n].at[o : o + TILE], into, o)

    @pl.when(pl.program_id(0) == 0)
    def _():
        finish(copies)

    def load(b):
        e_b = jnp.concatenate([turned[s, b] for s in range(share)], axis=1)
        out_ref[b] = (g_ref[b].astype(F32) + dot_nn(block(first + b), e_b)).astype(BF16)
        grad_ref[b] = dot_nt(x_ref[b], e_b).astype(BF16)

    each(per, load, 4)


def last_stage(place, pos, e_got, x_home, g_home, left_one):
    share = len(e_got)
    blocks, home, cut = e_got[0].shape
    _, size, tokens = x_home.shape
    per = math.gcd(home, 16)
    wide = pl.BlockSpec((per, size, tokens), lambda h, pos: (h, 0, 0))
    factor = pl.BlockSpec((per, size, size), lambda h, pos: (h, 0, 0))
    return call(
        functools.partial(last_kernel, place),
        (shape(g_home.shape), shape((home, size, size))),
        (home // per,),
        [pl.BlockSpec((blocks, per, cut), lambda h, pos: (0, h, 0))] * share + [wide, wide] + anywhere(len(left_one)),
        (wide, factor),
        [pltpu.VMEM((share, per, blocks, cut), BF16)] + whole_scratch([left_one]),
        (*e_got, x_home, g_home, *left_one),
        us=10,
        scalars=pos,
    )


def mixed_kernel(place, pos_ref, *refs):
    *s_refs, x_ref, out_ref = refs
    cut = s_refs[0].shape[2]
    for n, s_ref in enumerate(s_refs):
        lanes = pl.ds(pl.multiple_of(place.source(pos_ref, n) * cut, cut), cut)
        out_ref[:, :, lanes] = (x_ref[:, :, lanes].astype(F32) + s_ref[...].astype(F32)).astype(BF16)


def add_home(place, pos, s_got, x_home):
    home, blocks, cut = s_got[0].shape
    per = math.gcd(home, 8)
    wide = pl.BlockSpec((per,) + x_home.shape[1:], lambda h, pos: (h, 0, 0))
    return call(
        functools.partial(mixed_kernel, place),
        shape(x_home.shape),
        (home // per,),
        [pl.BlockSpec((per, blocks, cut), lambda h, pos: (h, 0, 0))] * len(s_got) + [wide],
        wide,
        [],
        (*s_got, x_home),
        us=6,
        scalars=pos,
    )


def back_two_kernel(place, pos_ref, *refs):
    share = place.far * place.near
    g_parts, factor = refs[:share], unflat(place, refs[share:-7])
    out_ref, turned, stage, g_all, g_sems, w_all, w_sems = refs[-7:]
    per = out_ref.shape[0]
    phase, j = pl.program_id(0), pl.program_id(1)

    @pl.when((phase == 0) & (j == 0))
    def _():
        copies = share_copies(place, pos_ref, g_parts, g_all, g_sems) + piece_copies(factor, w_all, w_sems)
        run(copies)
        finish(copies)

    @pl.when(phase == 0)
    def _():
        block = block_reader(place, pos_ref, w_all, j)

        def body(ks):
            out = dots_nn([block(k) for k in ks], [stacked(g_all, j * per + k) for k in ks])
            for k, y in zip(ks, out):
                stage[k] = y.astype(BF16)

        staged(per, body, stage, turned, j)

    @pl.when(phase == 1)
    def _():
        def body(k):
            out_ref[k] = turned[j * per + k]

        each(per, body)


def staged(per, body, stage, turned, j):
    for k in range(0, per, TILE):
        pairs(TILE, lambda ks: body([k + i for i in ks]))
        turn(stage.at[k : k + TILE], turned, j * per + k)


def middle_sizes(place, parts):
    blocks, home, cut = parts[0].shape
    return blocks, home, cut, len(parts)


def back_two(place, pos, g_mid, right_two):
    blocks, home, cut, share = middle_sizes(place, g_mid)
    at = during(1, share)
    return call(
        functools.partial(back_two_kernel, place),
        shape((blocks, blocks, cut)),
        (2, share),
        anywhere(share + len(flat(right_two))),
        pl.BlockSpec((home, blocks, cut), lambda p, j, pos: (at(p, j), 0, 0)),
        [
            pltpu.VMEM((blocks, blocks, cut), BF16),
            pltpu.VMEM((home, blocks, cut), BF16),
            pltpu.VMEM((share, blocks, home, cut), BF16),
            pltpu.SemaphoreType.DMA((share,)),
        ]
        + whole_scratch(right_two),
        (*g_mid, *flat(right_two)),
        us=10,
        scalars=pos,
    )


def either(place, pos_ref, j, keep_ref, send_ref, body):
    mine = lax.rem(j, place.near) == pos_ref[1]

    @pl.when(mine)
    def _():
        body(keep_ref)

    @pl.when(jnp.logical_not(mine))
    def _():
        body(send_ref)


def middle_kernel(place, pos_ref, *refs):
    share = place.far * place.near
    wide = (len(refs) - (2 * share + 15)) // 2
    s_parts, rest = refs[:share], refs[share:]
    one, two, rest = unflat(place, rest[:wide]), unflat(place, rest[wide : 2 * wide]), rest[2 * wide :]
    e_ref, act_ref, keep_two, send_two, keep_one, send_one, *rest = rest
    out_refs, rest = rest[:share], rest[share:]
    turned, hidden, e_one, s_all, s_sems, one_all, one_sems, two_all, two_sems = rest
    per, home = act_ref.shape[0], s_all.shape[2]
    phase, j = pl.program_id(0), pl.program_id(1)

    def second():
        return piece_copies(two, two_all, two_sems)

    @pl.when((phase == 0) & (j == 0))
    def _():
        run(group_copies(one, one_all, one_sems))
        for group in range(share):
            run(share_group(place, pos_ref, s_parts, s_all, s_sems, group, per))

    @pl.when((phase == 0) & (j == min(1, share - 1)))
    def _():
        run(second())

    @pl.when(phase == 0)
    def _():
        finish(copies_of_group(place, pos_ref, one, one_all, one_sems, j))
        finish(share_group(place, pos_ref, s_parts, s_all, s_sems, j, per))

    @pl.when(phase == 0)
    def _():
        block = block_reader(place, pos_ref, one_all, j)

        def body(ks):
            out = dots_tn([block(k) for k in ks], [stacked(s_all, j * per + k) for k in ks])
            for k, y in zip(ks, out):
                e_one[k] = y.astype(BF16)

        staged(per, body, e_one, turned, j)

    @pl.when((phase == 1) & (j == 0))
    def _():
        finish(second())

    @pl.when(phase == 1)
    def _():
        block = block_reader(place, pos_ref, two_all, j)

        def with_out(grad_ref):
            def body(ks):
                acts, slopes, es = [], [], [e_ref[k] for k in ks]
                for k in ks:
                    value, slope = gelu_both(turned[j * per + k].astype(F32))
                    acts.append(value.astype(BF16))
                    slopes.append(slope)
                    act_ref[k] = acts[-1]
                for k, slope, y in zip(ks, slopes, dots_nn([block(k) for k in ks], es)):
                    e_one[k] = (slope * y).astype(BF16)
                for k, y in zip(ks, dots_nt(acts, es)):
                    grad_ref[0, k] = y.astype(BF16)

            staged(per, body, e_one, hidden, j)

        either(place, pos_ref, j, keep_two, send_two, with_out)

    @pl.when(phase == 2)
    def _():
        block = block_reader(place, pos_ref, one_all, j)

        def with_out(grad_ref):
            def body(ks):
                hs = [hidden[j * per + k] for k in ks]
                for k, y in zip(ks, dots_nn([block(k) for k in ks], hs)):
                    e_one[k] = y.astype(BF16)
                for k, y in zip(ks, dots_nt([stacked(s_all, j * per + k) for k in ks], hs)):
                    grad_ref[0, k] = y.astype(BF16)

            pairs(per, body)

        either(place, pos_ref, j, keep_one, send_one, with_out)
        for n in range(share):
            at = pl.ds(pl.multiple_of(place.onward(pos_ref, n) * home, home), home)
            out_refs[n][...] = e_one[:, at, :]


def grad_specs(place, phase, home, size, share):
    at = during(phase, share)
    dims = shape((place.far, home, size, size))
    spec = pl.BlockSpec((1, home, size, size), lambda p, j, pos: (at(p, j) // place.near, 0, 0, 0))
    return [dims] * 2, [spec] * 2


def middle(place, pos, s_mid, e_mid, right_one, left_two):
    blocks, home, cut, share = middle_sizes(place, s_mid)
    at = [during(phase, share) for phase in range(3)]
    block = pl.BlockSpec((home, blocks, cut), lambda p, j, pos: (at[1](p, j), 0, 0))
    two, two_specs = grad_specs(place, 1, home, blocks, share)
    one, one_specs = grad_specs(place, 2, home, blocks, share)
    piece = pl.BlockSpec((home, home, cut), lambda p, j, pos: (at[2](p, j), 0, 0))
    out = call(
        functools.partial(middle_kernel, place),
        (shape((blocks, blocks, cut)), *two, *one) + (shape((blocks, home, cut)),) * share,
        (3, share),
        anywhere(share + 2 * len(flat(right_one))) + [block],
        (block, *two_specs, *one_specs) + (piece,) * share,
        [pltpu.VMEM((blocks, blocks, cut), BF16)] * 2
        + [
            pltpu.VMEM((home, blocks, cut), BF16),
            pltpu.VMEM((share, blocks, home, cut), BF16),
            pltpu.SemaphoreType.DMA((share, share)),
        ]
        + whole_scratch(right_one, True)
        + whole_scratch(left_two),
        (*s_mid, *flat(right_one), *flat(left_two), e_mid),
        us=26,
        scalars=pos,
    )
    return out[0], out[1:3], out[3:5], list(out[5:])


def forward_two_kernel(place, pos_ref, *refs):
    share = place.far * place.near
    wide = (len(refs) - (2 * share + 13)) // 2
    g_parts, rest = refs[:share], refs[share:]
    left, right, rest = unflat(place, rest[:wide]), unflat(place, rest[wide : 2 * wide]), rest[2 * wide :]
    act_ref, keep_ref, send_ref, *rest = rest
    out_refs, rest = rest[:share], rest[share:]
    turned, fourth, stage, g_all, g_sems, out_sems, left_all, left_sems, right_all, right_sems = rest
    per = act_ref.shape[0]
    phase, j = pl.program_id(0), pl.program_id(1)

    def second():
        return piece_copies(right, right_all, right_sems) + share_copies(place, pos_ref, g_parts, g_all, g_sems)

    @pl.when((phase == 0) & (j == 0))
    def _():
        run(group_copies(left, left_all, left_sems))

    @pl.when((phase == 0) & (j == min(1, share - 1)))
    def _():
        run(second())

    @pl.when(phase == 0)
    def _():
        finish(copies_of_group(place, pos_ref, left, left_all, left_sems, j))

    @pl.when(phase == 0)
    def _():
        block = block_reader(place, pos_ref, left_all, j)

        def body(ks):
            for k, y in zip(ks, dots_tn([block(k) for k in ks], [act_ref[k] for k in ks])):
                stage[k] = y.astype(BF16)

        staged(per, body, stage, turned, j)

    @pl.when((phase == 1) & (j == 0))
    def _():
        finish(second())

    @pl.when(phase == 1)
    def _():
        block = block_reader(place, pos_ref, right_all, j)

        def with_out(grad_ref):
            def body(ks):
                thirds = [turned[j * per + k] for k in ks]
                for k, y in zip(ks, dots_tn([block(k) for k in ks], thirds)):
                    stage[k] = y.astype(BF16)
                for k, y in zip(ks, dots_nt(thirds, [stacked(g_all, j * per + k) for k in ks])):
                    grad_ref[0, k] = y.astype(BF16)

            staged(per, body, stage, fourth, j)

        either(place, pos_ref, j, keep_ref, send_ref, with_out)

    @pl.when((phase == 1) & (j == share - 1))
    def _():
        copies = []
        for n in range(share):
            mine = fourth.at[pl.ds(place.onward(pos_ref, n) * per, per)]
            copies.append(pltpu.make_async_copy(mine, out_refs[n], out_sems.at[n]))
        run(copies)
        finish(copies)


def forward_two(place, pos, act, g_mid, left_two, right_two):
    blocks, home, cut, share = middle_sizes(place, g_mid)
    at = during(0, share)
    grad, grad_spec = grad_specs(place, 1, home, blocks, share)
    out = call(
        functools.partial(forward_two_kernel, place),
        (*grad,) + (shape((home, blocks, cut)),) * share,
        (2, share),
        anywhere(share + 2 * len(flat(left_two))) + [pl.BlockSpec((home, blocks, cut), lambda p, j, pos: (at(p, j), 0, 0))],
        (*grad_spec, *anywhere(share)),
        [pltpu.VMEM((blocks, blocks, cut), BF16)] * 2
        + [
            pltpu.VMEM((home, blocks, cut), BF16),
            pltpu.VMEM((share, blocks, home, cut), BF16),
            pltpu.SemaphoreType.DMA((share,)),
            pltpu.SemaphoreType.DMA((share,)),
        ]
        + whole_scratch(left_two, True)
        + whole_scratch(right_two),
        (*g_mid, *flat(left_two), *flat(right_two), act),
        us=20,
        scalars=pos,
    )
    return out[:2], list(out[2:])


def halves(size):
    low = 2 if size % 2 == 0 else 1
    return size // low, low


def cross(pieces):
    return lax.all_to_all(pieces, "tensor", split_axis=0, concat_axis=0, tiled=True)


def whole_tokens(x_home, g_home, factors, share, cut):
    home, size, tokens = x_home.shape
    first_left = factors[0]
    rows = first_left.shape[1]
    place = Place(share, lax.axis_size("dp"))
    pos = place.position()

    def gather(start, n):
        if n >= len(place.dp):
            return start
        got = [start] + place.dp[n].sends(start)
        return got if n == 0 else jnp.stack(got)

    def gather_far(start):
        for n in reversed(range(2, len(place.dp))):
            start = gather(start, n)
        return start

    def last_dp(start):
        return gather(start, 0) if place.dp else [start]

    def cores(piece):
        return [piece] + place.core.sends(piece)

    def by_core(own):
        return [[p[c] for p in own] for c in range(place.near)]

    def cross(pieces, n):
        return place.exchange(pieces, n) if n < share else None

    def from_y(start):
        return jnp.stack([start] + place.y.sends(start))

    n_one, n_two, n_three = (place.steps.index(step) if step in place.steps else share for step in [(0, 1), (1, 0), (1, 1)])
    one = gather_far(first_left)
    rest = from_y(jnp.stack([factors[3], factors[1], factors[2]]))
    g = {n: deal(place, pos, g_home, cut, n) for n in reversed(range(share))}
    got_three = cross(g, n_three)
    w_two = gather_far(after(rest[:, 0], g[share - 1]))
    one = last_dp(gather(one, 1))
    w_one = gather_far(rest[:, 1])
    w_two = gather(w_two, 1)
    got_three, one, w_two, w_one, rest, g = slot(place, (got_three, one, w_two, w_one, rest, g))

    got_two = cross(g, n_two)
    right_two = last_dp(w_two)
    w_one = gather(w_one, 1)
    w_left = gather_far(rest[:, 2])
    s = first_stage(place, pos, x_home, one, cut)
    got_two, right_two, w_one, w_left, one, s, pos = slot(place, (got_two, right_two, w_one, w_left, one, list(s), pos))

    s_three = cross(s, n_three)
    right_one = last_dp(w_one)
    w_left = gather(w_left, 1)
    right_two = by_core([cores(p) for p in right_two])
    s_one = cross(s, n_one)
    got_one = cross(g, n_one)
    s_three, s_one, right_one, w_left, right_two, g, got_one = slot(
        place, (s_three, s_one, right_one, w_left, right_two, g, got_one)
    )
    g_mid = [g[0], got_one, got_two, got_three][:share]

    s_two = cross(s, n_two)
    left_two = last_dp(w_left)
    left_core = cores(left_two[0])
    right_one = by_core([cores(p) for p in right_one])
    e_mid = back_two(place, pos, g_mid, right_two)
    s_two, left_two, left_core, right_one, e_mid = slot(place, (s_two, left_two, left_core, right_one, e_mid))
    s_mid = [s[0], s_one, s_two, s_three][:share]
    left_two = by_core([left_core] + [cores(p) for p in left_two[1:]])

    act, grad_two, grad_one, e = middle(place, pos, s_mid, e_mid, right_one, left_two)

    def start_sum(keep, send):
        arrays = [keep, place.core.send(send, 1)] if place.near > 1 else [keep]
        return Sum(arrays, [place.y, home] + place.dp[::-1], (rows, size))

    def hold(parts, arrays):
        for part, kept in zip(parts, arrays):
            part.arrays, part.ready = kept

    def arrays_of(*parts):
        return [(part.arrays, part.ready) for part in parts]

    x_step, near_step, far_step = (place.dp + [None] * 3)[:3]

    e_three = cross(e, n_three)
    two, one_part = start_sum(*grad_two), start_sum(*grad_one)
    grad_three, s = forward_two(place, pos, act, g_mid, left_two, right_two)
    two.prepare(x_step)
    one_part.prepare(near_step)
    e_three, kept, grad_three, s, e = slot(place, (e_three, arrays_of(two, one_part), grad_three, s, e))
    hold([two, one_part], kept)

    e_two = cross(e, n_two)
    two.step(x_step)
    one_part.step(near_step)
    three = start_sum(*grad_three)
    e_one = cross(e, n_one)
    three.prepare(x_step)
    e_two, e_one, kept, s = slot(place, (e_two, e_one, arrays_of(two, one_part, three), s))
    hold([two, one_part, three], kept)
    e_got = [e[0], e_one, e_two, e_three][:share]

    s_three = cross(s, n_three)
    three.step(x_step)
    one_part.step(far_step)
    two.step(near_step)
    input_grad, lone = last_stage(place, pos, e_got, x_home, g_home, one)
    lone = Sum([lone], [home] + place.dp[::-1], (rows, size))
    lone.prepare(x_step)
    s_three, kept, input_grad, s = slot(place, (s_three, arrays_of(two, one_part, three, lone), input_grad, s))
    hold([two, one_part, three, lone], kept)

    s_two = cross(s, n_two)
    lone.step(x_step)
    two.step(far_step)
    three.step(near_step)
    one_part.step(x_step)
    lone.step(near_step)
    three.step(far_step, lone.arrays[-1])
    s_one = cross(s, n_one)
    s_got = [s[0], s_one, s_two, s_three][:share]
    mixed = add_home(place, pos, s_got, x_home)
    grad_ltwo, grad_rone, grad_rtwo = finish_together([two, one_part, three], place.dp, place.y, mixed)
    grad_lone = lone.finish()
    return mixed, input_grad, grad_lone, grad_rone, grad_ltwo, grad_rtwo


def split_blocks(x_home, g_home, factors, share, cut):
    home, size, tokens = x_home.shape
    far, near = halves(share)
    outer, inner = halves(lax.axis_size("dp"))
    ring_y, ring_core = Ring("tensor", (near, far)), Ring("tensor", (1, near))
    ring_z, ring_x = Ring("dp", (inner, outer)), Ring("dp", (1, inner))
    rows = factors[0].shape[1]
    n_tensor = lax.axis_size("tensor")
    groups = n_tensor // share
    held = home * share
    same_tokens = [[group * share + part for group in range(groups)] for part in range(share)]

    def go(values):
        pieces = values.reshape(home, groups, held, share, cut).transpose(1, 3, 2, 0, 4)
        got = cross(pieces.reshape(n_tensor, held, home, cut))
        return got.transpose(1, 0, 2, 3).reshape(held, size, cut)

    def back(values):
        pieces = values.reshape(held, n_tensor, home, cut).transpose(1, 0, 2, 3)
        got = cross(pieces).reshape(groups, share, held, home, cut)
        return got.transpose(3, 0, 2, 1, 4).reshape(home, size, tokens)

    def turn(values):
        moved = lax.all_to_all(
            values.reshape(held, groups, held, cut), "tensor", split_axis=1, concat_axis=0, tiled=True, axis_index_groups=same_tokens
        )
        return jnp.swapaxes(moved.reshape(size, held, cut), 0, 1)

    def whole(factor):
        one = ring_z.gather(ring_y.gather(factor))
        all_rows = ring_core.gather(ring_x.gather(one))
        return all_rows.transpose(3, 0, 4, 2, 1, 5, 6).reshape(held, size, size)

    def own_sum(partial):
        split = partial.reshape(ring_y.size, ring_core.size, home, ring_z.size, ring_x.size, rows, size)
        terms = ring_core.scatter([split], 1)
        return total(ring_y.scatter(ring_z.scatter(ring_x.scatter(terms, 3), 2), 0))

    first_left, first_right, second_left, second_right = factors
    g_mid = go(g_home)
    left_one = ring_x.gather(ring_z.gather(first_left)).transpose(2, 1, 0, 3, 4).reshape(home, size, size)
    right_one, left_two, right_two = whole(first_right), whole(second_left), whole(second_right)

    s_one = go(product("bjt,bjo->bot", x_home, left_one).astype(BF16))
    s_two = turn(product("bit,bip->bpt", s_one, right_one).astype(BF16))
    act = gelu_value(s_two.astype(F32)).astype(BF16)
    e_three = turn(product("bot,bio->bit", g_mid, right_two).astype(BF16))
    h_mid = turn(gelu_back(s_two.astype(F32), product("bot,bjo->bjt", e_three, left_two)).astype(BF16))
    e_one = back(product("bpt,bip->bit", h_mid, right_one).astype(BF16))
    s_three = turn(product("bjt,bjo->bot", act, left_two).astype(BF16))
    s_four = back(product("bit,bio->bot", s_three, right_two).astype(BF16))
    mixed = (x_home.astype(F32) + s_four.astype(F32)).astype(BF16)

    grad_rtwo = own_sum(product("bit,bot->bio", s_three, g_mid))
    grad_ltwo = own_sum(product("bjt,bot->bjo", act, e_three))
    grad_rone = own_sum(product("bit,bpt->bip", s_one, h_mid))
    grad_lone = product("bjt,bot->bjo", x_home, e_one).reshape(home, ring_z.size, ring_x.size, rows, size)
    grad_lone = total(ring_z.scatter(ring_x.scatter([grad_lone], 2), 1))
    input_grad = (g_home.astype(F32) + product("bot,bjo->bjt", e_one, left_one)).astype(BF16)
    return mixed, input_grad, grad_lone, grad_rone, grad_ltwo, grad_rtwo


def per_device(inputs, cotangent, first_left, first_right, second_left, second_right):
    n_tensor = lax.axis_size("tensor")
    home, _, size = first_left.shape
    tokens = inputs.shape[1]
    share = math.gcd(n_tensor, max(1, tokens // LANES))
    cut = tokens // share
    plan = whole_tokens if share == n_tensor else split_blocks
    mixed, input_grad, *weight_grads = plan(
        inputs.reshape(home, size, tokens),
        cotangent.reshape(home, size, tokens),
        (first_left, first_right, second_left, second_right),
        share,
        cut,
    )
    return (mixed.reshape(inputs.shape), input_grad.reshape(inputs.shape), *weight_grads)


def solution(mesh):
    wide, factor = P("tensor", "dp"), P("tensor", "dp", None)
    return jax.shard_map(
        per_device,
        mesh=mesh,
        in_specs=(wide, wide, factor, factor, factor, factor),
        out_specs=(wide, wide, factor, factor, factor, factor),
        check_vma=False,
    )
```
